128 devices in a mesh: seq: 16 (over x_hi, z, core), fsdp: 8 (over x_lo, y).
Axes of the slice: x: 4 (x_hi: 2, x_lo: 2; x = x_hi * 2 + x_lo), y: 4, z: 4, core: 2. Of those that a mesh axis runs over, the one named last changes fastest.
Arguments:
- tokens: bfloat16 [8, 2048, 1024], P('fsdp', 'seq'), may hold values from -6 to 6
- out_grad: bfloat16 [8, 2048, 1024], P('fsdp', 'seq'), may hold values from -6 to 6
- w_query: bfloat16 [1024, 2048], P('fsdp'), may hold values from -0.1875 to 0.1875
- w_key: bfloat16 [1024, 1024], P('fsdp'), may hold values from -0.1875 to 0.1875
- w_value: bfloat16 [1024, 1024], P('fsdp'), may hold values from -0.1875 to 0.1875
- w_out: bfloat16 [2048, 1024], P('fsdp'), may hold values from -0.125 to 0.125
- w_gate: bfloat16 [1024, 3072], P('fsdp'), may hold values from -0.1875 to 0.1875
- w_up: bfloat16 [1024, 3072], P('fsdp'), may hold values from -0.1875 to 0.1875
- w_down: bfloat16 [3072, 1024], P('fsdp'), may hold values from -0.109375 to 0.109375
- gain_query: float32 [2048], replicated, may hold values from 0.25 to 1.75
- gain_key: float32 [1024], replicated, may hold values from 0.25 to 1.75
- gain_attn: float32 [1024], replicated, may hold values from 0.25 to 1.75
- gain_mlp: float32 [1024], replicated, may hold values from 0.25 to 1.75
Outputs:
- output: bfloat16 [8, 2048, 1024], P('fsdp', 'seq')
- input_grad: bfloat16 [8, 2048, 1024], P('fsdp', 'seq')
- grad_query: float32 [1024, 2048], P(('seq', 'fsdp'))
- grad_key: float32 [1024, 1024], P(('seq', 'fsdp'))
- grad_value: float32 [1024, 1024], P(('seq', 'fsdp'))
- grad_out: float32 [2048, 1024], P(('seq', 'fsdp'))
- grad_gate: float32 [1024, 3072], P(('seq', 'fsdp'))
- grad_up: float32 [1024, 3072], P(('seq', 'fsdp'))
- grad_down: float32 [3072, 1024], P(('seq', 'fsdp'))
- grad_gain_query: float32 [2048], P(('seq', 'fsdp'))
- grad_gain_key: float32 [1024], P(('seq', 'fsdp'))
- grad_gain_attn: float32 [1024], P(('seq', 'fsdp'))
- grad_gain_mlp: float32 [1024], P(('seq', 'fsdp'))
The draws below stay inside these ranges and needn't reach their ends.
All inputs are finite; a program needn't handle non-finite values.
Results may differ from the reference program's by a relative error of at most 0.039.
Values may be sent and summed in bfloat16 or wider, within the bound.
No kernel may reach another device: no remote copies, remote signals or barrier semaphores. Data moves between devices by JAX's collectives and lax.ppermute only.
A program may use at most 192 MiB of HBM per device.

```python
import jax
import jax.numpy as jnp
from jax import lax

D = 1024
HQ = 16
KV = 8
DH = 128
FF = 3072
QW = 2048
KW = 1024
SEQ_LEN = 2048
SEQS = 8


def block_scale(rng, extent, split, smallest, top_value):
    level, own = 1.0, jax.random.fold_in(rng, 6)
    for axis_at, parts in split:
        steps = jnp.exp(jax.random.uniform(jax.random.fold_in(own, axis_at), (parts,), jnp.float32, smallest / len(split), top_value / len(split)))
        level = level * jnp.repeat(steps, extent[axis_at] // parts).reshape([-1 if axis == axis_at else 1 for axis in range(len(extent))])
    return level


def scatter_about(stream_key, shape, deviation, bound, cuts=(), kind=jnp.bfloat16):
    loudness = block_scale(stream_key, shape, cuts, -0.22, 0.18) if cuts else 1.0
    entries = jax.random.normal(stream_key, shape, jnp.float32) * deviation * loudness
    return jnp.minimum(jnp.maximum(entries, -bound), bound).astype(kind)


def setup_inputs(seed: int = 0) -> dict:
    seeds = jax.random.split(jax.random.key(seed), 14)
    return {
        "tokens": scatter_about(seeds[0], (SEQS, SEQ_LEN, D), 1.0, 6.0, ((0, 8), (1, 16))),
        "out_grad": scatter_about(seeds[1], (SEQS, SEQ_LEN, D), 1.0, 6.0, ((0, 8), (1, 16))),
        "w_query": scatter_about(seeds[2], (D, QW), D ** -0.5, 0.1875, ((0, 8),)),
        "w_key": scatter_about(seeds[3], (D, KW), D ** -0.5, 0.1875, ((0, 8),)),
        "w_value": scatter_about(seeds[4], (D, KW), D ** -0.5, 0.1875, ((0, 8),)),
        "w_out": scatter_about(seeds[5], (QW, D), QW ** -0.5, 0.125, ((0, 8),)),
        "w_gate": scatter_about(seeds[6], (D, FF), D ** -0.5, 0.1875, ((0, 8),)),
        "w_up": scatter_about(seeds[7], (D, FF), D ** -0.5, 0.1875, ((0, 8),)),
        "w_down": scatter_about(seeds[8], (FF, D), FF ** -0.5, 0.109375, ((0, 8),)),
        "gain_query": jnp.clip(1.0 + 0.15 * jax.random.normal(seeds[9], (QW,), jnp.float32), 0.25, 1.75),
        "gain_key": jnp.clip(1.0 + 0.15 * jax.random.normal(seeds[10], (KW,), jnp.float32), 0.25, 1.75),
        "gain_attn": jnp.clip(1.0 + 0.15 * jax.random.normal(seeds[11], (D,), jnp.float32), 0.25, 1.75),
        "gain_mlp": jnp.clip(1.0 + 0.15 * jax.random.normal(seeds[12], (D,), jnp.float32), 0.25, 1.75),
    }


EPS = 1e-06
THETA = 1000000.0
MASKED = -1e+30

@jax.custom_vjp
def low(v):
    return lax.optimization_barrier(v.astype(jnp.bfloat16)).astype(jnp.float32)

@jax.custom_vjp
def low_back(v):
    return v

def low_keep(v):
    return (low(v), None)

def low_pass(kept, grad):
    return (grad,)

def back_keep(v):
    return (v, None)

def back_low(kept, grad):
    return (low(grad),)
low.defvjp(low_keep, low_pass)
low_back.defvjp(back_keep, back_low)

def matmul(left, right):
    return jnp.dot(left, right, precision=lax.Precision.HIGHEST)

def normalize(values, gain):
    return values * lax.rsqrt(lax.optimization_barrier(jnp.mean(values * values, axis=-1, keepdims=True)) + EPS) * gain

def rotary_tables(first, length):
    half = DH // 2
    places = (first + jnp.arange(length, dtype=jnp.int32)).astype(jnp.float32)
    inverse = THETA ** (-(jnp.arange(half, dtype=jnp.float32) * (2.0 / DH)))
    angles = places[:, None] * inverse[None, :]
    cosine = jnp.cos(angles)
    sine = jnp.sin(angles)
    return (jnp.concatenate([cosine, cosine], axis=-1)[:, None, :], jnp.concatenate([sine, sine], axis=-1)[:, None, :])

def rotate(values, cosine, sine):
    half = values.shape[-1] // 2
    turned = jnp.concatenate([-values[..., half:], values[..., :half]], axis=-1)
    return values * cosine + turned * sine

def attention(queries, keys, values_in):
    length = queries.shape[0]
    stride = min(512, length)
    pieces = length // stride
    factor = DH ** (-0.5)
    key_places = jnp.arange(length, dtype=jnp.int32)

    def one_piece(item):
        query_piece, offset = item
        scores = low_back(jnp.einsum('qhd,khd->hqk', query_piece, keys, precision=lax.Precision.HIGHEST) * factor)
        allowed = (offset + jnp.arange(stride, dtype=jnp.int32))[:, None] >= key_places[None, :]
        scores = jnp.where(allowed[None], scores, MASKED)
        highest = lax.optimization_barrier(jnp.max(scores, axis=-1, keepdims=True))
        weights = jnp.exp(scores - highest)
        chances = weights / lax.optimization_barrier(jnp.sum(weights, axis=-1, keepdims=True))
        return jnp.einsum('hqk,khd->qhd', low(chances), values_in, precision=lax.Precision.HIGHEST)
    query_pieces = queries.reshape(pieces, stride, HQ, DH)
    offsets = jnp.arange(pieces, dtype=jnp.int32) * stride
    return lax.map(jax.checkpoint(one_piece), (query_pieces, offsets)).reshape(length, HQ, DH)

def layer(inputs, query_w, key_w, value_w, out_w, gate_w, up_w, down_w, gain_query, gain_key, gain_attn, gain_mlp):
    length = inputs.shape[0]
    cosine, sine = rotary_tables(0, length)
    repeats = HQ // KV
    queries = normalize(low_back(matmul(inputs, query_w)), gain_query).reshape(length, HQ, DH)
    keys = normalize(low_back(matmul(inputs, key_w)), gain_key).reshape(length, KV, DH)
    values_in = low_back(matmul(inputs, value_w)).reshape(length, KV, DH)
    queries = low(low_back(rotate(queries, cosine, sine)))
    keys = low(low_back(jnp.repeat(rotate(keys, cosine, sine), repeats, axis=1)))
    values_in = low(low_back(jnp.repeat(values_in, repeats, axis=1)))
    mixed = low(low_back(attention(queries, keys, values_in))).reshape(length, QW)
    attended = low_back(matmul(mixed, out_w))
    hidden_state = inputs + normalize(attended, gain_attn)
    mlp_input = low(hidden_state)
    gate_raw = low_back(matmul(mlp_input, gate_w))
    up_raw = low_back(matmul(mlp_input, up_w))
    expanded = low(jax.nn.silu(gate_raw) * up_raw)
    projected = low_back(matmul(expanded, down_w))
    return hidden_state + normalize(projected, gain_mlp)

def reference(tokens, out_grad, w_query, w_key, w_value, w_out, w_gate, w_up, w_down, gain_query, gain_key, gain_attn, gain_mlp):
    weights = tuple((matrix.astype(jnp.float32) for matrix in (w_query, w_key, w_value, w_out, w_gate, w_up, w_down, gain_query, gain_key, gain_attn, gain_mlp)))

    def one_sequence(totals, pair):
        inputs, cotangent = pair
        result, pull = jax.vjp(layer, inputs, *weights)
        grads = pull(cotangent)
        summed = tuple((total + grad for total, grad in zip(totals, grads[1:])))
        return (summed, (result, grads[0]))
    zeros = tuple((jnp.zeros(matrix.shape, jnp.float32) for matrix in weights))
    totals, (outputs, input_grads) = lax.scan(one_sequence, zeros, (tokens.astype(jnp.float32), out_grad.astype(jnp.float32)))
    return (outputs.astype(jnp.bfloat16), input_grads.astype(jnp.bfloat16), totals[0], totals[1], totals[2], totals[3], totals[4], totals[5], totals[6], totals[7], totals[8], totals[9], totals[10])
```

```python
import functools
import math

import jax
import jax.numpy as jnp
from jax import lax
from jax.experimental import pallas as pl
from jax.experimental.pallas import tpu as pltpu
from jax.sharding import PartitionSpec as P

BF16 = jnp.bfloat16
F32 = jnp.float32
DH = 128
EPS = 1e-06
THETA = 1000000.0
MASKED = -1e30
LOG2E = math.log2(math.e)
QUERY_SCALE = DH ** (-0.5) * LOG2E
VMEM = pl.BlockSpec(memory_space=pltpu.VMEM)
SMEM = pl.BlockSpec(memory_space=pltpu.SMEM)
NT = (((1,), (1,)), ((), ()))

SEQ_PLACES = [(xh, z, c) for xh in range(2) for z in range(4) for c in range(2)]


def seq_index(xh, z, c):
    return xh * 8 + (z % 4) * 2 + c


CORE_SWAP = [(i, i ^ 1) for i in range(16)]
LOW_TO_HIGH = [(i, i + 8) for i in range(8)]
HIGH_TO_LOW = [(i + 8, i) for i in range(8)]
X_SWAP = [(i, i ^ 8) for i in range(16)]


def from_z(k):
    return [(seq_index(xh, z + k, c), seq_index(xh, z, c)) for xh, z, c in SEQ_PLACES]


def to_z(k):
    return [(seq_index(xh, z, c), seq_index(xh, z + k, c)) for xh, z, c in SEQ_PLACES]


def gather_group(block):
    mine = jnp.concatenate(
        [block] + [lax.ppermute(block, "seq", from_z(k)) for k in (1, 2, 3)], axis=0
    )
    return mine, lax.ppermute(mine, "seq", CORE_SWAP)


def scatter_group(mine, part):
    total = mine + lax.ppermute(part, "seq", CORE_SWAP).astype(F32)
    rows = total.shape[0] // 4
    out = total[:rows]
    for k in (2, 1, 3):
        piece = total[k * rows : (k + 1) * rows].astype(BF16)
        out = out + lax.ppermute(piece, "seq", to_z(k)).astype(F32)
    return out


def sum_group(rows):
    groups = rows.shape[0] // 8
    other = lax.ppermute(rows, "seq", CORE_SWAP).reshape(groups, 2, 4, 128)
    pair = rows.reshape(groups, 2, 4, 128) + jnp.concatenate([other[:, 1:], other[:, :1]], axis=1)
    total = pair
    for k in (2, 1, 3):
        got = lax.ppermute(pair, "seq", from_z(k))
        total = total + jnp.concatenate([got[:, :, 4 - k :], got[:, :, : 4 - k]], axis=2)
    return total.reshape(rows.shape)


def column(row):
    return jnp.transpose(jnp.broadcast_to(row, (128, 128)))


def row_sums(values):
    return jnp.sum(jnp.transpose(values), axis=0, keepdims=True)


def kernel_call(body, outs, ins, scratch=(), flops=0, nbytes=0):
    return pl.pallas_call(
        body,
        out_shape=outs,
        in_specs=ins,
        out_specs=jax.tree.map(lambda _: VMEM, outs),
        scratch_shapes=scratch,
        compiler_params=pltpu.CompilerParams(vmem_limit_bytes=48 * 1024 * 1024),
        cost_estimate=pl.CostEstimate(flops=flops, bytes_accessed=nbytes, transcendentals=0),
    )


def shaped(shape, dtype):
    return jax.ShapeDtypeStruct(shape, dtype)


def project_body(place, mine, part, *refs):
    blocks, (gain_q, gain_k, cos, sin) = refs[:8], refs[8:12]
    weight, q_raw, k_raw, q_rot, k_rot, values, squares = refs[12:]
    for j in range(8):
        at = pl.multiple_of((place[3] ^ j) * 128, 128)
        weight[pl.ds(at, 128), :] = blocks[j][...]
    for half, source in enumerate((mine, part)):

        def step(t, carry):
            at = pl.multiple_of(t * 128, 128)
            block = half * 4 + t
            rows = pl.ds(pl.multiple_of(block * 128, 128), 128)
            made = jnp.dot(source[pl.ds(at, 128), :], weight[...], preferred_element_type=F32)
            q, k = made[:, :256], made[:, 256:384]
            values[rows, :] = made[:, 384:].astype(BF16)
            q_raw[rows, :] = q
            k_raw[rows, :] = k
            squares[pl.ds(block, 1), :] = row_sums(
                q[:, :128] * q[:, :128] + q[:, 128:] * q[:, 128:]
            )
            squares[pl.ds(block + 8, 1), :] = row_sums(k * k)
            cosine, sine = cos[rows, :], sin[rows, :]
            for head in range(2):
                lanes = slice(head * 128, head * 128 + 128)
                turn = q[:, lanes] * gain_q[:, lanes]
                q_rot[rows, lanes] = (turn * cosine + pltpu.roll(turn, 64, 1) * sine).astype(BF16)
            turn = k * gain_k[...]
            k_rot[rows, :] = (turn * cosine + pltpu.roll(turn, 64, 1) * sine).astype(BF16)
            return carry

        lax.fori_loop(0, 4, step, 0)


def spot(place, block):
    z = lax.rem(place[1] + block % 4, 4)
    c = place[2] if block < 4 else 1 - place[2]
    return z, c


def attend_body(
    place, q_rot, k_rot, values, k_low, v_low, r_q, r_k, r_low,
    out_raw, out_low, q_tiles, keys, vals, logs, vals_t,
):
    for b in range(8):
        rows = slice(b * 128, b * 128 + 128)
        z, c = spot(place, b)
        r = column(r_q[b : b + 1, :]) * QUERY_SCALE
        inner = pl.ds(pl.multiple_of(c * 128, 128), 128)
        for head in range(2):
            q = q_rot[rows, head * 128 : head * 128 + 128].astype(F32)
            q_tiles[z * 2 + head, inner, :] = (q * r).astype(BF16)
        at = pl.ds(pl.multiple_of(1024 + z * 256 + c * 128, 128), 128)
        keys[at, :] = (k_rot[rows, :].astype(F32) * column(r_k[b : b + 1, :])).astype(BF16)
        vals[at, :] = values[rows, :]
        keys[rows, :] = (k_low[rows, :].astype(F32) * column(r_low[b : b + 1, :])).astype(BF16)
        vals[rows, :] = v_low[rows, :]
    for t in range(8):
        tile = vals[t * 256 : t * 256 + 256, :].astype(F32)
        vals_t[t] = jnp.transpose(tile).astype(BF16)
    allowed = lax.broadcasted_iota(jnp.int32, (256, 256), 0) <= lax.broadcasted_iota(
        jnp.int32, (256, 256), 1
    )

    def queries(i, carry):
        q = [q_tiles[i * 2 + head] for head in range(2)]

        def scores(t, head):
            k = keys[pl.ds(pl.multiple_of(t * 256, 256), 256), :]
            return lax.dot_general(k, q[head], NT, preferred_element_type=F32)

        state = []
        for head in range(2):
            s = jnp.where(allowed, scores(4 + i, head), MASKED)
            top = jnp.max(s, axis=0, keepdims=True)
            p = jnp.exp2(s - top)
            acc = jnp.dot(vals_t[4 + i], p.astype(BF16), preferred_element_type=F32)
            state += [top, jnp.sum(p, axis=0, keepdims=True), acc]

        def step(t, state):
            new = []
            for head in range(2):
                top, total, acc = state[3 * head : 3 * head + 3]
                s = scores(t, head)
                high = jnp.maximum(top, jnp.max(s, axis=0, keepdims=True))
                p = jnp.exp2(s - high)
                fade = jnp.exp2(top - high)
                acc = acc * fade + jnp.dot(vals_t[t], p.astype(BF16), preferred_element_type=F32)
                new += [high, total * fade + jnp.sum(p, axis=0, keepdims=True), acc]
            return tuple(new)

        state = lax.fori_loop(4 - 4 * place[0], 4 + i, step, tuple(state))
        for head in range(2):
            top, total, acc = state[3 * head : 3 * head + 3]
            out = jnp.transpose(acc / total)
            logs[pl.ds(i * 2 + head, 1), :] = top + jnp.log2(total)
            for c in range(2):
                block = lax.rem(i - place[1] + 4, 4) + 4 * jnp.abs(c - place[2])
                at = pl.ds(pl.multiple_of(block * 128, 128), 128)
                lanes = slice(head * 128, head * 128 + 128)
                out_raw[at, lanes] = out[c * 128 : c * 128 + 128, :]
                out_low[at, lanes] = out[c * 128 : c * 128 + 128, :].astype(BF16)
        return carry

    lax.fori_loop(0, 4, queries, 0)


def attend_back_body(
    place, q_tiles, keys, vals, logs, out_raw, d_out,
    dq, dk, dv, d_low, dots, keys_t, d_tiles, deltas, dk_acc, dv_acc,
):
    for t in range(8):
        tile = keys[t * 256 : t * 256 + 256, :].astype(F32)
        keys_t[t] = jnp.transpose(tile).astype(BF16)
    for b in range(8):
        rows = slice(b * 128, b * 128 + 128)
        z, c = spot(place, b)
        inner = pl.ds(pl.multiple_of(c * 128, 128), 128)
        for head in range(2):
            lanes = slice(head * 128, head * 128 + 128)
            grad = d_out[rows, lanes]
            d_tiles[z * 2 + head, inner, :] = grad
            deltas[z * 2 + head, pl.ds(c, 1), :] = row_sums(grad.astype(F32) * out_raw[rows, lanes])
    dk_acc[...] = jnp.zeros_like(dk_acc)
    dv_acc[...] = jnp.zeros_like(dv_acc)
    allowed = lax.broadcasted_iota(jnp.int32, (256, 256), 0) <= lax.broadcasted_iota(
        jnp.int32, (256, 256), 1
    )

    def queries(i, carry):
        q = [q_tiles[i * 2 + head] for head in range(2)]
        grad = [d_tiles[i * 2 + head] for head in range(2)]
        log = [logs[pl.ds(i * 2 + head, 1), :] for head in range(2)]
        delta = []
        for head in range(2):
            both = deltas[i * 2 + head]
            delta.append(jnp.concatenate([both[0:1, :], both[1:2, :]], axis=1))

        def tile(t, diagonal):
            at = pl.ds(pl.multiple_of(t * 256, 256), 256)
            k, v, made = keys[at, :], vals[at, :], []
            dk_tile, dv_tile = dk_acc[at, :], dv_acc[at, :]
            for head in range(2):
                s = lax.dot_general(k, q[head], NT, preferred_element_type=F32)
                p = jnp.exp2(s - log[head])
                if diagonal:
                    p = jnp.where(allowed, p, 0.0)
                dp = lax.dot_general(v, grad[head], NT, preferred_element_type=F32)
                ds = (p * (dp - delta[head])).astype(BF16)
                dv_tile += jnp.dot(p.astype(BF16), grad[head], preferred_element_type=F32)
                dk_tile += jnp.dot(ds, q[head], preferred_element_type=F32)
                made.append(jnp.dot(keys_t[t], ds, preferred_element_type=F32))
            dk_acc[at, :] = dk_tile
            dv_acc[at, :] = dv_tile
            return made

        first = tile(4 + i, True)
        total = lax.fori_loop(
            4 - 4 * place[0],
            4 + i,
            lambda t, acc: tuple(a + b for a, b in zip(acc, tile(t, False))),
            tuple(first),
        )
        dot = jnp.zeros((1, 256), F32)
        for head in range(2):
            out = jnp.transpose(total[head]) * DH ** (-0.5)
            dot += jnp.sum(total[head] * jnp.transpose(q[head].astype(F32)), axis=0, keepdims=True)
            for c in range(2):
                block = lax.rem(i - place[1] + 4, 4) + 4 * jnp.abs(c - place[2])
                at = pl.ds(pl.multiple_of(block * 128, 128), 128)
                dq[at, head * 128 : head * 128 + 128] = out[c * 128 : c * 128 + 128, :].astype(BF16)
        for c in range(2):
            block = lax.rem(i - place[1] + 4, 4) + 4 * jnp.abs(c - place[2])
            dots[pl.ds(block, 1), :] = dot[:, c * 128 : c * 128 + 128] * (1.0 / LOG2E)
        return carry

    lax.fori_loop(0, 4, queries, 0)
    for b in range(8):
        rows = slice(b * 128, b * 128 + 128)
        z, c = spot(place, b)
        at = pl.ds(pl.multiple_of(1024 + z * 256 + c * 128, 128), 128)
        key_grad = dk_acc[at, :] * (1.0 / LOG2E)
        dk[rows, :] = key_grad
        dv[rows, :] = dv_acc[at, :]
        dots[8 + b : 9 + b, :] = row_sums(key_grad * keys[at, :].astype(F32))
        key_grad = dk_acc[rows, :] * (1.0 / LOG2E)
        d_low[rows, :128] = key_grad.astype(BF16)
        d_low[rows, 128:] = dv_acc[rows, :].astype(BF16)
        dots[16 + b : 17 + b, :] = row_sums(key_grad * keys[rows, :].astype(F32))


def unproject_body(
    dq, dk, dv, d_got, q_raw, k_raw, r_q, r_k, t_q, t_k, cos, sin, gain_q, gain_k, weight,
    d_made, dx_mine, dx_part, gains_q, gains_k,
):
    gains_q[...] = jnp.zeros_like(gains_q)
    gains_k[...] = jnp.zeros_like(gains_k)
    for half in (1, 0):

        def step(t, carry):
            block = half * 4 + t
            rows = pl.ds(pl.multiple_of(block * 128, 128), 128)
            cosine, sine = cos[rows, :], sin[rows, :]
            r = column(r_q[pl.ds(block, 1), :])
            mean = column(t_q[pl.ds(block, 1), :]) * (1.0 / 2048.0)
            for head in range(2):
                lanes = slice(head * 128, head * 128 + 128)
                turn = dq[rows, lanes].astype(F32)
                d_norm = turn * cosine - pltpu.roll(turn, 64, 1) * sine
                hat = q_raw[rows, lanes] * r
                gains_q[:, lanes] += jnp.sum(d_norm * hat, axis=0, keepdims=True)
                d_made[rows, lanes] = (r * (d_norm * gain_q[:, lanes] - hat * mean)).astype(BF16)
            r = column(r_k[pl.ds(block, 1), :])
            mean = column(t_k[pl.ds(block, 1), :]) * (1.0 / 1024.0)
            turn = dk[rows, :] + d_got[rows, :128].astype(F32)
            d_norm = turn * cosine - pltpu.roll(turn, 64, 1) * sine
            hat = k_raw[rows, :] * r
            gains_k[...] += jnp.sum(d_norm * hat, axis=0, keepdims=True)
            d_made[rows, 256:384] = (r * (d_norm * gain_k[...] - hat * mean)).astype(BF16)
            d_made[rows, 384:] = (dv[rows, :] + d_got[rows, 128:].astype(F32)).astype(BF16)
            dx = lax.dot_general(d_made[rows, :], weight[...], NT, preferred_element_type=F32)
            at = pl.ds(pl.multiple_of(t * 128, 128), 128)
            if half:
                dx_part[at, :] = dx.astype(BF16)
            else:
                dx_mine[at, :] = dx
            return carry

        lax.fori_loop(0, 4, step, 0)


def norm_scale(values):
    return lax.rsqrt(jnp.mean(values * values, axis=-1, keepdims=True) + EPS)


def norm_back(upstream, normed, scaling):
    return scaling * (upstream - normed * jnp.mean(upstream * normed, axis=-1, keepdims=True))


def rotary_tables(first, z, c):
    half = DH // 2
    k = jnp.arange(4, dtype=jnp.int32)
    starts = jnp.concatenate([((z + k) % 4) * 256 + c * 128, ((z + k) % 4) * 256 + (1 - c) * 128])
    places = (first + starts[:, None] + jnp.arange(128, dtype=jnp.int32)[None, :]).reshape(1024)
    inverse = THETA ** (-(jnp.arange(half, dtype=F32) * (2.0 / DH)))
    angles = places.astype(F32)[:, None] * inverse[None, :]
    cosine, sine = jnp.cos(angles), jnp.sin(angles)
    return (
        jnp.concatenate([cosine, cosine], axis=-1),
        jnp.concatenate([-sine, sine], axis=-1),
    )


def dot(a, b):
    return jnp.dot(a, b, preferred_element_type=F32)


def dot_nt(a, b):
    return lax.dot_general(a, b, NT, preferred_element_type=F32)


def dot_tn(a, b):
    return lax.dot_general(a, b, (((0,), (0,)), ((), ())), preferred_element_type=F32)


def on_device(
    tokens, out_grad, w_query, w_key, w_value, w_out, w_gate, w_up, w_down,
    gain_query, gain_key, gain_attn, gain_mlp,
):
    seq, f = lax.axis_index("seq"), lax.axis_index("fsdp")
    xh, zc = seq // 8, seq % 8
    z, c = zc // 2, zc % 2
    place = jnp.stack([xh, z, c, f]).astype(jnp.int32)
    inputs = tokens[0]

    def columns(weight, width):
        return lax.dynamic_slice_in_dim(weight, zc * width, width, 1)

    x_mine, x_part = gather_group(inputs)
    w_slice = jnp.concatenate(
        [columns(w_query, 256), columns(w_key, 128), columns(w_value, 128)], axis=1
    )
    w_blocks = [w_slice] + [
        lax.ppermute(w_slice, "fsdp", [(i, i ^ j) for i in range(8)]) for j in range(1, 8)
    ]
    across = [(seq_index(xh_, 0, 0) + a, fs, seq_index(xh_, 0, 0) + fs, a)
              for xh_ in range(2) for a in range(8) for fs in range(8)]
    rows_both = lax.ppermute(
        jnp.concatenate([w_out, w_down], axis=0),
        ("seq", "fsdp"),
        [(s * 8 + fs, s2 * 8 + f2) for s, fs, s2, f2 in across],
    )
    w_out_rows, w_down_rows = rows_both[:256], rows_both[256:]
    w_gu = lax.all_gather(
        jnp.concatenate([columns(w_gate, 384), columns(w_up, 384)], axis=1),
        "fsdp", axis=0, tiled=True,
    )
    cosine, sine = rotary_tables(xh * 1024, z, c)
    gain_q = lax.dynamic_slice_in_dim(gain_query, zc * 256, 256, 0)[None]
    gain_k = lax.dynamic_slice_in_dim(gain_key, zc * 128, 128, 0)[None]

    weight, q_raw, k_raw, q_rot, k_rot, values, squares = kernel_call(
        project_body,
        (
            shaped((1024, 512), BF16), shaped((1024, 256), F32), shaped((1024, 128), F32),
            shaped((1024, 256), BF16), shaped((1024, 128), BF16), shaped((1024, 128), BF16),
            shaped((16, 128), F32),
        ),
        [SMEM] + [VMEM] * 14,
        flops=2 * 1024 * 1024 * 512, nbytes=9 << 20,
    )(place, x_mine, x_part, *w_blocks, gain_q, gain_k, cosine, sine)

    kv_low = lax.ppermute(jnp.concatenate([k_rot, values], axis=1), "seq", LOW_TO_HIGH)
    squares = sum_group(squares)
    r_q = lax.rsqrt(squares[:8] * (1.0 / 2048.0) + EPS)
    r_k = lax.rsqrt(squares[8:] * (1.0 / 1024.0) + EPS)
    r_low = lax.ppermute(r_k, "seq", LOW_TO_HIGH)

    out_raw, mixed, q_tiles, keys, vals, logs = kernel_call(
        attend_body,
        (
            shaped((1024, 256), F32), shaped((1024, 256), BF16), shaped((8, 256, 128), BF16),
            shaped((2048, 128), BF16), shaped((2048, 128), BF16), shaped((8, 256), F32),
        ),
        [SMEM] + [VMEM] * 8,
        [pltpu.VMEM((8, 128, 256), BF16)],
        flops=4 * 1024 * 2048 * 256, nbytes=6 << 20,
    )(place, q_rot, k_rot, values, kv_low[:, :128], kv_low[:, 128:], r_q, r_k, r_low)

    a_part = dot(mixed[512:], w_out_rows).astype(BF16)
    attended = scatter_group(dot(mixed[:512], w_out_rows), a_part)
    attn_scale = norm_scale(attended)
    attn_hat = attended * attn_scale
    hidden_state = inputs.astype(F32) + attn_hat * gain_attn
    h_mine, h_part = gather_group(hidden_state.astype(BF16))
    h_all = jnp.concatenate([h_mine, h_part], axis=0)
    w_gate_cols, w_up_cols = w_gu[:, :384], w_gu[:, 384:]
    gate = dot(h_all, w_gate_cols)
    up = dot(h_all, w_up_cols)
    expanded = (jax.nn.silu(gate) * up).astype(BF16)
    m_part = dot(expanded[512:], w_down_rows).astype(BF16)
    projected = scatter_group(dot(expanded[:512], w_down_rows), m_part)
    mlp_scale = norm_scale(projected)
    mlp_hat = projected * mlp_scale
    output = (hidden_state + mlp_hat * gain_mlp).astype(BF16)[None]

    upstream = out_grad[0].astype(F32)
    grad_gain_mlp = jnp.sum(upstream * mlp_hat, axis=0)
    d_projected = norm_back(upstream * gain_mlp, mlp_hat, mlp_scale).astype(BF16)
    dm_mine, dm_part = gather_group(d_projected)
    dm_all = jnp.concatenate([dm_mine, dm_part], axis=0)
    d_expanded = dot_nt(dm_all, w_down_rows)
    sig = jax.nn.sigmoid(gate)
    d_gate = (d_expanded * up * sig * (1.0 + gate * (1.0 - sig))).astype(BF16)
    d_up = (d_expanded * (gate * sig)).astype(BF16)
    d_gu = jnp.concatenate([d_gate, d_up], axis=1)
    dh_part = dot_nt(d_gu[512:], w_gu).astype(BF16)
    d_hidden = upstream + scatter_group(dot_nt(d_gu[:512], w_gu), dh_part)

    n = jnp.arange(1024, dtype=jnp.int32)
    source = ((n // 8) % 16) * 64 + (n // 128) * 8 + n % 8
    order = (n[:, None] == source[None, :]).astype(BF16)
    x_all = jnp.concatenate([x_mine, x_part], axis=0)
    x_turned = dot(x_all, order).astype(BF16)
    h_turned = dot(h_all, order).astype(BF16)
    grad_gu = dot_tn(h_turned, d_gu).astype(BF16)
    grad_gu = lax.psum_scatter(grad_gu, "fsdp", scatter_dimension=0, tiled=True)
    grad_down = dot_tn(expanded, dm_all).reshape(2, 8, 24, 1024)

    grad_gain_attn = jnp.sum(d_hidden * attn_hat, axis=0)
    d_attended = norm_back(d_hidden * gain_attn, attn_hat, attn_scale).astype(BF16)
    da_mine, da_part = gather_group(d_attended)
    da_all = jnp.concatenate([da_mine, da_part], axis=0)
    d_mixed = dot_nt(da_all, w_out_rows).astype(BF16)
    grad_out = dot_tn(mixed, da_all).reshape(2, 8, 16, 1024)
    grad_rows = jnp.swapaxes(
        jnp.concatenate([grad_down, grad_out], axis=2).astype(BF16), 0, 1
    ).reshape(8 * 80, 1024)
    grad_rows = lax.psum_scatter(grad_rows, "fsdp", scatter_dimension=0, tiled=True)
    grad_rows = grad_rows.reshape(2, 40, 1024)
    kept = jnp.where(xh == 0, grad_rows[0], grad_rows[1]).astype(F32)
    given = jnp.where(xh == 0, grad_rows[1], grad_rows[0])
    kept = kept + lax.ppermute(given, "seq", X_SWAP).astype(F32)
    kept = lax.ppermute(
        kept.astype(BF16), "seq", [(xh_ * 8 + a, 2 * a + xh_) for xh_ in range(2) for a in range(8)]
    ).astype(F32)

    dq, dk, dv, d_low, dots = kernel_call(
        attend_back_body,
        (
            shaped((1024, 256), BF16), shaped((1024, 128), F32), shaped((1024, 128), F32),
            shaped((1024, 256), BF16), shaped((24, 128), F32),
        ),
        [SMEM] + [VMEM] * 6,
        [
            pltpu.VMEM((8, 128, 256), BF16), pltpu.VMEM((8, 256, 128), BF16),
            pltpu.VMEM((8, 2, 128), F32), pltpu.VMEM((2048, 128), F32), pltpu.VMEM((2048, 128), F32),
        ],
        flops=10 * 1024 * 2048 * 256, nbytes=8 << 20,
    )(place, q_tiles, keys, vals, logs, out_raw, d_mixed)
    d_got = lax.ppermute(d_low, "seq", HIGH_TO_LOW)
    dots = sum_group(dots)
    t_k = dots[8:16] + lax.ppermute(dots[16:], "seq", HIGH_TO_LOW)

    d_made, dx_mine, dx_part, gains_q, gains_k = kernel_call(
        unproject_body,
        (
            shaped((1024, 512), BF16), shaped((512, 1024), F32), shaped((512, 1024), BF16),
            shaped((1, 256), F32), shaped((1, 128), F32),
        ),
        [VMEM] * 15,
        flops=2 * 1024 * 1024 * 512, nbytes=12 << 20,
    )(dq, dk, dv, d_got, q_raw, k_raw, r_q, r_k, dots[:8], t_k, cosine, sine, gain_q, gain_k, weight)
    d_inputs = d_hidden + scatter_group(dx_mine, dx_part)
    input_grad = d_inputs.astype(BF16)[None]

    grad_made = dot_tn(x_turned, d_made).astype(BF16).reshape(8, 128, 512)
    mine = (jnp.arange(8) == zc)[None, :, None, None]
    wide_q = jnp.where(mine, gains_q.reshape(2, 8, 16).swapaxes(0, 1)[:, None], 0.0)
    wide_k = jnp.where(mine, gains_k.reshape(2, 8, 8).swapaxes(0, 1)[:, None], 0.0)
    gains = jnp.concatenate(
        [
            wide_q.reshape(8, 16, 16),
            wide_k.reshape(8, 16, 8),
            grad_gain_attn.reshape(16, 8, 8).swapaxes(0, 1),
            grad_gain_mlp.reshape(16, 8, 8).swapaxes(0, 1),
        ],
        axis=2,
    ).astype(BF16)
    gains = jnp.pad(gains[:, :, None, :], ((0, 0), (0, 0), (0, 7), (0, 88))).reshape(8, 128, 128)
    sent = jnp.concatenate([grad_made, gains], axis=2)
    got = lax.all_to_all(sent, "fsdp", split_axis=0, concat_axis=0, tiled=True)
    grad_made = jnp.sum(got.astype(F32), axis=0).astype(BF16)
    sent = jnp.concatenate([grad_made, grad_gu], axis=1).reshape(16, 8, 1408)
    got = lax.all_to_all(sent, "seq", split_axis=0, concat_axis=0, tiled=True).astype(F32)
    summed = got[:8] + got[8:]

    def take(first, width):
        return summed[:, :, first : first + width].swapaxes(0, 1).reshape(8, 8 * width)

    gains = jnp.sum(summed[:, 0, 512:640], axis=0)
    return (
        output,
        input_grad,
        take(0, 256),
        take(256, 128),
        take(384, 128),
        kept[24:],
        take(640, 384),
        take(1024, 384),
        kept[:24],
        gains[:16],
        gains[16:24],
        gains[24:32],
        gains[32:40],
    )


def solution(mesh):
    rows = P("fsdp", "seq", None)
    weight = P("fsdp", None)
    grad = P(("seq", "fsdp"), None)
    gain = P(("seq", "fsdp"))
    return jax.shard_map(
        on_device,
        mesh=mesh,
        in_specs=(rows,) * 2 + (weight,) * 7 + (P(),) * 4,
        out_specs=(rows,) * 2 + (grad,) * 7 + (gain,) * 4,
        check_vma=False,
    )
```

```python
import functools
import math

import jax
import jax.numpy as jnp
from jax import lax
from jax.experimental import pallas as pl
from jax.experimental.pallas import tpu as pltpu
from jax.sharding import PartitionSpec as P

BF16 = jnp.bfloat16
F32 = jnp.float32
DH = 128
EPS = 1e-06
THETA = 1000000.0
MASKED = -1e30
LOG2E = math.log2(math.e)
QUERY_SCALE = DH ** (-0.5) * LOG2E
VMEM_BYTES = 40 * 1024 * 1024
VMEM = pl.BlockSpec(memory_space=pltpu.VMEM)
SMEM = pl.BlockSpec(memory_space=pltpu.SMEM)
ANY = pl.BlockSpec(memory_space=pl.ANY)
SMALL = 64 * 1024
NT = (((1,), (1,)), ((), ()))

SEQ_PLACES = [(xh, z, c) for xh in range(2) for z in range(4) for c in range(2)]


def seq_index(xh, z, c):
    return xh * 8 + (z % 4) * 2 + c


CORE_SWAP = [(i, i ^ 1) for i in range(16)]
LOW_TO_HIGH = [(i, i + 8) for i in range(8)]
HIGH_TO_LOW = [(i + 8, i) for i in range(8)]
X_SWAP = [(i, i ^ 8) for i in range(16)]


def from_z(k):
    return [(seq_index(xh, z + k, c), seq_index(xh, z, c)) for xh, z, c in SEQ_PLACES]


def to_z(k):
    return [(seq_index(xh, z, c), seq_index(xh, z + k, c)) for xh, z, c in SEQ_PLACES]


def across(pairs):
    return [(seq * 8 + f, to_seq * 8 + to_f) for seq, f, to_seq, to_f in pairs]


TURN = across(
    (xh * 8 + a, f, xh * 8 + f, a) for xh in range(2) for a in range(8) for f in range(8)
)
Z_SWAP = [(i, i ^ 2) for i in range(16)]
FAR_SWAP = [(i, i ^ 4) for i in range(16)]
OUT_HOME = [(xh * 8 + a, 2 * a + xh) for xh in range(2) for a in range(8)]
DOWN_HOME = across(
    (seq_index(xh, 2 * zh + zl, c), f, 2 * f + zl, 4 * c + 2 * xh + zh)
    for xh in range(2) for zh in range(2) for zl in range(2) for c in range(2) for f in range(8)
)


def swap(value, pairs):
    return lax.ppermute(value, "seq", pairs)


def after(value, *others):
    return lax.optimization_barrier((value, *others))[0]


def gather_group(block):
    far = {k: swap(block, from_z(k)) for k in (2, 1, 3)}
    mine = [block, far[1], far[2], far[3]]
    return mine + [swap(v, CORE_SWAP) for v in mine]


def scatter_group(mine, part):
    rows = [slice(k * 128, k * 128 + 128) for k in range(4)]
    out = None
    for k in (2, 1, 3, 0):
        piece = mine[rows[k]] + swap(part[rows[k]], CORE_SWAP).astype(F32)
        if k:
            piece = swap(piece.astype(BF16), to_z(k)).astype(F32)
        out = piece if out is None else out + piece
    return out


def gather_pair(block):
    mine = [block, swap(block, Z_SWAP)]
    return mine + [swap(v, CORE_SWAP) for v in mine]


def scatter_pair(mine, part, later=()):
    far = mine[128:] + swap(part[128:], CORE_SWAP).astype(F32)
    far, *later = lax.optimization_barrier((far.astype(BF16), *later))
    far = swap(far, Z_SWAP).astype(F32)
    return mine[:128] + swap(part[:128], CORE_SWAP).astype(F32) + far, later


def sum_group(rows):
    groups = rows.shape[0] // 8
    other = swap(rows, CORE_SWAP).reshape(groups, 2, 4, 128)
    pair = rows.reshape(groups, 2, 4, 128) + jnp.concatenate([other[:, 1:], other[:, :1]], axis=1)
    total = pair
    for k in (2, 1, 3):
        got = swap(pair, from_z(k))
        total = total + jnp.concatenate([got[:, :, 4 - k :], got[:, :, : 4 - k]], axis=2)
    return total.reshape(rows.shape)


def column(row):
    return jnp.transpose(jnp.broadcast_to(row, (128, 128)))


def row_sums(values):
    return jnp.sum(jnp.transpose(values), axis=0, keepdims=True)


def shaped(shape, dtype):
    return jax.ShapeDtypeStruct(shape, dtype)


def kernel_call(body, outs, inputs, scratch=(), flops=0, nbytes=0):
    groups = [x if isinstance(x, list) else [x] for x in inputs]
    flat = [a for group in groups for a in group]
    joined = [
        shaped((sum(a.shape[0] for a in group),) + group[0].shape[1:], group[0].dtype)
        for group in groups
    ]

    def large(s):
        return math.prod(s.shape) * s.dtype.itemsize >= SMALL

    def where(s):
        return ANY if large(s) else SMEM if s.dtype == jnp.int32 else VMEM

    out_shapes = [joined[o] if isinstance(o, int) else o for o in outs]
    in_buffers = [pltpu.VMEM(s.shape, s.dtype) for s in joined if large(s)]
    out_buffers = [
        pltpu.VMEM(o.shape, o.dtype) for o in outs if not isinstance(o, int) and large(o)
    ]

    def whole(*refs):
        refs = list(refs)

        def pull(count):
            taken = refs[:count]
            del refs[:count]
            return taken

        in_refs, out_refs = pull(len(flat)), pull(len(outs))
        in_space, out_space = pull(len(in_buffers)), pull(len(out_buffers))
        own, (in_sem, out_sem) = pull(len(scratch)), refs
        loads, ins, at = {}, [], 0
        for group, s in zip(groups, joined):
            if not large(s):
                ins.append(in_refs[at])
                at += 1
                continue
            space, row = in_space.pop(0), 0
            loads[id(space)] = []
            for a in group:
                copy = pltpu.make_async_copy(
                    in_refs[at], space.at[pl.ds(row, a.shape[0])], in_sem.at[at]
                )
                copy.start()
                loads[id(space)].append(copy)
                row, at = row + a.shape[0], at + 1
            ins.append(space)
        made, stores = [], {}
        for k, (o, s, ref) in enumerate(zip(outs, out_shapes, out_refs)):
            if not large(s):
                made.append(ref)
                continue
            space = ins[o] if isinstance(o, int) else out_space.pop(0)
            stores[id(space)] = pltpu.make_async_copy(space, ref, out_sem.at[k])
            if not isinstance(o, int):
                made.append(space)
        started = []

        def ready(*spaces):
            for space in spaces:
                for copy in loads.pop(id(space), ()):
                    copy.wait()

        def done(*spaces):
            for space in spaces:
                copy = stores.pop(id(space))
                copy.start()
                started.append(copy)

        body(ready, done, *ins, *made, *own)
        for key in list(stores):
            copy = stores.pop(key)
            copy.start()
            started.append(copy)
        for copy in started:
            copy.wait()

    return pl.pallas_call(
        whole,
        out_shape=tuple(out_shapes),
        in_specs=[where(s) for group, s in zip(groups, joined) for _ in group],
        out_specs=tuple(where(s) for s in out_shapes),
        scratch_shapes=[
            *in_buffers, *out_buffers, *scratch,
            pltpu.SemaphoreType.DMA((len(flat),)), pltpu.SemaphoreType.DMA((len(outs),)),
        ],
        compiler_params=pltpu.CompilerParams(vmem_limit_bytes=VMEM_BYTES),
        cost_estimate=pl.CostEstimate(flops=flops, bytes_accessed=nbytes, transcendentals=0),
    )(*flat)


def root(total, width):
    return lax.rsqrt(total * (1.0 / width) + EPS)


def project_body(
    ready, done, x_all, weight, gain_q, gain_k, cos, sin,
    q_raw, k_raw, q_rot, kv_rot, squares,
):
    ready(x_all, weight, cos, sin)
    done(x_all)

    def step(t, carry):
        at = pl.multiple_of(t * 256, 256)
        made = jnp.dot(x_all[pl.ds(at, 256), :], weight[...], preferred_element_type=F32)
        for part in range(2):
            rows = pl.ds(at + part * 128, 128)
            block = t * 2 + part
            here = made[part * 128 : part * 128 + 128]
            q, k = here[:, :256], here[:, 256:384]
            kv_rot[rows, 128:] = here[:, 384:].astype(BF16)
            q_raw[rows, :] = q
            k_raw[rows, :] = k
            squares[pl.ds(block, 1), :] = row_sums(
                q[:, :128] * q[:, :128] + q[:, 128:] * q[:, 128:]
            )
            squares[pl.ds(block + 8, 1), :] = row_sums(k * k)
            cosine, sine = cos[rows, :], sin[rows, :]
            for head in range(2):
                lanes = slice(head * 128, head * 128 + 128)
                turn = q[:, lanes] * gain_q[:, lanes]
                q_rot[rows, lanes] = (turn * cosine + pltpu.roll(turn, 64, 1) * sine).astype(BF16)
            turn = k * gain_k[...]
            kv_rot[rows, :128] = (turn * cosine + pltpu.roll(turn, 64, 1) * sine).astype(BF16)
        return carry

    lax.fori_loop(0, 4, step, 0)


def spot(place, block):
    z = lax.rem(place[1] + block % 4, 4)
    c = place[2] if block < 4 else 1 - place[2]
    return z, c


def attend_body(
    ready, done, place, q_rot, kv_rot, kv_low, squares, squares_low, w_out,
    out_raw, out_low, q_tiles, keys, vals, logs, a_mine, a_part, vals_t,
):
    ready(q_rot, kv_rot, kv_low)
    for b in range(8):
        rows = slice(b * 128, b * 128 + 128)
        z, c = spot(place, b)
        r = column(root(squares[b : b + 1, :], 2048.0)) * QUERY_SCALE
        inner = pl.ds(pl.multiple_of(c * 128, 128), 128)
        for head in range(2):
            q = q_rot[rows, head * 128 : head * 128 + 128].astype(F32)
            q_tiles[z * 2 + head, inner, :] = (q * r).astype(BF16)
        at = pl.ds(pl.multiple_of(1024 + z * 256 + c * 128, 128), 128)
        r = column(root(squares[8 + b : 9 + b, :], 1024.0))
        keys[at, :] = (kv_rot[rows, :128].astype(F32) * r).astype(BF16)
        vals[at, :] = kv_rot[rows, 128:]
        r = column(root(squares_low[b : b + 1, :], 1024.0))
        keys[rows, :] = (kv_low[rows, :128].astype(F32) * r).astype(BF16)
        vals[rows, :] = kv_low[rows, 128:]
    done(q_tiles, keys, vals)
    vals_t[...] = jnp.transpose(vals[...].astype(F32)).astype(BF16)
    allowed = lax.broadcasted_iota(jnp.int32, (256, 256), 0) <= lax.broadcasted_iota(
        jnp.int32, (256, 256), 1
    )

    def queries(first, i):
        at_diagonal = 1024 + i * 256
        ranges = [(first, at_diagonal)] if at_diagonal > first else []
        for head in range(2):
            q = q_tiles[i * 2 + head]
            scores = [
                lax.dot_general(keys[lo:hi, :], q, NT, preferred_element_type=F32)
                for lo, hi in ranges + [(at_diagonal, at_diagonal + 256)]
            ]
            scores[-1] = jnp.where(allowed, scores[-1], MASKED)
            tops = [jnp.max(s, axis=0, keepdims=True) for s in scores]
            top = functools.reduce(jnp.maximum, tops)
            total, acc = 0.0, 0.0
            for s, (lo, hi) in zip(scores, ranges + [(at_diagonal, at_diagonal + 256)]):
                p = jnp.exp2(s - top)
                total = total + jnp.sum(p, axis=0, keepdims=True)
                acc = acc + jnp.dot(
                    vals_t[:, lo:hi], p.astype(BF16), preferred_element_type=F32
                )
            out = jnp.transpose(acc / total)
            logs[i * 2 + head : i * 2 + head + 1, :] = top + jnp.log2(total)
            for c in range(2):
                block = lax.rem(i - place[1] + 4, 4) + 4 * jnp.abs(c - place[2])
                at = pl.ds(pl.multiple_of(block * 128, 128), 128)
                lanes = slice(head * 128, head * 128 + 128)
                out_raw[at, lanes] = out[c * 128 : c * 128 + 128, :]
                out_low[at, lanes] = out[c * 128 : c * 128 + 128, :].astype(BF16)

    @pl.when(place[0] == 1)
    def _():
        for i in range(4):
            queries(0, i)

    @pl.when(place[0] == 0)
    def _():
        for i in range(4):
            queries(1024, i)

    done(out_raw, out_low)
    ready(w_out)

    def project(t, carry):
        at = pl.ds(pl.multiple_of(t * 256, 256), 256)
        far = pl.ds(pl.multiple_of(512 + t * 256, 256), 256)
        a_part[at, :] = jnp.dot(out_low[far, :], w_out[...], preferred_element_type=F32).astype(BF16)
        a_mine[at, :] = jnp.dot(out_low[at, :], w_out[...], preferred_element_type=F32)
        return carry

    lax.fori_loop(0, 2, project, 0)


def attend_back_body(
    ready, done, place, q_tiles, keys, vals, logs, out_raw, w_out, da_all,
    dq, dk, dv, d_low, dots, keys_t, d_tiles, deltas, dk_acc, dv_acc,
):
    ready(keys)
    keys_t[...] = jnp.transpose(keys[...].astype(F32)).astype(BF16)
    ready(q_tiles, vals, out_raw, w_out, da_all)
    done(da_all)
    for b in range(8):
        rows = slice(b * 128, b * 128 + 128)
        z, c = spot(place, b)
        inner = pl.ds(pl.multiple_of(c * 128, 128), 128)
        d_out = lax.dot_general(
            da_all[rows, :], w_out[...], NT, preferred_element_type=F32
        ).astype(BF16)
        for head in range(2):
            lanes = slice(head * 128, head * 128 + 128)
            grad = d_out[:, lanes]
            d_tiles[z * 2 + head, inner, :] = grad
            deltas[z * 2 + head, pl.ds(c, 1), :] = row_sums(grad.astype(F32) * out_raw[rows, lanes])
    dk_acc[...] = jnp.zeros_like(dk_acc)
    dv_acc[...] = jnp.zeros_like(dv_acc)
    allowed = lax.broadcasted_iota(jnp.int32, (256, 256), 0) <= lax.broadcasted_iota(
        jnp.int32, (256, 256), 1
    )

    def queries(first, i):
        at_diagonal = 1024 + i * 256
        q = [q_tiles[i * 2 + head] for head in range(2)]
        grad = [d_tiles[i * 2 + head] for head in range(2)]
        log = [logs[i * 2 + head : i * 2 + head + 1, :] for head in range(2)]
        delta = [
            jnp.concatenate([deltas[i * 2 + head, 0:1, :], deltas[i * 2 + head, 1:2, :]], axis=1)
            for head in range(2)
        ]
        total = [0.0, 0.0]
        for lo in range(first, at_diagonal + 256, 256):
            at = slice(lo, lo + 256)
            k, v = keys[at, :], vals[at, :]
            dk_tile, dv_tile = dk_acc[at, :], dv_acc[at, :]
            for head in range(2):
                s = lax.dot_general(k, q[head], NT, preferred_element_type=F32)
                p = jnp.exp2(s - log[head])
                if lo == at_diagonal:
                    p = jnp.where(allowed, p, 0.0)
                dp = lax.dot_general(v, grad[head], NT, preferred_element_type=F32)
                ds = (p * (dp - delta[head])).astype(BF16)
                dv_tile += jnp.dot(p.astype(BF16), grad[head], preferred_element_type=F32)
                dk_tile += jnp.dot(ds, q[head], preferred_element_type=F32)
                total[head] = total[head] + jnp.dot(
                    keys_t[:, at], ds, preferred_element_type=F32
                )
            dk_acc[at, :] = dk_tile
            dv_acc[at, :] = dv_tile
        dot = jnp.zeros((1, 256), F32)
        for head in range(2):
            out = jnp.transpose(total[head]) * DH ** (-0.5)
            dot += jnp.sum(total[head] * jnp.transpose(q[head].astype(F32)), axis=0, keepdims=True)
            for c in range(2):
                block = lax.rem(i - place[1] + 4, 4) + 4 * jnp.abs(c - place[2])
                at = pl.ds(pl.multiple_of(block * 128, 128), 128)
                dq[at, head * 128 : head * 128 + 128] = out[c * 128 : c * 128 + 128, :].astype(BF16)
        for c in range(2):
            block = lax.rem(i - place[1] + 4, 4) + 4 * jnp.abs(c - place[2])
            dots[pl.ds(block, 1), :] = dot[:, c * 128 : c * 128 + 128] * (1.0 / LOG2E)

    @pl.when(place[0] == 1)
    def _():
        for i in range(4):
            queries(0, i)

    @pl.when(place[0] == 0)
    def _():
        for i in range(4):
            queries(1024, i)

    for b in range(8):
        rows = slice(b * 128, b * 128 + 128)
        z, c = spot(place, b)
        at = pl.ds(pl.multiple_of(1024 + z * 256 + c * 128, 128), 128)
        key_grad = dk_acc[at, :] * (1.0 / LOG2E)
        dk[rows, :] = key_grad
        dv[rows, :] = dv_acc[at, :]
        dots[8 + b : 9 + b, :] = row_sums(key_grad * keys[at, :].astype(F32))
        key_grad = dk_acc[rows, :] * (1.0 / LOG2E)
        d_low[rows, :128] = key_grad.astype(BF16)
        d_low[rows, 128:] = dv_acc[rows, :].astype(BF16)
        dots[16 + b : 17 + b, :] = row_sums(key_grad * keys[rows, :].astype(F32))


def unproject_body(
    ready, done, place, dq, dk, dv, d_got, q_raw, k_raw, squares, dots, dots_got, cos, sin,
    gain_q, gain_k, x_turned, gains, d_made, sent, sums,
):
    sums[...] = jnp.zeros_like(sums)
    ready(dq, dk, dv, d_got, q_raw, k_raw, cos, sin)

    def step(b, carry):
        rows = pl.ds(pl.multiple_of(b * 128, 128), 128)
        cosine, sine = cos[rows, :], sin[rows, :]
        r = column(root(squares[pl.ds(b, 1), :], 2048.0))
        mean = column(dots[pl.ds(b, 1), :]) * (1.0 / 2048.0)
        for head in range(2):
            lanes = slice(head * 128, head * 128 + 128)
            turn = dq[rows, lanes].astype(F32)
            d_norm = turn * cosine - pltpu.roll(turn, 64, 1) * sine
            hat = q_raw[rows, lanes] * r
            sums[0:1, lanes] += jnp.sum(d_norm * hat, axis=0, keepdims=True)
            d_made[rows, lanes] = (r * (d_norm * gain_q[:, lanes] - hat * mean)).astype(BF16)
        r = column(root(squares[pl.ds(b + 8, 1), :], 1024.0))
        mean = column(dots[pl.ds(b + 8, 1), :] + dots_got[pl.ds(b, 1), :]) * (1.0 / 1024.0)
        turn = dk[rows, :] + d_got[rows, :128].astype(F32)
        d_norm = turn * cosine - pltpu.roll(turn, 64, 1) * sine
        hat = k_raw[rows, :] * r
        sums[0:1, 256:] += jnp.sum(d_norm * hat, axis=0, keepdims=True)
        d_made[rows, 256:384] = (r * (d_norm * gain_k[...] - hat * mean)).astype(BF16)
        d_made[rows, 384:] = (dv[rows, :] + d_got[rows, 128:].astype(F32)).astype(BF16)
        return carry

    lax.fori_loop(0, 8, step, 0)
    done(d_made)
    ready(x_turned, gains)

    def grad(t, carry):
        rows = pl.ds(pl.multiple_of(t * 256, 256), 256)
        sent[rows, :512] = jnp.dot(
            x_turned[rows, :], d_made[...], preferred_element_type=F32
        ).astype(BF16)
        sent[rows, 512:] = gains[rows, :]
        return carry

    lax.fori_loop(0, 4, grad, 0)
    extra = 0.0
    for lo, width, each, first in ((0, 256, 16, 0), (256, 128, 8, 16)):
        row = lax.broadcasted_iota(jnp.int32, (128, width), 0) // 8
        lane = lax.broadcasted_iota(jnp.int32, (128, width), 1) // each
        spread = jnp.where(row == lane, sums[0:1, lo : lo + width], 0.0).astype(BF16)
        lane = lax.broadcasted_iota(jnp.int32, (width, 128), 0) % each + first
        pick = jnp.where(lane == lax.broadcasted_iota(jnp.int32, (width, 128), 1), 1.0, 0.0)
        extra = extra + jnp.dot(spread, pick.astype(BF16), preferred_element_type=F32)
    rows = pl.ds(pl.multiple_of((place[1] * 2 + place[2]) * 128, 128), 128)
    sent[rows, 512:] = (gains[rows, :].astype(F32) + extra).astype(BF16)


def input_body(ready, done, d_made, weight, dx_mine, dx_part):
    ready(d_made, weight)

    def step(t, carry):
        at = pl.ds(pl.multiple_of(t * 256, 256), 256)
        far = pl.ds(pl.multiple_of(512 + t * 256, 256), 256)
        dx_part[at, :] = lax.dot_general(
            d_made[far, :], weight[...], NT, preferred_element_type=F32
        ).astype(BF16)
        dx_mine[at, :] = lax.dot_general(
            d_made[at, :], weight[...], NT, preferred_element_type=F32
        )
        return carry

    lax.fori_loop(0, 2, step, 0)


def expand_body(ready, done, h_all, weight, gate, up, expanded, m_mine, m_part, down):
    ready(weight)
    for f in range(8):
        down[f * 96 : f * 96 + 96, :768] = weight[f * 128 : f * 128 + 96, 1536:]
        for m in range(3):
            down[f * 96 + m * 32 : f * 96 + m * 32 + 32, 768:] = weight[
                f * 128 + 96 : f * 128 + 128, 1536 + m * 256 : 1792 + m * 256
            ]

    done(down)
    ready(h_all)
    done(h_all)

    def widen(n, carry):
        lanes = pl.ds(pl.multiple_of(n * 256, 256), 256)
        upper = pl.ds(pl.multiple_of(768 + n * 256, 256), 256)
        g = jnp.dot(h_all[...], weight[:, lanes], preferred_element_type=F32)
        u = jnp.dot(h_all[...], weight[:, upper], preferred_element_type=F32)
        gate[:, lanes] = g
        up[:, lanes] = u
        expanded[:, lanes] = (g * jax.nn.sigmoid(g) * u).astype(BF16)
        return carry

    lax.fori_loop(0, 3, widen, 0)
    done(gate, up, expanded)

    def narrow(n, carry):
        lanes = pl.ds(pl.multiple_of(n * 256, 256), 256)
        m = jnp.dot(expanded[...], down[:, lanes], preferred_element_type=F32)
        m_mine[:, lanes] = m[:256]
        m_part[:, lanes] = m[256:].astype(BF16)
        return carry

    lax.fori_loop(0, 4, narrow, 0)


def expand_back_body(ready, done, dm_all, gate, up, weight, down, d_gu, dh_mine, dh_part):
    ready(dm_all, gate, up, down)
    done(dm_all)

    def widen(n, carry):
        lanes = pl.ds(pl.multiple_of(n * 256, 256), 256)
        upper = pl.ds(pl.multiple_of(768 + n * 256, 256), 256)
        de = lax.dot_general(dm_all[...], down[lanes, :], NT, preferred_element_type=F32)
        g = gate[:, lanes]
        sig = jax.nn.sigmoid(g)
        d_gu[:, lanes] = (de * up[:, lanes] * sig * (1.0 + g * (1.0 - sig))).astype(BF16)
        d_gu[:, upper] = (de * (g * sig)).astype(BF16)
        return carry

    lax.fori_loop(0, 3, widen, 0)
    done(d_gu)
    ready(weight)

    def narrow(n, carry):
        lanes = pl.ds(pl.multiple_of(n * 256, 256), 256)
        dh = lax.dot_general(d_gu[...], weight[lanes, :1536], NT, preferred_element_type=F32)
        dh_mine[:, lanes] = dh[:256]
        dh_part[:, lanes] = dh[256:].astype(BF16)
        return carry

    lax.fori_loop(0, 4, narrow, 0)


def expand_grad_body(ready, done, h_turned, d_gu, expanded, dm_all, out, expanded_t):
    ready(expanded)
    expanded_t[...] = jnp.transpose(expanded[...].astype(F32)).astype(BF16)

    ready(h_turned, d_gu, dm_all)

    def widen(n, carry):
        lanes = pl.ds(pl.multiple_of(n * 256, 256), 256)
        out[:, lanes] = jnp.dot(
            h_turned[...], d_gu[:, lanes], preferred_element_type=F32
        ).astype(BF16)
        return carry

    lax.fori_loop(0, 6, widen, 0)
    for n in range(4):
        made = jnp.dot(
            expanded_t[...], dm_all[:, n * 256 : n * 256 + 256], preferred_element_type=F32
        ).astype(BF16)
        for f in range(8):
            for m in range(3):
                rows = slice(f * 96 + m * 32, f * 96 + m * 32 + 32)
                if n < 3:
                    to, lanes = f * 128 + m * 32, 1536 + n * 256
                else:
                    to, lanes = f * 128 + 96, 1536 + m * 256
                out[to : to + 32, lanes : lanes + 256] = made[rows]


def norm_scale(values):
    return lax.rsqrt(jnp.mean(values * values, axis=-1, keepdims=True) + EPS)


def norm_back(upstream, normed, scaling):
    return scaling * (upstream - normed * jnp.mean(upstream * normed, axis=-1, keepdims=True))


def rotary_tables(first, z, c):
    half = DH // 2
    k = jnp.arange(4, dtype=jnp.int32)
    starts = jnp.concatenate([((z + k) % 4) * 256 + c * 128, ((z + k) % 4) * 256 + (1 - c) * 128])
    places = (first + starts[:, None] + jnp.arange(128, dtype=jnp.int32)[None, :]).reshape(1024)
    inverse = THETA ** (-(jnp.arange(half, dtype=F32) * (2.0 / DH)))
    angles = places.astype(F32)[:, None] * inverse[None, :]
    cosine, sine = jnp.cos(angles), jnp.sin(angles)
    return (
        jnp.concatenate([cosine, cosine], axis=-1),
        jnp.concatenate([-sine, sine], axis=-1),
    )


def dot(a, b):
    return jnp.dot(a, b, preferred_element_type=F32)


def dot_nt(a, b):
    return lax.dot_general(a, b, NT, preferred_element_type=F32)


def dot_tn(a, b):
    return lax.dot_general(a, b, (((0,), (0,)), ((), ())), preferred_element_type=F32)


def on_device(
    tokens, out_grad, w_query, w_key, w_value, w_out, w_gate, w_up, w_down,
    gain_query, gain_key, gain_attn, gain_mlp,
):
    seq = lax.axis_index("seq")
    xh, zc = seq // 8, seq % 8
    z, c = zc // 2, zc % 2
    quarter = (z % 2) * 2 + c
    place = jnp.stack([xh, z, c]).astype(jnp.int32)
    inputs = tokens[0]

    def columns(weight, width):
        return lax.dynamic_slice_in_dim(weight, zc * width, width, 1)

    def spread(block):
        return lax.all_to_all(
            jnp.broadcast_to(block[None], (8,) + block.shape),
            "fsdp", split_axis=0, concat_axis=0, tiled=True,
        ).reshape(8 * block.shape[0], block.shape[1])

    x_blocks = gather_group(inputs)
    weight = spread(
        jnp.concatenate(
            [columns(w_query, 256), columns(w_key, 128), columns(w_value, 128)], axis=1
        )
    )
    w_out_rows = lax.ppermute(
        lax.dynamic_slice_in_dim(w_out, zc * 32, 32, 0), ("seq", "fsdp"), TURN
    )
    weight, w_out_rows, w_gate, w_up, w_down = lax.optimization_barrier(
        (weight, w_out_rows, w_gate, w_up, w_down)
    )
    w_out_rows = spread(w_out_rows)

    def quarters(weight):
        part = lax.dynamic_slice_in_dim(weight.reshape(128, 8, 384), quarter * 96, 96, 2)
        return part.reshape(128, 768)

    down = lax.dynamic_slice_in_dim(w_down, quarter * 96, 96, 0)
    packed = jnp.concatenate(
        [
            down[:, :768],
            jnp.concatenate([down[m * 32 : m * 32 + 32, 768:] for m in range(3)], axis=1),
        ],
        axis=0,
    )
    w_mlp = lax.all_gather(
        jnp.concatenate([quarters(w_gate), quarters(w_up), packed], axis=1),
        "fsdp", axis=0, tiled=True,
    )

    cosine, sine = rotary_tables(xh * 1024, z, c)
    gain_q = lax.dynamic_slice_in_dim(gain_query, zc * 256, 256, 0)[None]
    gain_k = lax.dynamic_slice_in_dim(gain_key, zc * 128, 128, 0)[None]
    x_all, q_raw, k_raw, q_rot, kv_rot, squares = kernel_call(
        project_body,
        [
            0, shaped((1024, 256), F32), shaped((1024, 128), F32),
            shaped((1024, 256), BF16), shaped((1024, 256), BF16), shaped((16, 128), F32),
        ],
        [x_blocks, weight, gain_q, gain_k, cosine, sine],
        flops=2 * 1024 * 1024 * 512, nbytes=9 << 20,
    )

    kv_low = swap(kv_rot, LOW_TO_HIGH)
    squares = sum_group(squares)
    squares_low = swap(squares[8:], LOW_TO_HIGH)
    out_raw, mixed, q_tiles, keys, vals, logs, a_mine, a_part = kernel_call(
        attend_body,
        [
            shaped((1024, 256), F32), shaped((1024, 256), BF16), shaped((8, 256, 128), BF16),
            shaped((2048, 128), BF16), shaped((2048, 128), BF16), shaped((8, 256), F32),
            shaped((512, 1024), F32), shaped((512, 1024), BF16),
        ],
        [place, q_rot, kv_rot, kv_low, squares, squares_low, w_out_rows],
        [pltpu.VMEM((128, 2048), BF16)],
        flops=4 * 1024 * 2048 * 256, nbytes=9 << 20,
    )
    x_turned = x_all.T

    attended = scatter_group(a_mine, a_part)
    attended, w_mlp, x_turned = lax.optimization_barrier((attended, w_mlp, x_turned))
    attn_scale = norm_scale(attended)
    attn_hat = attended * attn_scale
    hidden_state = inputs.astype(F32) + attn_hat * gain_attn
    h_all, gate, up, expanded, m_mine, m_part, w_down_rows = kernel_call(
        expand_body,
        [
            0, shaped((512, 768), F32), shaped((512, 768), F32), shaped((512, 768), BF16),
            shaped((256, 1024), F32), shaped((256, 1024), BF16), shaped((768, 1024), BF16),
        ],
        [gather_pair(hidden_state.astype(BF16)), w_mlp],
        flops=2 * 512 * 2304 * 1024, nbytes=12 << 20,
    )
    projected, _ = scatter_pair(m_mine, m_part)
    mlp_scale = norm_scale(projected)
    mlp_hat = projected * mlp_scale
    output = (hidden_state + mlp_hat * gain_mlp).astype(BF16)[None]

    upstream = out_grad[0].astype(F32)
    grad_gain_mlp = jnp.sum(upstream * mlp_hat, axis=0)
    d_projected = norm_back(upstream * gain_mlp, mlp_hat, mlp_scale).astype(BF16)
    n = jnp.arange(1024, dtype=jnp.int32)
    source = ((n // 8) % 16) * 64 + (n // 128) * 8 + n % 8
    order = (n[None, :] == source[:, None]).astype(BF16)
    h_turned = dot_nt(order, h_all).astype(BF16)
    d_blocks = gather_pair(d_projected)
    d_blocks[3], h_turned = lax.optimization_barrier((d_blocks[3], h_turned))
    dm_all, d_gu, dh_mine, dh_part = kernel_call(
        expand_back_body,
        [
            0, shaped((512, 1536), BF16), shaped((256, 1024), F32), shaped((256, 1024), BF16),
        ],
        [d_blocks, gate, up, w_mlp, w_down_rows],
        flops=2 * 512 * 2304 * 1024, nbytes=12 << 20,
    )

    far = dh_mine[128:] + swap(dh_part[128:], CORE_SWAP).astype(F32)
    far, d_gu, dm_all = lax.optimization_barrier((far.astype(BF16), d_gu, dm_all))
    far = swap(far, Z_SWAP)
    (grad_mlp,) = kernel_call(
        expand_grad_body,
        [shaped((1024, 2304), BF16)],
        [h_turned, d_gu, expanded, dm_all],
        [pltpu.VMEM((768, 512), BF16)],
        flops=2 * 512 * 2304 * 1024, nbytes=9 << 20,
    )
    far, grad_mlp = lax.optimization_barrier((far, grad_mlp))
    grad_mlp = lax.psum_scatter(grad_mlp, "fsdp", scatter_dimension=0, tiled=True)
    d_hidden = upstream + dh_mine[:128] + swap(dh_part[:128], CORE_SWAP).astype(F32)
    d_hidden = d_hidden + far.astype(F32)

    grad_gain_attn = jnp.sum(d_hidden * attn_hat, axis=0)
    d_attended = norm_back(d_hidden * gain_attn, attn_hat, attn_scale).astype(BF16)
    dq, dk, dv, d_low, dots, da_all = kernel_call(
        attend_back_body,
        [
            shaped((1024, 256), BF16), shaped((1024, 128), F32), shaped((1024, 128), F32),
            shaped((1024, 256), BF16), shaped((24, 128), F32), 7,
        ],
        [place, q_tiles, keys, vals, logs, out_raw, w_out_rows, gather_group(d_attended)],
        [
            pltpu.VMEM((128, 2048), BF16), pltpu.VMEM((8, 256, 128), BF16),
            pltpu.VMEM((8, 2, 128), F32), pltpu.VMEM((2048, 128), F32), pltpu.VMEM((2048, 128), F32),
        ],
        flops=10 * 1024 * 2048 * 256, nbytes=8 << 20,
    )
    d_got = swap(d_low, HIGH_TO_LOW)
    dots = sum_group(dots)
    dots_got = swap(dots[16:], HIGH_TO_LOW)

    gains = jnp.concatenate([grad_gain_attn.reshape(128, 8), grad_gain_mlp.reshape(128, 8)], axis=1)
    gains = jnp.broadcast_to(
        jnp.pad(gains.astype(BF16), ((0, 0), (24, 88)))[:, None, :], (128, 8, 128)
    ).reshape(1024, 128)
    d_made, sent = kernel_call(
        unproject_body,
        [shaped((1024, 512), BF16), shaped((1024, 640), BF16)],
        [
            place, dq, dk, dv, d_got, q_raw, k_raw, squares, dots, dots_got, cosine, sine,
            gain_q, gain_k, x_turned, gains,
        ],
        [pltpu.VMEM((8, 384), F32)],
        flops=2 * 1024 * 1024 * 512, nbytes=9 << 20,
    )
    got_made = lax.all_to_all(
        sent.reshape(128, 8, 640), ("seq", "fsdp"), split_axis=0, concat_axis=0, tiled=True
    )
    dx_mine, dx_part = kernel_call(
        input_body,
        [shaped((512, 1024), F32), shaped((512, 1024), BF16)],
        [after(d_made, sent), weight],
        flops=2 * 1024 * 1024 * 512, nbytes=5 << 20,
    )
    d_inputs = scatter_group(dx_mine, dx_part)

    grad_out = dot_tn(mixed, after(da_all, d_got)).astype(BF16).reshape(2, 8, 16, 1024)
    grad_out = lax.all_to_all(
        jnp.swapaxes(grad_out, 0, 1), "fsdp", split_axis=0, concat_axis=0, tiled=True
    )
    grad_out = jnp.sum(grad_out.astype(F32), axis=0)
    given = jnp.where(xh == 0, grad_out[1], grad_out[0]).astype(BF16)
    grad_out = jnp.where(xh == 0, grad_out[0], grad_out[1]) + swap(given, X_SWAP).astype(F32)
    grad_out = swap(grad_out.astype(BF16), OUT_HOME)

    packed = grad_mlp[:, 1536:]
    grad_down = jnp.concatenate(
        [
            packed[:96],
            jnp.concatenate([packed[96:, m * 256 : m * 256 + 256] for m in range(3)], axis=0),
        ],
        axis=1,
    )
    given = jnp.where(xh == 0, grad_down[48:], grad_down[:48])
    grad_down = jnp.where(xh == 0, grad_down[:48], grad_down[48:]).astype(F32)
    grad_down = grad_down + swap(given, X_SWAP).astype(F32)
    given = jnp.where(z < 2, grad_down[24:], grad_down[:24]).astype(BF16)
    grad_down = jnp.where(z < 2, grad_down[:24], grad_down[24:]) + swap(given, FAR_SWAP).astype(F32)
    grad_down = lax.ppermute(grad_down.astype(BF16), ("seq", "fsdp"), DOWN_HOME)
    got_wide = lax.all_to_all(
        grad_mlp[:, :1536].reshape(16, 8, 1536), "seq", split_axis=0, concat_axis=0, tiled=True
    )

    got_made, got_wide, grad_down, grad_out, d_inputs = lax.optimization_barrier(
        (got_made, got_wide, grad_down, grad_out, d_inputs)
    )
    summed = jnp.sum(got_made.reshape(2, 8, 8, 8, 640).astype(F32), axis=(0, 2))
    gains = jnp.sum(summed[:, 0, 512:], axis=0)

    def take(first, width):
        return summed[:, :, first : first + width].swapaxes(0, 1).reshape(8, 8 * width)

    wide = jnp.sum(got_wide.reshape(2, 2, 4, 8, 2, 8, 96).astype(F32), axis=(0, 1))
    wide = wide.transpose(2, 1, 3, 0, 4).reshape(2, 8, 3072)
    return (
        output,
        (d_hidden + d_inputs).astype(BF16)[None],
        take(0, 256),
        take(256, 128),
        take(384, 128),
        grad_out.astype(F32),
        wide[0],
        wide[1],
        grad_down.astype(F32),
        gains[:16],
        gains[16:24],
        gains[24:32],
        gains[32:40],
    )


def solution(mesh):
    rows = P("fsdp", "seq", None)
    weight = P("fsdp", None)
    grad = P(("seq", "fsdp"), None)
    gain = P(("seq", "fsdp"))
    return jax.shard_map(
        on_device,
        mesh=mesh,
        in_specs=(rows,) * 2 + (weight,) * 7 + (P(),) * 4,
        out_specs=(rows,) * 2 + (grad,) * 7 + (gain,) * 4,
        check_vma=False,
    )
```

```python
import functools
import math

import jax
import jax.numpy as jnp
from jax import lax
from jax.experimental import pallas as pl
from jax.experimental.pallas import tpu as pltpu
from jax.sharding import PartitionSpec as P

BF16 = jnp.bfloat16
F32 = jnp.float32
DH = 128
EPS = 1e-06
THETA = 1000000.0
MASKED = -1e30
LOG2E = math.log2(math.e)
QUERY_SCALE = DH ** (-0.5) * LOG2E
VMEM_BYTES = 40 * 1024 * 1024
VMEM = pl.BlockSpec(memory_space=pltpu.VMEM)
SMEM = pl.BlockSpec(memory_space=pltpu.SMEM)
HBM = pl.BlockSpec(memory_space=pltpu.HBM)
SMALL = 64 * 1024
NT = (((1,), (1,)), ((), ()))

SEQ_PLACES = [(xh, z, c) for xh in range(2) for z in range(4) for c in range(2)]


def seq_index(xh, z, c):
    return xh * 8 + (z % 4) * 2 + c


CORE_SWAP = [(i, i ^ 1) for i in range(16)]
LOW_TO_HIGH = [(i, i + 8) for i in range(8)]
HIGH_TO_LOW = [(i + 8, i) for i in range(8)]
X_SWAP = [(i, i ^ 8) for i in range(16)]


def from_z(k):
    return [(seq_index(xh, z + k, c), seq_index(xh, z, c)) for xh, z, c in SEQ_PLACES]


def to_z(k):
    return [(seq_index(xh, z, c), seq_index(xh, z + k, c)) for xh, z, c in SEQ_PLACES]


def across(pairs):
    return [(seq * 8 + f, to_seq * 8 + to_f) for seq, f, to_seq, to_f in pairs]


TURN = across(
    (xh * 8 + a, f, xh * 8 + f, a) for xh in range(2) for a in range(8) for f in range(8)
)
Z_SWAP = [(i, i ^ 2) for i in range(16)]
FAR_SWAP = [(i, i ^ 4) for i in range(16)]
OUT_HOME = [(xh * 8 + a, 2 * a + xh) for xh in range(2) for a in range(8)]
DOWN_HOME = across(
    (seq_index(xh, 2 * zh + zl, c), f, 2 * f + zl, 4 * c + 2 * xh + zh)
    for xh in range(2) for zh in range(2) for zl in range(2) for c in range(2) for f in range(8)
)


def swap(value, pairs):
    return lax.ppermute(value, "seq", pairs)


def after(value, *others):
    return lax.optimization_barrier((value, *others))[0]


def gather_group(block):
    far = {k: swap(block, from_z(k)) for k in (2, 1, 3)}
    mine = [block, far[1], far[2], far[3]]
    return mine + [swap(v, CORE_SWAP) for v in mine]


def scatter_group(mine, part):
    rows = [slice(k * 128, k * 128 + 128) for k in range(4)]
    out = None
    for k in (2, 1, 3, 0):
        piece = mine[rows[k]] + swap(part[rows[k]], CORE_SWAP).astype(F32)
        if k:
            piece = swap(piece.astype(BF16), to_z(k)).astype(F32)
        out = piece if out is None else out + piece
    return out


def gather_pair(block):
    mine = [block, swap(block, Z_SWAP)]
    return mine + [swap(v, CORE_SWAP) for v in mine]


def scatter_pair(mine, part, later=()):
    far = mine[128:] + swap(part[128:], CORE_SWAP).astype(F32)
    far, *later = lax.optimization_barrier((far.astype(BF16), *later))
    far = swap(far, Z_SWAP).astype(F32)
    return mine[:128] + swap(part[:128], CORE_SWAP).astype(F32) + far, later


def sum_group(rows):
    groups = rows.shape[0] // 8
    other = swap(rows, CORE_SWAP).reshape(groups, 2, 4, 128)
    pair = rows.reshape(groups, 2, 4, 128) + jnp.concatenate([other[:, 1:], other[:, :1]], axis=1)
    total = pair
    for k in (2, 1, 3):
        got = swap(pair, from_z(k))
        total = total + jnp.concatenate([got[:, :, 4 - k :], got[:, :, : 4 - k]], axis=2)
    return total.reshape(rows.shape)


def column(row):
    return jnp.transpose(jnp.broadcast_to(row, (128, 128)))


def row_sums(values):
    return jnp.sum(jnp.transpose(values), axis=0, keepdims=True)


def shaped(shape, dtype):
    return jax.ShapeDtypeStruct(shape, dtype)


def kernel_call(body, outs, inputs, scratch=(), flops=0, nbytes=0):
    groups = [x if isinstance(x, list) else [x] for x in inputs]
    flat = [a for group in groups for a in group]
    joined = [
        shaped((sum(a.shape[0] for a in group),) + group[0].shape[1:], group[0].dtype)
        for group in groups
    ]

    def large(s):
        return math.prod(s.shape) * s.dtype.itemsize >= SMALL

    def where(s):
        return HBM if large(s) else SMEM if s.dtype == jnp.int32 else VMEM

    out_shapes = [joined[o] if isinstance(o, int) else o for o in outs]
    in_buffers = [pltpu.VMEM(s.shape, s.dtype) for s in joined if large(s)]
    out_buffers = [
        pltpu.VMEM(o.shape, o.dtype) for o in outs if not isinstance(o, int) and large(o)
    ]

    def whole(*refs):
        refs = list(refs)

        def pull(count):
            taken = refs[:count]
            del refs[:count]
            return taken

        in_refs, out_refs = pull(len(flat)), pull(len(outs))
        in_space, out_space = pull(len(in_buffers)), pull(len(out_buffers))
        own, (in_sem, out_sem) = pull(len(scratch)), refs
        loads, ins, at = {}, [], 0
        for group, s in zip(groups, joined):
            if not large(s):
                ins.append(in_refs[at])
                at += 1
                continue
            space, row = in_space.pop(0), 0
            loads[id(space)] = []
            for a in group:
                copy = pltpu.make_async_copy(
                    in_refs[at], space.at[pl.ds(row, a.shape[0])], in_sem.at[at]
                )
                copy.start()
                loads[id(space)].append(copy)
                row, at = row + a.shape[0], at + 1
            ins.append(space)
        made, stores = [], {}
        for k, (o, s, ref) in enumerate(zip(outs, out_shapes, out_refs)):
            if not large(s):
                made.append(ref)
                continue
            space = ins[o] if isinstance(o, int) else out_space.pop(0)
            stores[id(space)] = pltpu.make_async_copy(space, ref, out_sem.at[k])
            if not isinstance(o, int):
                made.append(space)
        started = []

        def ready(*spaces):
            for space in spaces:
                for copy in loads.pop(id(space), ()):
                    copy.wait()

        def done(*spaces):
            for space in spaces:
                copy = stores.pop(id(space))
                copy.start()
                started.append(copy)

        body(ready, done, *ins, *made, *own)
        for key in list(stores):
            copy = stores.pop(key)
            copy.start()
            started.append(copy)
        for copy in started:
            copy.wait()

    return pl.pallas_call(
        whole,
        out_shape=tuple(pltpu.HBM(s.shape, s.dtype) if large(s) else s for s in out_shapes),
        in_specs=[where(s) for group, s in zip(groups, joined) for _ in group],
        out_specs=tuple(where(s) for s in out_shapes),
        scratch_shapes=[
            *in_buffers, *out_buffers, *scratch,
            pltpu.SemaphoreType.DMA((len(flat),)), pltpu.SemaphoreType.DMA((len(outs),)),
        ],
        compiler_params=pltpu.CompilerParams(vmem_limit_bytes=VMEM_BYTES),
        cost_estimate=pl.CostEstimate(flops=flops, bytes_accessed=nbytes, transcendentals=0),
    )(
        *[
            pltpu.with_memory_space_constraint(a, pltpu.HBM) if large(s) else a
            for group, s in zip(groups, joined)
            for a in group
        ]
    )


def root(total, width):
    return lax.rsqrt(total * (1.0 / width) + EPS)


def project_body(
    ready, done, x_all, weight, gain_q, gain_k, cos, sin,
    q_raw, k_raw, q_rot, kv_rot, squares,
):
    ready(x_all, weight, cos, sin)
    done(x_all)

    def step(t, carry):
        at = pl.multiple_of(t * 256, 256)
        made = jnp.dot(x_all[pl.ds(at, 256), :], weight[...], preferred_element_type=F32)
        for part in range(2):
            rows = pl.ds(at + part * 128, 128)
            block = t * 2 + part
            here = made[part * 128 : part * 128 + 128]
            q, k = here[:, :256], here[:, 256:384]
            kv_rot[rows, 128:] = here[:, 384:].astype(BF16)
            q_raw[rows, :] = q
            k_raw[rows, :] = k
            squares[pl.ds(block, 1), :] = row_sums(
                q[:, :128] * q[:, :128] + q[:, 128:] * q[:, 128:]
            )
            squares[pl.ds(block + 8, 1), :] = row_sums(k * k)
            cosine, sine = cos[rows, :], sin[rows, :]
            for head in range(2):
                lanes = slice(head * 128, head * 128 + 128)
                turn = q[:, lanes] * gain_q[:, lanes]
                q_rot[rows, lanes] = (turn * cosine + pltpu.roll(turn, 64, 1) * sine).astype(BF16)
            turn = k * gain_k[...]
            kv_rot[rows, :128] = (turn * cosine + pltpu.roll(turn, 64, 1) * sine).astype(BF16)
        return carry

    lax.fori_loop(0, 4, step, 0)


def spot(place, block):
    z = lax.rem(place[1] + block % 4, 4)
    c = place[2] if block < 4 else 1 - place[2]
    return z, c


def attend_body(
    ready, done, place, q_rot, kv_rot, kv_low, squares, squares_low,
    out_raw, out_low, q_tiles, keys, vals, logs, vals_t,
):
    ready(q_rot, kv_rot, kv_low)
    for b in range(8):
        rows = slice(b * 128, b * 128 + 128)
        z, c = spot(place, b)
        r = column(root(squares[b : b + 1, :], 2048.0)) * QUERY_SCALE
        inner = pl.ds(pl.multiple_of(c * 128, 128), 128)
        for head in range(2):
            q = q_rot[rows, head * 128 : head * 128 + 128].astype(F32)
            q_tiles[z * 2 + head, inner, :] = (q * r).astype(BF16)
        at = pl.ds(pl.multiple_of(1024 + z * 256 + c * 128, 128), 128)
        r = column(root(squares[8 + b : 9 + b, :], 1024.0))
        keys[at, :] = (kv_rot[rows, :128].astype(F32) * r).astype(BF16)
        vals[at, :] = kv_rot[rows, 128:]
        r = column(root(squares_low[b : b + 1, :], 1024.0))
        keys[rows, :] = (kv_low[rows, :128].astype(F32) * r).astype(BF16)
        vals[rows, :] = kv_low[rows, 128:]
    done(q_tiles, keys, vals)
    vals_t[...] = jnp.transpose(vals[...].astype(F32)).astype(BF16)
    allowed = lax.broadcasted_iota(jnp.int32, (256, 256), 0) <= lax.broadcasted_iota(
        jnp.int32, (256, 256), 1
    )

    def queries(first, i):
        at_diagonal = 1024 + i * 256
        ranges = [(first, at_diagonal)] if at_diagonal > first else []
        for head in range(2):
            q = q_tiles[i * 2 + head]
            scores = [
                lax.dot_general(keys[lo:hi, :], q, NT, preferred_element_type=F32)
                for lo, hi in ranges + [(at_diagonal, at_diagonal + 256)]
            ]
            scores[-1] = jnp.where(allowed, scores[-1], MASKED)
            tops = [jnp.max(s, axis=0, keepdims=True) for s in scores]
            top = functools.reduce(jnp.maximum, tops)
            total, acc = 0.0, 0.0
            for s, (lo, hi) in zip(scores, ranges + [(at_diagonal, at_diagonal + 256)]):
                p = jnp.exp2(s - top)
                total = total + jnp.sum(p, axis=0, keepdims=True)
                acc = acc + jnp.dot(
                    vals_t[:, lo:hi], p.astype(BF16), preferred_element_type=F32
                )
            out = jnp.transpose(acc / total)
            logs[i * 2 + head : i * 2 + head + 1, :] = top + jnp.log2(total)
            for c in range(2):
                block = lax.rem(i - place[1] + 4, 4) + 4 * jnp.abs(c - place[2])
                at = pl.ds(pl.multiple_of(block * 128, 128), 128)
                lanes = slice(head * 128, head * 128 + 128)
                out_raw[at, lanes] = out[c * 128 : c * 128 + 128, :]
                out_low[at, lanes] = out[c * 128 : c * 128 + 128, :].astype(BF16)

    @pl.when(place[0] == 1)
    def _():
        for i in range(4):
            queries(0, i)

    @pl.when(place[0] == 0)
    def _():
        for i in range(4):
            queries(1024, i)

    done(out_raw, out_low)


def output_body(ready, done, mixed, packed, a_mine, a_part, w_out):
    ready(packed)
    for f in range(8):
        for m in range(4):
            w_out[f * 32 : f * 32 + 32, m * 256 : m * 256 + 256] = packed[
                f * 128 + m * 32 : f * 128 + m * 32 + 32, :
            ]
    done(w_out)
    ready(mixed)

    def project(t, carry):
        at = pl.ds(pl.multiple_of(t * 256, 256), 256)
        far = pl.ds(pl.multiple_of(512 + t * 256, 256), 256)
        a_part[at, :] = jnp.dot(mixed[far, :], w_out[...], preferred_element_type=F32).astype(BF16)
        a_mine[at, :] = jnp.dot(mixed[at, :], w_out[...], preferred_element_type=F32)
        return carry

    lax.fori_loop(0, 2, project, 0)


def attend_back_body(
    ready, done, place, q_tiles, keys, vals, logs, out_raw, w_out, da_all,
    dq, dk, dv, d_low, dots, keys_t, d_tiles, deltas, dk_acc, dv_acc,
):
    ready(keys)
    keys_t[...] = jnp.transpose(keys[...].astype(F32)).astype(BF16)
    ready(q_tiles, vals, out_raw, w_out, da_all)
    done(da_all)
    for b in range(8):
        rows = slice(b * 128, b * 128 + 128)
        z, c = spot(place, b)
        inner = pl.ds(pl.multiple_of(c * 128, 128), 128)
        d_out = lax.dot_general(
            da_all[rows, :], w_out[...], NT, preferred_element_type=F32
        ).astype(BF16)
        for head in range(2):
            lanes = slice(head * 128, head * 128 + 128)
            grad = d_out[:, lanes]
            d_tiles[z * 2 + head, inner, :] = grad
            deltas[z * 2 + head, pl.ds(c, 1), :] = row_sums(grad.astype(F32) * out_raw[rows, lanes])
    dk_acc[...] = jnp.zeros_like(dk_acc)
    dv_acc[...] = jnp.zeros_like(dv_acc)
    allowed = lax.broadcasted_iota(jnp.int32, (256, 256), 0) <= lax.broadcasted_iota(
        jnp.int32, (256, 256), 1
    )

    def queries(first, i):
        at_diagonal = 1024 + i * 256
        q = [q_tiles[i * 2 + head] for head in range(2)]
        grad = [d_tiles[i * 2 + head] for head in range(2)]
        log = [logs[i * 2 + head : i * 2 + head + 1, :] for head in range(2)]
        delta = [
            jnp.concatenate([deltas[i * 2 + head, 0:1, :], deltas[i * 2 + head, 1:2, :]], axis=1)
            for head in range(2)
        ]
        total = [0.0, 0.0]
        for lo in range(first, at_diagonal + 256, 256):
            at = slice(lo, lo + 256)
            k, v = keys[at, :], vals[at, :]
            dk_tile, dv_tile = dk_acc[at, :], dv_acc[at, :]
            for head in range(2):
                s = lax.dot_general(k, q[head], NT, preferred_element_type=F32)
                p = jnp.exp2(s - log[head])
                if lo == at_diagonal:
                    p = jnp.where(allowed, p, 0.0)
                dp = lax.dot_general(v, grad[head], NT, preferred_element_type=F32)
                ds = (p * (dp - delta[head])).astype(BF16)
                dv_tile += jnp.dot(p.astype(BF16), grad[head], preferred_element_type=F32)
                dk_tile += jnp.dot(ds, q[head], preferred_element_type=F32)
                total[head] = total[head] + jnp.dot(
                    keys_t[:, at], ds, preferred_element_type=F32
                )
            dk_acc[at, :] = dk_tile
            dv_acc[at, :] = dv_tile
        dot = jnp.zeros((1, 256), F32)
        for head in range(2):
            out = jnp.transpose(total[head]) * DH ** (-0.5)
            dot += jnp.sum(total[head] * jnp.transpose(q[head].astype(F32)), axis=0, keepdims=True)
            for c in range(2):
                block = lax.rem(i - place[1] + 4, 4) + 4 * jnp.abs(c - place[2])
                at = pl.ds(pl.multiple_of(block * 128, 128), 128)
                dq[at, head * 128 : head * 128 + 128] = out[c * 128 : c * 128 + 128, :].astype(BF16)
        for c in range(2):
            block = lax.rem(i - place[1] + 4, 4) + 4 * jnp.abs(c - place[2])
            dots[pl.ds(block, 1), :] = dot[:, c * 128 : c * 128 + 128] * (1.0 / LOG2E)

    @pl.when(place[0] == 1)
    def _():
        for i in range(4):
            queries(0, i)

    @pl.when(place[0] == 0)
    def _():
        for i in range(4):
            queries(1024, i)

    for b in range(8):
        rows = slice(b * 128, b * 128 + 128)
        z, c = spot(place, b)
        at = pl.ds(pl.multiple_of(1024 + z * 256 + c * 128, 128), 128)
        key_grad = dk_acc[at, :] * (1.0 / LOG2E)
        dk[rows, :] = key_grad
        dv[rows, :] = dv_acc[at, :]
        dots[8 + b : 9 + b, :] = row_sums(key_grad * keys[at, :].astype(F32))
        key_grad = dk_acc[rows, :] * (1.0 / LOG2E)
        d_low[rows, :128] = key_grad.astype(BF16)
        d_low[rows, 128:] = dv_acc[rows, :].astype(BF16)
        dots[16 + b : 17 + b, :] = row_sums(key_grad * keys[rows, :].astype(F32))


def unproject_body(
    ready, done, place, dq, dk, dv, d_got, q_raw, k_raw, squares, dots, dots_got, cos, sin,
    gain_q, gain_k, x_turned, gains, d_made, sent, sums,
):
    sums[...] = jnp.zeros_like(sums)
    ready(dq, dk, dv, d_got, q_raw, k_raw, cos, sin)

    def step(b, carry):
        rows = pl.ds(pl.multiple_of(b * 128, 128), 128)
        cosine, sine = cos[rows, :], sin[rows, :]
        r = column(root(squares[pl.ds(b, 1), :], 2048.0))
        mean = column(dots[pl.ds(b, 1), :]) * (1.0 / 2048.0)
        for head in range(2):
            lanes = slice(head * 128, head * 128 + 128)
            turn = dq[rows, lanes].astype(F32)
            d_norm = turn * cosine - pltpu.roll(turn, 64, 1) * sine
            hat = q_raw[rows, lanes] * r
            sums[0:1, lanes] += jnp.sum(d_norm * hat, axis=0, keepdims=True)
            d_made[rows, lanes] = (r * (d_norm * gain_q[:, lanes] - hat * mean)).astype(BF16)
        r = column(root(squares[pl.ds(b + 8, 1), :], 1024.0))
        mean = column(dots[pl.ds(b + 8, 1), :] + dots_got[pl.ds(b, 1), :]) * (1.0 / 1024.0)
        turn = dk[rows, :] + d_got[rows, :128].astype(F32)
        d_norm = turn * cosine - pltpu.roll(turn, 64, 1) * sine
        hat = k_raw[rows, :] * r
        sums[0:1, 256:] += jnp.sum(d_norm * hat, axis=0, keepdims=True)
        d_made[rows, 256:384] = (r * (d_norm * gain_k[...] - hat * mean)).astype(BF16)
        d_made[rows, 384:] = (dv[rows, :] + d_got[rows, 128:].astype(F32)).astype(BF16)
        return carry

    lax.fori_loop(0, 8, step, 0)
    done(d_made)
    ready(x_turned, gains)

    def grad(t, carry):
        rows = pl.ds(pl.multiple_of(t * 256, 256), 256)
        sent[rows, :512] = jnp.dot(
            x_turned[rows, :], d_made[...], preferred_element_type=F32
        ).astype(BF16)
        sent[rows, 512:] = gains[rows, :]
        return carry

    lax.fori_loop(0, 4, grad, 0)
    extra = 0.0
    for lo, width, each, first in ((0, 256, 16, 0), (256, 128, 8, 16)):
        row = lax.broadcasted_iota(jnp.int32, (128, width), 0) // 8
        lane = lax.broadcasted_iota(jnp.int32, (128, width), 1) // each
        spread = jnp.where(row == lane, sums[0:1, lo : lo + width], 0.0).astype(BF16)
        lane = lax.broadcasted_iota(jnp.int32, (width, 128), 0) % each + first
        pick = jnp.where(lane == lax.broadcasted_iota(jnp.int32, (width, 128), 1), 1.0, 0.0)
        extra = extra + jnp.dot(spread, pick.astype(BF16), preferred_element_type=F32)
    rows = pl.ds(pl.multiple_of((place[1] * 2 + place[2]) * 128, 128), 128)
    sent[rows, 512:] = (gains[rows, :].astype(F32) + extra).astype(BF16)


def input_body(ready, done, d_made, weight, dx_mine, dx_part):
    ready(d_made, weight)

    def step(t, carry):
        at = pl.ds(pl.multiple_of(t * 256, 256), 256)
        far = pl.ds(pl.multiple_of(512 + t * 256, 256), 256)
        dx_part[at, :] = lax.dot_general(
            d_made[far, :], weight[...], NT, preferred_element_type=F32
        ).astype(BF16)
        dx_mine[at, :] = lax.dot_general(
            d_made[at, :], weight[...], NT, preferred_element_type=F32
        )
        return carry

    lax.fori_loop(0, 2, step, 0)


def expand_body(ready, done, h_all, weight, gate, up, expanded, m_mine, m_part, down):
    ready(weight)
    for f in range(8):
        down[f * 96 : f * 96 + 96, :768] = weight[f * 128 : f * 128 + 96, 1536:2304]
        for m in range(3):
            down[f * 96 + m * 32 : f * 96 + m * 32 + 32, 768:] = weight[
                f * 128 + 96 : f * 128 + 128, 1536 + m * 256 : 1792 + m * 256
            ]

    done(down)
    ready(h_all)
    done(h_all)

    def widen(n, carry):
        lanes = pl.ds(pl.multiple_of(n * 256, 256), 256)
        upper = pl.ds(pl.multiple_of(768 + n * 256, 256), 256)
        g = jnp.dot(h_all[...], weight[:, lanes], preferred_element_type=F32)
        u = jnp.dot(h_all[...], weight[:, upper], preferred_element_type=F32)
        gate[:, lanes] = g
        up[:, lanes] = u
        expanded[:, lanes] = (g * jax.nn.sigmoid(g) * u).astype(BF16)
        return carry

    lax.fori_loop(0, 3, widen, 0)
    done(gate, up, expanded)

    def narrow(n, carry):
        lanes = pl.ds(pl.multiple_of(n * 256, 256), 256)
        m = jnp.dot(expanded[...], down[:, lanes], preferred_element_type=F32)
        m_mine[:, lanes] = m[:256]
        m_part[:, lanes] = m[256:].astype(BF16)
        return carry

    lax.fori_loop(0, 4, narrow, 0)


def expand_back_body(ready, done, dm_all, gate, up, weight, down, d_gu, dh_mine, dh_part):
    ready(dm_all, gate, up, down)
    done(dm_all)

    def widen(n, carry):
        lanes = pl.ds(pl.multiple_of(n * 256, 256), 256)
        upper = pl.ds(pl.multiple_of(768 + n * 256, 256), 256)
        de = lax.dot_general(dm_all[...], down[lanes, :], NT, preferred_element_type=F32)
        g = gate[:, lanes]
        sig = jax.nn.sigmoid(g)
        d_gu[:, lanes] = (de * up[:, lanes] * sig * (1.0 + g * (1.0 - sig))).astype(BF16)
        d_gu[:, upper] = (de * (g * sig)).astype(BF16)
        return carry

    lax.fori_loop(0, 3, widen, 0)
    done(d_gu)
    ready(weight)

    def narrow(n, carry):
        lanes = pl.ds(pl.multiple_of(n * 256, 256), 256)
        dh = lax.dot_general(d_gu[...], weight[lanes, :1536], NT, preferred_element_type=F32)
        dh_mine[:, lanes] = dh[:256]
        dh_part[:, lanes] = dh[256:].astype(BF16)
        return carry

    lax.fori_loop(0, 4, narrow, 0)


def expand_grad_body(ready, done, h_turned, d_gu, expanded, dm_all, out, expanded_t):
    ready(expanded)
    expanded_t[...] = jnp.transpose(expanded[...].astype(F32)).astype(BF16)

    ready(h_turned, d_gu, dm_all)

    def widen(n, carry):
        lanes = pl.ds(pl.multiple_of(n * 256, 256), 256)
        out[:, lanes] = jnp.dot(
            h_turned[...], d_gu[:, lanes], preferred_element_type=F32
        ).astype(BF16)
        return carry

    lax.fori_loop(0, 6, widen, 0)
    for n in range(4):
        made = jnp.dot(
            expanded_t[...], dm_all[:, n * 256 : n * 256 + 256], preferred_element_type=F32
        ).astype(BF16)
        for f in range(16):
            if n < 3:
                out[f * 64 : f * 64 + 48, 1536 + n * 256 : 1792 + n * 256] = made[
                    f * 48 : f * 48 + 48
                ]
                continue
            for m in range(3):
                out[f * 64 + 48 : f * 64 + 64, 1536 + m * 256 : 1792 + m * 256] = made[
                    f * 48 + m * 16 : f * 48 + m * 16 + 16
                ]


def norm_scale(values):
    return lax.rsqrt(jnp.mean(values * values, axis=-1, keepdims=True) + EPS)


def norm_back(upstream, normed, scaling):
    return scaling * (upstream - normed * jnp.mean(upstream * normed, axis=-1, keepdims=True))


def rotary_tables(first, z, c):
    half = DH // 2
    k = jnp.arange(4, dtype=jnp.int32)
    starts = jnp.concatenate([((z + k) % 4) * 256 + c * 128, ((z + k) % 4) * 256 + (1 - c) * 128])
    places = (first + starts[:, None] + jnp.arange(128, dtype=jnp.int32)[None, :]).reshape(1024)
    inverse = THETA ** (-(jnp.arange(half, dtype=F32) * (2.0 / DH)))
    angles = places.astype(F32)[:, None] * inverse[None, :]
    cosine, sine = jnp.cos(angles), jnp.sin(angles)
    return (
        jnp.concatenate([cosine, cosine], axis=-1),
        jnp.concatenate([-sine, sine], axis=-1),
    )


def dot(a, b):
    return jnp.dot(a, b, preferred_element_type=F32)


def dot_nt(a, b):
    return lax.dot_general(a, b, NT, preferred_element_type=F32)


def dot_tn(a, b):
    return lax.dot_general(a, b, (((0,), (0,)), ((), ())), preferred_element_type=F32)


def on_device(
    tokens, out_grad, w_query, w_key, w_value, w_out, w_gate, w_up, w_down,
    gain_query, gain_key, gain_attn, gain_mlp,
):
    seq = lax.axis_index("seq")
    xh, zc = seq // 8, seq % 8
    z, c = zc // 2, zc % 2
    quarter = (z % 2) * 2 + c
    place = jnp.stack([xh, z, c]).astype(jnp.int32)
    inputs = tokens[0]

    def columns(weight, width):
        return lax.dynamic_slice_in_dim(weight, zc * width, width, 1)

    def spread(block):
        return lax.all_to_all(
            jnp.broadcast_to(block[None], (8,) + block.shape),
            "fsdp", split_axis=0, concat_axis=0, tiled=True,
        ).reshape(8 * block.shape[0], block.shape[1])

    x_blocks = gather_group(inputs)
    weight = spread(
        jnp.concatenate(
            [columns(w_query, 256), columns(w_key, 128), columns(w_value, 128)], axis=1
        )
    )
    w_out_rows = lax.ppermute(
        lax.dynamic_slice_in_dim(w_out, zc * 32, 32, 0), ("seq", "fsdp"), TURN
    )
    x_blocks[2], w_gate, w_up, w_down = lax.optimization_barrier(
        (x_blocks[2], w_gate, w_up, w_down)
    )

    def quarters(weight):
        part = lax.dynamic_slice_in_dim(weight.reshape(128, 8, 384), quarter * 96, 96, 2)
        return part.reshape(128, 768)

    down = lax.dynamic_slice_in_dim(w_down, quarter * 96, 96, 0)
    packed = jnp.concatenate(
        [
            down[:, :768],
            jnp.concatenate([down[m * 32 : m * 32 + 32, 768:] for m in range(3)], axis=1),
        ],
        axis=0,
    )
    w_mlp = lax.all_gather(
        jnp.concatenate(
            [
                quarters(w_gate),
                quarters(w_up),
                packed,
                jnp.concatenate([w_out_rows[:, m * 256 : m * 256 + 256] for m in range(4)], axis=0),
            ],
            axis=1,
        ),
        "fsdp", axis=0, tiled=True,
    )

    cosine, sine = rotary_tables(xh * 1024, z, c)
    gain_q = lax.dynamic_slice_in_dim(gain_query, zc * 256, 256, 0)[None]
    gain_k = lax.dynamic_slice_in_dim(gain_key, zc * 128, 128, 0)[None]
    x_all, q_raw, k_raw, q_rot, kv_rot, squares = kernel_call(
        project_body,
        [
            0, shaped((1024, 256), F32), shaped((1024, 128), F32),
            shaped((1024, 256), BF16), shaped((1024, 256), BF16), shaped((16, 128), F32),
        ],
        [x_blocks, weight, gain_q, gain_k, cosine, sine],
        flops=2 * 1024 * 1024 * 512, nbytes=9 << 20,
    )

    kv_low = swap(kv_rot, LOW_TO_HIGH)
    squares = sum_group(squares)
    squares_low = swap(squares[8:], LOW_TO_HIGH)
    out_raw, mixed, q_tiles, keys, vals, logs = kernel_call(
        attend_body,
        [
            shaped((1024, 256), F32), shaped((1024, 256), BF16), shaped((8, 256, 128), BF16),
            shaped((2048, 128), BF16), shaped((2048, 128), BF16), shaped((8, 256), F32),
        ],
        [place, q_rot, kv_rot, kv_low, squares, squares_low],
        [pltpu.VMEM((128, 2048), BF16)],
        flops=4 * 1024 * 2048 * 256, nbytes=9 << 20,
    )
    a_mine, a_part, w_out_rows = kernel_call(
        output_body,
        [shaped((512, 1024), F32), shaped((512, 1024), BF16), shaped((256, 1024), BF16)],
        [mixed, w_mlp[:, 2304:]],
        flops=2 * 1024 * 1024 * 256, nbytes=5 << 20,
    )
    x_turned = x_all.T

    attended = scatter_group(a_mine, a_part)
    attended, x_turned = lax.optimization_barrier((attended, x_turned))
    attn_scale = norm_scale(attended)
    attn_hat = attended * attn_scale
    hidden_state = inputs.astype(F32) + attn_hat * gain_attn
    h_all, gate, up, expanded, m_mine, m_part, w_down_rows = kernel_call(
        expand_body,
        [
            0, shaped((512, 768), F32), shaped((512, 768), F32), shaped((512, 768), BF16),
            shaped((256, 1024), F32), shaped((256, 1024), BF16), shaped((768, 1024), BF16),
        ],
        [gather_pair(hidden_state.astype(BF16)), w_mlp],
        flops=2 * 512 * 2304 * 1024, nbytes=12 << 20,
    )
    projected, _ = scatter_pair(m_mine, m_part)
    mlp_scale = norm_scale(projected)
    mlp_hat = projected * mlp_scale
    output = (hidden_state + mlp_hat * gain_mlp).astype(BF16)[None]

    upstream = out_grad[0].astype(F32)
    grad_gain_mlp = jnp.sum(upstream * mlp_hat, axis=0)
    d_projected = norm_back(upstream * gain_mlp, mlp_hat, mlp_scale).astype(BF16)
    n = jnp.arange(1024, dtype=jnp.int32)
    source = ((n // 8) % 16) * 64 + (n // 128) * 8 + n % 8
    order = (n[None, :] == source[:, None]).astype(BF16)
    h_turned = dot_nt(order, h_all).astype(BF16)
    d_blocks = gather_pair(d_projected)
    d_blocks[3], h_turned = lax.optimization_barrier((d_blocks[3], h_turned))
    dm_all, d_gu, dh_mine, dh_part = kernel_call(
        expand_back_body,
        [
            0, shaped((512, 1536), BF16), shaped((256, 1024), F32), shaped((256, 1024), BF16),
        ],
        [d_blocks, gate, up, w_mlp, w_down_rows],
        flops=2 * 512 * 2304 * 1024, nbytes=12 << 20,
    )

    far = dh_mine[128:] + swap(dh_part[128:], CORE_SWAP).astype(F32)
    far, d_gu, dm_all = lax.optimization_barrier((far.astype(BF16), d_gu, dm_all))
    far = swap(far, Z_SWAP)
    (grad_mlp,) = kernel_call(
        expand_grad_body,
        [shaped((1024, 2304), BF16)],
        [h_turned, d_gu, expanded, dm_all],
        [pltpu.VMEM((768, 512), BF16)],
        flops=2 * 512 * 2304 * 1024, nbytes=9 << 20,
    )
    far, grad_mlp = lax.optimization_barrier((far, grad_mlp))
    grad_mlp = lax.psum_scatter(grad_mlp, "fsdp", scatter_dimension=0, tiled=True)
    d_hidden = upstream + dh_mine[:128] + swap(dh_part[:128], CORE_SWAP).astype(F32)
    d_hidden = d_hidden + far.astype(F32)

    grad_gain_attn = jnp.sum(d_hidden * attn_hat, axis=0)
    d_attended = norm_back(d_hidden * gain_attn, attn_hat, attn_scale).astype(BF16)
    dq, dk, dv, d_low, dots, da_all = kernel_call(
        attend_back_body,
        [
            shaped((1024, 256), BF16), shaped((1024, 128), F32), shaped((1024, 128), F32),
            shaped((1024, 256), BF16), shaped((24, 128), F32), 7,
        ],
        [place, q_tiles, keys, vals, logs, out_raw, w_out_rows, gather_group(d_attended)],
        [
            pltpu.VMEM((128, 2048), BF16), pltpu.VMEM((8, 256, 128), BF16),
            pltpu.VMEM((8, 2, 128), F32), pltpu.VMEM((2048, 128), F32), pltpu.VMEM((2048, 128), F32),
        ],
        flops=10 * 1024 * 2048 * 256, nbytes=8 << 20,
    )
    grad_out = dot_tn(mixed, da_all).astype(BF16).reshape(2, 8, 16, 1024)
    grad_out = lax.psum_scatter(
        jnp.swapaxes(grad_out, 0, 1).reshape(256, 1024), "fsdp", scatter_dimension=0, tiled=True
    ).reshape(2, 16, 1024)
    d_got = swap(d_low, HIGH_TO_LOW)
    dots = sum_group(dots)
    dots_got = swap(dots[16:], HIGH_TO_LOW)

    gains = jnp.concatenate([grad_gain_attn.reshape(128, 8), grad_gain_mlp.reshape(128, 8)], axis=1)
    gains = jnp.broadcast_to(
        jnp.pad(gains.astype(BF16), ((0, 0), (24, 88)))[:, None, :], (128, 8, 128)
    ).reshape(1024, 128)
    d_made, sent = kernel_call(
        unproject_body,
        [shaped((1024, 512), BF16), shaped((1024, 640), BF16)],
        [
            place, dq, dk, dv, d_got, q_raw, k_raw, squares, dots, dots_got, cosine, sine,
            gain_q, gain_k, x_turned, gains,
        ],
        [pltpu.VMEM((8, 384), F32)],
        flops=2 * 1024 * 1024 * 512, nbytes=9 << 20,
    )
    got_made = lax.all_to_all(
        sent.reshape(128, 8, 640), ("seq", "fsdp"), split_axis=0, concat_axis=0, tiled=True
    )
    dx_mine, dx_part = kernel_call(
        input_body,
        [shaped((512, 1024), F32), shaped((512, 1024), BF16)],
        [after(d_made, sent), weight],
        flops=2 * 1024 * 1024 * 512, nbytes=5 << 20,
    )
    d_inputs = scatter_group(dx_mine, dx_part)

    given = jnp.where(xh == 0, grad_out[1], grad_out[0])
    grad_out = jnp.where(xh == 0, grad_out[0], grad_out[1]).astype(F32)
    grad_out = grad_out + swap(given, X_SWAP).astype(F32)
    grad_out = swap(grad_out.astype(BF16), OUT_HOME)

    def halves(value, upper):
        low, high = value[: value.shape[0] // 2], value[value.shape[0] // 2 :]
        return jnp.where(upper, high, low), jnp.where(upper, low, high)

    kept, given = halves(grad_mlp, xh == 1)
    kept = kept.astype(F32) + swap(given, X_SWAP).astype(F32)
    grad_down = jnp.concatenate(
        [
            kept[:48, 1536:],
            jnp.concatenate([kept[48:, 1536 + m * 256 : 1792 + m * 256] for m in range(3)], axis=0),
        ],
        axis=1,
    )
    grad_down, given = halves(grad_down, z >= 2)
    grad_down = grad_down + swap(given.astype(BF16), FAR_SWAP).astype(F32)
    grad_down = lax.ppermute(grad_down.astype(BF16), ("seq", "fsdp"), DOWN_HOME)
    kept, given = halves(kept[:, :1536], z >= 2)
    kept = (kept + swap(given.astype(BF16), FAR_SWAP).astype(F32)).astype(BF16)
    kept, given = halves(kept, z % 2 == 1)
    got = swap(given, Z_SWAP)
    kept = jnp.stack([jnp.where(z % 2 == 1, got, kept), jnp.where(z % 2 == 1, kept, got)])
    kept = kept.reshape(2, 2, 8, 1536)
    given = jnp.where(c == 1, kept[:, 0], kept[:, 1])
    kept = jnp.where(c == 1, kept[:, 1], kept[:, 0])
    got = swap(given, CORE_SWAP)
    got_wide = jnp.stack([jnp.where(c == 1, got, kept), jnp.where(c == 1, kept, got)], axis=1)

    got_made, got_wide, grad_down, grad_out, d_inputs = lax.optimization_barrier(
        (got_made, got_wide, grad_down, grad_out, d_inputs)
    )
    summed = jnp.sum(got_made.reshape(2, 8, 8, 8, 640).astype(F32), axis=(0, 2))
    gains = jnp.sum(summed[:, 0, 512:], axis=0)

    def take(first, width):
        return summed[:, :, first : first + width].swapaxes(0, 1).reshape(8, 8 * width)

    wide = got_wide.astype(F32).reshape(4, 8, 2, 8, 96)
    wide = wide.transpose(2, 1, 3, 0, 4).reshape(2, 8, 3072)
    return (
        output,
        (d_hidden + d_inputs).astype(BF16)[None],
        take(0, 256),
        take(256, 128),
        take(384, 128),
        grad_out.astype(F32),
        wide[0],
        wide[1],
        grad_down.astype(F32),
        gains[:16],
        gains[16:24],
        gains[24:32],
        gains[32:40],
    )


def solution(mesh):
    rows = P("fsdp", "seq", None)
    weight = P("fsdp", None)
    grad = P(("seq", "fsdp"), None)
    gain = P(("seq", "fsdp"))
    return jax.shard_map(
        on_device,
        mesh=mesh,
        in_specs=(rows,) * 2 + (weight,) * 7 + (P(),) * 4,
        out_specs=(rows,) * 2 + (grad,) * 7 + (gain,) * 4,
        check_vma=False,
    )
```

```python
import functools
import math

import jax
import jax.numpy as jnp
from jax import lax
from jax.experimental import pallas as pl
from jax.experimental.pallas import tpu as pltpu
from jax.sharding import PartitionSpec as P

BF16 = jnp.bfloat16
F32 = jnp.float32
DH = 128
EPS = 1e-06
THETA = 1000000.0
MASKED = -1e30
LOG2E = math.log2(math.e)
QUERY_SCALE = DH ** (-0.5) * LOG2E
VMEM_BYTES = 40 * 1024 * 1024
VMEM = pl.BlockSpec(memory_space=pltpu.VMEM)
SMEM = pl.BlockSpec(memory_space=pltpu.SMEM)
ANY = pl.BlockSpec(memory_space=pl.ANY)
SMALL = 64 * 1024
NT = (((1,), (1,)), ((), ()))

SEQ_PLACES = [(xh, z, c) for xh in range(2) for z in range(4) for c in range(2)]


def seq_index(xh, z, c):
    return xh * 8 + (z % 4) * 2 + c


CORE_SWAP = [(i, i ^ 1) for i in range(16)]
LOW_TO_HIGH = [(i, i + 8) for i in range(8)]
HIGH_TO_LOW = [(i + 8, i) for i in range(8)]
X_SWAP = [(i, i ^ 8) for i in range(16)]


def from_z(k):
    return [(seq_index(xh, z + k, c), seq_index(xh, z, c)) for xh, z, c in SEQ_PLACES]


def to_z(k):
    return [(seq_index(xh, z, c), seq_index(xh, z + k, c)) for xh, z, c in SEQ_PLACES]


def across(pairs):
    return [(seq * 8 + f, to_seq * 8 + to_f) for seq, f, to_seq, to_f in pairs]


TURN = across(
    (xh * 8 + a, f, xh * 8 + f, a) for xh in range(2) for a in range(8) for f in range(8)
)
Z_SWAP = [(i, i ^ 2) for i in range(16)]
FAR_SWAP = [(i, i ^ 4) for i in range(16)]
OUT_HOME = [(xh * 8 + a, 2 * a + xh) for xh in range(2) for a in range(8)]
DOWN_HOME = across(
    (seq_index(xh, 2 * zh + zl, c), f, 2 * f + zl, 4 * c + 2 * xh + zh)
    for xh in range(2) for zh in range(2) for zl in range(2) for c in range(2) for f in range(8)
)


def swap(value, pairs):
    return lax.ppermute(value, "seq", pairs)


def after(value, *others):
    return lax.optimization_barrier((value, *others))[0]


def gather_group(block):
    far = {k: swap(block, from_z(k)) for k in (2, 1, 3)}
    mine = [block, far[1], far[2], far[3]]
    return mine + [swap(v, CORE_SWAP) for v in mine]


def scatter_group(mine, part):
    rows = [slice(k * 128, k * 128 + 128) for k in range(4)]
    out = None
    for k in (2, 1, 3, 0):
        piece = mine[rows[k]] + swap(part[rows[k]], CORE_SWAP).astype(F32)
        if k:
            piece = swap(piece.astype(BF16), to_z(k)).astype(F32)
        out = piece if out is None else out + piece
    return out


def gather_pair(block):
    mine = [block, swap(block, Z_SWAP)]
    return mine + [swap(v, CORE_SWAP) for v in mine]


def scatter_pair(mine, part, later=()):
    far = mine[128:] + swap(part[128:], CORE_SWAP).astype(F32)
    far, *later = lax.optimization_barrier((far.astype(BF16), *later))
    far = swap(far, Z_SWAP).astype(F32)
    return mine[:128] + swap(part[:128], CORE_SWAP).astype(F32) + far, later


def sum_group(rows):
    groups = rows.shape[0] // 8
    other = swap(rows, CORE_SWAP).reshape(groups, 2, 4, 128)
    pair = rows.reshape(groups, 2, 4, 128) + jnp.concatenate([other[:, 1:], other[:, :1]], axis=1)
    total = pair
    for k in (2, 1, 3):
        got = swap(pair, from_z(k))
        total = total + jnp.concatenate([got[:, :, 4 - k :], got[:, :, : 4 - k]], axis=2)
    return total.reshape(rows.shape)


def column(row):
    return jnp.transpose(jnp.broadcast_to(row, (128, 128)))


def row_sums(values):
    return jnp.sum(jnp.transpose(values), axis=0, keepdims=True)


def shaped(shape, dtype):
    return jax.ShapeDtypeStruct(shape, dtype)


class Kept:
    def __init__(self, value):
        self.value = value


def in_hbm(*values):
    return [Kept(v) for v in values]


def kernel_call(body, outs, inputs, scratch=(), flops=0, nbytes=0):
    hbm_outs = [isinstance(o, Kept) for o in outs]
    hbm_ins = [isinstance(x, Kept) for x in inputs]
    outs = [o.value if isinstance(o, Kept) else o for o in outs]
    inputs = [x.value if isinstance(x, Kept) else x for x in inputs]
    groups = [x if isinstance(x, list) else [x] for x in inputs]
    flat = [a for group in groups for a in group]
    joined = [
        shaped((sum(a.shape[0] for a in group),) + group[0].shape[1:], group[0].dtype)
        for group in groups
    ]

    def large(s):
        return math.prod(s.shape) * s.dtype.itemsize >= SMALL

    def where(s):
        return ANY if large(s) else SMEM if s.dtype == jnp.int32 else VMEM

    out_shapes = [joined[o] if isinstance(o, int) else o for o in outs]
    in_buffers = [pltpu.VMEM(s.shape, s.dtype) for s in joined if large(s)]
    out_buffers = [
        pltpu.VMEM(o.shape, o.dtype) for o in outs if not isinstance(o, int) and large(o)
    ]

    def whole(*refs):
        refs = list(refs)

        def pull(count):
            taken = refs[:count]
            del refs[:count]
            return taken

        in_refs, out_refs = pull(len(flat)), pull(len(outs))
        in_space, out_space = pull(len(in_buffers)), pull(len(out_buffers))
        own, (in_sem, out_sem) = pull(len(scratch)), refs
        loads, ins, at = {}, [], 0
        for group, s in zip(groups, joined):
            if not large(s):
                ins.append(in_refs[at])
                at += 1
                continue
            space, row = in_space.pop(0), 0
            loads[id(space)] = []
            for a in group:
                copy = pltpu.make_async_copy(
                    in_refs[at], space.at[pl.ds(row, a.shape[0])], in_sem.at[at]
                )
                copy.start()
                loads[id(space)].append(copy)
                row, at = row + a.shape[0], at + 1
            ins.append(space)
        made, stores = [], {}
        for k, (o, s, ref) in enumerate(zip(outs, out_shapes, out_refs)):
            if not large(s):
                made.append(ref)
                continue
            space = ins[o] if isinstance(o, int) else out_space.pop(0)
            stores[id(space)] = pltpu.make_async_copy(space, ref, out_sem.at[k])
            if not isinstance(o, int):
                made.append(space)
        started = []

        def ready(*spaces):
            for space in spaces:
                for copy in loads.pop(id(space), ()):
                    copy.wait()

        def done(*spaces):
            for space in spaces:
                copy = stores.pop(id(space))
                copy.start()
                started.append(copy)

        body(ready, done, *ins, *made, *own)
        for key in list(stores):
            copy = stores.pop(key)
            copy.start()
            started.append(copy)
        for copy in started:
            copy.wait()

    return pl.pallas_call(
        whole,
        out_shape=tuple(
            pltpu.HBM(s.shape, s.dtype) if hbm else s for s, hbm in zip(out_shapes, hbm_outs)
        ),
        in_specs=[where(s) for group, s in zip(groups, joined) for _ in group],
        out_specs=tuple(where(s) for s in out_shapes),
        scratch_shapes=[
            *in_buffers, *out_buffers, *scratch,
            pltpu.SemaphoreType.DMA((len(flat),)), pltpu.SemaphoreType.DMA((len(outs),)),
        ],
        compiler_params=pltpu.CompilerParams(vmem_limit_bytes=VMEM_BYTES),
        cost_estimate=pl.CostEstimate(flops=flops, bytes_accessed=nbytes, transcendentals=0),
    )(
        *[
            pltpu.with_memory_space_constraint(a, pltpu.HBM) if hbm else a
            for group, hbm in zip(groups, hbm_ins)
            for a in group
        ]
    )


def root(total, width):
    return lax.rsqrt(total * (1.0 / width) + EPS)


def project_body(
    ready, done, x_all, weight, gain_q, gain_k, cos, sin,
    q_raw, k_raw, q_rot, kv_rot, squares,
):
    ready(x_all, weight, cos, sin)
    done(x_all)

    def step(t, carry):
        at = pl.multiple_of(t * 256, 256)
        made = jnp.dot(x_all[pl.ds(at, 256), :], weight[...], preferred_element_type=F32)
        for part in range(2):
            rows = pl.ds(at + part * 128, 128)
            block = t * 2 + part
            here = made[part * 128 : part * 128 + 128]
            q, k = here[:, :256], here[:, 256:384]
            kv_rot[rows, 128:] = here[:, 384:].astype(BF16)
            q_raw[rows, :] = q
            k_raw[rows, :] = k
            squares[pl.ds(block, 1), :] = row_sums(
                q[:, :128] * q[:, :128] + q[:, 128:] * q[:, 128:]
            )
            squares[pl.ds(block + 8, 1), :] = row_sums(k * k)
            cosine, sine = cos[rows, :], sin[rows, :]
            for head in range(2):
                lanes = slice(head * 128, head * 128 + 128)
                turn = q[:, lanes] * gain_q[:, lanes]
                q_rot[rows, lanes] = (turn * cosine + pltpu.roll(turn, 64, 1) * sine).astype(BF16)
            turn = k * gain_k[...]
            kv_rot[rows, :128] = (turn * cosine + pltpu.roll(turn, 64, 1) * sine).astype(BF16)
        return carry

    lax.fori_loop(0, 4, step, 0)


def spot(place, block):
    z = lax.rem(place[1] + block % 4, 4)
    c = place[2] if block < 4 else 1 - place[2]
    return z, c


def attend_body(
    ready, done, place, q_rot, kv_rot, kv_low, squares, squares_low,
    out_raw, out_low, q_tiles, keys, vals, logs, vals_t,
):
    ready(q_rot, kv_rot, kv_low)
    for b in range(8):
        rows = slice(b * 128, b * 128 + 128)
        z, c = spot(place, b)
        r = column(root(squares[b : b + 1, :], 2048.0)) * QUERY_SCALE
        inner = pl.ds(pl.multiple_of(c * 128, 128), 128)
        for head in range(2):
            q = q_rot[rows, head * 128 : head * 128 + 128].astype(F32)
            q_tiles[z * 2 + head, inner, :] = (q * r).astype(BF16)
        at = pl.ds(pl.multiple_of(1024 + z * 256 + c * 128, 128), 128)
        r = column(root(squares[8 + b : 9 + b, :], 1024.0))
        keys[at, :] = (kv_rot[rows, :128].astype(F32) * r).astype(BF16)
        vals[at, :] = kv_rot[rows, 128:]
        r = column(root(squares_low[b : b + 1, :], 1024.0))
        keys[rows, :] = (kv_low[rows, :128].astype(F32) * r).astype(BF16)
        vals[rows, :] = kv_low[rows, 128:]
    done(q_tiles, keys, vals)
    vals_t[...] = jnp.transpose(vals[...].astype(F32)).astype(BF16)
    allowed = lax.broadcasted_iota(jnp.int32, (256, 256), 0) <= lax.broadcasted_iota(
        jnp.int32, (256, 256), 1
    )

    def queries(first, i):
        at_diagonal = 1024 + i * 256
        ranges = [(first, at_diagonal)] if at_diagonal > first else []
        for head in range(2):
            q = q_tiles[i * 2 + head]
            scores = [
                lax.dot_general(keys[lo:hi, :], q, NT, preferred_element_type=F32)
                for lo, hi in ranges + [(at_diagonal, at_diagonal + 256)]
            ]
            scores[-1] = jnp.where(allowed, scores[-1], MASKED)
            tops = [jnp.max(s, axis=0, keepdims=True) for s in scores]
            top = functools.reduce(jnp.maximum, tops)
            total, acc = 0.0, 0.0
            for s, (lo, hi) in zip(scores, ranges + [(at_diagonal, at_diagonal + 256)]):
                p = jnp.exp2(s - top)
                total = total + jnp.sum(p, axis=0, keepdims=True)
                acc = acc + jnp.dot(
                    vals_t[:, lo:hi], p.astype(BF16), preferred_element_type=F32
                )
            out = jnp.transpose(acc / total)
            logs[i * 2 + head : i * 2 + head + 1, :] = top + jnp.log2(total)
            for c in range(2):
                block = lax.rem(i - place[1] + 4, 4) + 4 * jnp.abs(c - place[2])
                at = pl.ds(pl.multiple_of(block * 128, 128), 128)
                lanes = slice(head * 128, head * 128 + 128)
                out_raw[at, lanes] = out[c * 128 : c * 128 + 128, :]
                out_low[at, lanes] = out[c * 128 : c * 128 + 128, :].astype(BF16)

    @pl.when(place[0] == 1)
    def _():
        for i in range(4):
            queries(0, i)

    @pl.when(place[0] == 0)
    def _():
        for i in range(4):
            queries(1024, i)

    done(out_raw, out_low)


def output_body(ready, done, mixed, w_out, a_mine, a_part):
    ready(mixed, w_out)

    def project(t, carry):
        at = pl.ds(pl.multiple_of(t * 256, 256), 256)
        far = pl.ds(pl.multiple_of(512 + t * 256, 256), 256)
        a_part[at, :] = jnp.dot(mixed[far, :], w_out[...], preferred_element_type=F32).astype(BF16)
        a_mine[at, :] = jnp.dot(mixed[at, :], w_out[...], preferred_element_type=F32)
        return carry

    lax.fori_loop(0, 2, project, 0)


def attend_back_body(
    ready, done, place, q_tiles, keys, vals, logs, out_raw, w_out, da_all,
    dq, dk, dv, d_low, dots, keys_t, d_tiles, deltas, dk_acc, dv_acc,
):
    ready(keys)
    keys_t[...] = jnp.transpose(keys[...].astype(F32)).astype(BF16)
    ready(q_tiles, vals, out_raw, w_out, da_all)
    done(da_all)
    for b in range(8):
        rows = slice(b * 128, b * 128 + 128)
        z, c = spot(place, b)
        inner = pl.ds(pl.multiple_of(c * 128, 128), 128)
        d_out = lax.dot_general(
            da_all[rows, :], w_out[...], NT, preferred_element_type=F32
        ).astype(BF16)
        for head in range(2):
            lanes = slice(head * 128, head * 128 + 128)
            grad = d_out[:, lanes]
            d_tiles[z * 2 + head, inner, :] = grad
            deltas[z * 2 + head, pl.ds(c, 1), :] = row_sums(grad.astype(F32) * out_raw[rows, lanes])
    dk_acc[...] = jnp.zeros_like(dk_acc)
    dv_acc[...] = jnp.zeros_like(dv_acc)
    allowed = lax.broadcasted_iota(jnp.int32, (256, 256), 0) <= lax.broadcasted_iota(
        jnp.int32, (256, 256), 1
    )

    def queries(first, i):
        at_diagonal = 1024 + i * 256
        q = [q_tiles[i * 2 + head] for head in range(2)]
        grad = [d_tiles[i * 2 + head] for head in range(2)]
        log = [logs[i * 2 + head : i * 2 + head + 1, :] for head in range(2)]
        delta = [
            jnp.concatenate([deltas[i * 2 + head, 0:1, :], deltas[i * 2 + head, 1:2, :]], axis=1)
            for head in range(2)
        ]
        total = [0.0, 0.0]
        for lo in range(first, at_diagonal + 256, 256):
            at = slice(lo, lo + 256)
            k, v = keys[at, :], vals[at, :]
            dk_tile, dv_tile = dk_acc[at, :], dv_acc[at, :]
            for head in range(2):
                s = lax.dot_general(k, q[head], NT, preferred_element_type=F32)
                p = jnp.exp2(s - log[head])
                if lo == at_diagonal:
                    p = jnp.where(allowed, p, 0.0)
                dp = lax.dot_general(v, grad[head], NT, preferred_element_type=F32)
                ds = (p * (dp - delta[head])).astype(BF16)
                dv_tile += jnp.dot(p.astype(BF16), grad[head], preferred_element_type=F32)
                dk_tile += jnp.dot(ds, q[head], preferred_element_type=F32)
                total[head] = total[head] + jnp.dot(
                    keys_t[:, at], ds, preferred_element_type=F32
                )
            dk_acc[at, :] = dk_tile
            dv_acc[at, :] = dv_tile
        dot = jnp.zeros((1, 256), F32)
        for head in range(2):
            out = jnp.transpose(total[head]) * DH ** (-0.5)
            dot += jnp.sum(total[head] * jnp.transpose(q[head].astype(F32)), axis=0, keepdims=True)
            for c in range(2):
                block = lax.rem(i - place[1] + 4, 4) + 4 * jnp.abs(c - place[2])
                at = pl.ds(pl.multiple_of(block * 128, 128), 128)
                dq[at, head * 128 : head * 128 + 128] = out[c * 128 : c * 128 + 128, :].astype(BF16)
        for c in range(2):
            block = lax.rem(i - place[1] + 4, 4) + 4 * jnp.abs(c - place[2])
            dots[pl.ds(block, 1), :] = dot[:, c * 128 : c * 128 + 128] * (1.0 / LOG2E)

    @pl.when(place[0] == 1)
    def _():
        for i in range(4):
            queries(0, i)

    @pl.when(place[0] == 0)
    def _():
        for i in range(4):
            queries(1024, i)

    for b in range(8):
        rows = slice(b * 128, b * 128 + 128)
        z, c = spot(place, b)
        at = pl.ds(pl.multiple_of(1024 + z * 256 + c * 128, 128), 128)
        key_grad = dk_acc[at, :] * (1.0 / LOG2E)
        dk[rows, :] = key_grad
        dv[rows, :] = dv_acc[at, :]
        dots[8 + b : 9 + b, :] = row_sums(key_grad * keys[at, :].astype(F32))
        key_grad = dk_acc[rows, :] * (1.0 / LOG2E)
        d_low[rows, :128] = key_grad.astype(BF16)
        d_low[rows, 128:] = dv_acc[rows, :].astype(BF16)
        dots[16 + b : 17 + b, :] = row_sums(key_grad * keys[rows, :].astype(F32))


def unproject_body(
    ready, done, place, dq, dk, dv, d_got, q_raw, k_raw, squares, dots, dots_got, cos, sin,
    gain_q, gain_k, x_turned, gains, d_made, sent, sums,
):
    sums[...] = jnp.zeros_like(sums)
    ready(dq, dk, dv, d_got, q_raw, k_raw, cos, sin)

    def step(b, carry):
        rows = pl.ds(pl.multiple_of(b * 128, 128), 128)
        cosine, sine = cos[rows, :], sin[rows, :]
        r = column(root(squares[pl.ds(b, 1), :], 2048.0))
        mean = column(dots[pl.ds(b, 1), :]) * (1.0 / 2048.0)
        for head in range(2):
            lanes = slice(head * 128, head * 128 + 128)
            turn = dq[rows, lanes].astype(F32)
            d_norm = turn * cosine - pltpu.roll(turn, 64, 1) * sine
            hat = q_raw[rows, lanes] * r
            sums[0:1, lanes] += jnp.sum(d_norm * hat, axis=0, keepdims=True)
            d_made[rows, lanes] = (r * (d_norm * gain_q[:, lanes] - hat * mean)).astype(BF16)
        r = column(root(squares[pl.ds(b + 8, 1), :], 1024.0))
        mean = column(dots[pl.ds(b + 8, 1), :] + dots_got[pl.ds(b, 1), :]) * (1.0 / 1024.0)
        turn = dk[rows, :] + d_got[rows, :128].astype(F32)
        d_norm = turn * cosine - pltpu.roll(turn, 64, 1) * sine
        hat = k_raw[rows, :] * r
        sums[0:1, 256:] += jnp.sum(d_norm * hat, axis=0, keepdims=True)
        d_made[rows, 256:384] = (r * (d_norm * gain_k[...] - hat * mean)).astype(BF16)
        d_made[rows, 384:] = (dv[rows, :] + d_got[rows, 128:].astype(F32)).astype(BF16)
        return carry

    lax.fori_loop(0, 8, step, 0)
    done(d_made)
    ready(x_turned, gains)

    def grad(t, carry):
        rows = pl.ds(pl.multiple_of(t * 256, 256), 256)
        sent[rows, :512] = jnp.dot(
            x_turned[rows, :], d_made[...], preferred_element_type=F32
        ).astype(BF16)
        sent[rows, 512:] = gains[rows, :]
        return carry

    lax.fori_loop(0, 4, grad, 0)
    extra = 0.0
    for lo, width, each, first in ((0, 256, 16, 0), (256, 128, 8, 16)):
        row = lax.broadcasted_iota(jnp.int32, (128, width), 0) // 8
        lane = lax.broadcasted_iota(jnp.int32, (128, width), 1) // each
        spread = jnp.where(row == lane, sums[0:1, lo : lo + width], 0.0).astype(BF16)
        lane = lax.broadcasted_iota(jnp.int32, (width, 128), 0) % each + first
        pick = jnp.where(lane == lax.broadcasted_iota(jnp.int32, (width, 128), 1), 1.0, 0.0)
        extra = extra + jnp.dot(spread, pick.astype(BF16), preferred_element_type=F32)
    rows = pl.ds(pl.multiple_of((place[1] * 2 + place[2]) * 128, 128), 128)
    sent[rows, 512:] = (gains[rows, :].astype(F32) + extra).astype(BF16)


def input_body(ready, done, d_made, weight, dx_mine, dx_part):
    ready(d_made, weight)

    def step(t, carry):
        at = pl.ds(pl.multiple_of(t * 256, 256), 256)
        far = pl.ds(pl.multiple_of(512 + t * 256, 256), 256)
        dx_part[at, :] = lax.dot_general(
            d_made[far, :], weight[...], NT, preferred_element_type=F32
        ).astype(BF16)
        dx_mine[at, :] = lax.dot_general(
            d_made[at, :], weight[...], NT, preferred_element_type=F32
        )
        return carry

    lax.fori_loop(0, 2, step, 0)


def expand_body(ready, done, h_all, weight, gate, up, expanded, m_mine, m_part, down):
    ready(weight)
    for f in range(8):
        down[f * 96 : f * 96 + 96, :768] = weight[f * 128 : f * 128 + 96, 1536:2304]
        for m in range(3):
            down[f * 96 + m * 32 : f * 96 + m * 32 + 32, 768:] = weight[
                f * 128 + 96 : f * 128 + 128, 1536 + m * 256 : 1792 + m * 256
            ]

    done(down)
    ready(h_all)
    done(h_all)

    def widen(n, carry):
        lanes = pl.ds(pl.multiple_of(n * 256, 256), 256)
        upper = pl.ds(pl.multiple_of(768 + n * 256, 256), 256)
        g = jnp.dot(h_all[...], weight[:, lanes], preferred_element_type=F32)
        u = jnp.dot(h_all[...], weight[:, upper], preferred_element_type=F32)
        gate[:, lanes] = g
        up[:, lanes] = u
        expanded[:, lanes] = (g * jax.nn.sigmoid(g) * u).astype(BF16)
        return carry

    lax.fori_loop(0, 3, widen, 0)
    done(gate, up, expanded)

    def narrow(n, carry):
        lanes = pl.ds(pl.multiple_of(n * 256, 256), 256)
        m = jnp.dot(expanded[...], down[:, lanes], preferred_element_type=F32)
        m_mine[:, lanes] = m[:256]
        m_part[:, lanes] = m[256:].astype(BF16)
        return carry

    lax.fori_loop(0, 4, narrow, 0)


def expand_back_body(ready, done, dm_all, gate, up, weight, down, d_gu, dh_mine, dh_part):
    ready(dm_all, gate, up, down)
    done(dm_all)

    def widen(n, carry):
        lanes = pl.ds(pl.multiple_of(n * 256, 256), 256)
        upper = pl.ds(pl.multiple_of(768 + n * 256, 256), 256)
        de = lax.dot_general(dm_all[...], down[lanes, :], NT, preferred_element_type=F32)
        g = gate[:, lanes]
        sig = jax.nn.sigmoid(g)
        d_gu[:, lanes] = (de * up[:, lanes] * sig * (1.0 + g * (1.0 - sig))).astype(BF16)
        d_gu[:, upper] = (de * (g * sig)).astype(BF16)
        return carry

    lax.fori_loop(0, 3, widen, 0)
    done(d_gu)
    ready(weight)

    def narrow(n, carry):
        lanes = pl.ds(pl.multiple_of(n * 256, 256), 256)
        dh = lax.dot_general(d_gu[...], weight[lanes, :1536], NT, preferred_element_type=F32)
        dh_mine[:, lanes] = dh[:256]
        dh_part[:, lanes] = dh[256:].astype(BF16)
        return carry

    lax.fori_loop(0, 4, narrow, 0)


def expand_grad_body(ready, done, h_turned, d_gu, expanded, dm_all, out, expanded_t):
    ready(expanded)
    expanded_t[...] = jnp.transpose(expanded[...].astype(F32)).astype(BF16)

    ready(h_turned, d_gu, dm_all)

    def widen(n, carry):
        lanes = pl.ds(pl.multiple_of(n * 256, 256), 256)
        out[:, lanes] = jnp.dot(
            h_turned[...], d_gu[:, lanes], preferred_element_type=F32
        ).astype(BF16)
        return carry

    lax.fori_loop(0, 6, widen, 0)
    for n in range(4):
        made = jnp.dot(
            expanded_t[...], dm_all[:, n * 256 : n * 256 + 256], preferred_element_type=F32
        ).astype(BF16)
        for f in range(16):
            if n < 3:
                out[f * 64 : f * 64 + 48, 1536 + n * 256 : 1792 + n * 256] = made[
                    f * 48 : f * 48 + 48
                ]
                continue
            for m in range(3):
                out[f * 64 + 48 : f * 64 + 64, 1536 + m * 256 : 1792 + m * 256] = made[
                    f * 48 + m * 16 : f * 48 + m * 16 + 16
                ]


def norm_scale(values):
    return lax.rsqrt(jnp.mean(values * values, axis=-1, keepdims=True) + EPS)


def norm_back(upstream, normed, scaling):
    return scaling * (upstream - normed * jnp.mean(upstream * normed, axis=-1, keepdims=True))


def rotary_tables(first, z, c):
    half = DH // 2
    k = jnp.arange(4, dtype=jnp.int32)
    starts = jnp.concatenate([((z + k) % 4) * 256 + c * 128, ((z + k) % 4) * 256 + (1 - c) * 128])
    places = (first + starts[:, None] + jnp.arange(128, dtype=jnp.int32)[None, :]).reshape(1024)
    inverse = THETA ** (-(jnp.arange(half, dtype=F32) * (2.0 / DH)))
    angles = places.astype(F32)[:, None] * inverse[None, :]
    cosine, sine = jnp.cos(angles), jnp.sin(angles)
    return (
        jnp.concatenate([cosine, cosine], axis=-1),
        jnp.concatenate([-sine, sine], axis=-1),
    )


def dot(a, b):
    return jnp.dot(a, b, preferred_element_type=F32)


def dot_nt(a, b):
    return lax.dot_general(a, b, NT, preferred_element_type=F32)


def dot_tn(a, b):
    return lax.dot_general(a, b, (((0,), (0,)), ((), ())), preferred_element_type=F32)


def on_device(
    tokens, out_grad, w_query, w_key, w_value, w_out, w_gate, w_up, w_down,
    gain_query, gain_key, gain_attn, gain_mlp,
):
    seq = lax.axis_index("seq")
    xh, zc = seq // 8, seq % 8
    z, c = zc // 2, zc % 2
    quarter = (z % 2) * 2 + c
    place = jnp.stack([xh, z, c]).astype(jnp.int32)
    inputs = tokens[0]

    def columns(weight, width):
        return lax.dynamic_slice_in_dim(weight, zc * width, width, 1)

    def spread(block):
        return lax.all_to_all(
            jnp.broadcast_to(block[None], (8,) + block.shape),
            "fsdp", split_axis=0, concat_axis=0, tiled=True,
        ).reshape(8 * block.shape[0], block.shape[1])

    x_blocks = gather_group(inputs)
    weight = spread(
        jnp.concatenate(
            [columns(w_query, 256), columns(w_key, 128), columns(w_value, 128)], axis=1
        )
    )
    w_out_rows = lax.ppermute(
        lax.dynamic_slice_in_dim(w_out, zc * 32, 32, 0), ("seq", "fsdp"), TURN
    )
    x_blocks[1:4], weight, w_out_rows, w_gate, w_up, w_down = lax.optimization_barrier(
        (x_blocks[1:4], weight, w_out_rows, w_gate, w_up, w_down)
    )

    def quarters(weight):
        part = lax.dynamic_slice_in_dim(weight.reshape(128, 8, 384), quarter * 96, 96, 2)
        return part.reshape(128, 768)

    down = lax.dynamic_slice_in_dim(w_down, quarter * 96, 96, 0)
    packed = jnp.concatenate(
        [
            down[:, :768],
            jnp.concatenate([down[m * 32 : m * 32 + 32, 768:] for m in range(3)], axis=1),
        ],
        axis=0,
    )
    w_mlp = lax.all_gather(
        jnp.concatenate(
            [
                quarters(w_gate),
                quarters(w_up),
                packed,
            ],
            axis=1,
        ),
        "fsdp", axis=0, tiled=True,
    )

    cosine, sine = rotary_tables(xh * 1024, z, c)
    gain_q = lax.dynamic_slice_in_dim(gain_query, zc * 256, 256, 0)[None]
    gain_k = lax.dynamic_slice_in_dim(gain_key, zc * 128, 128, 0)[None]
    x_all, q_raw, k_raw, q_rot, kv_rot, squares = kernel_call(
        project_body,
        [
            *in_hbm(0, shaped((1024, 256), F32), shaped((1024, 128), F32)),
            shaped((1024, 256), BF16), shaped((1024, 256), BF16), shaped((16, 128), F32),
        ],
        [x_blocks, weight, gain_q, gain_k, cosine, sine],
        flops=2 * 1024 * 1024 * 512, nbytes=9 << 20,
    )

    kv_low = swap(kv_rot, LOW_TO_HIGH)
    squares = sum_group(squares)
    squares, w_out_rows = lax.optimization_barrier((squares, w_out_rows))
    squares_low = swap(squares[8:], LOW_TO_HIGH)
    w_out_rows = spread(w_out_rows)
    out_raw, mixed, q_tiles, keys, vals, logs = kernel_call(
        attend_body,
        [
            *in_hbm(
                shaped((1024, 256), F32), shaped((1024, 256), BF16), shaped((8, 256, 128), BF16),
                shaped((2048, 128), BF16), shaped((2048, 128), BF16),
            ),
            shaped((8, 256), F32),
        ],
        [place, q_rot, kv_rot, kv_low, squares, squares_low],
        [pltpu.VMEM((128, 2048), BF16)],
        flops=4 * 1024 * 2048 * 256, nbytes=9 << 20,
    )
    a_mine, a_part = kernel_call(
        output_body,
        [shaped((512, 1024), F32), shaped((512, 1024), BF16)],
        [*in_hbm(mixed), w_out_rows],
        flops=2 * 1024 * 1024 * 256, nbytes=5 << 20,
    )
    x_turned = x_all.T

    attended = scatter_group(a_mine, a_part)
    attended, x_turned = lax.optimization_barrier((attended, x_turned))
    attn_scale = norm_scale(attended)
    attn_hat = attended * attn_scale
    hidden_state = inputs.astype(F32) + attn_hat * gain_attn
    h_all, gate, up, expanded, m_mine, m_part, w_down_rows = kernel_call(
        expand_body,
        [
            0, shaped((512, 768), F32), shaped((512, 768), F32), shaped((512, 768), BF16),
            shaped((256, 1024), F32), shaped((256, 1024), BF16), shaped((768, 1024), BF16),
        ],
        [gather_pair(hidden_state.astype(BF16)), w_mlp],
        flops=2 * 512 * 2304 * 1024, nbytes=12 << 20,
    )
    projected, _ = scatter_pair(m_mine, m_part)
    mlp_scale = norm_scale(projected)
    mlp_hat = projected * mlp_scale
    output = (hidden_state + mlp_hat * gain_mlp).astype(BF16)[None]

    upstream = out_grad[0].astype(F32)
    grad_gain_mlp = jnp.sum(upstream * mlp_hat, axis=0)
    d_projected = norm_back(upstream * gain_mlp, mlp_hat, mlp_scale).astype(BF16)
    n = jnp.arange(1024, dtype=jnp.int32)
    source = ((n // 8) % 16) * 64 + (n // 128) * 8 + n % 8
    order = (n[None, :] == source[:, None]).astype(BF16)
    h_turned = dot_nt(order, h_all).astype(BF16)
    d_blocks = gather_pair(d_projected)
    d_blocks[3], h_turned = lax.optimization_barrier((d_blocks[3], h_turned))
    dm_all, d_gu, dh_mine, dh_part = kernel_call(
        expand_back_body,
        [
            0, shaped((512, 1536), BF16), shaped((256, 1024), F32), shaped((256, 1024), BF16),
        ],
        [d_blocks, gate, up, w_mlp, w_down_rows],
        flops=2 * 512 * 2304 * 1024, nbytes=12 << 20,
    )

    far = dh_mine[128:] + swap(dh_part[128:], CORE_SWAP).astype(F32)
    far, d_gu, dm_all = lax.optimization_barrier((far.astype(BF16), d_gu, dm_all))
    far = swap(far, Z_SWAP)
    (grad_mlp,) = kernel_call(
        expand_grad_body,
        [shaped((1024, 2304), BF16)],
        [h_turned, d_gu, expanded, dm_all],
        [pltpu.VMEM((768, 512), BF16)],
        flops=2 * 512 * 2304 * 1024, nbytes=9 << 20,
    )
    far, grad_mlp = lax.optimization_barrier((far, grad_mlp))
    grad_mlp = lax.psum_scatter(grad_mlp, "fsdp", scatter_dimension=0, tiled=True)
    d_hidden = upstream + dh_mine[:128] + swap(dh_part[:128], CORE_SWAP).astype(F32)
    d_hidden = d_hidden + far.astype(F32)

    grad_gain_attn = jnp.sum(d_hidden * attn_hat, axis=0)
    d_attended = norm_back(d_hidden * gain_attn, attn_hat, attn_scale).astype(BF16)
    dq, dk, dv, d_low, dots, da_all = kernel_call(
        attend_back_body,
        [
            shaped((1024, 256), BF16), shaped((1024, 128), F32), shaped((1024, 128), F32),
            shaped((1024, 256), BF16), shaped((24, 128), F32), 7,
        ],
        [
            place, *in_hbm(q_tiles, keys, vals), logs, *in_hbm(out_raw), w_out_rows,
            gather_group(d_attended),
        ],
        [
            pltpu.VMEM((128, 2048), BF16), pltpu.VMEM((8, 256, 128), BF16),
            pltpu.VMEM((8, 2, 128), F32), pltpu.VMEM((2048, 128), F32), pltpu.VMEM((2048, 128), F32),
        ],
        flops=10 * 1024 * 2048 * 256, nbytes=8 << 20,
    )
    grad_out = dot_tn(mixed, da_all).astype(BF16).reshape(2, 8, 16, 1024)
    grad_mlp, grad_out = lax.optimization_barrier((grad_mlp, grad_out))
    grad_out = lax.psum_scatter(
        jnp.swapaxes(grad_out, 0, 1).reshape(256, 1024), "fsdp", scatter_dimension=0, tiled=True
    ).reshape(2, 16, 1024)
    d_got = swap(d_low, HIGH_TO_LOW)
    dots = sum_group(dots)
    dots_got = swap(dots[16:], HIGH_TO_LOW)

    gains = jnp.concatenate([grad_gain_attn.reshape(128, 8), grad_gain_mlp.reshape(128, 8)], axis=1)
    gains = jnp.broadcast_to(
        jnp.pad(gains.astype(BF16), ((0, 0), (24, 88)))[:, None, :], (128, 8, 128)
    ).reshape(1024, 128)
    d_made, sent = kernel_call(
        unproject_body,
        [shaped((1024, 512), BF16), shaped((1024, 640), BF16)],
        [
            place, dq, dk, dv, d_got, *in_hbm(q_raw, k_raw), squares, dots, dots_got, cosine, sine,
            gain_q, gain_k, *in_hbm(x_turned), gains,
        ],
        [pltpu.VMEM((8, 384), F32)],
        flops=2 * 1024 * 1024 * 512, nbytes=9 << 20,
    )
    got_made = lax.all_to_all(
        sent.reshape(128, 8, 640), ("seq", "fsdp"), split_axis=0, concat_axis=0, tiled=True
    )
    dx_mine, dx_part = kernel_call(
        input_body,
        [shaped((512, 1024), F32), shaped((512, 1024), BF16)],
        [after(d_made, sent), weight],
        flops=2 * 1024 * 1024 * 512, nbytes=5 << 20,
    )
    d_inputs = scatter_group(dx_mine, dx_part)

    given = jnp.where(xh == 0, grad_out[1], grad_out[0])
    grad_out = jnp.where(xh == 0, grad_out[0], grad_out[1]).astype(F32)
    grad_out = grad_out + swap(given, X_SWAP).astype(F32)
    grad_out = swap(grad_out.astype(BF16), OUT_HOME)

    def halves(value, upper):
        low, high = value[: value.shape[0] // 2], value[value.shape[0] // 2 :]
        return jnp.where(upper, high, low), jnp.where(upper, low, high)

    kept, given = halves(grad_mlp, xh == 1)
    kept = kept.astype(F32) + swap(given, X_SWAP).astype(F32)
    grad_down = jnp.concatenate(
        [
            kept[:48, 1536:],
            jnp.concatenate([kept[48:, 1536 + m * 256 : 1792 + m * 256] for m in range(3)], axis=0),
        ],
        axis=1,
    )
    grad_down, given = halves(grad_down, z >= 2)
    grad_down = grad_down + swap(given.astype(BF16), FAR_SWAP).astype(F32)
    grad_down = lax.ppermute(grad_down.astype(BF16), ("seq", "fsdp"), DOWN_HOME)
    kept, given = halves(kept[:, :1536], z >= 2)
    kept = (kept + swap(given.astype(BF16), FAR_SWAP).astype(F32)).astype(BF16)
    kept, given = halves(kept, z % 2 == 1)
    got = swap(given, Z_SWAP)
    kept = jnp.stack([jnp.where(z % 2 == 1, got, kept), jnp.where(z % 2 == 1, kept, got)])
    kept = kept.reshape(2, 2, 8, 1536)
    given = jnp.where(c == 1, kept[:, 0], kept[:, 1])
    kept = jnp.where(c == 1, kept[:, 1], kept[:, 0])
    got = swap(given, CORE_SWAP)
    got_wide = jnp.stack([jnp.where(c == 1, got, kept), jnp.where(c == 1, kept, got)], axis=1)

    got_made, got_wide, grad_down, grad_out, d_inputs = lax.optimization_barrier(
        (got_made, got_wide, grad_down, grad_out, d_inputs)
    )
    summed = jnp.sum(got_made.reshape(2, 8, 8, 8, 640).astype(F32), axis=(0, 2))
    gains = jnp.sum(summed[:, 0, 512:], axis=0)

    def take(first, width):
        return summed[:, :, first : first + width].swapaxes(0, 1).reshape(8, 8 * width)

    wide = got_wide.astype(F32).reshape(4, 8, 2, 8, 96)
    wide = wide.transpose(2, 1, 3, 0, 4).reshape(2, 8, 3072)
    return (
        output,
        (d_hidden + d_inputs).astype(BF16)[None],
        take(0, 256),
        take(256, 128),
        take(384, 128),
        grad_out.astype(F32),
        wide[0],
        wide[1],
        grad_down.astype(F32),
        gains[:16],
        gains[16:24],
        gains[24:32],
        gains[32:40],
    )


def solution(mesh):
    rows = P("fsdp", "seq", None)
    weight = P("fsdp", None)
    grad = P(("seq", "fsdp"), None)
    gain = P(("seq", "fsdp"))
    return jax.shard_map(
        on_device,
        mesh=mesh,
        in_specs=(rows,) * 2 + (weight,) * 7 + (P(),) * 4,
        out_specs=(rows,) * 2 + (grad,) * 7 + (gain,) * 4,
        check_vma=False,
    )
```

```python
import functools
import math

import jax
import jax.numpy as jnp
from jax import lax
from jax.experimental import pallas as pl
from jax.experimental.pallas import tpu as pltpu
from jax.sharding import PartitionSpec as P

BF16 = jnp.bfloat16
F32 = jnp.float32
DH = 128
EPS = 1e-06
THETA = 1000000.0
MASKED = -1e30
LOG2E = math.log2(math.e)
QUERY_SCALE = DH ** (-0.5) * LOG2E
VMEM_BYTES = 20 * 1024 * 1024
VMEM = pl.BlockSpec(memory_space=pltpu.VMEM)
SMEM = pl.BlockSpec(memory_space=pltpu.SMEM)
ANY = pl.BlockSpec(memory_space=pl.ANY)
SMALL = 64 * 1024
NT = (((1,), (1,)), ((), ()))

SEQ_PLACES = [(xh, z, c) for xh in range(2) for z in range(4) for c in range(2)]


def seq_index(xh, z, c):
    return xh * 8 + (z % 4) * 2 + c


CORE_SWAP = [(i, i ^ 1) for i in range(16)]
LOW_TO_HIGH = [(i, i + 8) for i in range(8)]
HIGH_TO_LOW = [(i + 8, i) for i in range(8)]
X_SWAP = [(i, i ^ 8) for i in range(16)]


def from_z(k):
    return [(seq_index(xh, z + k, c), seq_index(xh, z, c)) for xh, z, c in SEQ_PLACES]


def to_z(k):
    return [(seq_index(xh, z, c), seq_index(xh, z + k, c)) for xh, z, c in SEQ_PLACES]


def across(pairs):
    return [(seq * 8 + f, to_seq * 8 + to_f) for seq, f, to_seq, to_f in pairs]


TURN = across(
    (xh * 8 + a, f, xh * 8 + f, a) for xh in range(2) for a in range(8) for f in range(8)
)
Z_SWAP = [(i, i ^ 2) for i in range(16)]
FAR_SWAP = [(i, i ^ 4) for i in range(16)]
OUT_HOME = [(xh * 8 + a, 2 * a + xh) for xh in range(2) for a in range(8)]
DOWN_HOME = across(
    (seq_index(xh, 2 * zh + zl, c), f, 2 * f + zl, 4 * c + 2 * xh + zh)
    for xh in range(2) for zh in range(2) for zl in range(2) for c in range(2) for f in range(8)
)


def swap(value, pairs):
    return lax.ppermute(value, "seq", pairs)


def after(value, *others):
    return lax.optimization_barrier((value, *others))[0]


def gather_group(block):
    far = {k: swap(block, from_z(k)) for k in (2, 1, 3)}
    mine = [block, far[1], far[2], far[3]]
    return mine + [swap(v, CORE_SWAP) for v in mine]


def scatter_group(mine, part):
    rows = [slice(k * 128, k * 128 + 128) for k in range(4)]
    out = None
    for k in (2, 1, 3, 0):
        piece = mine[rows[k]] + swap(part[rows[k]], CORE_SWAP).astype(F32)
        if k:
            piece = swap(piece.astype(BF16), to_z(k)).astype(F32)
        out = piece if out is None else out + piece
    return out


def gather_pair(block):
    mine = [block, swap(block, Z_SWAP)]
    return mine + [swap(v, CORE_SWAP) for v in mine]


def scatter_pair(mine, part, later=()):
    far = mine[128:] + swap(part[128:], CORE_SWAP).astype(F32)
    far, *later = lax.optimization_barrier((far.astype(BF16), *later))
    far = swap(far, Z_SWAP).astype(F32)
    return mine[:128] + swap(part[:128], CORE_SWAP).astype(F32) + far, later


def sum_group(rows):
    groups = rows.shape[0] // 8
    other = swap(rows, CORE_SWAP).reshape(groups, 2, 4, 128)
    pair = rows.reshape(groups, 2, 4, 128) + jnp.concatenate([other[:, 1:], other[:, :1]], axis=1)
    total = pair
    for k in (2, 1, 3):
        got = swap(pair, from_z(k))
        total = total + jnp.concatenate([got[:, :, 4 - k :], got[:, :, : 4 - k]], axis=2)
    return total.reshape(rows.shape)


def column(row):
    return jnp.transpose(jnp.broadcast_to(row, (128, 128)))


def row_sums(values):
    return jnp.sum(jnp.transpose(values), axis=0, keepdims=True)


def shaped(shape, dtype):
    return jax.ShapeDtypeStruct(shape, dtype)


class Kept:
    def __init__(self, value):
        self.value = value


def in_hbm(*values):
    return [Kept(v) for v in values]


def kernel_call(body, outs, inputs, scratch=(), flops=0, nbytes=0):
    hbm_outs = [isinstance(o, Kept) for o in outs]
    hbm_ins = [isinstance(x, Kept) for x in inputs]
    outs = [o.value if isinstance(o, Kept) else o for o in outs]
    inputs = [x.value if isinstance(x, Kept) else x for x in inputs]
    groups = [x if isinstance(x, list) else [x] for x in inputs]
    flat = [a for group in groups for a in group]
    joined = [
        shaped((sum(a.shape[0] for a in group),) + group[0].shape[1:], group[0].dtype)
        for group in groups
    ]

    def large(s):
        return math.prod(s.shape) * s.dtype.itemsize >= SMALL

    def where(s):
        return ANY if large(s) else SMEM if s.dtype == jnp.int32 else VMEM

    out_shapes = [joined[o] if isinstance(o, int) else o for o in outs]
    in_buffers = [pltpu.VMEM(s.shape, s.dtype) for s in joined if large(s)]
    out_buffers = [
        pltpu.VMEM(o.shape, o.dtype) for o in outs if not isinstance(o, int) and large(o)
    ]

    def whole(*refs):
        refs = list(refs)

        def pull(count):
            taken = refs[:count]
            del refs[:count]
            return taken

        in_refs, out_refs = pull(len(flat)), pull(len(outs))
        in_space, out_space = pull(len(in_buffers)), pull(len(out_buffers))
        own, (in_sem, out_sem) = pull(len(scratch)), refs
        loads, ins, at = {}, [], 0
        for group, s in zip(groups, joined):
            if not large(s):
                ins.append(in_refs[at])
                at += 1
                continue
            space, row = in_space.pop(0), 0
            loads[id(space)] = []
            for a in group:
                copy = pltpu.make_async_copy(
                    in_refs[at], space.at[pl.ds(row, a.shape[0])], in_sem.at[at]
                )
                copy.start()
                loads[id(space)].append(copy)
                row, at = row + a.shape[0], at + 1
            ins.append(space)
        made, stores = [], {}
        for k, (o, s, ref) in enumerate(zip(outs, out_shapes, out_refs)):
            if not large(s):
                made.append(ref)
                continue
            space = ins[o] if isinstance(o, int) else out_space.pop(0)
            stores[id(space)] = pltpu.make_async_copy(space, ref, out_sem.at[k])
            if not isinstance(o, int):
                made.append(space)
        started = []

        def ready(*spaces):
            for space in spaces:
                for copy in loads.pop(id(space), ()):
                    copy.wait()

        def done(*spaces):
            for space in spaces:
                copy = stores.pop(id(space))
                copy.start()
                started.append(copy)

        body(ready, done, *ins, *made, *own)
        for key in list(stores):
            copy = stores.pop(key)
            copy.start()
            started.append(copy)
        for copy in started:
            copy.wait()

    return pl.pallas_call(
        whole,
        out_shape=tuple(
            pltpu.HBM(s.shape, s.dtype) if hbm else s for s, hbm in zip(out_shapes, hbm_outs)
        ),
        in_specs=[where(s) for group, s in zip(groups, joined) for _ in group],
        out_specs=tuple(where(s) for s in out_shapes),
        scratch_shapes=[
            *in_buffers, *out_buffers, *scratch,
            pltpu.SemaphoreType.DMA((len(flat),)), pltpu.SemaphoreType.DMA((len(outs),)),
        ],
        compiler_params=pltpu.CompilerParams(vmem_limit_bytes=VMEM_BYTES),
        cost_estimate=pl.CostEstimate(flops=flops, bytes_accessed=nbytes, transcendentals=0),
    )(
        *[
            pltpu.with_memory_space_constraint(a, pltpu.HBM) if hbm else a
            for group, hbm in zip(groups, hbm_ins)
            for a in group
        ]
    )


def root(total, width):
    return lax.rsqrt(total * (1.0 / width) + EPS)


def project_body(
    ready, done, x_all, weight, gain_q, gain_k, cos, sin,
    q_raw, k_raw, q_rot, kv_rot, squares,
):
    ready(x_all, weight, cos, sin)
    done(x_all)

    def step(t, carry):
        at = pl.multiple_of(t * 256, 256)
        made = jnp.dot(x_all[pl.ds(at, 256), :], weight[...], preferred_element_type=F32)
        for part in range(2):
            rows = pl.ds(at + part * 128, 128)
            block = t * 2 + part
            here = made[part * 128 : part * 128 + 128]
            q, k = here[:, :256], here[:, 256:384]
            kv_rot[rows, 128:] = here[:, 384:].astype(BF16)
            q_raw[rows, :] = q
            k_raw[rows, :] = k
            squares[pl.ds(block, 1), :] = row_sums(
                q[:, :128] * q[:, :128] + q[:, 128:] * q[:, 128:]
            )
            squares[pl.ds(block + 8, 1), :] = row_sums(k * k)
            cosine, sine = cos[rows, :], sin[rows, :]
            for head in range(2):
                lanes = slice(head * 128, head * 128 + 128)
                turn = q[:, lanes] * gain_q[:, lanes]
                q_rot[rows, lanes] = (turn * cosine + pltpu.roll(turn, 64, 1) * sine).astype(BF16)
            turn = k * gain_k[...]
            kv_rot[rows, :128] = (turn * cosine + pltpu.roll(turn, 64, 1) * sine).astype(BF16)
        return carry

    lax.fori_loop(0, 4, step, 0)


def spot(place, block):
    z = lax.rem(place[1] + block % 4, 4)
    c = place[2] if block < 4 else 1 - place[2]
    return z, c


def attend_body(
    ready, done, place, q_rot, kv_rot, kv_low, squares, squares_low,
    out_raw, out_low, q_tiles, keys, vals, logs, vals_t,
):
    ready(q_rot, kv_rot, kv_low)
    for b in range(8):
        rows = slice(b * 128, b * 128 + 128)
        z, c = spot(place, b)
        r = column(root(squares[b : b + 1, :], 2048.0)) * QUERY_SCALE
        inner = pl.ds(pl.multiple_of(c * 128, 128), 128)
        for head in range(2):
            q = q_rot[rows, head * 128 : head * 128 + 128].astype(F32)
            q_tiles[z * 2 + head, inner, :] = (q * r).astype(BF16)
        at = pl.ds(pl.multiple_of(1024 + z * 256 + c * 128, 128), 128)
        r = column(root(squares[8 + b : 9 + b, :], 1024.0))
        keys[at, :] = (kv_rot[rows, :128].astype(F32) * r).astype(BF16)
        vals[at, :] = kv_rot[rows, 128:]
        r = column(root(squares_low[b : b + 1, :], 1024.0))
        keys[rows, :] = (kv_low[rows, :128].astype(F32) * r).astype(BF16)
        vals[rows, :] = kv_low[rows, 128:]
    done(q_tiles, keys, vals)
    vals_t[...] = jnp.transpose(vals[...].astype(F32)).astype(BF16)
    allowed = lax.broadcasted_iota(jnp.int32, (256, 256), 0) <= lax.broadcasted_iota(
        jnp.int32, (256, 256), 1
    )

    def queries(first, i):
        at_diagonal = 1024 + i * 256
        ranges = [(first, at_diagonal)] if at_diagonal > first else []
        for head in range(2):
            q = q_tiles[i * 2 + head]
            scores = [
                lax.dot_general(keys[lo:hi, :], q, NT, preferred_element_type=F32)
                for lo, hi in ranges + [(at_diagonal, at_diagonal + 256)]
            ]
            scores[-1] = jnp.where(allowed, scores[-1], MASKED)
            tops = [jnp.max(s, axis=0, keepdims=True) for s in scores]
            top = functools.reduce(jnp.maximum, tops)
            total, acc = 0.0, 0.0
            for s, (lo, hi) in zip(scores, ranges + [(at_diagonal, at_diagonal + 256)]):
                p = jnp.exp2(s - top)
                total = total + jnp.sum(p, axis=0, keepdims=True)
                acc = acc + jnp.dot(
                    vals_t[:, lo:hi], p.astype(BF16), preferred_element_type=F32
                )
            out = jnp.transpose(acc / total)
            logs[i * 2 + head : i * 2 + head + 1, :] = top + jnp.log2(total)
            for c in range(2):
                block = lax.rem(i - place[1] + 4, 4) + 4 * jnp.abs(c - place[2])
                at = pl.ds(pl.multiple_of(block * 128, 128), 128)
                lanes = slice(head * 128, head * 128 + 128)
                out_raw[at, lanes] = out[c * 128 : c * 128 + 128, :]
                out_low[at, lanes] = out[c * 128 : c * 128 + 128, :].astype(BF16)

    @pl.when(place[0] == 1)
    def _():
        for i in range(4):
            queries(0, i)

    @pl.when(place[0] == 0)
    def _():
        for i in range(4):
            queries(1024, i)

    done(out_raw, out_low)


def output_body(ready, done, mixed, w_out, a_mine, a_part):
    ready(mixed, w_out)

    def project(t, carry):
        at = pl.ds(pl.multiple_of(t * 256, 256), 256)
        far = pl.ds(pl.multiple_of(512 + t * 256, 256), 256)
        a_part[at, :] = jnp.dot(mixed[far, :], w_out[...], preferred_element_type=F32).astype(BF16)
        a_mine[at, :] = jnp.dot(mixed[at, :], w_out[...], preferred_element_type=F32)
        return carry

    lax.fori_loop(0, 2, project, 0)


def attend_back_body(
    ready, done, place, q_tiles, keys, vals, logs, out_raw, w_out, da_all,
    dq, dk, dv, d_low, dots, keys_t, d_tiles, deltas, dk_acc, dv_acc,
):
    ready(keys)
    keys_t[...] = jnp.transpose(keys[...].astype(F32)).astype(BF16)
    ready(q_tiles, vals, out_raw, w_out, da_all)
    done(da_all)
    for b in range(8):
        rows = slice(b * 128, b * 128 + 128)
        z, c = spot(place, b)
        inner = pl.ds(pl.multiple_of(c * 128, 128), 128)
        d_out = lax.dot_general(
            da_all[rows, :], w_out[...], NT, preferred_element_type=F32
        ).astype(BF16)
        for head in range(2):
            lanes = slice(head * 128, head * 128 + 128)
            grad = d_out[:, lanes]
            d_tiles[z * 2 + head, inner, :] = grad
            deltas[z * 2 + head, pl.ds(c, 1), :] = row_sums(grad.astype(F32) * out_raw[rows, lanes])
    dk_acc[...] = jnp.zeros_like(dk_acc)
    dv_acc[...] = jnp.zeros_like(dv_acc)
    allowed = lax.broadcasted_iota(jnp.int32, (256, 256), 0) <= lax.broadcasted_iota(
        jnp.int32, (256, 256), 1
    )

    def queries(first, i):
        at_diagonal = 1024 + i * 256
        q = [q_tiles[i * 2 + head] for head in range(2)]
        grad = [d_tiles[i * 2 + head] for head in range(2)]
        log = [logs[i * 2 + head : i * 2 + head + 1, :] for head in range(2)]
        delta = [
            jnp.concatenate([deltas[i * 2 + head, 0:1, :], deltas[i * 2 + head, 1:2, :]], axis=1)
            for head in range(2)
        ]
        total = [0.0, 0.0]
        for lo in range(first, at_diagonal + 256, 256):
            at = slice(lo, lo + 256)
            k, v = keys[at, :], vals[at, :]
            dk_tile, dv_tile = dk_acc[at, :], dv_acc[at, :]
            for head in range(2):
                s = lax.dot_general(k, q[head], NT, preferred_element_type=F32)
                p = jnp.exp2(s - log[head])
                if lo == at_diagonal:
                    p = jnp.where(allowed, p, 0.0)
                dp = lax.dot_general(v, grad[head], NT, preferred_element_type=F32)
                ds = (p * (dp - delta[head])).astype(BF16)
                dv_tile += jnp.dot(p.astype(BF16), grad[head], preferred_element_type=F32)
                dk_tile += jnp.dot(ds, q[head], preferred_element_type=F32)
                total[head] = total[head] + jnp.dot(
                    keys_t[:, at], ds, preferred_element_type=F32
                )
            dk_acc[at, :] = dk_tile
            dv_acc[at, :] = dv_tile
        dot = jnp.zeros((1, 256), F32)
        for head in range(2):
            out = jnp.transpose(total[head]) * DH ** (-0.5)
            dot += jnp.sum(total[head] * jnp.transpose(q[head].astype(F32)), axis=0, keepdims=True)
            for c in range(2):
                block = lax.rem(i - place[1] + 4, 4) + 4 * jnp.abs(c - place[2])
                at = pl.ds(pl.multiple_of(block * 128, 128), 128)
                dq[at, head * 128 : head * 128 + 128] = out[c * 128 : c * 128 + 128, :].astype(BF16)
        for c in range(2):
            block = lax.rem(i - place[1] + 4, 4) + 4 * jnp.abs(c - place[2])
            dots[pl.ds(block, 1), :] = dot[:, c * 128 : c * 128 + 128] * (1.0 / LOG2E)

    @pl.when(place[0] == 1)
    def _():
        for i in range(4):
            queries(0, i)

    @pl.when(place[0] == 0)
    def _():
        for i in range(4):
            queries(1024, i)

    for b in range(8):
        rows = slice(b * 128, b * 128 + 128)
        z, c = spot(place, b)
        at = pl.ds(pl.multiple_of(1024 + z * 256 + c * 128, 128), 128)
        key_grad = dk_acc[at, :] * (1.0 / LOG2E)
        dk[rows, :] = key_grad
        dv[rows, :] = dv_acc[at, :]
        dots[8 + b : 9 + b, :] = row_sums(key_grad * keys[at, :].astype(F32))
        key_grad = dk_acc[rows, :] * (1.0 / LOG2E)
        d_low[rows, :128] = key_grad.astype(BF16)
        d_low[rows, 128:] = dv_acc[rows, :].astype(BF16)
        dots[16 + b : 17 + b, :] = row_sums(key_grad * keys[rows, :].astype(F32))


def unproject_body(
    ready, done, place, dq, dk, dv, d_got, q_raw, k_raw, squares, dots, dots_got, cos, sin,
    gain_q, gain_k, x_turned, gains, d_made, sent, sums,
):
    sums[...] = jnp.zeros_like(sums)
    ready(dq, dk, dv, d_got, q_raw, k_raw, cos, sin)

    def step(b, carry):
        rows = pl.ds(pl.multiple_of(b * 128, 128), 128)
        cosine, sine = cos[rows, :], sin[rows, :]
        r = column(root(squares[pl.ds(b, 1), :], 2048.0))
        mean = column(dots[pl.ds(b, 1), :]) * (1.0 / 2048.0)
        for head in range(2):
            lanes = slice(head * 128, head * 128 + 128)
            turn = dq[rows, lanes].astype(F32)
            d_norm = turn * cosine - pltpu.roll(turn, 64, 1) * sine
            hat = q_raw[rows, lanes] * r
            sums[0:1, lanes] += jnp.sum(d_norm * hat, axis=0, keepdims=True)
            d_made[rows, lanes] = (r * (d_norm * gain_q[:, lanes] - hat * mean)).astype(BF16)
        r = column(root(squares[pl.ds(b + 8, 1), :], 1024.0))
        mean = column(dots[pl.ds(b + 8, 1), :] + dots_got[pl.ds(b, 1), :]) * (1.0 / 1024.0)
        turn = dk[rows, :] + d_got[rows, :128].astype(F32)
        d_norm = turn * cosine - pltpu.roll(turn, 64, 1) * sine
        hat = k_raw[rows, :] * r
        sums[0:1, 256:] += jnp.sum(d_norm * hat, axis=0, keepdims=True)
        d_made[rows, 256:384] = (r * (d_norm * gain_k[...] - hat * mean)).astype(BF16)
        d_made[rows, 384:] = (dv[rows, :] + d_got[rows, 128:].astype(F32)).astype(BF16)
        return carry

    lax.fori_loop(0, 8, step, 0)
    done(d_made)
    ready(x_turned, gains)

    def grad(t, carry):
        rows = pl.ds(pl.multiple_of(t * 256, 256), 256)
        sent[rows, :512] = jnp.dot(
            x_turned[rows, :], d_made[...], preferred_element_type=F32
        ).astype(BF16)
        sent[rows, 512:] = gains[rows, :]
        return carry

    lax.fori_loop(0, 4, grad, 0)
    extra = 0.0
    for lo, width, each, first in ((0, 256, 16, 0), (256, 128, 8, 16)):
        row = lax.broadcasted_iota(jnp.int32, (128, width), 0) // 8
        lane = lax.broadcasted_iota(jnp.int32, (128, width), 1) // each
        spread = jnp.where(row == lane, sums[0:1, lo : lo + width], 0.0).astype(BF16)
        lane = lax.broadcasted_iota(jnp.int32, (width, 128), 0) % each + first
        pick = jnp.where(lane == lax.broadcasted_iota(jnp.int32, (width, 128), 1), 1.0, 0.0)
        extra = extra + jnp.dot(spread, pick.astype(BF16), preferred_element_type=F32)
    rows = pl.ds(pl.multiple_of((place[1] * 2 + place[2]) * 128, 128), 128)
    sent[rows, 512:] = (gains[rows, :].astype(F32) + extra).astype(BF16)


def input_body(ready, done, d_made, weight, dx_mine, dx_part):
    ready(d_made, weight)

    def step(t, carry):
        at = pl.ds(pl.multiple_of(t * 256, 256), 256)
        far = pl.ds(pl.multiple_of(512 + t * 256, 256), 256)
        dx_part[at, :] = lax.dot_general(
            d_made[far, :], weight[...], NT, preferred_element_type=F32
        ).astype(BF16)
        dx_mine[at, :] = lax.dot_general(
            d_made[at, :], weight[...], NT, preferred_element_type=F32
        )
        return carry

    lax.fori_loop(0, 2, step, 0)


def expand_body(ready, done, h_all, weight, gate, up, expanded, m_mine, m_part, down):
    ready(weight)
    for f in range(8):
        down[f * 96 : f * 96 + 96, :768] = weight[f * 128 : f * 128 + 96, 1536:2304]
        for m in range(3):
            down[f * 96 + m * 32 : f * 96 + m * 32 + 32, 768:] = weight[
                f * 128 + 96 : f * 128 + 128, 1536 + m * 256 : 1792 + m * 256
            ]

    done(down)
    ready(h_all)
    done(h_all)

    def widen(n, carry):
        lanes = pl.ds(pl.multiple_of(n * 256, 256), 256)
        upper = pl.ds(pl.multiple_of(768 + n * 256, 256), 256)
        g = jnp.dot(h_all[...], weight[:, lanes], preferred_element_type=F32)
        u = jnp.dot(h_all[...], weight[:, upper], preferred_element_type=F32)
        gate[:, lanes] = g
        up[:, lanes] = u
        expanded[:, lanes] = (g * jax.nn.sigmoid(g) * u).astype(BF16)
        return carry

    lax.fori_loop(0, 3, widen, 0)
    done(gate, up, expanded)

    def narrow(n, carry):
        lanes = pl.ds(pl.multiple_of(n * 256, 256), 256)
        m = jnp.dot(expanded[...], down[:, lanes], preferred_element_type=F32)
        m_mine[:, lanes] = m[:256]
        m_part[:, lanes] = m[256:].astype(BF16)
        return carry

    lax.fori_loop(0, 4, narrow, 0)


def expand_back_body(ready, done, dm_all, gate, up, weight, down, d_gu, dh_mine, dh_part):
    ready(dm_all, gate, up, down)
    done(dm_all)

    def widen(n, carry):
        lanes = pl.ds(pl.multiple_of(n * 256, 256), 256)
        upper = pl.ds(pl.multiple_of(768 + n * 256, 256), 256)
        de = lax.dot_general(dm_all[...], down[lanes, :], NT, preferred_element_type=F32)
        g = gate[:, lanes]
        sig = jax.nn.sigmoid(g)
        d_gu[:, lanes] = (de * up[:, lanes] * sig * (1.0 + g * (1.0 - sig))).astype(BF16)
        d_gu[:, upper] = (de * (g * sig)).astype(BF16)
        return carry

    lax.fori_loop(0, 3, widen, 0)
    done(d_gu)
    ready(weight)

    def narrow(n, carry):
        lanes = pl.ds(pl.multiple_of(n * 256, 256), 256)
        dh = lax.dot_general(d_gu[...], weight[lanes, :1536], NT, preferred_element_type=F32)
        dh_mine[:, lanes] = dh[:256]
        dh_part[:, lanes] = dh[256:].astype(BF16)
        return carry

    lax.fori_loop(0, 4, narrow, 0)


def expand_grad_body(ready, done, h_turned, d_gu, expanded, dm_all, out, expanded_t):
    ready(expanded)
    expanded_t[...] = jnp.transpose(expanded[...].astype(F32)).astype(BF16)

    ready(h_turned, d_gu, dm_all)

    def widen(n, carry):
        lanes = pl.ds(pl.multiple_of(n * 256, 256), 256)
        out[:, lanes] = jnp.dot(
            h_turned[...], d_gu[:, lanes], preferred_element_type=F32
        ).astype(BF16)
        return carry

    lax.fori_loop(0, 6, widen, 0)
    for n in range(4):
        made = jnp.dot(
            expanded_t[...], dm_all[:, n * 256 : n * 256 + 256], preferred_element_type=F32
        ).astype(BF16)
        for f in range(16):
            if n < 3:
                out[f * 64 : f * 64 + 48, 1536 + n * 256 : 1792 + n * 256] = made[
                    f * 48 : f * 48 + 48
                ]
                continue
            for m in range(3):
                out[f * 64 + 48 : f * 64 + 64, 1536 + m * 256 : 1792 + m * 256] = made[
                    f * 48 + m * 16 : f * 48 + m * 16 + 16
                ]


def norm_scale(values):
    return lax.rsqrt(jnp.mean(values * values, axis=-1, keepdims=True) + EPS)


def norm_back(upstream, normed, scaling):
    return scaling * (upstream - normed * jnp.mean(upstream * normed, axis=-1, keepdims=True))


def rotary_tables(first, z, c):
    half = DH // 2
    k = jnp.arange(4, dtype=jnp.int32)
    starts = jnp.concatenate([((z + k) % 4) * 256 + c * 128, ((z + k) % 4) * 256 + (1 - c) * 128])
    places = (first + starts[:, None] + jnp.arange(128, dtype=jnp.int32)[None, :]).reshape(1024)
    inverse = THETA ** (-(jnp.arange(half, dtype=F32) * (2.0 / DH)))
    angles = places.astype(F32)[:, None] * inverse[None, :]
    cosine, sine = jnp.cos(angles), jnp.sin(angles)
    return (
        jnp.concatenate([cosine, cosine], axis=-1),
        jnp.concatenate([-sine, sine], axis=-1),
    )


def dot(a, b):
    return jnp.dot(a, b, preferred_element_type=F32)


def dot_nt(a, b):
    return lax.dot_general(a, b, NT, preferred_element_type=F32)


def dot_tn(a, b):
    return lax.dot_general(a, b, (((0,), (0,)), ((), ())), preferred_element_type=F32)


def on_device(
    tokens, out_grad, w_query, w_key, w_value, w_out, w_gate, w_up, w_down,
    gain_query, gain_key, gain_attn, gain_mlp,
):
    seq = lax.axis_index("seq")
    xh, zc = seq // 8, seq % 8
    z, c = zc // 2, zc % 2
    quarter = (z % 2) * 2 + c
    place = jnp.stack([xh, z, c]).astype(jnp.int32)
    inputs = tokens[0]

    def columns(weight, width):
        return lax.dynamic_slice_in_dim(weight, zc * width, width, 1)

    def spread(block):
        return lax.all_to_all(
            jnp.broadcast_to(block[None], (8,) + block.shape),
            "fsdp", split_axis=0, concat_axis=0, tiled=True,
        ).reshape(8 * block.shape[0], block.shape[1])

    x_blocks = gather_group(inputs)
    weight = spread(
        jnp.concatenate(
            [columns(w_query, 256), columns(w_key, 128), columns(w_value, 128)], axis=1
        )
    )
    w_out_rows = lax.ppermute(
        lax.dynamic_slice_in_dim(w_out, zc * 32, 32, 0), ("seq", "fsdp"), TURN
    )
    x_blocks[1:4], weight, w_out_rows = lax.optimization_barrier(
        (x_blocks[1:4], weight, w_out_rows)
    )
    w_out_rows = spread(w_out_rows)

    def quarters(weight):
        part = lax.dynamic_slice_in_dim(weight.reshape(128, 8, 384), quarter * 96, 96, 2)
        return part.reshape(128, 768)

    down = lax.dynamic_slice_in_dim(w_down, quarter * 96, 96, 0)
    packed = jnp.concatenate(
        [
            down[:, :768],
            jnp.concatenate([down[m * 32 : m * 32 + 32, 768:] for m in range(3)], axis=1),
        ],
        axis=0,
    )
    w_mlp = jnp.concatenate([quarters(w_gate), quarters(w_up), packed], axis=1)
    weight, w_mlp = lax.optimization_barrier((weight, w_mlp))
    w_mlp = lax.all_gather(after(w_mlp, w_out_rows), "fsdp", axis=0, tiled=True)

    cosine, sine = rotary_tables(xh * 1024, z, c)
    gain_q = lax.dynamic_slice_in_dim(gain_query, zc * 256, 256, 0)[None]
    gain_k = lax.dynamic_slice_in_dim(gain_key, zc * 128, 128, 0)[None]
    x_all, q_raw, k_raw, q_rot, kv_rot, squares = kernel_call(
        project_body,
        [
            *in_hbm(0, shaped((1024, 256), F32), shaped((1024, 128), F32)),
            shaped((1024, 256), BF16), shaped((1024, 256), BF16), shaped((16, 128), F32),
        ],
        [x_blocks, weight, gain_q, gain_k, cosine, sine],
        flops=2 * 1024 * 1024 * 512, nbytes=9 << 20,
    )

    kv_low = swap(kv_rot, LOW_TO_HIGH)
    squares = sum_group(squares)
    squares, w_out_rows = lax.optimization_barrier((squares, w_out_rows))
    squares_low = swap(squares[8:], LOW_TO_HIGH)
    out_raw, mixed, q_tiles, keys, vals, logs = kernel_call(
        attend_body,
        [
            *in_hbm(
                shaped((1024, 256), F32), shaped((1024, 256), BF16), shaped((8, 256, 128), BF16),
                shaped((2048, 128), BF16), shaped((2048, 128), BF16),
            ),
            shaped((8, 256), F32),
        ],
        [place, q_rot, kv_rot, kv_low, squares, squares_low],
        [pltpu.VMEM((128, 2048), BF16)],
        flops=4 * 1024 * 2048 * 256, nbytes=9 << 20,
    )
    a_mine, a_part = kernel_call(
        output_body,
        [shaped((512, 1024), F32), shaped((512, 1024), BF16)],
        [*in_hbm(mixed), w_out_rows],
        flops=2 * 1024 * 1024 * 256, nbytes=5 << 20,
    )
    x_turned = x_all.T

    attended = scatter_group(a_mine, a_part)
    attended, x_turned = lax.optimization_barrier((attended, x_turned))
    attn_scale = norm_scale(attended)
    attn_hat = attended * attn_scale
    hidden_state = inputs.astype(F32) + attn_hat * gain_attn
    h_all, gate, up, expanded, m_mine, m_part, w_down_rows = kernel_call(
        expand_body,
        [
            0, shaped((512, 768), F32), shaped((512, 768), F32), shaped((512, 768), BF16),
            shaped((256, 1024), F32), shaped((256, 1024), BF16), shaped((768, 1024), BF16),
        ],
        [gather_pair(hidden_state.astype(BF16)), w_mlp],
        flops=2 * 512 * 2304 * 1024, nbytes=12 << 20,
    )
    projected, _ = scatter_pair(m_mine, m_part)
    mlp_scale = norm_scale(projected)
    mlp_hat = projected * mlp_scale
    output = (hidden_state + mlp_hat * gain_mlp).astype(BF16)[None]

    upstream = out_grad[0].astype(F32)
    grad_gain_mlp = jnp.sum(upstream * mlp_hat, axis=0)
    d_projected = norm_back(upstream * gain_mlp, mlp_hat, mlp_scale).astype(BF16)
    n = jnp.arange(1024, dtype=jnp.int32)
    source = ((n // 8) % 16) * 64 + (n // 128) * 8 + n % 8
    order = (n[None, :] == source[:, None]).astype(BF16)
    h_turned = dot_nt(order, h_all).astype(BF16)
    d_blocks = gather_pair(d_projected)
    d_blocks[3], h_turned = lax.optimization_barrier((d_blocks[3], h_turned))
    dm_all, d_gu, dh_mine, dh_part = kernel_call(
        expand_back_body,
        [
            0, shaped((512, 1536), BF16), shaped((256, 1024), F32), shaped((256, 1024), BF16),
        ],
        [d_blocks, gate, up, w_mlp, w_down_rows],
        flops=2 * 512 * 2304 * 1024, nbytes=12 << 20,
    )

    far = dh_mine[128:] + swap(dh_part[128:], CORE_SWAP).astype(F32)
    far, d_gu, dm_all = lax.optimization_barrier((far.astype(BF16), d_gu, dm_all))
    far = swap(far, Z_SWAP)
    (grad_mlp,) = kernel_call(
        expand_grad_body,
        [shaped((1024, 2304), BF16)],
        [h_turned, d_gu, expanded, dm_all],
        [pltpu.VMEM((768, 512), BF16)],
        flops=2 * 512 * 2304 * 1024, nbytes=9 << 20,
    )
    far, grad_mlp = lax.optimization_barrier((far, grad_mlp))
    grad_mlp = lax.psum_scatter(grad_mlp, "fsdp", scatter_dimension=0, tiled=True)
    d_hidden = upstream + dh_mine[:128] + swap(dh_part[:128], CORE_SWAP).astype(F32)
    d_hidden = d_hidden + far.astype(F32)

    grad_gain_attn = jnp.sum(d_hidden * attn_hat, axis=0)
    d_attended = norm_back(d_hidden * gain_attn, attn_hat, attn_scale).astype(BF16)
    dq, dk, dv, d_low, dots, da_all = kernel_call(
        attend_back_body,
        [
            shaped((1024, 256), BF16), shaped((1024, 128), F32), shaped((1024, 128), F32),
            shaped((1024, 256), BF16), shaped((24, 128), F32), 7,
        ],
        [
            place, *in_hbm(q_tiles, keys, vals), logs, *in_hbm(out_raw), w_out_rows,
            gather_group(d_attended),
        ],
        [
            pltpu.VMEM((128, 2048), BF16), pltpu.VMEM((8, 256, 128), BF16),
            pltpu.VMEM((8, 2, 128), F32), pltpu.VMEM((2048, 128), F32), pltpu.VMEM((2048, 128), F32),
        ],
        flops=10 * 1024 * 2048 * 256, nbytes=8 << 20,
    )
    grad_out = dot_tn(mixed, da_all).astype(BF16).reshape(2, 8, 16, 1024)
    grad_mlp, grad_out = lax.optimization_barrier((grad_mlp, grad_out))
    grad_out = jnp.swapaxes(grad_out, 0, 1).reshape(256, 1024)
    dq, grad_out = lax.optimization_barrier((dq, grad_out))
    grad_out = lax.psum_scatter(grad_out, "fsdp", scatter_dimension=0, tiled=True)
    grad_out = grad_out.reshape(2, 16, 1024)
    d_got = swap(d_low, HIGH_TO_LOW)
    dots = sum_group(dots)
    dots_got = swap(dots[16:], HIGH_TO_LOW)

    gains = jnp.concatenate([grad_gain_attn.reshape(128, 8), grad_gain_mlp.reshape(128, 8)], axis=1)
    gains = jnp.broadcast_to(
        jnp.pad(gains.astype(BF16), ((0, 0), (24, 88)))[:, None, :], (128, 8, 128)
    ).reshape(1024, 128)
    d_made, sent = kernel_call(
        unproject_body,
        [shaped((1024, 512), BF16), shaped((1024, 640), BF16)],
        [
            place, dq, dk, dv, d_got, *in_hbm(q_raw, k_raw), squares, dots, dots_got, cosine, sine,
            gain_q, gain_k, *in_hbm(x_turned), gains,
        ],
        [pltpu.VMEM((8, 384), F32)],
        flops=2 * 1024 * 1024 * 512, nbytes=9 << 20,
    )
    got_made = lax.all_to_all(
        sent.reshape(128, 8, 640), ("seq", "fsdp"), split_axis=0, concat_axis=0, tiled=True
    )
    dx_mine, dx_part = kernel_call(
        input_body,
        [shaped((512, 1024), F32), shaped((512, 1024), BF16)],
        [after(d_made, sent), weight],
        flops=2 * 1024 * 1024 * 512, nbytes=5 << 20,
    )

    given = jnp.where(xh == 0, grad_out[1], grad_out[0])
    grad_out = jnp.where(xh == 0, grad_out[0], grad_out[1]).astype(F32)
    grad_out = grad_out + swap(given, X_SWAP).astype(F32)
    grad_out = swap(grad_out.astype(BF16), OUT_HOME)

    def halves(value, upper):
        low, high = value[: value.shape[0] // 2], value[value.shape[0] // 2 :]
        return jnp.where(upper, high, low), jnp.where(upper, low, high)

    kept, given = halves(grad_mlp, xh == 1)
    kept = kept.astype(F32) + swap(given, X_SWAP).astype(F32)
    grad_down = jnp.concatenate(
        [
            kept[:48, 1536:],
            jnp.concatenate([kept[48:, 1536 + m * 256 : 1792 + m * 256] for m in range(3)], axis=0),
        ],
        axis=1,
    )
    grad_down, given = halves(grad_down, z >= 2)
    grad_down = grad_down + swap(given.astype(BF16), FAR_SWAP).astype(F32)
    grad_down = lax.ppermute(grad_down.astype(BF16), ("seq", "fsdp"), DOWN_HOME)
    kept, given = halves(kept[:, :1536], z >= 2)
    kept = (kept + swap(given.astype(BF16), FAR_SWAP).astype(F32)).astype(BF16)
    kept, given = halves(kept, z % 2 == 1)
    got = swap(given, Z_SWAP)
    kept = jnp.stack([jnp.where(z % 2 == 1, got, kept), jnp.where(z % 2 == 1, kept, got)])
    kept = kept.reshape(2, 2, 8, 1536)
    given = jnp.where(c == 1, kept[:, 0], kept[:, 1])
    kept = jnp.where(c == 1, kept[:, 1], kept[:, 0])
    got = swap(given, CORE_SWAP)
    got_wide = jnp.stack([jnp.where(c == 1, got, kept), jnp.where(c == 1, kept, got)], axis=1)

    got_made, got_wide, grad_down, dx_part = lax.optimization_barrier(
        (got_made, got_wide, grad_down, dx_part)
    )
    d_inputs = scatter_group(dx_mine, dx_part)
    summed = jnp.sum(got_made.reshape(2, 8, 8, 8, 640).astype(F32), axis=(0, 2))
    gains = jnp.sum(summed[:, 0, 512:], axis=0)

    def take(first, width):
        return summed[:, :, first : first + width].swapaxes(0, 1).reshape(8, 8 * width)

    wide = got_wide.astype(F32).reshape(4, 8, 2, 8, 96)
    wide = wide.transpose(2, 1, 3, 0, 4).reshape(2, 8, 3072)
    return (
        output,
        (d_hidden + d_inputs).astype(BF16)[None],
        take(0, 256),
        take(256, 128),
        take(384, 128),
        grad_out.astype(F32),
        wide[0],
        wide[1],
        grad_down.astype(F32),
        gains[:16],
        gains[16:24],
        gains[24:32],
        gains[32:40],
    )


def solution(mesh):
    rows = P("fsdp", "seq", None)
    weight = P("fsdp", None)
    grad = P(("seq", "fsdp"), None)
    gain = P(("seq", "fsdp"))
    return jax.shard_map(
        on_device,
        mesh=mesh,
        in_specs=(rows,) * 2 + (weight,) * 7 + (P(),) * 4,
        out_specs=(rows,) * 2 + (grad,) * 7 + (gain,) * 4,
        check_vma=False,
    )
```

```python
import functools
import math

import jax
import jax.numpy as jnp
from jax import lax
from jax.experimental import pallas as pl
from jax.experimental.pallas import tpu as pltpu
from jax.sharding import PartitionSpec as P

BF16 = jnp.bfloat16
F32 = jnp.float32
DH = 128
EPS = 1e-06
THETA = 1000000.0
MASKED = -1e30
LOG2E = math.log2(math.e)
QUERY_SCALE = DH ** (-0.5) * LOG2E
VMEM_BYTES = 20 * 1024 * 1024
VMEM = pl.BlockSpec(memory_space=pltpu.VMEM)
SMEM = pl.BlockSpec(memory_space=pltpu.SMEM)
ANY = pl.BlockSpec(memory_space=pl.ANY)
SMALL = 64 * 1024
NT = (((1,), (1,)), ((), ()))

SEQ_PLACES = [(xh, z, c) for xh in range(2) for z in range(4) for c in range(2)]


def seq_index(xh, z, c):
    return xh * 8 + (z % 4) * 2 + c


CORE_SWAP = [(i, i ^ 1) for i in range(16)]
LOW_TO_HIGH = [(i, i + 8) for i in range(8)]
HIGH_TO_LOW = [(i + 8, i) for i in range(8)]
X_SWAP = [(i, i ^ 8) for i in range(16)]


def from_z(k):
    return [(seq_index(xh, z + k, c), seq_index(xh, z, c)) for xh, z, c in SEQ_PLACES]


def to_z(k):
    return [(seq_index(xh, z, c), seq_index(xh, z + k, c)) for xh, z, c in SEQ_PLACES]


def across(pairs):
    return [(seq * 8 + f, to_seq * 8 + to_f) for seq, f, to_seq, to_f in pairs]


TURN = across(
    (xh * 8 + a, f, xh * 8 + f, a) for xh in range(2) for a in range(8) for f in range(8)
)
Z_SWAP = [(i, i ^ 2) for i in range(16)]
FAR_SWAP = [(i, i ^ 4) for i in range(16)]
OUT_HOME = [(xh * 8 + a, 2 * a + xh) for xh in range(2) for a in range(8)]
DOWN_HOME = across(
    (seq_index(xh, 2 * zh + zl, c), f, 2 * f + zl, 4 * c + 2 * xh + zh)
    for xh in range(2) for zh in range(2) for zl in range(2) for c in range(2) for f in range(8)
)


def swap(value, pairs):
    return lax.ppermute(value, "seq", pairs)


def after(value, *others):
    return lax.optimization_barrier((value, *others))[0]


def gather_group(block):
    far = {k: swap(block, from_z(k)) for k in (2, 1, 3)}
    mine = [block, far[1], far[2], far[3]]
    return mine + [swap(v, CORE_SWAP) for v in mine]


def scatter_group(mine, part):
    rows = [slice(k * 128, k * 128 + 128) for k in range(4)]
    out = None
    for k in (2, 1, 3, 0):
        piece = mine[rows[k]] + swap(part[rows[k]], CORE_SWAP).astype(F32)
        if k:
            piece = swap(piece.astype(BF16), to_z(k)).astype(F32)
        out = piece if out is None else out + piece
    return out


def gather_pair(block):
    mine = [block, swap(block, Z_SWAP)]
    return mine + [swap(v, CORE_SWAP) for v in mine]


def scatter_pair(mine, part, later=()):
    far = mine[128:] + swap(part[128:], CORE_SWAP).astype(F32)
    far, *later = lax.optimization_barrier((far.astype(BF16), *later))
    far = swap(far, Z_SWAP).astype(F32)
    return mine[:128] + swap(part[:128], CORE_SWAP).astype(F32) + far, later


def sum_group(rows):
    groups = rows.shape[0] // 8
    other = swap(rows, CORE_SWAP).reshape(groups, 2, 4, 128)
    pair = rows.reshape(groups, 2, 4, 128) + jnp.concatenate([other[:, 1:], other[:, :1]], axis=1)
    total = pair
    for k in (2, 1, 3):
        got = swap(pair, from_z(k))
        total = total + jnp.concatenate([got[:, :, 4 - k :], got[:, :, : 4 - k]], axis=2)
    return total.reshape(rows.shape)


def column(row):
    return jnp.transpose(jnp.broadcast_to(row, (128, 128)))


def row_sums(values):
    return jnp.sum(jnp.transpose(values), axis=0, keepdims=True)


def shaped(shape, dtype):
    return jax.ShapeDtypeStruct(shape, dtype)


class Kept:
    def __init__(self, value, lanes=None):
        self.value, self.lanes = value, lanes


def in_hbm(*values):
    return [Kept(v) for v in values]


def kernel_call(body, outs, inputs, scratch=(), flops=0, nbytes=0):
    hbm_outs = [isinstance(o, Kept) for o in outs]
    hbm_ins = [isinstance(x, Kept) for x in inputs]
    lanes = [x.lanes if isinstance(x, Kept) else None for x in inputs]
    outs = [o.value if isinstance(o, Kept) else o for o in outs]
    inputs = [x.value if isinstance(x, Kept) else x for x in inputs]
    groups = [x if isinstance(x, list) else [x] for x in inputs]
    flat = [a for group in groups for a in group]
    joined = [
        shaped(
            (sum(a.shape[0] for a in group),)
            + (group[0].shape[1:] if part is None else (part.stop - part.start,)),
            group[0].dtype,
        )
        for group, part in zip(groups, lanes)
    ]

    def large(s):
        return math.prod(s.shape) * s.dtype.itemsize >= SMALL

    def where(s):
        return ANY if large(s) else SMEM if s.dtype == jnp.int32 else VMEM

    out_shapes = [joined[o] if isinstance(o, int) else o for o in outs]
    in_buffers = [pltpu.VMEM(s.shape, s.dtype) for s in joined if large(s)]
    out_buffers = [
        pltpu.VMEM(o.shape, o.dtype) for o in outs if not isinstance(o, int) and large(o)
    ]

    def whole(*refs):
        refs = list(refs)

        def pull(count):
            taken = refs[:count]
            del refs[:count]
            return taken

        in_refs, out_refs = pull(len(flat)), pull(len(outs))
        in_space, out_space = pull(len(in_buffers)), pull(len(out_buffers))
        own, (in_sem, out_sem) = pull(len(scratch)), refs
        loads, ins, at = {}, [], 0
        for group, s, part in zip(groups, joined, lanes):
            if not large(s):
                ins.append(in_refs[at])
                at += 1
                continue
            space, row = in_space.pop(0), 0
            loads[id(space)] = []
            for a in group:
                source = in_refs[at]
                if part is not None:
                    source = source.at[:, pl.ds(part.start, part.stop - part.start)]
                copy = pltpu.make_async_copy(
                    source, space.at[pl.ds(row, a.shape[0])], in_sem.at[at]
                )
                copy.start()
                loads[id(space)].append(copy)
                row, at = row + a.shape[0], at + 1
            ins.append(space)
        made, stores = [], {}
        for k, (o, s, ref) in enumerate(zip(outs, out_shapes, out_refs)):
            if not large(s):
                made.append(ref)
                continue
            space = ins[o] if isinstance(o, int) else out_space.pop(0)
            stores[id(space)] = pltpu.make_async_copy(space, ref, out_sem.at[k])
            if not isinstance(o, int):
                made.append(space)
        started = []

        def ready(*spaces):
            for space in spaces:
                for copy in loads.pop(id(space), ()):
                    copy.wait()

        def done(*spaces):
            for space in spaces:
                copy = stores.pop(id(space))
                copy.start()
                started.append(copy)

        body(ready, done, *ins, *made, *own)
        for key in list(stores):
            copy = stores.pop(key)
            copy.start()
            started.append(copy)
        for copy in started:
            copy.wait()

    return pl.pallas_call(
        whole,
        out_shape=tuple(
            pltpu.HBM(s.shape, s.dtype) if hbm else s for s, hbm in zip(out_shapes, hbm_outs)
        ),
        in_specs=[where(s) for group, s in zip(groups, joined) for _ in group],
        out_specs=tuple(where(s) for s in out_shapes),
        scratch_shapes=[
            *in_buffers, *out_buffers, *scratch,
            pltpu.SemaphoreType.DMA((len(flat),)), pltpu.SemaphoreType.DMA((len(outs),)),
        ],
        compiler_params=pltpu.CompilerParams(vmem_limit_bytes=VMEM_BYTES),
        cost_estimate=pl.CostEstimate(flops=flops, bytes_accessed=nbytes, transcendentals=0),
    )(
        *[
            pltpu.with_memory_space_constraint(a, pltpu.HBM) if hbm else a
            for group, hbm in zip(groups, hbm_ins)
            for a in group
        ]
    )


def root(total, width):
    return lax.rsqrt(total * (1.0 / width) + EPS)


def project_body(
    ready, done, x_all, weight, gain_q, gain_k, cos, sin,
    q_raw, k_raw, q_rot, kv_rot, squares,
):
    ready(x_all, weight, cos, sin)
    done(x_all)

    def step(t, carry):
        at = pl.multiple_of(t * 256, 256)
        made = jnp.dot(x_all[pl.ds(at, 256), :], weight[...], preferred_element_type=F32)
        for part in range(2):
            rows = pl.ds(at + part * 128, 128)
            block = t * 2 + part
            here = made[part * 128 : part * 128 + 128]
            q, k = here[:, :256], here[:, 256:384]
            kv_rot[rows, 128:] = here[:, 384:].astype(BF16)
            q_raw[rows, :] = q
            k_raw[rows, :] = k
            squares[pl.ds(block, 1), :] = row_sums(
                q[:, :128] * q[:, :128] + q[:, 128:] * q[:, 128:]
            )
            squares[pl.ds(block + 8, 1), :] = row_sums(k * k)
            cosine, sine = cos[rows, :], sin[rows, :]
            for head in range(2):
                lanes = slice(head * 128, head * 128 + 128)
                turn = q[:, lanes] * gain_q[:, lanes]
                q_rot[rows, lanes] = (turn * cosine + pltpu.roll(turn, 64, 1) * sine).astype(BF16)
            turn = k * gain_k[...]
            kv_rot[rows, :128] = (turn * cosine + pltpu.roll(turn, 64, 1) * sine).astype(BF16)
        return carry

    lax.fori_loop(0, 4, step, 0)


def spot(place, block):
    z = lax.rem(place[1] + block % 4, 4)
    c = place[2] if block < 4 else 1 - place[2]
    return z, c


def attend_body(
    ready, done, place, q_rot, kv_rot, kv_low, squares, squares_low,
    out_raw, out_low, q_tiles, keys, vals, logs, vals_t,
):
    ready(q_rot, kv_rot, kv_low)
    for b in range(8):
        rows = slice(b * 128, b * 128 + 128)
        z, c = spot(place, b)
        r = column(root(squares[b : b + 1, :], 2048.0)) * QUERY_SCALE
        inner = pl.ds(pl.multiple_of(c * 128, 128), 128)
        for head in range(2):
            q = q_rot[rows, head * 128 : head * 128 + 128].astype(F32)
            q_tiles[z * 2 + head, inner, :] = (q * r).astype(BF16)
        at = pl.ds(pl.multiple_of(1024 + z * 256 + c * 128, 128), 128)
        r = column(root(squares[8 + b : 9 + b, :], 1024.0))
        keys[at, :] = (kv_rot[rows, :128].astype(F32) * r).astype(BF16)
        vals[at, :] = kv_rot[rows, 128:]
        r = column(root(squares_low[b : b + 1, :], 1024.0))
        keys[rows, :] = (kv_low[rows, :128].astype(F32) * r).astype(BF16)
        vals[rows, :] = kv_low[rows, 128:]
    done(q_tiles, keys, vals)
    vals_t[...] = jnp.transpose(vals[...].astype(F32)).astype(BF16)
    allowed = lax.broadcasted_iota(jnp.int32, (256, 256), 0) <= lax.broadcasted_iota(
        jnp.int32, (256, 256), 1
    )

    def queries(first, i):
        at_diagonal = 1024 + i * 256
        ranges = [(first, at_diagonal)] if at_diagonal > first else []
        for head in range(2):
            q = q_tiles[i * 2 + head]
            scores = [
                lax.dot_general(keys[lo:hi, :], q, NT, preferred_element_type=F32)
                for lo, hi in ranges + [(at_diagonal, at_diagonal + 256)]
            ]
            scores[-1] = jnp.where(allowed, scores[-1], MASKED)
            tops = [jnp.max(s, axis=0, keepdims=True) for s in scores]
            top = functools.reduce(jnp.maximum, tops)
            total, acc = 0.0, 0.0
            for s, (lo, hi) in zip(scores, ranges + [(at_diagonal, at_diagonal + 256)]):
                p = jnp.exp2(s - top)
                total = total + jnp.sum(p, axis=0, keepdims=True)
                acc = acc + jnp.dot(
                    vals_t[:, lo:hi], p.astype(BF16), preferred_element_type=F32
                )
            out = jnp.transpose(acc / total)
            logs[i * 2 + head : i * 2 + head + 1, :] = top + jnp.log2(total)
            for c in range(2):
                block = lax.rem(i - place[1] + 4, 4) + 4 * jnp.abs(c - place[2])
                at = pl.ds(pl.multiple_of(block * 128, 128), 128)
                lanes = slice(head * 128, head * 128 + 128)
                out_raw[at, lanes] = out[c * 128 : c * 128 + 128, :]
                out_low[at, lanes] = out[c * 128 : c * 128 + 128, :].astype(BF16)

    @pl.when(place[0] == 1)
    def _():
        for i in range(4):
            queries(0, i)

    @pl.when(place[0] == 0)
    def _():
        for i in range(4):
            queries(1024, i)

    done(out_raw, out_low)


def output_body(ready, done, mixed, packed, a_mine, a_part, w_out):
    ready(packed)
    for f in range(8):
        for m in range(4):
            w_out[f * 32 : f * 32 + 32, m * 256 : m * 256 + 256] = packed[
                f * 128 + m * 32 : f * 128 + m * 32 + 32, :
            ]
    done(w_out)
    ready(mixed)

    def project(t, carry):
        at = pl.ds(pl.multiple_of(t * 256, 256), 256)
        far = pl.ds(pl.multiple_of(512 + t * 256, 256), 256)
        a_part[at, :] = jnp.dot(mixed[far, :], w_out[...], preferred_element_type=F32).astype(BF16)
        a_mine[at, :] = jnp.dot(mixed[at, :], w_out[...], preferred_element_type=F32)
        return carry

    lax.fori_loop(0, 2, project, 0)


def attend_back_body(
    ready, done, place, q_tiles, keys, vals, logs, out_raw, w_out, da_all,
    dq, dk, dv, d_low, dots, keys_t, d_tiles, deltas, dk_acc, dv_acc,
):
    ready(keys)
    keys_t[...] = jnp.transpose(keys[...].astype(F32)).astype(BF16)
    ready(q_tiles, vals, out_raw, w_out, da_all)
    done(da_all)
    for b in range(8):
        rows = slice(b * 128, b * 128 + 128)
        z, c = spot(place, b)
        inner = pl.ds(pl.multiple_of(c * 128, 128), 128)
        d_out = lax.dot_general(
            da_all[rows, :], w_out[...], NT, preferred_element_type=F32
        ).astype(BF16)
        for head in range(2):
            lanes = slice(head * 128, head * 128 + 128)
            grad = d_out[:, lanes]
            d_tiles[z * 2 + head, inner, :] = grad
            deltas[z * 2 + head, pl.ds(c, 1), :] = row_sums(grad.astype(F32) * out_raw[rows, lanes])
    dk_acc[...] = jnp.zeros_like(dk_acc)
    dv_acc[...] = jnp.zeros_like(dv_acc)
    allowed = lax.broadcasted_iota(jnp.int32, (256, 256), 0) <= lax.broadcasted_iota(
        jnp.int32, (256, 256), 1
    )

    def queries(first, i):
        at_diagonal = 1024 + i * 256
        q = [q_tiles[i * 2 + head] for head in range(2)]
        grad = [d_tiles[i * 2 + head] for head in range(2)]
        log = [logs[i * 2 + head : i * 2 + head + 1, :] for head in range(2)]
        delta = [
            jnp.concatenate([deltas[i * 2 + head, 0:1, :], deltas[i * 2 + head, 1:2, :]], axis=1)
            for head in range(2)
        ]
        total = [0.0, 0.0]
        for lo in range(first, at_diagonal + 256, 256):
            at = slice(lo, lo + 256)
            k, v = keys[at, :], vals[at, :]
            dk_tile, dv_tile = dk_acc[at, :], dv_acc[at, :]
            for head in range(2):
                s = lax.dot_general(k, q[head], NT, preferred_element_type=F32)
                p = jnp.exp2(s - log[head])
                if lo == at_diagonal:
                    p = jnp.where(allowed, p, 0.0)
                dp = lax.dot_general(v, grad[head], NT, preferred_element_type=F32)
                ds = (p * (dp - delta[head])).astype(BF16)
                dv_tile += jnp.dot(p.astype(BF16), grad[head], preferred_element_type=F32)
                dk_tile += jnp.dot(ds, q[head], preferred_element_type=F32)
                total[head] = total[head] + jnp.dot(
                    keys_t[:, at], ds, preferred_element_type=F32
                )
            dk_acc[at, :] = dk_tile
            dv_acc[at, :] = dv_tile
        dot = jnp.zeros((1, 256), F32)
        for head in range(2):
            out = jnp.transpose(total[head]) * DH ** (-0.5)
            dot += jnp.sum(total[head] * jnp.transpose(q[head].astype(F32)), axis=0, keepdims=True)
            for c in range(2):
                block = lax.rem(i - place[1] + 4, 4) + 4 * jnp.abs(c - place[2])
                at = pl.ds(pl.multiple_of(block * 128, 128), 128)
                dq[at, head * 128 : head * 128 + 128] = out[c * 128 : c * 128 + 128, :].astype(BF16)
        for c in range(2):
            block = lax.rem(i - place[1] + 4, 4) + 4 * jnp.abs(c - place[2])
            dots[pl.ds(block, 1), :] = dot[:, c * 128 : c * 128 + 128] * (1.0 / LOG2E)

    @pl.when(place[0] == 1)
    def _():
        for i in range(4):
            queries(0, i)

    @pl.when(place[0] == 0)
    def _():
        for i in range(4):
            queries(1024, i)

    for b in range(8):
        rows = slice(b * 128, b * 128 + 128)
        z, c = spot(place, b)
        at = pl.ds(pl.multiple_of(1024 + z * 256 + c * 128, 128), 128)
        key_grad = dk_acc[at, :] * (1.0 / LOG2E)
        dk[rows, :] = key_grad
        dv[rows, :] = dv_acc[at, :]
        dots[8 + b : 9 + b, :] = row_sums(key_grad * keys[at, :].astype(F32))
        key_grad = dk_acc[rows, :] * (1.0 / LOG2E)
        d_low[rows, :128] = key_grad.astype(BF16)
        d_low[rows, 128:] = dv_acc[rows, :].astype(BF16)
        dots[16 + b : 17 + b, :] = row_sums(key_grad * keys[rows, :].astype(F32))


def unproject_body(
    ready, done, place, dq, dk, dv, d_got, q_raw, k_raw, squares, dots, dots_got, cos, sin,
    gain_q, gain_k, x_turned, gains, d_made, sent, sums,
):
    sums[...] = jnp.zeros_like(sums)
    ready(dq, dk, dv, d_got, q_raw, k_raw, cos, sin)

    def step(b, carry):
        rows = pl.ds(pl.multiple_of(b * 128, 128), 128)
        cosine, sine = cos[rows, :], sin[rows, :]
        r = column(root(squares[pl.ds(b, 1), :], 2048.0))
        mean = column(dots[pl.ds(b, 1), :]) * (1.0 / 2048.0)
        for head in range(2):
            lanes = slice(head * 128, head * 128 + 128)
            turn = dq[rows, lanes].astype(F32)
            d_norm = turn * cosine - pltpu.roll(turn, 64, 1) * sine
            hat = q_raw[rows, lanes] * r
            sums[0:1, lanes] += jnp.sum(d_norm * hat, axis=0, keepdims=True)
            d_made[rows, lanes] = (r * (d_norm * gain_q[:, lanes] - hat * mean)).astype(BF16)
        r = column(root(squares[pl.ds(b + 8, 1), :], 1024.0))
        mean = column(dots[pl.ds(b + 8, 1), :] + dots_got[pl.ds(b, 1), :]) * (1.0 / 1024.0)
        turn = dk[rows, :] + d_got[rows, :128].astype(F32)
        d_norm = turn * cosine - pltpu.roll(turn, 64, 1) * sine
        hat = k_raw[rows, :] * r
        sums[0:1, 256:] += jnp.sum(d_norm * hat, axis=0, keepdims=True)
        d_made[rows, 256:384] = (r * (d_norm * gain_k[...] - hat * mean)).astype(BF16)
        d_made[rows, 384:] = (dv[rows, :] + d_got[rows, 128:].astype(F32)).astype(BF16)
        return carry

    lax.fori_loop(0, 8, step, 0)
    done(d_made)
    ready(x_turned, gains)

    def grad(t, carry):
        rows = pl.ds(pl.multiple_of(t * 256, 256), 256)
        sent[rows, :512] = jnp.dot(
            x_turned[rows, :], d_made[...], preferred_element_type=F32
        ).astype(BF16)
        sent[rows, 512:] = gains[rows, :]
        return carry

    lax.fori_loop(0, 4, grad, 0)
    extra = 0.0
    for lo, width, each, first in ((0, 256, 16, 0), (256, 128, 8, 16)):
        row = lax.broadcasted_iota(jnp.int32, (128, width), 0) // 8
        lane = lax.broadcasted_iota(jnp.int32, (128, width), 1) // each
        spread = jnp.where(row == lane, sums[0:1, lo : lo + width], 0.0).astype(BF16)
        lane = lax.broadcasted_iota(jnp.int32, (width, 128), 0) % each + first
        pick = jnp.where(lane == lax.broadcasted_iota(jnp.int32, (width, 128), 1), 1.0, 0.0)
        extra = extra + jnp.dot(spread, pick.astype(BF16), preferred_element_type=F32)
    rows = pl.ds(pl.multiple_of((place[1] * 2 + place[2]) * 128, 128), 128)
    sent[rows, 512:] = (gains[rows, :].astype(F32) + extra).astype(BF16)


def input_body(ready, done, d_made, weight, dx_mine, dx_part):
    ready(d_made, weight)

    def step(t, carry):
        at = pl.ds(pl.multiple_of(t * 256, 256), 256)
        far = pl.ds(pl.multiple_of(512 + t * 256, 256), 256)
        dx_part[at, :] = lax.dot_general(
            d_made[far, :], weight[...], NT, preferred_element_type=F32
        ).astype(BF16)
        dx_mine[at, :] = lax.dot_general(
            d_made[at, :], weight[...], NT, preferred_element_type=F32
        )
        return carry

    lax.fori_loop(0, 2, step, 0)


def expand_body(ready, done, h_all, weight, packed, gate, up, expanded, m_mine, m_part, down):
    ready(packed)
    for f in range(8):
        down[f * 96 : f * 96 + 96, :768] = packed[f * 128 : f * 128 + 96, :]
        for m in range(3):
            down[f * 96 + m * 32 : f * 96 + m * 32 + 32, 768:] = packed[
                f * 128 + 96 : f * 128 + 128, m * 256 : m * 256 + 256
            ]

    done(down)
    ready(h_all, weight)
    done(h_all)

    def widen(n, carry):
        lanes = pl.ds(pl.multiple_of(n * 256, 256), 256)
        upper = pl.ds(pl.multiple_of(768 + n * 256, 256), 256)
        g = jnp.dot(h_all[...], weight[:, lanes], preferred_element_type=F32)
        u = jnp.dot(h_all[...], weight[:, upper], preferred_element_type=F32)
        gate[:, lanes] = g
        up[:, lanes] = u
        expanded[:, lanes] = (g * jax.nn.sigmoid(g) * u).astype(BF16)
        return carry

    lax.fori_loop(0, 3, widen, 0)
    done(gate, up, expanded)

    def narrow(n, carry):
        lanes = pl.ds(pl.multiple_of(n * 256, 256), 256)
        m = jnp.dot(expanded[...], down[:, lanes], preferred_element_type=F32)
        m_mine[:, lanes] = m[:256]
        m_part[:, lanes] = m[256:].astype(BF16)
        return carry

    lax.fori_loop(0, 4, narrow, 0)


def expand_back_body(ready, done, dm_all, gate, up, weight, down, d_gu, dh_mine, dh_part):
    ready(dm_all, gate, up, down)
    done(dm_all)

    def widen(n, carry):
        lanes = pl.ds(pl.multiple_of(n * 256, 256), 256)
        upper = pl.ds(pl.multiple_of(768 + n * 256, 256), 256)
        de = lax.dot_general(dm_all[...], down[lanes, :], NT, preferred_element_type=F32)
        g = gate[:, lanes]
        sig = jax.nn.sigmoid(g)
        d_gu[:, lanes] = (de * up[:, lanes] * sig * (1.0 + g * (1.0 - sig))).astype(BF16)
        d_gu[:, upper] = (de * (g * sig)).astype(BF16)
        return carry

    lax.fori_loop(0, 3, widen, 0)
    done(d_gu)
    ready(weight)

    def narrow(n, carry):
        lanes = pl.ds(pl.multiple_of(n * 256, 256), 256)
        dh = lax.dot_general(d_gu[...], weight[lanes, :], NT, preferred_element_type=F32)
        dh_mine[:, lanes] = dh[:256]
        dh_part[:, lanes] = dh[256:].astype(BF16)
        return carry

    lax.fori_loop(0, 4, narrow, 0)


def expand_grad_body(ready, done, h_turned, d_gu, expanded, dm_all, out, expanded_t):
    ready(expanded)
    expanded_t[...] = jnp.transpose(expanded[...].astype(F32)).astype(BF16)

    ready(h_turned, d_gu, dm_all)

    def widen(n, carry):
        lanes = pl.ds(pl.multiple_of(n * 256, 256), 256)
        out[:, lanes] = jnp.dot(
            h_turned[...], d_gu[:, lanes], preferred_element_type=F32
        ).astype(BF16)
        return carry

    lax.fori_loop(0, 6, widen, 0)
    for n in range(4):
        made = jnp.dot(
            expanded_t[...], dm_all[:, n * 256 : n * 256 + 256], preferred_element_type=F32
        ).astype(BF16)
        for f in range(16):
            if n < 3:
                out[f * 64 : f * 64 + 48, 1536 + n * 256 : 1792 + n * 256] = made[
                    f * 48 : f * 48 + 48
                ]
                continue
            for m in range(3):
                out[f * 64 + 48 : f * 64 + 64, 1536 + m * 256 : 1792 + m * 256] = made[
                    f * 48 + m * 16 : f * 48 + m * 16 + 16
                ]


def norm_scale(values):
    return lax.rsqrt(jnp.mean(values * values, axis=-1, keepdims=True) + EPS)


def norm_back(upstream, normed, scaling):
    return scaling * (upstream - normed * jnp.mean(upstream * normed, axis=-1, keepdims=True))


def rotary_tables(first, z, c):
    half = DH // 2
    k = jnp.arange(4, dtype=jnp.int32)
    starts = jnp.concatenate([((z + k) % 4) * 256 + c * 128, ((z + k) % 4) * 256 + (1 - c) * 128])
    places = (first + starts[:, None] + jnp.arange(128, dtype=jnp.int32)[None, :]).reshape(1024)
    inverse = THETA ** (-(jnp.arange(half, dtype=F32) * (2.0 / DH)))
    angles = places.astype(F32)[:, None] * inverse[None, :]
    cosine, sine = jnp.cos(angles), jnp.sin(angles)
    return (
        jnp.concatenate([cosine, cosine], axis=-1),
        jnp.concatenate([-sine, sine], axis=-1),
    )


def dot(a, b):
    return jnp.dot(a, b, preferred_element_type=F32)


def dot_nt(a, b):
    return lax.dot_general(a, b, NT, preferred_element_type=F32)


def dot_tn(a, b):
    return lax.dot_general(a, b, (((0,), (0,)), ((), ())), preferred_element_type=F32)


def on_device(
    tokens, out_grad, w_query, w_key, w_value, w_out, w_gate, w_up, w_down,
    gain_query, gain_key, gain_attn, gain_mlp,
):
    seq = lax.axis_index("seq")
    xh, zc = seq // 8, seq % 8
    z, c = zc // 2, zc % 2
    quarter = (z % 2) * 2 + c
    place = jnp.stack([xh, z, c]).astype(jnp.int32)
    inputs = tokens[0]

    def columns(weight, width):
        return lax.dynamic_slice_in_dim(weight, zc * width, width, 1)

    def spread(block):
        return lax.all_to_all(
            jnp.broadcast_to(block[None], (8,) + block.shape),
            "fsdp", split_axis=0, concat_axis=0, tiled=True,
        ).reshape(8 * block.shape[0], block.shape[1])

    x_blocks = gather_group(inputs)
    weight = spread(
        jnp.concatenate(
            [columns(w_query, 256), columns(w_key, 128), columns(w_value, 128)], axis=1
        )
    )
    w_out_rows = lax.ppermute(
        lax.dynamic_slice_in_dim(w_out, zc * 32, 32, 0), ("seq", "fsdp"), TURN
    )

    def quarters(weight):
        part = lax.dynamic_slice_in_dim(weight.reshape(128, 8, 384), quarter * 96, 96, 2)
        return part.reshape(128, 768)

    down = lax.dynamic_slice_in_dim(w_down, quarter * 96, 96, 0)
    packed = jnp.concatenate(
        [
            down[:, :768],
            jnp.concatenate([down[m * 32 : m * 32 + 32, 768:] for m in range(3)], axis=1),
        ],
        axis=0,
    )
    packed = jnp.concatenate(
        [packed]
        + [jnp.concatenate([w_out_rows[:, m * 256 : m * 256 + 256] for m in range(4)], axis=0)],
        axis=1,
    )
    w_narrow = lax.all_gather(packed, "fsdp", axis=0, tiled=True)
    w_wide = jnp.concatenate([quarters(w_gate), quarters(w_up)], axis=1)
    weight, w_wide = lax.optimization_barrier((weight, w_wide))

    cosine, sine = rotary_tables(xh * 1024, z, c)
    gain_q = lax.dynamic_slice_in_dim(gain_query, zc * 256, 256, 0)[None]
    gain_k = lax.dynamic_slice_in_dim(gain_key, zc * 128, 128, 0)[None]
    x_all, q_raw, k_raw, q_rot, kv_rot, squares = kernel_call(
        project_body,
        [
            *in_hbm(0, shaped((1024, 256), F32), shaped((1024, 128), F32)),
            shaped((1024, 256), BF16), shaped((1024, 256), BF16), shaped((16, 128), F32),
        ],
        [x_blocks, weight, gain_q, gain_k, cosine, sine],
        flops=2 * 1024 * 1024 * 512, nbytes=9 << 20,
    )

    kv_low = swap(kv_rot, LOW_TO_HIGH)
    squares = sum_group(squares)
    squares_low = swap(squares[8:], LOW_TO_HIGH)
    w_wide, kv_low = lax.optimization_barrier((w_wide, kv_low))
    w_wide = lax.all_gather(w_wide, "fsdp", axis=0, tiled=True)
    out_raw, mixed, q_tiles, keys, vals, logs = kernel_call(
        attend_body,
        [
            *in_hbm(
                shaped((1024, 256), F32), shaped((1024, 256), BF16), shaped((8, 256, 128), BF16),
                shaped((2048, 128), BF16), shaped((2048, 128), BF16),
            ),
            shaped((8, 256), F32),
        ],
        [place, q_rot, kv_rot, kv_low, squares, squares_low],
        [pltpu.VMEM((128, 2048), BF16)],
        flops=4 * 1024 * 2048 * 256, nbytes=9 << 20,
    )
    a_mine, a_part, w_out_rows = kernel_call(
        output_body,
        [shaped((512, 1024), F32), shaped((512, 1024), BF16), *in_hbm(shaped((256, 1024), BF16))],
        [*in_hbm(mixed), Kept(w_narrow, slice(768, 1024))],
        flops=2 * 1024 * 1024 * 256, nbytes=5 << 20,
    )
    x_turned = x_all.T

    attended = scatter_group(a_mine, a_part)
    attended, x_turned = lax.optimization_barrier((attended, x_turned))
    attn_scale = norm_scale(attended)
    attn_hat = attended * attn_scale
    hidden_state = inputs.astype(F32) + attn_hat * gain_attn
    h_all, gate, up, expanded, m_mine, m_part, w_down_rows = kernel_call(
        expand_body,
        [
            0, shaped((512, 768), F32), shaped((512, 768), F32), shaped((512, 768), BF16),
            shaped((256, 1024), F32), shaped((256, 1024), BF16), shaped((768, 1024), BF16),
        ],
        [
            gather_pair(hidden_state.astype(BF16)), *in_hbm(w_wide), Kept(w_narrow, slice(0, 768)),
        ],
        flops=2 * 512 * 2304 * 1024, nbytes=12 << 20,
    )
    projected, _ = scatter_pair(m_mine, m_part)
    mlp_scale = norm_scale(projected)
    mlp_hat = projected * mlp_scale
    output = (hidden_state + mlp_hat * gain_mlp).astype(BF16)[None]

    upstream = out_grad[0].astype(F32)
    grad_gain_mlp = jnp.sum(upstream * mlp_hat, axis=0)
    d_projected = norm_back(upstream * gain_mlp, mlp_hat, mlp_scale).astype(BF16)
    n = jnp.arange(1024, dtype=jnp.int32)
    source = ((n // 8) % 16) * 64 + (n // 128) * 8 + n % 8
    order = (n[None, :] == source[:, None]).astype(BF16)
    h_turned = dot_nt(order, h_all).astype(BF16)
    d_blocks = gather_pair(d_projected)
    d_blocks[3], h_turned = lax.optimization_barrier((d_blocks[3], h_turned))
    dm_all, d_gu, dh_mine, dh_part = kernel_call(
        expand_back_body,
        [
            0, shaped((512, 1536), BF16), shaped((256, 1024), F32), shaped((256, 1024), BF16),
        ],
        [d_blocks, gate, up, w_wide, w_down_rows],
        flops=2 * 512 * 2304 * 1024, nbytes=12 << 20,
    )

    far = dh_mine[128:] + swap(dh_part[128:], CORE_SWAP).astype(F32)
    far, d_gu, dm_all = lax.optimization_barrier((far.astype(BF16), d_gu, dm_all))
    far = swap(far, Z_SWAP)
    (grad_mlp,) = kernel_call(
        expand_grad_body,
        in_hbm(shaped((1024, 2304), BF16)),
        [h_turned, d_gu, expanded, dm_all],
        [pltpu.VMEM((768, 512), BF16)],
        flops=2 * 512 * 2304 * 1024, nbytes=9 << 20,
    )
    far, grad_mlp = lax.optimization_barrier((far, grad_mlp))
    grad_mlp = lax.psum_scatter(grad_mlp, "fsdp", scatter_dimension=0, tiled=True)
    d_hidden = upstream + dh_mine[:128] + swap(dh_part[:128], CORE_SWAP).astype(F32)
    d_hidden = d_hidden + far.astype(F32)

    grad_gain_attn = jnp.sum(d_hidden * attn_hat, axis=0)
    d_attended = norm_back(d_hidden * gain_attn, attn_hat, attn_scale).astype(BF16)
    dq, dk, dv, d_low, dots, da_all = kernel_call(
        attend_back_body,
        [
            shaped((1024, 256), BF16), shaped((1024, 128), F32), shaped((1024, 128), F32),
            shaped((1024, 256), BF16), shaped((24, 128), F32), 7,
        ],
        [
            place, *in_hbm(q_tiles, keys, vals), logs,
            *in_hbm(out_raw, w_out_rows, gather_group(d_attended)),
        ],
        [
            pltpu.VMEM((128, 2048), BF16), pltpu.VMEM((8, 256, 128), BF16),
            pltpu.VMEM((8, 2, 128), F32), pltpu.VMEM((2048, 128), F32), pltpu.VMEM((2048, 128), F32),
        ],
        flops=10 * 1024 * 2048 * 256, nbytes=8 << 20,
    )
    grad_out = dot_tn(mixed, da_all).astype(BF16).reshape(2, 8, 16, 1024)
    grad_mlp, grad_out = lax.optimization_barrier((grad_mlp, grad_out))
    grad_out = jnp.swapaxes(grad_out, 0, 1).reshape(256, 1024)
    dq, grad_out = lax.optimization_barrier((dq, grad_out))
    grad_out = lax.psum_scatter(grad_out, "fsdp", scatter_dimension=0, tiled=True)
    grad_out = grad_out.reshape(2, 16, 1024)
    d_got = swap(d_low, HIGH_TO_LOW)
    dots = sum_group(dots)
    dots_got = swap(dots[16:], HIGH_TO_LOW)

    gains = jnp.concatenate([grad_gain_attn.reshape(128, 8), grad_gain_mlp.reshape(128, 8)], axis=1)
    gains = jnp.broadcast_to(
        jnp.pad(gains.astype(BF16), ((0, 0), (24, 88)))[:, None, :], (128, 8, 128)
    ).reshape(1024, 128)
    d_made, sent = kernel_call(
        unproject_body,
        [shaped((1024, 512), BF16), shaped((1024, 640), BF16)],
        [
            place, dq, dk, dv, d_got, *in_hbm(q_raw, k_raw), squares, dots, dots_got, cosine, sine,
            gain_q, gain_k, *in_hbm(x_turned), gains,
        ],
        [pltpu.VMEM((8, 384), F32)],
        flops=2 * 1024 * 1024 * 512, nbytes=9 << 20,
    )
    got_made = lax.all_to_all(
        sent.reshape(128, 8, 640), ("seq", "fsdp"), split_axis=0, concat_axis=0, tiled=True
    )
    given = jnp.where(xh == 0, grad_out[1], grad_out[0])
    grad_out = jnp.where(xh == 0, grad_out[0], grad_out[1]).astype(F32)
    grad_out = grad_out + swap(given, X_SWAP).astype(F32)
    grad_out = swap(grad_out.astype(BF16), OUT_HOME)

    def halves(value, upper):
        low, high = value[: value.shape[0] // 2], value[value.shape[0] // 2 :]
        return jnp.where(upper, high, low), jnp.where(upper, low, high)

    kept, given = halves(grad_mlp, xh == 1)
    kept = kept.astype(F32) + swap(given, X_SWAP).astype(F32)
    dx_mine, dx_part = kernel_call(
        input_body,
        [shaped((512, 1024), F32), shaped((512, 1024), BF16)],
        [after(d_made, kept), weight],
        flops=2 * 1024 * 1024 * 512, nbytes=5 << 20,
    )

    rows = [slice(k * 128, k * 128 + 128) for k in range(4)]
    pieces = [dx_mine[r] + swap(dx_part[r], CORE_SWAP).astype(F32) for r in rows]
    far = [piece.astype(BF16) for piece in pieces[1:]]
    kept, grad_out = after(kept, *far), after(grad_out, *far)
    d_inputs = pieces[0] + sum(
        swap(piece, to_z(k)).astype(F32) for k, piece in enumerate(far, 1)
    )
    grad_down = jnp.concatenate(
        [
            kept[:48, 1536:],
            jnp.concatenate([kept[48:, 1536 + m * 256 : 1792 + m * 256] for m in range(3)], axis=0),
        ],
        axis=1,
    )
    grad_down, given = halves(grad_down, z >= 2)
    grad_down = grad_down + swap(given.astype(BF16), FAR_SWAP).astype(F32)
    grad_down = lax.ppermute(grad_down.astype(BF16), ("seq", "fsdp"), DOWN_HOME)
    kept, given = halves(kept[:, :1536], z >= 2)
    kept = (kept + swap(given.astype(BF16), FAR_SWAP).astype(F32)).astype(BF16)
    kept, given = halves(kept, z % 2 == 1)
    got = swap(given, Z_SWAP)
    kept = jnp.stack([jnp.where(z % 2 == 1, got, kept), jnp.where(z % 2 == 1, kept, got)])
    kept = kept.reshape(2, 2, 8, 1536)
    given = jnp.where(c == 1, kept[:, 0], kept[:, 1])
    kept = jnp.where(c == 1, kept[:, 1], kept[:, 0])
    got = swap(given, CORE_SWAP)
    got_wide = jnp.stack([jnp.where(c == 1, got, kept), jnp.where(c == 1, kept, got)], axis=1)

    got_made, got_wide, grad_down, grad_out, d_inputs = lax.optimization_barrier(
        (got_made, got_wide, grad_down, grad_out, d_inputs)
    )
    summed = jnp.sum(got_made.reshape(2, 8, 8, 8, 640).astype(F32), axis=(0, 2))
    gains = jnp.sum(summed[:, 0, 512:], axis=0)

    def take(first, width):
        return summed[:, :, first : first + width].swapaxes(0, 1).reshape(8, 8 * width)

    wide = got_wide.astype(F32).reshape(4, 8, 2, 8, 96)
    wide = wide.transpose(2, 1, 3, 0, 4).reshape(2, 8, 3072)
    return (
        output,
        (d_hidden + d_inputs).astype(BF16)[None],
        take(0, 256),
        take(256, 128),
        take(384, 128),
        grad_out.astype(F32),
        wide[0],
        wide[1],
        grad_down.astype(F32),
        gains[:16],
        gains[16:24],
        gains[24:32],
        gains[32:40],
    )


def solution(mesh):
    rows = P("fsdp", "seq", None)
    weight = P("fsdp", None)
    grad = P(("seq", "fsdp"), None)
    gain = P(("seq", "fsdp"))
    return jax.shard_map(
        on_device,
        mesh=mesh,
        in_specs=(rows,) * 2 + (weight,) * 7 + (P(),) * 4,
        out_specs=(rows,) * 2 + (grad,) * 7 + (gain,) * 4,
        check_vma=False,
    )
```

```python
import functools
import math

import jax
import jax.numpy as jnp
from jax import lax
from jax.experimental import pallas as pl
from jax.experimental.pallas import tpu as pltpu
from jax.sharding import PartitionSpec as P

BF16 = jnp.bfloat16
F32 = jnp.float32
DH = 128
EPS = 1e-06
THETA = 1000000.0
MASKED = -1e30
LOG2E = math.log2(math.e)
QUERY_SCALE = DH ** (-0.5) * LOG2E
VMEM_BYTES = 20 * 1024 * 1024
VMEM = pl.BlockSpec(memory_space=pltpu.VMEM)
SMEM = pl.BlockSpec(memory_space=pltpu.SMEM)
ANY = pl.BlockSpec(memory_space=pl.ANY)
SMALL = 64 * 1024
NT = (((1,), (1,)), ((), ()))

SEQ_PLACES = [(xh, z, c) for xh in range(2) for z in range(4) for c in range(2)]


def seq_index(xh, z, c):
    return xh * 8 + (z % 4) * 2 + c


CORE_SWAP = [(i, i ^ 1) for i in range(16)]
LOW_TO_HIGH = [(i, i + 8) for i in range(8)]
HIGH_TO_LOW = [(i + 8, i) for i in range(8)]
X_SWAP = [(i, i ^ 8) for i in range(16)]


def from_z(k):
    return [(seq_index(xh, z + k, c), seq_index(xh, z, c)) for xh, z, c in SEQ_PLACES]


def to_z(k):
    return [(seq_index(xh, z, c), seq_index(xh, z + k, c)) for xh, z, c in SEQ_PLACES]


def across(pairs):
    return [(seq * 8 + f, to_seq * 8 + to_f) for seq, f, to_seq, to_f in pairs]


TURN = across(
    (xh * 8 + a, f, xh * 8 + f, a) for xh in range(2) for a in range(8) for f in range(8)
)
Z_SWAP = [(i, i ^ 2) for i in range(16)]
FAR_SWAP = [(i, i ^ 4) for i in range(16)]
OUT_HOME = [(xh * 8 + a, 2 * a + xh) for xh in range(2) for a in range(8)]
DOWN_HOME = across(
    (seq_index(xh, 2 * zh + zl, c), f, 2 * f + zl, 4 * c + 2 * xh + zh)
    for xh in range(2) for zh in range(2) for zl in range(2) for c in range(2) for f in range(8)
)


def swap(value, pairs):
    return lax.ppermute(value, "seq", pairs)


def after(value, *others):
    return lax.optimization_barrier((value, *others))[0]


def gather_group(block):
    far = {k: swap(block, from_z(k)) for k in (2, 1, 3)}
    mine = [block, far[1], far[2], far[3]]
    return mine + [swap(v, CORE_SWAP) for v in mine]


def scatter_group(mine, part):
    rows = [slice(k * 128, k * 128 + 128) for k in range(4)]
    out = None
    for k in (2, 1, 3, 0):
        piece = mine[rows[k]] + swap(part[rows[k]], CORE_SWAP).astype(F32)
        if k:
            piece = swap(piece.astype(BF16), to_z(k)).astype(F32)
        out = piece if out is None else out + piece
    return out


def gather_pair(block):
    mine = [block, swap(block, Z_SWAP)]
    return mine + [swap(v, CORE_SWAP) for v in mine]


def scatter_pair(mine, part, later=()):
    far = mine[128:] + swap(part[128:], CORE_SWAP).astype(F32)
    far, *later = lax.optimization_barrier((far.astype(BF16), *later))
    far = swap(far, Z_SWAP).astype(F32)
    return mine[:128] + swap(part[:128], CORE_SWAP).astype(F32) + far, later


def sum_group(rows):
    groups = rows.shape[0] // 8
    other = swap(rows, CORE_SWAP).reshape(groups, 2, 4, 128)
    pair = rows.reshape(groups, 2, 4, 128) + jnp.concatenate([other[:, 1:], other[:, :1]], axis=1)
    total = pair
    for k in (2, 1, 3):
        got = swap(pair, from_z(k))
        total = total + jnp.concatenate([got[:, :, 4 - k :], got[:, :, : 4 - k]], axis=2)
    return total.reshape(rows.shape)


def column(row):
    return jnp.transpose(jnp.broadcast_to(row, (128, 128)))


def row_sums(values):
    return jnp.sum(jnp.transpose(values), axis=0, keepdims=True)


def shaped(shape, dtype):
    return jax.ShapeDtypeStruct(shape, dtype)


class Kept:
    def __init__(self, value):
        self.value = value


def in_hbm(*values):
    return [Kept(v) for v in values]


def kernel_call(body, outs, inputs, scratch=(), flops=0, nbytes=0):
    hbm_outs = [isinstance(o, Kept) for o in outs]
    hbm_ins = [isinstance(x, Kept) for x in inputs]
    outs = [o.value if isinstance(o, Kept) else o for o in outs]
    inputs = [x.value if isinstance(x, Kept) else x for x in inputs]
    groups = [x if isinstance(x, list) else [x] for x in inputs]
    flat = [a for group in groups for a in group]
    joined = [
        shaped((sum(a.shape[0] for a in group),) + group[0].shape[1:], group[0].dtype)
        for group in groups
    ]

    def large(s):
        return math.prod(s.shape) * s.dtype.itemsize >= SMALL

    def where(s):
        return ANY if large(s) else SMEM if s.dtype == jnp.int32 else VMEM

    out_shapes = [joined[o] if isinstance(o, int) else o for o in outs]
    in_buffers = [pltpu.VMEM(s.shape, s.dtype) for s in joined if large(s)]
    out_buffers = [
        pltpu.VMEM(o.shape, o.dtype) for o in outs if not isinstance(o, int) and large(o)
    ]

    def whole(*refs):
        refs = list(refs)

        def pull(count):
            taken = refs[:count]
            del refs[:count]
            return taken

        in_refs, out_refs = pull(len(flat)), pull(len(outs))
        in_space, out_space = pull(len(in_buffers)), pull(len(out_buffers))
        own, (in_sem, out_sem) = pull(len(scratch)), refs
        loads, ins, at = {}, [], 0
        for group, s in zip(groups, joined):
            if not large(s):
                ins.append(in_refs[at])
                at += 1
                continue
            space, row = in_space.pop(0), 0
            loads[id(space)] = []
            for a in group:
                copy = pltpu.make_async_copy(
                    in_refs[at], space.at[pl.ds(row, a.shape[0])], in_sem.at[at]
                )
                copy.start()
                loads[id(space)].append(copy)
                row, at = row + a.shape[0], at + 1
            ins.append(space)
        made, stores = [], {}
        for k, (o, s, ref) in enumerate(zip(outs, out_shapes, out_refs)):
            if not large(s):
                made.append(ref)
                continue
            space = ins[o] if isinstance(o, int) else out_space.pop(0)
            stores[id(space)] = pltpu.make_async_copy(space, ref, out_sem.at[k])
            if not isinstance(o, int):
                made.append(space)
        started = []

        def ready(*spaces):
            for space in spaces:
                for copy in loads.pop(id(space), ()):
                    copy.wait()

        def done(*spaces):
            for space in spaces:
                copy = stores.pop(id(space))
                copy.start()
                started.append(copy)

        body(ready, done, *ins, *made, *own)
        for key in list(stores):
            copy = stores.pop(key)
            copy.start()
            started.append(copy)
        for copy in started:
            copy.wait()

    return pl.pallas_call(
        whole,
        out_shape=tuple(
            pltpu.HBM(s.shape, s.dtype) if hbm else s for s, hbm in zip(out_shapes, hbm_outs)
        ),
        in_specs=[where(s) for group, s in zip(groups, joined) for _ in group],
        out_specs=tuple(where(s) for s in out_shapes),
        scratch_shapes=[
            *in_buffers, *out_buffers, *scratch,
            pltpu.SemaphoreType.DMA((len(flat),)), pltpu.SemaphoreType.DMA((len(outs),)),
        ],
        compiler_params=pltpu.CompilerParams(vmem_limit_bytes=VMEM_BYTES),
        cost_estimate=pl.CostEstimate(flops=flops, bytes_accessed=nbytes, transcendentals=0),
    )(
        *[
            pltpu.with_memory_space_constraint(a, pltpu.HBM) if hbm else a
            for group, hbm in zip(groups, hbm_ins)
            for a in group
        ]
    )


def root(total, width):
    return lax.rsqrt(total * (1.0 / width) + EPS)


def project_body(
    ready, done, x_all, weight, gain_q, gain_k, cos, sin,
    q_raw, k_raw, q_rot, kv_rot, squares,
):
    ready(x_all, weight, cos, sin)
    done(x_all)

    def step(t, carry):
        at = pl.multiple_of(t * 256, 256)
        made = jnp.dot(x_all[pl.ds(at, 256), :], weight[...], preferred_element_type=F32)
        for part in range(2):
            rows = pl.ds(at + part * 128, 128)
            block = t * 2 + part
            here = made[part * 128 : part * 128 + 128]
            q, k = here[:, :256], here[:, 256:384]
            kv_rot[rows, 128:] = here[:, 384:].astype(BF16)
            q_raw[rows, :] = q
            k_raw[rows, :] = k
            squares[pl.ds(block, 1), :] = row_sums(
                q[:, :128] * q[:, :128] + q[:, 128:] * q[:, 128:]
            )
            squares[pl.ds(block + 8, 1), :] = row_sums(k * k)
            cosine, sine = cos[rows, :], sin[rows, :]
            for head in range(2):
                lanes = slice(head * 128, head * 128 + 128)
                turn = q[:, lanes] * gain_q[:, lanes]
                q_rot[rows, lanes] = (turn * cosine + pltpu.roll(turn, 64, 1) * sine).astype(BF16)
            turn = k * gain_k[...]
            kv_rot[rows, :128] = (turn * cosine + pltpu.roll(turn, 64, 1) * sine).astype(BF16)
        return carry

    lax.fori_loop(0, 4, step, 0)


def spot(place, block):
    z = lax.rem(place[1] + block % 4, 4)
    c = place[2] if block < 4 else 1 - place[2]
    return z, c


def attend_body(
    ready, done, place, q_rot, kv_rot, kv_low, squares, squares_low,
    out_raw, out_low, q_tiles, keys, vals, logs, vals_t,
):
    ready(q_rot, kv_rot, kv_low)
    for b in range(8):
        rows = slice(b * 128, b * 128 + 128)
        z, c = spot(place, b)
        r = column(root(squares[b : b + 1, :], 2048.0)) * QUERY_SCALE
        inner = pl.ds(pl.multiple_of(c * 128, 128), 128)
        for head in range(2):
            q = q_rot[rows, head * 128 : head * 128 + 128].astype(F32)
            q_tiles[z * 2 + head, inner, :] = (q * r).astype(BF16)
        at = pl.ds(pl.multiple_of(1024 + z * 256 + c * 128, 128), 128)
        r = column(root(squares[8 + b : 9 + b, :], 1024.0))
        keys[at, :] = (kv_rot[rows, :128].astype(F32) * r).astype(BF16)
        vals[at, :] = kv_rot[rows, 128:]
        r = column(root(squares_low[b : b + 1, :], 1024.0))
        keys[rows, :] = (kv_low[rows, :128].astype(F32) * r).astype(BF16)
        vals[rows, :] = kv_low[rows, 128:]
    done(q_tiles, keys, vals)
    vals_t[...] = jnp.transpose(vals[...].astype(F32)).astype(BF16)
    allowed = lax.broadcasted_iota(jnp.int32, (256, 256), 0) <= lax.broadcasted_iota(
        jnp.int32, (256, 256), 1
    )

    def queries(first, i):
        at_diagonal = 1024 + i * 256
        ranges = [(first, at_diagonal)] if at_diagonal > first else []
        for head in range(2):
            q = q_tiles[i * 2 + head]
            scores = [
                lax.dot_general(keys[lo:hi, :], q, NT, preferred_element_type=F32)
                for lo, hi in ranges + [(at_diagonal, at_diagonal + 256)]
            ]
            scores[-1] = jnp.where(allowed, scores[-1], MASKED)
            tops = [jnp.max(s, axis=0, keepdims=True) for s in scores]
            top = functools.reduce(jnp.maximum, tops)
            total, acc = 0.0, 0.0
            for s, (lo, hi) in zip(scores, ranges + [(at_diagonal, at_diagonal + 256)]):
                p = jnp.exp2(s - top)
                total = total + jnp.sum(p, axis=0, keepdims=True)
                acc = acc + jnp.dot(
                    vals_t[:, lo:hi], p.astype(BF16), preferred_element_type=F32
                )
            out = jnp.transpose(acc / total)
            logs[i * 2 + head : i * 2 + head + 1, :] = top + jnp.log2(total)
            for c in range(2):
                block = lax.rem(i - place[1] + 4, 4) + 4 * jnp.abs(c - place[2])
                at = pl.ds(pl.multiple_of(block * 128, 128), 128)
                lanes = slice(head * 128, head * 128 + 128)
                out_raw[at, lanes] = out[c * 128 : c * 128 + 128, :]
                out_low[at, lanes] = out[c * 128 : c * 128 + 128, :].astype(BF16)

    @pl.when(place[0] == 1)
    def _():
        for i in range(4):
            queries(0, i)

    @pl.when(place[0] == 0)
    def _():
        for i in range(4):
            queries(1024, i)

    done(out_raw, out_low)


def output_body(ready, done, mixed, w_out, a_mine, a_part):
    ready(mixed, w_out)

    def project(t, carry):
        at = pl.ds(pl.multiple_of(t * 256, 256), 256)
        far = pl.ds(pl.multiple_of(512 + t * 256, 256), 256)
        a_part[at, :] = jnp.dot(mixed[far, :], w_out[...], preferred_element_type=F32).astype(BF16)
        a_mine[at, :] = jnp.dot(mixed[at, :], w_out[...], preferred_element_type=F32)
        return carry

    lax.fori_loop(0, 2, project, 0)


def attend_back_body(
    ready, done, place, q_tiles, keys, vals, logs, out_raw, w_out, da_all,
    dq, dk, dv, d_low, dots, keys_t, d_tiles, deltas, dk_acc, dv_acc,
):
    ready(keys)
    keys_t[...] = jnp.transpose(keys[...].astype(F32)).astype(BF16)
    ready(q_tiles, vals, out_raw, w_out, da_all)
    done(da_all)
    for b in range(8):
        rows = slice(b * 128, b * 128 + 128)
        z, c = spot(place, b)
        inner = pl.ds(pl.multiple_of(c * 128, 128), 128)
        d_out = lax.dot_general(
            da_all[rows, :], w_out[...], NT, preferred_element_type=F32
        ).astype(BF16)
        for head in range(2):
            lanes = slice(head * 128, head * 128 + 128)
            grad = d_out[:, lanes]
            d_tiles[z * 2 + head, inner, :] = grad
            deltas[z * 2 + head, pl.ds(c, 1), :] = row_sums(grad.astype(F32) * out_raw[rows, lanes])
    dk_acc[...] = jnp.zeros_like(dk_acc)
    dv_acc[...] = jnp.zeros_like(dv_acc)
    allowed = lax.broadcasted_iota(jnp.int32, (256, 256), 0) <= lax.broadcasted_iota(
        jnp.int32, (256, 256), 1
    )

    def queries(first, i):
        at_diagonal = 1024 + i * 256
        q = [q_tiles[i * 2 + head] for head in range(2)]
        grad = [d_tiles[i * 2 + head] for head in range(2)]
        log = [logs[i * 2 + head : i * 2 + head + 1, :] for head in range(2)]
        delta = [
            jnp.concatenate([deltas[i * 2 + head, 0:1, :], deltas[i * 2 + head, 1:2, :]], axis=1)
            for head in range(2)
        ]
        total = [0.0, 0.0]
        for lo in range(first, at_diagonal + 256, 256):
            at = slice(lo, lo + 256)
            k, v = keys[at, :], vals[at, :]
            dk_tile, dv_tile = dk_acc[at, :], dv_acc[at, :]
            for head in range(2):
                s = lax.dot_general(k, q[head], NT, preferred_element_type=F32)
                p = jnp.exp2(s - log[head])
                if lo == at_diagonal:
                    p = jnp.where(allowed, p, 0.0)
                dp = lax.dot_general(v, grad[head], NT, preferred_element_type=F32)
                ds = (p * (dp - delta[head])).astype(BF16)
                dv_tile += jnp.dot(p.astype(BF16), grad[head], preferred_element_type=F32)
                dk_tile += jnp.dot(ds, q[head], preferred_element_type=F32)
                total[head] = total[head] + jnp.dot(
                    keys_t[:, at], ds, preferred_element_type=F32
                )
            dk_acc[at, :] = dk_tile
            dv_acc[at, :] = dv_tile
        dot = jnp.zeros((1, 256), F32)
        for head in range(2):
            out = jnp.transpose(total[head]) * DH ** (-0.5)
            dot += jnp.sum(total[head] * jnp.transpose(q[head].astype(F32)), axis=0, keepdims=True)
            for c in range(2):
                block = lax.rem(i - place[1] + 4, 4) + 4 * jnp.abs(c - place[2])
                at = pl.ds(pl.multiple_of(block * 128, 128), 128)
                dq[at, head * 128 : head * 128 + 128] = out[c * 128 : c * 128 + 128, :].astype(BF16)
        for c in range(2):
            block = lax.rem(i - place[1] + 4, 4) + 4 * jnp.abs(c - place[2])
            dots[pl.ds(block, 1), :] = dot[:, c * 128 : c * 128 + 128] * (1.0 / LOG2E)

    @pl.when(place[0] == 1)
    def _():
        for i in range(4):
            queries(0, i)

    @pl.when(place[0] == 0)
    def _():
        for i in range(4):
            queries(1024, i)

    for b in range(8):
        rows = slice(b * 128, b * 128 + 128)
        z, c = spot(place, b)
        at = pl.ds(pl.multiple_of(1024 + z * 256 + c * 128, 128), 128)
        key_grad = dk_acc[at, :] * (1.0 / LOG2E)
        dk[rows, :] = key_grad
        dv[rows, :] = dv_acc[at, :]
        dots[8 + b : 9 + b, :] = row_sums(key_grad * keys[at, :].astype(F32))
        key_grad = dk_acc[rows, :] * (1.0 / LOG2E)
        d_low[rows, :128] = key_grad.astype(BF16)
        d_low[rows, 128:] = dv_acc[rows, :].astype(BF16)
        dots[16 + b : 17 + b, :] = row_sums(key_grad * keys[rows, :].astype(F32))


def unproject_body(
    ready, done, place, dq, dk, dv, d_got, q_raw, k_raw, squares, dots, dots_got, cos, sin,
    gain_q, gain_k, x_turned, gains, d_made, sent, sums,
):
    sums[...] = jnp.zeros_like(sums)
    ready(dq, dk, dv, d_got, q_raw, k_raw, cos, sin)

    def step(b, carry):
        rows = pl.ds(pl.multiple_of(b * 128, 128), 128)
        cosine, sine = cos[rows, :], sin[rows, :]
        r = column(root(squares[pl.ds(b, 1), :], 2048.0))
        mean = column(dots[pl.ds(b, 1), :]) * (1.0 / 2048.0)
        for head in range(2):
            lanes = slice(head * 128, head * 128 + 128)
            turn = dq[rows, lanes].astype(F32)
            d_norm = turn * cosine - pltpu.roll(turn, 64, 1) * sine
            hat = q_raw[rows, lanes] * r
            sums[0:1, lanes] += jnp.sum(d_norm * hat, axis=0, keepdims=True)
            d_made[rows, lanes] = (r * (d_norm * gain_q[:, lanes] - hat * mean)).astype(BF16)
        r = column(root(squares[pl.ds(b + 8, 1), :], 1024.0))
        mean = column(dots[pl.ds(b + 8, 1), :] + dots_got[pl.ds(b, 1), :]) * (1.0 / 1024.0)
        turn = dk[rows, :] + d_got[rows, :128].astype(F32)
        d_norm = turn * cosine - pltpu.roll(turn, 64, 1) * sine
        hat = k_raw[rows, :] * r
        sums[0:1, 256:] += jnp.sum(d_norm * hat, axis=0, keepdims=True)
        d_made[rows, 256:384] = (r * (d_norm * gain_k[...] - hat * mean)).astype(BF16)
        d_made[rows, 384:] = (dv[rows, :] + d_got[rows, 128:].astype(F32)).astype(BF16)
        return carry

    lax.fori_loop(0, 8, step, 0)
    done(d_made)
    ready(x_turned, gains)

    def grad(t, carry):
        rows = pl.ds(pl.multiple_of(t * 256, 256), 256)
        sent[rows, :512] = jnp.dot(
            x_turned[rows, :], d_made[...], preferred_element_type=F32
        ).astype(BF16)
        sent[rows, 512:] = gains[rows, :]
        return carry

    lax.fori_loop(0, 4, grad, 0)
    extra = 0.0
    for lo, width, each, first in ((0, 256, 16, 0), (256, 128, 8, 16)):
        row = lax.broadcasted_iota(jnp.int32, (128, width), 0) // 8
        lane = lax.broadcasted_iota(jnp.int32, (128, width), 1) // each
        spread = jnp.where(row == lane, sums[0:1, lo : lo + width], 0.0).astype(BF16)
        lane = lax.broadcasted_iota(jnp.int32, (width, 128), 0) % each + first
        pick = jnp.where(lane == lax.broadcasted_iota(jnp.int32, (width, 128), 1), 1.0, 0.0)
        extra = extra + jnp.dot(spread, pick.astype(BF16), preferred_element_type=F32)
    rows = pl.ds(pl.multiple_of((place[1] * 2 + place[2]) * 128, 128), 128)
    sent[rows, 512:] = (gains[rows, :].astype(F32) + extra).astype(BF16)


def input_body(ready, done, d_made, weight, dx_mine, dx_part):
    ready(d_made, weight)

    def step(t, carry):
        at = pl.ds(pl.multiple_of(t * 256, 256), 256)
        far = pl.ds(pl.multiple_of(512 + t * 256, 256), 256)
        dx_part[at, :] = lax.dot_general(
            d_made[far, :], weight[...], NT, preferred_element_type=F32
        ).astype(BF16)
        dx_mine[at, :] = lax.dot_general(
            d_made[at, :], weight[...], NT, preferred_element_type=F32
        )
        return carry

    lax.fori_loop(0, 2, step, 0)


def expand_body(ready, done, h_all, weight, packed, gate, up, expanded, m_mine, m_part, down):
    ready(packed)
    for f in range(8):
        down[f * 96 : f * 96 + 96, :768] = packed[f * 128 : f * 128 + 96, :]
        for m in range(3):
            down[f * 96 + m * 32 : f * 96 + m * 32 + 32, 768:] = packed[
                f * 128 + 96 : f * 128 + 128, m * 256 : m * 256 + 256
            ]

    done(down)
    ready(h_all, weight)
    done(h_all)

    def widen(n, carry):
        lanes = pl.ds(pl.multiple_of(n * 256, 256), 256)
        upper = pl.ds(pl.multiple_of(768 + n * 256, 256), 256)
        g = jnp.dot(h_all[...], weight[:, lanes], preferred_element_type=F32)
        u = jnp.dot(h_all[...], weight[:, upper], preferred_element_type=F32)
        gate[:, lanes] = g
        up[:, lanes] = u
        expanded[:, lanes] = (g * jax.nn.sigmoid(g) * u).astype(BF16)
        return carry

    lax.fori_loop(0, 3, widen, 0)
    done(gate, up, expanded)

    def narrow(n, carry):
        lanes = pl.ds(pl.multiple_of(n * 256, 256), 256)
        m = jnp.dot(expanded[...], down[:, lanes], preferred_element_type=F32)
        m_mine[:, lanes] = m[:256]
        m_part[:, lanes] = m[256:].astype(BF16)
        return carry

    lax.fori_loop(0, 4, narrow, 0)


def expand_back_body(ready, done, dm_all, gate, up, weight, down, d_gu, dh_mine, dh_part):
    ready(dm_all, gate, up, down)
    done(dm_all)

    def widen(n, carry):
        lanes = pl.ds(pl.multiple_of(n * 256, 256), 256)
        upper = pl.ds(pl.multiple_of(768 + n * 256, 256), 256)
        de = lax.dot_general(dm_all[...], down[lanes, :], NT, preferred_element_type=F32)
        g = gate[:, lanes]
        sig = jax.nn.sigmoid(g)
        d_gu[:, lanes] = (de * up[:, lanes] * sig * (1.0 + g * (1.0 - sig))).astype(BF16)
        d_gu[:, upper] = (de * (g * sig)).astype(BF16)
        return carry

    lax.fori_loop(0, 3, widen, 0)
    done(d_gu)
    ready(weight)

    def narrow(n, carry):
        lanes = pl.ds(pl.multiple_of(n * 256, 256), 256)
        dh = lax.dot_general(d_gu[...], weight[lanes, :], NT, preferred_element_type=F32)
        dh_mine[:, lanes] = dh[:256]
        dh_part[:, lanes] = dh[256:].astype(BF16)
        return carry

    lax.fori_loop(0, 4, narrow, 0)


def expand_grad_body(ready, done, h_turned, d_gu, expanded, dm_all, out, expanded_t):
    ready(expanded)
    expanded_t[...] = jnp.transpose(expanded[...].astype(F32)).astype(BF16)

    ready(h_turned, d_gu, dm_all)

    def widen(n, carry):
        lanes = pl.ds(pl.multiple_of(n * 256, 256), 256)
        out[:, lanes] = jnp.dot(
            h_turned[...], d_gu[:, lanes], preferred_element_type=F32
        ).astype(BF16)
        return carry

    lax.fori_loop(0, 6, widen, 0)
    for n in range(4):
        made = jnp.dot(
            expanded_t[...], dm_all[:, n * 256 : n * 256 + 256], preferred_element_type=F32
        ).astype(BF16)
        for f in range(16):
            if n < 3:
                out[f * 64 : f * 64 + 48, 1536 + n * 256 : 1792 + n * 256] = made[
                    f * 48 : f * 48 + 48
                ]
                continue
            for m in range(3):
                out[f * 64 + 48 : f * 64 + 64, 1536 + m * 256 : 1792 + m * 256] = made[
                    f * 48 + m * 16 : f * 48 + m * 16 + 16
                ]


def norm_scale(values):
    return lax.rsqrt(jnp.mean(values * values, axis=-1, keepdims=True) + EPS)


def norm_back(upstream, normed, scaling):
    return scaling * (upstream - normed * jnp.mean(upstream * normed, axis=-1, keepdims=True))


def rotary_tables(first, z, c):
    half = DH // 2
    k = jnp.arange(4, dtype=jnp.int32)
    starts = jnp.concatenate([((z + k) % 4) * 256 + c * 128, ((z + k) % 4) * 256 + (1 - c) * 128])
    places = (first + starts[:, None] + jnp.arange(128, dtype=jnp.int32)[None, :]).reshape(1024)
    inverse = THETA ** (-(jnp.arange(half, dtype=F32) * (2.0 / DH)))
    angles = places.astype(F32)[:, None] * inverse[None, :]
    cosine, sine = jnp.cos(angles), jnp.sin(angles)
    return (
        jnp.concatenate([cosine, cosine], axis=-1),
        jnp.concatenate([-sine, sine], axis=-1),
    )


def dot(a, b):
    return jnp.dot(a, b, preferred_element_type=F32)


def dot_nt(a, b):
    return lax.dot_general(a, b, NT, preferred_element_type=F32)


def dot_tn(a, b):
    return lax.dot_general(a, b, (((0,), (0,)), ((), ())), preferred_element_type=F32)


def on_device(
    tokens, out_grad, w_query, w_key, w_value, w_out, w_gate, w_up, w_down,
    gain_query, gain_key, gain_attn, gain_mlp,
):
    seq = lax.axis_index("seq")
    xh, zc = seq // 8, seq % 8
    z, c = zc // 2, zc % 2
    quarter = (z % 2) * 2 + c
    place = jnp.stack([xh, z, c]).astype(jnp.int32)
    inputs = tokens[0]

    def columns(weight, width):
        return lax.dynamic_slice_in_dim(weight, zc * width, width, 1)

    def spread(block):
        return lax.all_to_all(
            jnp.broadcast_to(block[None], (8,) + block.shape),
            "fsdp", split_axis=0, concat_axis=0, tiled=True,
        ).reshape(8 * block.shape[0], block.shape[1])

    x_blocks = gather_group(inputs)
    weight = spread(
        jnp.concatenate(
            [columns(w_query, 256), columns(w_key, 128), columns(w_value, 128)], axis=1
        )
    )
    w_out_rows = lax.ppermute(
        lax.dynamic_slice_in_dim(w_out, zc * 32, 32, 0), ("seq", "fsdp"), TURN
    )

    def quarters(weight):
        part = lax.dynamic_slice_in_dim(weight.reshape(128, 8, 384), quarter * 96, 96, 2)
        return part.reshape(128, 768)

    down = lax.dynamic_slice_in_dim(w_down, quarter * 96, 96, 0)
    packed = jnp.concatenate(
        [
            down[:, :768],
            jnp.concatenate([down[m * 32 : m * 32 + 32, 768:] for m in range(3)], axis=1),
        ],
        axis=0,
    )
    w_narrow = lax.all_gather(packed, "fsdp", axis=0, tiled=True)
    w_wide = jnp.concatenate([quarters(w_gate), quarters(w_up)], axis=1)
    weight, w_wide = lax.optimization_barrier((weight, w_wide))
    w_out_rows = spread(w_out_rows)

    cosine, sine = rotary_tables(xh * 1024, z, c)
    gain_q = lax.dynamic_slice_in_dim(gain_query, zc * 256, 256, 0)[None]
    gain_k = lax.dynamic_slice_in_dim(gain_key, zc * 128, 128, 0)[None]
    x_all, q_raw, k_raw, q_rot, kv_rot, squares = kernel_call(
        project_body,
        [
            *in_hbm(0, shaped((1024, 256), F32), shaped((1024, 128), F32)),
            shaped((1024, 256), BF16), shaped((1024, 256), BF16), shaped((16, 128), F32),
        ],
        [x_blocks, weight, gain_q, gain_k, cosine, sine],
        flops=2 * 1024 * 1024 * 512, nbytes=9 << 20,
    )

    kv_low = swap(kv_rot, LOW_TO_HIGH)
    squares = sum_group(squares)
    squares_low = swap(squares[8:], LOW_TO_HIGH)
    w_wide = after(w_wide, kv_low, squares, w_narrow)
    w_wide = lax.all_gather(w_wide, "fsdp", axis=0, tiled=True)
    out_raw, mixed, q_tiles, keys, vals, logs = kernel_call(
        attend_body,
        [
            *in_hbm(
                shaped((1024, 256), F32), shaped((1024, 256), BF16), shaped((8, 256, 128), BF16),
                shaped((2048, 128), BF16), shaped((2048, 128), BF16),
            ),
            shaped((8, 256), F32),
        ],
        [place, q_rot, kv_rot, kv_low, squares, squares_low],
        [pltpu.VMEM((128, 2048), BF16)],
        flops=4 * 1024 * 2048 * 256, nbytes=9 << 20,
    )
    a_mine, a_part = kernel_call(
        output_body,
        [shaped((512, 1024), F32), shaped((512, 1024), BF16)],
        [*in_hbm(mixed), w_out_rows],
        flops=2 * 1024 * 1024 * 256, nbytes=5 << 20,
    )
    x_turned = x_all.T

    attended = scatter_group(a_mine, a_part)
    attended, x_turned = lax.optimization_barrier((attended, x_turned))
    attn_scale = norm_scale(attended)
    attn_hat = attended * attn_scale
    hidden_state = inputs.astype(F32) + attn_hat * gain_attn
    h_all, gate, up, expanded, m_mine, m_part, w_down_rows = kernel_call(
        expand_body,
        [
            0, shaped((512, 768), F32), shaped((512, 768), F32), shaped((512, 768), BF16),
            shaped((256, 1024), F32), shaped((256, 1024), BF16), shaped((768, 1024), BF16),
        ],
        [
            gather_pair(hidden_state.astype(BF16)), *in_hbm(w_wide), *in_hbm(w_narrow),
        ],
        flops=2 * 512 * 2304 * 1024, nbytes=12 << 20,
    )
    projected, _ = scatter_pair(m_mine, m_part)
    mlp_scale = norm_scale(projected)
    mlp_hat = projected * mlp_scale
    output = (hidden_state + mlp_hat * gain_mlp).astype(BF16)[None]

    upstream = out_grad[0].astype(F32)
    grad_gain_mlp = jnp.sum(upstream * mlp_hat, axis=0)
    d_projected = norm_back(upstream * gain_mlp, mlp_hat, mlp_scale).astype(BF16)
    n = jnp.arange(1024, dtype=jnp.int32)
    source = ((n // 8) % 16) * 64 + (n // 128) * 8 + n % 8
    order = (n[None, :] == source[:, None]).astype(BF16)
    h_turned = dot_nt(order, h_all).astype(BF16)
    d_blocks = gather_pair(d_projected)
    d_blocks[3], h_turned = lax.optimization_barrier((d_blocks[3], h_turned))
    dm_all, d_gu, dh_mine, dh_part = kernel_call(
        expand_back_body,
        [
            0, shaped((512, 1536), BF16), shaped((256, 1024), F32), shaped((256, 1024), BF16),
        ],
        [d_blocks, gate, up, w_wide, w_down_rows],
        flops=2 * 512 * 2304 * 1024, nbytes=12 << 20,
    )

    far = dh_mine[128:] + swap(dh_part[128:], CORE_SWAP).astype(F32)
    far, d_gu, dm_all = lax.optimization_barrier((far.astype(BF16), d_gu, dm_all))
    far = swap(far, Z_SWAP)
    (grad_mlp,) = kernel_call(
        expand_grad_body,
        in_hbm(shaped((1024, 2304), BF16)),
        [h_turned, d_gu, expanded, dm_all],
        [pltpu.VMEM((768, 512), BF16)],
        flops=2 * 512 * 2304 * 1024, nbytes=9 << 20,
    )
    far, grad_mlp = lax.optimization_barrier((far, grad_mlp))
    grad_mlp = lax.psum_scatter(grad_mlp, "fsdp", scatter_dimension=0, tiled=True)
    d_hidden = upstream + dh_mine[:128] + swap(dh_part[:128], CORE_SWAP).astype(F32)
    d_hidden = d_hidden + far.astype(F32)

    grad_gain_attn = jnp.sum(d_hidden * attn_hat, axis=0)
    d_attended = norm_back(d_hidden * gain_attn, attn_hat, attn_scale).astype(BF16)
    dq, dk, dv, d_low, dots, da_all = kernel_call(
        attend_back_body,
        [
            shaped((1024, 256), BF16), shaped((1024, 128), F32), shaped((1024, 128), F32),
            shaped((1024, 256), BF16), shaped((24, 128), F32), 7,
        ],
        [
            place, *in_hbm(q_tiles, keys, vals), logs,
            *in_hbm(out_raw, w_out_rows, gather_group(d_attended)),
        ],
        [
            pltpu.VMEM((128, 2048), BF16), pltpu.VMEM((8, 256, 128), BF16),
            pltpu.VMEM((8, 2, 128), F32), pltpu.VMEM((2048, 128), F32), pltpu.VMEM((2048, 128), F32),
        ],
        flops=10 * 1024 * 2048 * 256, nbytes=8 << 20,
    )
    grad_out = dot_tn(mixed, da_all).astype(BF16).reshape(2, 8, 16, 1024)
    grad_mlp, grad_out = lax.optimization_barrier((grad_mlp, grad_out))
    grad_out = jnp.swapaxes(grad_out, 0, 1).reshape(256, 1024)
    dq, grad_out = lax.optimization_barrier((dq, grad_out))
    grad_out = lax.psum_scatter(grad_out, "fsdp", scatter_dimension=0, tiled=True)
    grad_out = grad_out.reshape(2, 16, 1024)
    d_got = swap(d_low, HIGH_TO_LOW)
    dots = sum_group(dots)
    dots_got = swap(dots[16:], HIGH_TO_LOW)

    gains = jnp.concatenate([grad_gain_attn.reshape(128, 8), grad_gain_mlp.reshape(128, 8)], axis=1)
    gains = jnp.broadcast_to(
        jnp.pad(gains.astype(BF16), ((0, 0), (24, 88)))[:, None, :], (128, 8, 128)
    ).reshape(1024, 128)
    d_made, sent = kernel_call(
        unproject_body,
        [shaped((1024, 512), BF16), shaped((1024, 640), BF16)],
        [
            place, dq, dk, dv, d_got, *in_hbm(q_raw, k_raw), squares, dots, dots_got, cosine, sine,
            gain_q, gain_k, *in_hbm(x_turned), gains,
        ],
        [pltpu.VMEM((8, 384), F32)],
        flops=2 * 1024 * 1024 * 512, nbytes=9 << 20,
    )

    def halves(value, upper):
        low, high = value[: value.shape[0] // 2], value[value.shape[0] // 2 :]
        return jnp.where(upper, high, low), jnp.where(upper, low, high)

    mine, given = halves(grad_mlp, xh == 1)
    mine = mine.astype(F32) + swap(given, X_SWAP).astype(F32)
    grad_down = jnp.concatenate(
        [
            mine[:48, 1536:],
            jnp.concatenate([mine[48:, 1536 + m * 256 : 1792 + m * 256] for m in range(3)], axis=0),
        ],
        axis=1,
    )
    grad_down, given_down = halves(grad_down, z >= 2)
    mine, given = halves(mine[:, :1536], z >= 2)
    given = swap(
        jnp.concatenate([given.reshape(48, 1024), given_down], axis=0).astype(BF16), FAR_SWAP
    ).astype(F32)
    mine = (mine + given[:48].reshape(32, 1536)).astype(BF16)
    grad_down = (grad_down + given[48:]).astype(BF16)
    sent, mine, grad_down = lax.optimization_barrier((sent, mine, grad_down))

    got_made = lax.all_to_all(
        sent.reshape(128, 8, 640), ("seq", "fsdp"), split_axis=0, concat_axis=0, tiled=True
    )
    dx_mine, dx_part = kernel_call(
        input_body,
        [shaped((512, 1024), F32), shaped((512, 1024), BF16)],
        [after(d_made, mine), weight],
        flops=2 * 1024 * 1024 * 512, nbytes=5 << 20,
    )
    rows = [slice(k * 128, k * 128 + 128) for k in range(4)]
    pieces = [dx_mine[r] + swap(dx_part[r], CORE_SWAP).astype(F32) for r in rows]
    far = [piece.astype(BF16) for piece in pieces[1:]]
    mine, grad_out, grad_down = after(mine, *far), after(grad_out, *far), after(grad_down, *far)
    d_inputs = pieces[0] + sum(
        swap(piece, to_z(k)).astype(F32) for k, piece in enumerate(far, 1)
    )

    grad_down = lax.ppermute(grad_down, ("seq", "fsdp"), DOWN_HOME)
    mine, given = halves(mine, z % 2 == 1)
    got = swap(given, Z_SWAP)
    mine = jnp.stack([jnp.where(z % 2 == 1, got, mine), jnp.where(z % 2 == 1, mine, got)])
    mine = mine.reshape(2, 2, 8, 1536)
    given = jnp.where(c == 1, mine[:, 0], mine[:, 1])
    mine = jnp.where(c == 1, mine[:, 1], mine[:, 0])
    got = swap(given, CORE_SWAP)
    got_wide = jnp.stack([jnp.where(c == 1, got, mine), jnp.where(c == 1, mine, got)], axis=1)

    given = jnp.where(xh == 0, grad_out[1], grad_out[0])
    grad_out = jnp.where(xh == 0, grad_out[0], grad_out[1]).astype(F32)
    grad_out = grad_out + swap(given, X_SWAP).astype(F32)
    grad_out = swap(grad_out.astype(BF16), OUT_HOME)

    got_made, got_wide, grad_down, grad_out, d_inputs = lax.optimization_barrier(
        (got_made, got_wide, grad_down, grad_out, d_inputs)
    )
    summed = jnp.sum(got_made.reshape(2, 8, 8, 8, 640).astype(F32), axis=(0, 2))
    gains = jnp.sum(summed[:, 0, 512:], axis=0)

    def take(first, width):
        return summed[:, :, first : first + width].swapaxes(0, 1).reshape(8, 8 * width)

    wide = got_wide.astype(F32).reshape(4, 8, 2, 8, 96)
    wide = wide.transpose(2, 1, 3, 0, 4).reshape(2, 8, 3072)
    return (
        output,
        (d_hidden + d_inputs).astype(BF16)[None],
        take(0, 256),
        take(256, 128),
        take(384, 128),
        grad_out.astype(F32),
        wide[0],
        wide[1],
        grad_down.astype(F32),
        gains[:16],
        gains[16:24],
        gains[24:32],
        gains[32:40],
    )


def solution(mesh):
    rows = P("fsdp", "seq", None)
    weight = P("fsdp", None)
    grad = P(("seq", "fsdp"), None)
    gain = P(("seq", "fsdp"))
    return jax.shard_map(
        on_device,
        mesh=mesh,
        in_specs=(rows,) * 2 + (weight,) * 7 + (P(),) * 4,
        out_specs=(rows,) * 2 + (grad,) * 7 + (gain,) * 4,
        check_vma=False,
    )
```

```python
import functools
import math

import jax
import jax.numpy as jnp
from jax import lax
from jax.experimental import pallas as pl
from jax.experimental.pallas import tpu as pltpu
from jax.sharding import PartitionSpec as P

BF16 = jnp.bfloat16
F32 = jnp.float32
DH = 128
EPS = 1e-06
THETA = 1000000.0
MASKED = -1e30
LOG2E = math.log2(math.e)
QUERY_SCALE = DH ** (-0.5) * LOG2E
VMEM_BYTES = 20 * 1024 * 1024
VMEM = pl.BlockSpec(memory_space=pltpu.VMEM)
SMEM = pl.BlockSpec(memory_space=pltpu.SMEM)
ANY = pl.BlockSpec(memory_space=pl.ANY)
SMALL = 64 * 1024
NT = (((1,), (1,)), ((), ()))

SEQ_PLACES = [(xh, z, c) for xh in range(2) for z in range(4) for c in range(2)]


def seq_index(xh, z, c):
    return xh * 8 + (z % 4) * 2 + c


CORE_SWAP = [(i, i ^ 1) for i in range(16)]
LOW_TO_HIGH = [(i, i + 8) for i in range(8)]
HIGH_TO_LOW = [(i + 8, i) for i in range(8)]
X_SWAP = [(i, i ^ 8) for i in range(16)]


def from_z(k):
    return [(seq_index(xh, z + k, c), seq_index(xh, z, c)) for xh, z, c in SEQ_PLACES]


def to_z(k):
    return [(seq_index(xh, z, c), seq_index(xh, z + k, c)) for xh, z, c in SEQ_PLACES]


def across(pairs):
    return [(seq * 8 + f, to_seq * 8 + to_f) for seq, f, to_seq, to_f in pairs]


TURN = across(
    (xh * 8 + a, f, xh * 8 + f, a) for xh in range(2) for a in range(8) for f in range(8)
)
Z_SWAP = [(i, i ^ 2) for i in range(16)]
FAR_SWAP = [(i, i ^ 4) for i in range(16)]
OUT_HOME = [(xh * 8 + a, 2 * a + xh) for xh in range(2) for a in range(8)]
DOWN_HOME = across(
    (seq_index(xh, 2 * zh + zl, c), f, 2 * f + zl, 4 * c + 2 * xh + zh)
    for xh in range(2) for zh in range(2) for zl in range(2) for c in range(2) for f in range(8)
)


def swap(value, pairs):
    return lax.ppermute(value, "seq", pairs)


def after(value, *others):
    return lax.optimization_barrier((value, *others))[0]


def gather_group(block):
    far = {k: swap(block, from_z(k)) for k in (2, 1, 3)}
    mine = [block, far[1], far[2], far[3]]
    return mine + [swap(v, CORE_SWAP) for v in mine]


def scatter_group(mine, part):
    rows = [slice(k * 128, k * 128 + 128) for k in range(4)]
    out = None
    for k in (2, 1, 3, 0):
        piece = mine[rows[k]] + swap(part[rows[k]], CORE_SWAP).astype(F32)
        if k:
            piece = swap(piece.astype(BF16), to_z(k)).astype(F32)
        out = piece if out is None else out + piece
    return out


def gather_pair(block):
    mine = [block, swap(block, Z_SWAP)]
    return mine + [swap(v, CORE_SWAP) for v in mine]


def scatter_pair(mine, part, later=()):
    far = mine[128:] + swap(part[128:], CORE_SWAP).astype(F32)
    far, *later = lax.optimization_barrier((far.astype(BF16), *later))
    far = swap(far, Z_SWAP).astype(F32)
    return mine[:128] + swap(part[:128], CORE_SWAP).astype(F32) + far, later


def sum_group(rows):
    groups = rows.shape[0] // 8
    other = swap(rows, CORE_SWAP).reshape(groups, 2, 4, 128)
    pair = rows.reshape(groups, 2, 4, 128) + jnp.concatenate([other[:, 1:], other[:, :1]], axis=1)
    total = pair
    for k in (2, 1, 3):
        got = swap(pair, from_z(k))
        total = total + jnp.concatenate([got[:, :, 4 - k :], got[:, :, : 4 - k]], axis=2)
    return total.reshape(rows.shape)


def column(row):
    return jnp.transpose(jnp.broadcast_to(row, (128, 128)))


def row_sums(values):
    return jnp.sum(jnp.transpose(values), axis=0, keepdims=True)


def shaped(shape, dtype):
    return jax.ShapeDtypeStruct(shape, dtype)


class Kept:
    def __init__(self, value):
        self.value = value


class Stripe:
    def __init__(self, first, width):
        self.lanes, self.width = pl.ds(first, width), width


def in_hbm(*values):
    return [Kept(v) for v in values]


def kernel_call(body, outs, inputs, scratch=(), flops=0, nbytes=0):
    hbm_outs = [isinstance(o, Kept) for o in outs]
    hbm_ins = [isinstance(x, Kept) for x in inputs]
    outs = [o.value if isinstance(o, Kept) else o for o in outs]
    inputs = [x.value if isinstance(x, Kept) else x for x in inputs]
    stripe = next((k for k, o in enumerate(outs) if isinstance(o, Stripe)), None)
    lanes, whole_array = None, []
    if stripe is not None:
        lanes, whole_array = outs[stripe].lanes, [inputs[-1]]
        outs[stripe] = shaped((inputs[-1].shape[0], outs[stripe].width), inputs[-1].dtype)
        inputs = inputs[:-1]
    groups = [x if isinstance(x, list) else [x] for x in inputs]
    flat = [a for group in groups for a in group]
    joined = [
        shaped((sum(a.shape[0] for a in group),) + group[0].shape[1:], group[0].dtype)
        for group in groups
    ]

    def large(s):
        return math.prod(s.shape) * s.dtype.itemsize >= SMALL

    def where(s):
        return ANY if large(s) else SMEM if s.dtype == jnp.int32 else VMEM

    out_shapes = [joined[o] if isinstance(o, int) else o for o in outs]
    in_buffers = [pltpu.VMEM(s.shape, s.dtype) for s in joined if large(s)]
    out_buffers = [
        pltpu.VMEM(o.shape, o.dtype) for o in outs if not isinstance(o, int) and large(o)
    ]

    def whole(*refs):
        refs = list(refs)

        def pull(count):
            taken = refs[:count]
            del refs[:count]
            return taken

        in_refs = pull(len(flat) + len(whole_array))[: len(flat)]
        out_refs = pull(len(outs))
        if stripe is not None:
            out_refs[stripe] = out_refs[stripe].at[:, lanes]
        in_space, out_space = pull(len(in_buffers)), pull(len(out_buffers))
        own, (in_sem, out_sem) = pull(len(scratch)), refs
        loads, ins, at = {}, [], 0
        for group, s in zip(groups, joined):
            if not large(s):
                ins.append(in_refs[at])
                at += 1
                continue
            space, row = in_space.pop(0), 0
            loads[id(space)] = []
            for a in group:
                copy = pltpu.make_async_copy(
                    in_refs[at], space.at[pl.ds(row, a.shape[0])], in_sem.at[at]
                )
                copy.start()
                loads[id(space)].append(copy)
                row, at = row + a.shape[0], at + 1
            ins.append(space)
        made, stores = [], {}
        for k, (o, s, ref) in enumerate(zip(outs, out_shapes, out_refs)):
            if not large(s):
                made.append(ref)
                continue
            space = ins[o] if isinstance(o, int) else out_space.pop(0)
            stores[id(space)] = pltpu.make_async_copy(space, ref, out_sem.at[k])
            if not isinstance(o, int):
                made.append(space)
        started = []

        def ready(*spaces):
            for space in spaces:
                for copy in loads.pop(id(space), ()):
                    copy.wait()

        def done(*spaces):
            for space in spaces:
                copy = stores.pop(id(space))
                copy.start()
                started.append(copy)

        body(ready, done, *ins, *made, *own)
        for key in list(stores):
            copy = stores.pop(key)
            copy.start()
            started.append(copy)
        for copy in started:
            copy.wait()

    shapes = [pltpu.HBM(s.shape, s.dtype) if hbm else s for s, hbm in zip(out_shapes, hbm_outs)]
    if stripe is not None:
        shapes[stripe] = pltpu.HBM(whole_array[0].shape, whole_array[0].dtype)
    return pl.pallas_call(
        whole,
        out_shape=tuple(shapes),
        in_specs=[where(s) for group, s in zip(groups, joined) for _ in group]
        + [ANY] * len(whole_array),
        out_specs=tuple(where(s) for s in out_shapes),
        scratch_shapes=[
            *in_buffers, *out_buffers, *scratch,
            pltpu.SemaphoreType.DMA((len(flat),)), pltpu.SemaphoreType.DMA((len(outs),)),
        ],
        compiler_params=pltpu.CompilerParams(vmem_limit_bytes=VMEM_BYTES),
        input_output_aliases={} if stripe is None else {len(flat): stripe},
        cost_estimate=pl.CostEstimate(flops=flops, bytes_accessed=nbytes, transcendentals=0),
    )(
        *[
            pltpu.with_memory_space_constraint(a, pltpu.HBM) if hbm else a
            for group, hbm in zip(groups, hbm_ins)
            for a in group
        ],
        *[pltpu.with_memory_space_constraint(a, pltpu.HBM) for a in whole_array],
    )


def root(total, width):
    return lax.rsqrt(total * (1.0 / width) + EPS)


def project_body(
    ready, done, x_all, weight, gain_q, gain_k, cos, sin,
    q_raw, k_raw, q_rot, kv_rot, squares,
):
    ready(x_all, weight, cos, sin)
    done(x_all)

    def step(t, carry):
        at = pl.multiple_of(t * 256, 256)
        made = jnp.dot(x_all[pl.ds(at, 256), :], weight[...], preferred_element_type=F32)
        for part in range(2):
            rows = pl.ds(at + part * 128, 128)
            block = t * 2 + part
            here = made[part * 128 : part * 128 + 128]
            q, k = here[:, :256], here[:, 256:384]
            kv_rot[rows, 128:] = here[:, 384:].astype(BF16)
            q_raw[rows, :] = q
            k_raw[rows, :] = k
            squares[pl.ds(block, 1), :] = row_sums(
                q[:, :128] * q[:, :128] + q[:, 128:] * q[:, 128:]
            )
            squares[pl.ds(block + 8, 1), :] = row_sums(k * k)
            cosine, sine = cos[rows, :], sin[rows, :]
            for head in range(2):
                lanes = slice(head * 128, head * 128 + 128)
                turn = q[:, lanes] * gain_q[:, lanes]
                q_rot[rows, lanes] = (turn * cosine + pltpu.roll(turn, 64, 1) * sine).astype(BF16)
            turn = k * gain_k[...]
            kv_rot[rows, :128] = (turn * cosine + pltpu.roll(turn, 64, 1) * sine).astype(BF16)
        return carry

    lax.fori_loop(0, 4, step, 0)


def spot(place, block):
    z = lax.rem(place[1] + block % 4, 4)
    c = place[2] if block < 4 else 1 - place[2]
    return z, c


def attend_body(
    ready, done, place, q_rot, kv_rot, kv_low, squares, squares_low,
    out_raw, out_low, out_turned, q_tiles, keys, vals, logs, vals_t,
):
    ready(q_rot, kv_rot, kv_low)
    for b in range(8):
        rows = slice(b * 128, b * 128 + 128)
        z, c = spot(place, b)
        r = column(root(squares[b : b + 1, :], 2048.0)) * QUERY_SCALE
        inner = pl.ds(pl.multiple_of(c * 128, 128), 128)
        for head in range(2):
            q = q_rot[rows, head * 128 : head * 128 + 128].astype(F32)
            q_tiles[z * 2 + head, inner, :] = (q * r).astype(BF16)
        at = pl.ds(pl.multiple_of(1024 + z * 256 + c * 128, 128), 128)
        r = column(root(squares[8 + b : 9 + b, :], 1024.0))
        keys[at, :] = (kv_rot[rows, :128].astype(F32) * r).astype(BF16)
        vals[at, :] = kv_rot[rows, 128:]
        r = column(root(squares_low[b : b + 1, :], 1024.0))
        keys[rows, :] = (kv_low[rows, :128].astype(F32) * r).astype(BF16)
        vals[rows, :] = kv_low[rows, 128:]
    done(q_tiles, keys, vals)
    vals_t[...] = jnp.transpose(vals[...].astype(F32)).astype(BF16)
    allowed = lax.broadcasted_iota(jnp.int32, (256, 256), 0) <= lax.broadcasted_iota(
        jnp.int32, (256, 256), 1
    )

    def queries(first, i):
        at_diagonal = 1024 + i * 256
        ranges = [(first, at_diagonal)] if at_diagonal > first else []
        for head in range(2):
            q = q_tiles[i * 2 + head]
            scores = [
                lax.dot_general(keys[lo:hi, :], q, NT, preferred_element_type=F32)
                for lo, hi in ranges + [(at_diagonal, at_diagonal + 256)]
            ]
            scores[-1] = jnp.where(allowed, scores[-1], MASKED)
            tops = [jnp.max(s, axis=0, keepdims=True) for s in scores]
            top = functools.reduce(jnp.maximum, tops)
            total, acc = 0.0, 0.0
            for s, (lo, hi) in zip(scores, ranges + [(at_diagonal, at_diagonal + 256)]):
                p = jnp.exp2(s - top)
                total = total + jnp.sum(p, axis=0, keepdims=True)
                acc = acc + jnp.dot(
                    vals_t[:, lo:hi], p.astype(BF16), preferred_element_type=F32
                )
            turned = acc / total
            out = jnp.transpose(turned)
            turned = turned.astype(BF16)
            logs[i * 2 + head : i * 2 + head + 1, :] = top + jnp.log2(total)
            for c in range(2):
                block = lax.rem(i - place[1] + 4, 4) + 4 * jnp.abs(c - place[2])
                at = pl.ds(pl.multiple_of(block * 128, 128), 128)
                lanes = slice(head * 128, head * 128 + 128)
                out_raw[at, lanes] = out[c * 128 : c * 128 + 128, :]
                out_low[at, lanes] = out[c * 128 : c * 128 + 128, :].astype(BF16)
                out_turned[lanes, at] = turned[:, c * 128 : c * 128 + 128]

    @pl.when(place[0] == 1)
    def _():
        for i in range(4):
            queries(0, i)

    @pl.when(place[0] == 0)
    def _():
        for i in range(4):
            queries(1024, i)

    done(out_raw, out_low, out_turned)


def output_body(ready, done, mixed, w_out, a_mine, a_part):
    ready(mixed, w_out)

    def project(t, carry):
        at = pl.ds(pl.multiple_of(t * 256, 256), 256)
        far = pl.ds(pl.multiple_of(512 + t * 256, 256), 256)
        a_part[at, :] = jnp.dot(mixed[far, :], w_out[...], preferred_element_type=F32).astype(BF16)
        a_mine[at, :] = jnp.dot(mixed[at, :], w_out[...], preferred_element_type=F32)
        return carry

    lax.fori_loop(0, 2, project, 0)


def output_back_body(
    ready, done, place, out_raw, w_out, da_all, mixed_turned, d_tiles, deltas, stripe
):
    ready(out_raw, w_out, da_all)
    for b in range(8):
        rows = slice(b * 128, b * 128 + 128)
        z, c = spot(place, b)
        inner = pl.ds(pl.multiple_of(c * 128, 128), 128)
        d_out = lax.dot_general(
            da_all[rows, :], w_out[...], NT, preferred_element_type=F32
        ).astype(BF16)
        for head in range(2):
            lanes = slice(head * 128, head * 128 + 128)
            grad = d_out[:, lanes]
            d_tiles[z * 2 + head, inner, :] = grad
            deltas[z * 2 + head, pl.ds(c, 1), :] = row_sums(grad.astype(F32) * out_raw[rows, lanes])
    done(d_tiles)
    ready(mixed_turned)
    for m in range(4):
        lanes = slice(m * 256, m * 256 + 256)
        made = jnp.dot(mixed_turned[...], da_all[:, lanes], preferred_element_type=F32).astype(BF16)
        for j in range(2):
            for f in range(8):
                to, at = f * 128 + j * 64 + m * 16, j * 128 + f * 16
                stripe[to : to + 16, :] = made[at : at + 16]


def attend_back_body(
    ready, done, place, q_tiles, keys, vals, logs, d_tiles, deltas,
    dq, dk, dv, d_low, dots, keys_t, dk_acc, dv_acc,
):
    ready(keys)
    keys_t[...] = jnp.transpose(keys[...].astype(F32)).astype(BF16)
    ready(q_tiles, vals, d_tiles)
    dk_acc[...] = jnp.zeros_like(dk_acc)
    dv_acc[...] = jnp.zeros_like(dv_acc)
    allowed = lax.broadcasted_iota(jnp.int32, (256, 256), 0) <= lax.broadcasted_iota(
        jnp.int32, (256, 256), 1
    )

    def queries(first, i):
        at_diagonal = 1024 + i * 256
        q = [q_tiles[i * 2 + head] for head in range(2)]
        grad = [d_tiles[i * 2 + head] for head in range(2)]
        log = [logs[i * 2 + head : i * 2 + head + 1, :] for head in range(2)]
        delta = [
            jnp.concatenate([deltas[i * 2 + head, 0:1, :], deltas[i * 2 + head, 1:2, :]], axis=1)
            for head in range(2)
        ]
        total = [0.0, 0.0]
        for lo in range(first, at_diagonal + 256, 256):
            at = slice(lo, lo + 256)
            k, v = keys[at, :], vals[at, :]
            dk_tile, dv_tile = dk_acc[at, :], dv_acc[at, :]
            for head in range(2):
                s = lax.dot_general(k, q[head], NT, preferred_element_type=F32)
                p = jnp.exp2(s - log[head])
                if lo == at_diagonal:
                    p = jnp.where(allowed, p, 0.0)
                dp = lax.dot_general(v, grad[head], NT, preferred_element_type=F32)
                ds = (p * (dp - delta[head])).astype(BF16)
                dv_tile += jnp.dot(p.astype(BF16), grad[head], preferred_element_type=F32)
                dk_tile += jnp.dot(ds, q[head], preferred_element_type=F32)
                total[head] = total[head] + jnp.dot(
                    keys_t[:, at], ds, preferred_element_type=F32
                )
            dk_acc[at, :] = dk_tile
            dv_acc[at, :] = dv_tile
        dot = jnp.zeros((1, 256), F32)
        for head in range(2):
            out = jnp.transpose(total[head]) * DH ** (-0.5)
            dot += jnp.sum(total[head] * jnp.transpose(q[head].astype(F32)), axis=0, keepdims=True)
            for c in range(2):
                block = lax.rem(i - place[1] + 4, 4) + 4 * jnp.abs(c - place[2])
                at = pl.ds(pl.multiple_of(block * 128, 128), 128)
                dq[at, head * 128 : head * 128 + 128] = out[c * 128 : c * 128 + 128, :].astype(BF16)
        for c in range(2):
            block = lax.rem(i - place[1] + 4, 4) + 4 * jnp.abs(c - place[2])
            dots[pl.ds(block, 1), :] = dot[:, c * 128 : c * 128 + 128] * (1.0 / LOG2E)

    @pl.when(place[0] == 1)
    def _():
        for i in range(4):
            queries(0, i)

    @pl.when(place[0] == 0)
    def _():
        for i in range(4):
            queries(1024, i)

    for b in range(8):
        rows = slice(b * 128, b * 128 + 128)
        z, c = spot(place, b)
        at = pl.ds(pl.multiple_of(1024 + z * 256 + c * 128, 128), 128)
        key_grad = dk_acc[at, :] * (1.0 / LOG2E)
        dk[rows, :] = key_grad
        dv[rows, :] = dv_acc[at, :]
        dots[8 + b : 9 + b, :] = row_sums(key_grad * keys[at, :].astype(F32))
        key_grad = dk_acc[rows, :] * (1.0 / LOG2E)
        d_low[rows, :128] = key_grad.astype(BF16)
        d_low[rows, 128:] = dv_acc[rows, :].astype(BF16)
        dots[16 + b : 17 + b, :] = row_sums(key_grad * keys[rows, :].astype(F32))


def unproject_body(
    ready, done, place, dq, dk, dv, d_got, q_raw, k_raw, squares, dots, dots_got, cos, sin,
    gain_q, gain_k, x_turned, gains, d_made, sent, sums,
):
    sums[...] = jnp.zeros_like(sums)
    ready(dq, dk, dv, d_got, q_raw, k_raw, cos, sin)

    def step(b, carry):
        rows = pl.ds(pl.multiple_of(b * 128, 128), 128)
        cosine, sine = cos[rows, :], sin[rows, :]
        r = column(root(squares[pl.ds(b, 1), :], 2048.0))
        mean = column(dots[pl.ds(b, 1), :]) * (1.0 / 2048.0)
        for head in range(2):
            lanes = slice(head * 128, head * 128 + 128)
            turn = dq[rows, lanes].astype(F32)
            d_norm = turn * cosine - pltpu.roll(turn, 64, 1) * sine
            hat = q_raw[rows, lanes] * r
            sums[0:1, lanes] += jnp.sum(d_norm * hat, axis=0, keepdims=True)
            d_made[rows, lanes] = (r * (d_norm * gain_q[:, lanes] - hat * mean)).astype(BF16)
        r = column(root(squares[pl.ds(b + 8, 1), :], 1024.0))
        mean = column(dots[pl.ds(b + 8, 1), :] + dots_got[pl.ds(b, 1), :]) * (1.0 / 1024.0)
        turn = dk[rows, :] + d_got[rows, :128].astype(F32)
        d_norm = turn * cosine - pltpu.roll(turn, 64, 1) * sine
        hat = k_raw[rows, :] * r
        sums[0:1, 256:] += jnp.sum(d_norm * hat, axis=0, keepdims=True)
        d_made[rows, 256:384] = (r * (d_norm * gain_k[...] - hat * mean)).astype(BF16)
        d_made[rows, 384:] = (dv[rows, :] + d_got[rows, 128:].astype(F32)).astype(BF16)
        return carry

    lax.fori_loop(0, 8, step, 0)
    done(d_made)
    ready(x_turned, gains)

    def grad(t, carry):
        rows = pl.ds(pl.multiple_of(t * 256, 256), 256)
        sent[rows, :512] = jnp.dot(
            x_turned[rows, :], d_made[...], preferred_element_type=F32
        ).astype(BF16)
        sent[rows, 512:] = gains[rows, :]
        return carry

    lax.fori_loop(0, 4, grad, 0)
    extra = 0.0
    for lo, width, each, first in ((0, 256, 16, 0), (256, 128, 8, 16)):
        row = lax.broadcasted_iota(jnp.int32, (128, width), 0) // 8
        lane = lax.broadcasted_iota(jnp.int32, (128, width), 1) // each
        spread = jnp.where(row == lane, sums[0:1, lo : lo + width], 0.0).astype(BF16)
        lane = lax.broadcasted_iota(jnp.int32, (width, 128), 0) % each + first
        pick = jnp.where(lane == lax.broadcasted_iota(jnp.int32, (width, 128), 1), 1.0, 0.0)
        extra = extra + jnp.dot(spread, pick.astype(BF16), preferred_element_type=F32)
    rows = pl.ds(pl.multiple_of((place[1] * 2 + place[2]) * 128, 128), 128)
    sent[rows, 512:] = (gains[rows, :].astype(F32) + extra).astype(BF16)


def input_body(ready, done, d_made, weight, dx_mine, dx_part):
    ready(d_made, weight)

    def step(t, carry):
        at = pl.ds(pl.multiple_of(t * 256, 256), 256)
        far = pl.ds(pl.multiple_of(512 + t * 256, 256), 256)
        dx_part[at, :] = lax.dot_general(
            d_made[far, :], weight[...], NT, preferred_element_type=F32
        ).astype(BF16)
        dx_mine[at, :] = lax.dot_general(
            d_made[at, :], weight[...], NT, preferred_element_type=F32
        )
        return carry

    lax.fori_loop(0, 2, step, 0)


def expand_body(ready, done, h_all, weight, packed, gate, up, expanded, m_mine, m_part, down):
    ready(packed)
    for f in range(8):
        down[f * 96 : f * 96 + 96, :768] = packed[f * 128 : f * 128 + 96, :]
        for m in range(3):
            down[f * 96 + m * 32 : f * 96 + m * 32 + 32, 768:] = packed[
                f * 128 + 96 : f * 128 + 128, m * 256 : m * 256 + 256
            ]

    done(down)
    ready(h_all, weight)
    done(h_all)

    def widen(n, carry):
        lanes = pl.ds(pl.multiple_of(n * 256, 256), 256)
        upper = pl.ds(pl.multiple_of(768 + n * 256, 256), 256)
        g = jnp.dot(h_all[...], weight[:, lanes], preferred_element_type=F32)
        u = jnp.dot(h_all[...], weight[:, upper], preferred_element_type=F32)
        gate[:, lanes] = g
        up[:, lanes] = u
        expanded[:, lanes] = (g * jax.nn.sigmoid(g) * u).astype(BF16)
        return carry

    lax.fori_loop(0, 3, widen, 0)
    done(gate, up, expanded)

    def narrow(n, carry):
        lanes = pl.ds(pl.multiple_of(n * 256, 256), 256)
        m = jnp.dot(expanded[...], down[:, lanes], preferred_element_type=F32)
        m_mine[:, lanes] = m[:256]
        m_part[:, lanes] = m[256:].astype(BF16)
        return carry

    lax.fori_loop(0, 4, narrow, 0)


def expand_back_body(ready, done, dm_all, gate, up, weight, down, d_gu, dh_mine, dh_part):
    ready(dm_all, gate, up, down)
    done(dm_all)

    def widen(n, carry):
        lanes = pl.ds(pl.multiple_of(n * 256, 256), 256)
        upper = pl.ds(pl.multiple_of(768 + n * 256, 256), 256)
        de = lax.dot_general(dm_all[...], down[lanes, :], NT, preferred_element_type=F32)
        g = gate[:, lanes]
        sig = jax.nn.sigmoid(g)
        d_gu[:, lanes] = (de * up[:, lanes] * sig * (1.0 + g * (1.0 - sig))).astype(BF16)
        d_gu[:, upper] = (de * (g * sig)).astype(BF16)
        return carry

    lax.fori_loop(0, 3, widen, 0)
    done(d_gu)
    ready(weight)

    def narrow(n, carry):
        lanes = pl.ds(pl.multiple_of(n * 256, 256), 256)
        dh = lax.dot_general(d_gu[...], weight[lanes, :], NT, preferred_element_type=F32)
        dh_mine[:, lanes] = dh[:256]
        dh_part[:, lanes] = dh[256:].astype(BF16)
        return carry

    lax.fori_loop(0, 4, narrow, 0)


def expand_grad_body(ready, done, h_turned, d_gu, expanded, dm_all, out, expanded_t):
    ready(expanded)
    expanded_t[...] = jnp.transpose(expanded[...].astype(F32)).astype(BF16)

    ready(h_turned, d_gu, dm_all)

    def widen(n, carry):
        lanes = pl.ds(pl.multiple_of(n * 256, 256), 256)
        out[:, lanes] = jnp.dot(
            h_turned[...], d_gu[:, lanes], preferred_element_type=F32
        ).astype(BF16)
        return carry

    lax.fori_loop(0, 6, widen, 0)
    for n in range(4):
        made = jnp.dot(
            expanded_t[...], dm_all[:, n * 256 : n * 256 + 256], preferred_element_type=F32
        ).astype(BF16)
        for f in range(16):
            if n < 3:
                out[f * 64 : f * 64 + 48, 1536 + n * 256 : 1792 + n * 256] = made[
                    f * 48 : f * 48 + 48
                ]
                continue
            for m in range(3):
                out[f * 64 + 48 : f * 64 + 64, 1536 + m * 256 : 1792 + m * 256] = made[
                    f * 48 + m * 16 : f * 48 + m * 16 + 16
                ]


def norm_scale(values):
    return lax.rsqrt(jnp.mean(values * values, axis=-1, keepdims=True) + EPS)


def norm_back(upstream, normed, scaling):
    return scaling * (upstream - normed * jnp.mean(upstream * normed, axis=-1, keepdims=True))


def rotary_tables(first, z, c):
    half = DH // 2
    k = jnp.arange(4, dtype=jnp.int32)
    starts = jnp.concatenate([((z + k) % 4) * 256 + c * 128, ((z + k) % 4) * 256 + (1 - c) * 128])
    places = (first + starts[:, None] + jnp.arange(128, dtype=jnp.int32)[None, :]).reshape(1024)
    inverse = THETA ** (-(jnp.arange(half, dtype=F32) * (2.0 / DH)))
    angles = places.astype(F32)[:, None] * inverse[None, :]
    cosine, sine = jnp.cos(angles), jnp.sin(angles)
    return (
        jnp.concatenate([cosine, cosine], axis=-1),
        jnp.concatenate([-sine, sine], axis=-1),
    )


def dot(a, b):
    return jnp.dot(a, b, preferred_element_type=F32)


def dot_nt(a, b):
    return lax.dot_general(a, b, NT, preferred_element_type=F32)


def dot_tn(a, b):
    return lax.dot_general(a, b, (((0,), (0,)), ((), ())), preferred_element_type=F32)


def on_device(
    tokens, out_grad, w_query, w_key, w_value, w_out, w_gate, w_up, w_down,
    gain_query, gain_key, gain_attn, gain_mlp,
):
    seq = lax.axis_index("seq")
    xh, zc = seq // 8, seq % 8
    z, c = zc // 2, zc % 2
    quarter = (z % 2) * 2 + c
    place = jnp.stack([xh, z, c]).astype(jnp.int32)
    inputs = tokens[0]

    def columns(weight, width):
        return lax.dynamic_slice_in_dim(weight, zc * width, width, 1)

    def spread(block):
        return lax.all_to_all(
            jnp.broadcast_to(block[None], (8,) + block.shape),
            "fsdp", split_axis=0, concat_axis=0, tiled=True,
        ).reshape(8 * block.shape[0], block.shape[1])

    x_blocks = gather_group(inputs)
    weight = spread(
        jnp.concatenate(
            [columns(w_query, 256), columns(w_key, 128), columns(w_value, 128)], axis=1
        )
    )
    w_out_rows = lax.ppermute(
        after(lax.dynamic_slice_in_dim(w_out, zc * 32, 32, 0), *x_blocks[1:4]),
        ("seq", "fsdp"),
        TURN,
    )

    def quarters(weight):
        part = lax.dynamic_slice_in_dim(weight.reshape(128, 8, 384), quarter * 96, 96, 2)
        return part.reshape(128, 768)

    down = lax.dynamic_slice_in_dim(w_down, quarter * 96, 96, 0)
    packed = jnp.concatenate(
        [
            down[:, :768],
            jnp.concatenate([down[m * 32 : m * 32 + 32, 768:] for m in range(3)], axis=1),
        ],
        axis=0,
    )
    w_narrow = lax.all_gather(packed, "fsdp", axis=0, tiled=True)
    w_wide = jnp.concatenate([quarters(w_gate), quarters(w_up)], axis=1)
    weight, w_wide, w_out_rows = lax.optimization_barrier((weight, w_wide, w_out_rows))

    cosine, sine = rotary_tables(xh * 1024, z, c)
    gain_q = lax.dynamic_slice_in_dim(gain_query, zc * 256, 256, 0)[None]
    gain_k = lax.dynamic_slice_in_dim(gain_key, zc * 128, 128, 0)[None]
    x_all, q_raw, k_raw, q_rot, kv_rot, squares = kernel_call(
        project_body,
        [
            *in_hbm(
                0, shaped((1024, 256), F32), shaped((1024, 128), F32),
                shaped((1024, 256), BF16), shaped((1024, 256), BF16),
            ),
            shaped((16, 128), F32),
        ],
        [x_blocks, weight, gain_q, gain_k, cosine, sine],
        flops=2 * 1024 * 1024 * 512, nbytes=9 << 20,
    )

    kv_low = swap(kv_rot, LOW_TO_HIGH)
    squares = sum_group(squares)
    squares_low = swap(squares[8:], LOW_TO_HIGH)
    kv_low, squares, squares_low, w_wide, w_narrow, w_out_rows = lax.optimization_barrier(
        (kv_low, squares, squares_low, w_wide, w_narrow, w_out_rows)
    )
    w_wide = lax.all_gather(w_wide, "fsdp", axis=0, tiled=True)
    w_out_rows = spread(w_out_rows)
    out_raw, mixed, mixed_turned, q_tiles, keys, vals, logs = kernel_call(
        attend_body,
        [
            *in_hbm(
                shaped((1024, 256), F32), shaped((1024, 256), BF16), shaped((256, 1024), BF16),
                shaped((8, 256, 128), BF16), shaped((2048, 128), BF16), shaped((2048, 128), BF16),
            ),
            shaped((8, 256), F32),
        ],
        [place, *in_hbm(q_rot, kv_rot), kv_low, squares, squares_low],
        [pltpu.VMEM((128, 2048), BF16)],
        flops=4 * 1024 * 2048 * 256, nbytes=9 << 20,
    )
    a_mine, a_part = kernel_call(
        output_body,
        [shaped((512, 1024), F32), shaped((512, 1024), BF16)],
        [*in_hbm(mixed), w_out_rows],
        flops=2 * 1024 * 1024 * 256, nbytes=5 << 20,
    )
    x_turned = x_all.T

    attended = scatter_group(a_mine, a_part)
    attended, x_turned = lax.optimization_barrier((attended, x_turned))
    attn_scale = norm_scale(attended)
    attn_hat = attended * attn_scale
    hidden_state = inputs.astype(F32) + attn_hat * gain_attn
    h_all, gate, up, expanded, m_mine, m_part, w_down_rows = kernel_call(
        expand_body,
        [
            0, shaped((512, 768), F32), shaped((512, 768), F32), shaped((512, 768), BF16),
            shaped((256, 1024), F32), shaped((256, 1024), BF16), shaped((768, 1024), BF16),
        ],
        [
            gather_pair(hidden_state.astype(BF16)), *in_hbm(w_wide), *in_hbm(w_narrow),
        ],
        flops=2 * 512 * 2304 * 1024, nbytes=12 << 20,
    )
    projected, _ = scatter_pair(m_mine, m_part)
    mlp_scale = norm_scale(projected)
    mlp_hat = projected * mlp_scale
    output = (hidden_state + mlp_hat * gain_mlp).astype(BF16)[None]

    upstream = out_grad[0].astype(F32)
    grad_gain_mlp = jnp.sum(upstream * mlp_hat, axis=0)
    d_projected = norm_back(upstream * gain_mlp, mlp_hat, mlp_scale).astype(BF16)
    n = jnp.arange(1024, dtype=jnp.int32)
    source = ((n // 8) % 16) * 64 + (n // 128) * 8 + n % 8
    order = (n[None, :] == source[:, None]).astype(BF16)
    h_turned = dot_nt(order, h_all).astype(BF16)
    d_blocks = gather_pair(d_projected)
    d_blocks[3], h_turned = lax.optimization_barrier((d_blocks[3], h_turned))
    dm_all, d_gu, dh_mine, dh_part = kernel_call(
        expand_back_body,
        [
            0, shaped((512, 1536), BF16), shaped((256, 1024), F32), shaped((256, 1024), BF16),
        ],
        [d_blocks, gate, up, w_wide, w_down_rows],
        flops=2 * 512 * 2304 * 1024, nbytes=12 << 20,
    )

    far = dh_mine[128:] + swap(dh_part[128:], CORE_SWAP).astype(F32)
    far, d_gu, dm_all = lax.optimization_barrier((far.astype(BF16), d_gu, dm_all))
    far = swap(far, Z_SWAP)
    (grad_mlp,) = kernel_call(
        expand_grad_body,
        in_hbm(shaped((1024, 2560), BF16)),
        [h_turned, d_gu, expanded, dm_all],
        [pltpu.VMEM((768, 512), BF16)],
        flops=2 * 512 * 2304 * 1024, nbytes=9 << 20,
    )
    far, grad_mlp = lax.optimization_barrier((far, grad_mlp))
    d_hidden = upstream + dh_mine[:128] + swap(dh_part[:128], CORE_SWAP).astype(F32)
    d_hidden = d_hidden + far.astype(F32)

    grad_gain_attn = jnp.sum(d_hidden * attn_hat, axis=0)
    d_attended = norm_back(d_hidden * gain_attn, attn_hat, attn_scale).astype(BF16)
    d_tiles, deltas, grad_mlp = kernel_call(
        output_back_body,
        [shaped((8, 256, 128), BF16), shaped((8, 2, 128), F32), Stripe(2304, 256)],
        [
            place, *in_hbm(out_raw, w_out_rows, gather_group(d_attended), mixed_turned),
            grad_mlp,
        ],
        flops=4 * 1024 * 1024 * 256, nbytes=6 << 20,
    )
    grad_mlp = lax.psum_scatter(grad_mlp, "fsdp", scatter_dimension=0, tiled=True)
    dq, dk, dv, d_low, dots = kernel_call(
        attend_back_body,
        [
            *in_hbm(
                shaped((1024, 256), BF16), shaped((1024, 128), F32), shaped((1024, 128), F32),
                shaped((1024, 256), BF16),
            ),
            shaped((24, 128), F32),
        ],
        [place, *in_hbm(q_tiles, keys, vals), logs, d_tiles, deltas],
        [
            pltpu.VMEM((128, 2048), BF16), pltpu.VMEM((2048, 128), F32),
            pltpu.VMEM((2048, 128), F32),
        ],
        flops=10 * 1024 * 2048 * 256, nbytes=8 << 20,
    )
    d_got = swap(d_low, HIGH_TO_LOW)
    dots = sum_group(dots)
    dots_got = swap(dots[16:], HIGH_TO_LOW)

    gains = jnp.concatenate([grad_gain_attn.reshape(128, 8), grad_gain_mlp.reshape(128, 8)], axis=1)
    gains = jnp.broadcast_to(
        jnp.pad(gains.astype(BF16), ((0, 0), (24, 88)))[:, None, :], (128, 8, 128)
    ).reshape(1024, 128)
    d_made, sent = kernel_call(
        unproject_body,
        [shaped((1024, 512), BF16), shaped((1024, 640), BF16)],
        [
            place, *in_hbm(dq, dk, dv), d_got, *in_hbm(q_raw, k_raw), squares, dots, dots_got, cosine, sine,
            gain_q, gain_k, *in_hbm(x_turned), gains,
        ],
        [pltpu.VMEM((8, 384), F32)],
        flops=2 * 1024 * 1024 * 512, nbytes=9 << 20,
    )

    def halves(value, upper):
        low, high = value[: value.shape[0] // 2], value[value.shape[0] // 2 :]
        return jnp.where(upper, high, low), jnp.where(upper, low, high)

    mine, given = halves(grad_mlp, xh == 1)
    mine = mine.astype(F32) + swap(given, X_SWAP).astype(F32)
    got_made = lax.all_to_all(
        sent.reshape(128, 8, 640), ("seq", "fsdp"), split_axis=0, concat_axis=0, tiled=True
    )
    dx_mine, dx_part = kernel_call(
        input_body,
        [shaped((512, 1024), F32), shaped((512, 1024), BF16)],
        [after(d_made, sent), weight],
        flops=2 * 1024 * 1024 * 512, nbytes=5 << 20,
    )
    rows = [slice(k * 128, k * 128 + 128) for k in range(4)]
    pieces = [dx_mine[r] + swap(dx_part[r], CORE_SWAP).astype(F32) for r in rows]
    far = [piece.astype(BF16) for piece in pieces[1:]]
    d_inputs = pieces[0] + sum(
        swap(piece, to_z(k)).astype(F32) for k, piece in enumerate(far, 1)
    )
    got_made, mine, d_inputs = lax.optimization_barrier((got_made, mine, d_inputs))

    grad_down = jnp.concatenate(
        [
            mine[:48, 1536:2304],
            jnp.concatenate([mine[48:, 1536 + m * 256 : 1792 + m * 256] for m in range(3)], axis=0),
        ],
        axis=1,
    )
    grad_out = jnp.concatenate([mine[m * 16 : m * 16 + 16, 2304:] for m in range(4)], axis=1)
    grad_out = swap(grad_out.astype(BF16), OUT_HOME)
    grad_down, given_down = halves(grad_down, z >= 2)
    mine, given = halves(mine[:, :1536], z >= 2)
    given = swap(
        jnp.concatenate([given.reshape(48, 1024), given_down], axis=0).astype(BF16), FAR_SWAP
    ).astype(F32)
    mine = (mine + given[:48].reshape(32, 1536)).astype(BF16)
    grad_down = (grad_down + given[48:]).astype(BF16)

    grad_down = lax.ppermute(grad_down, ("seq", "fsdp"), DOWN_HOME)
    mine, given = halves(mine, z % 2 == 1)
    got = swap(given, Z_SWAP)
    mine = jnp.stack([jnp.where(z % 2 == 1, got, mine), jnp.where(z % 2 == 1, mine, got)])
    mine = mine.reshape(2, 2, 8, 1536)
    given = jnp.where(c == 1, mine[:, 0], mine[:, 1])
    mine = jnp.where(c == 1, mine[:, 1], mine[:, 0])
    got = swap(given, CORE_SWAP)
    got_wide = jnp.stack([jnp.where(c == 1, got, mine), jnp.where(c == 1, mine, got)], axis=1)

    summed = jnp.sum(got_made.reshape(2, 8, 8, 8, 640).astype(F32), axis=(0, 2))
    gains = jnp.sum(summed[:, 0, 512:], axis=0)

    def take(first, width):
        return summed[:, :, first : first + width].swapaxes(0, 1).reshape(8, 8 * width)

    wide = got_wide.astype(F32).reshape(4, 8, 2, 8, 96)
    wide = wide.transpose(2, 1, 3, 0, 4).reshape(2, 8, 3072)
    return (
        output,
        (d_hidden + d_inputs).astype(BF16)[None],
        take(0, 256),
        take(256, 128),
        take(384, 128),
        grad_out.astype(F32),
        wide[0],
        wide[1],
        grad_down.astype(F32),
        gains[:16],
        gains[16:24],
        gains[24:32],
        gains[32:40],
    )


def solution(mesh):
    rows = P("fsdp", "seq", None)
    weight = P("fsdp", None)
    grad = P(("seq", "fsdp"), None)
    gain = P(("seq", "fsdp"))
    return jax.shard_map(
        on_device,
        mesh=mesh,
        in_specs=(rows,) * 2 + (weight,) * 7 + (P(),) * 4,
        out_specs=(rows,) * 2 + (grad,) * 7 + (gain,) * 4,
        check_vma=False,
    )
```

```python
import functools
import math

import jax
import jax.numpy as jnp
from jax import lax
from jax.experimental import pallas as pl
from jax.experimental.pallas import tpu as pltpu
from jax.sharding import PartitionSpec as P

BF16 = jnp.bfloat16
F32 = jnp.float32
DH = 128
EPS = 1e-06
THETA = 1000000.0
MASKED = -1e30
LOG2E = math.log2(math.e)
QUERY_SCALE = DH ** (-0.5) * LOG2E
VMEM_BYTES = 20 * 1024 * 1024
VMEM = pl.BlockSpec(memory_space=pltpu.VMEM)
SMEM = pl.BlockSpec(memory_space=pltpu.SMEM)
ANY = pl.BlockSpec(memory_space=pl.ANY)
SMALL = 64 * 1024
NT = (((1,), (1,)), ((), ()))

SEQ_PLACES = [(xh, z, c) for xh in range(2) for z in range(4) for c in range(2)]


def seq_index(xh, z, c):
    return xh * 8 + (z % 4) * 2 + c


CORE_SWAP = [(i, i ^ 1) for i in range(16)]
LOW_TO_HIGH = [(i, i + 8) for i in range(8)]
HIGH_TO_LOW = [(i + 8, i) for i in range(8)]
X_SWAP = [(i, i ^ 8) for i in range(16)]


def from_z(k):
    return [(seq_index(xh, z + k, c), seq_index(xh, z, c)) for xh, z, c in SEQ_PLACES]


def to_z(k):
    return [(seq_index(xh, z, c), seq_index(xh, z + k, c)) for xh, z, c in SEQ_PLACES]


def across(pairs):
    return [(seq * 8 + f, to_seq * 8 + to_f) for seq, f, to_seq, to_f in pairs]


TURN = across(
    (xh * 8 + a, f, xh * 8 + f, a) for xh in range(2) for a in range(8) for f in range(8)
)
Z_SWAP = [(i, i ^ 2) for i in range(16)]
FAR_SWAP = [(i, i ^ 4) for i in range(16)]
OUT_HOME = [(xh * 8 + a, 2 * a + xh) for xh in range(2) for a in range(8)]
DOWN_HOME = across(
    (seq_index(xh, 2 * zh + zl, c), f, 2 * f + zl, 4 * c + 2 * xh + zh)
    for xh in range(2) for zh in range(2) for zl in range(2) for c in range(2) for f in range(8)
)


def swap(value, pairs):
    return lax.ppermute(value, "seq", pairs)


def after(value, *others):
    return lax.optimization_barrier((value, *others))[0]


def gather_group(block):
    far = {k: swap(block, from_z(k)) for k in (2, 1, 3)}
    mine = [block, far[1], far[2], far[3]]
    return mine + [swap(v, CORE_SWAP) for v in mine]


def scatter_group(mine, part):
    rows = [slice(k * 128, k * 128 + 128) for k in range(4)]
    out = None
    for k in (2, 1, 3, 0):
        piece = mine[rows[k]] + swap(part[rows[k]], CORE_SWAP).astype(F32)
        if k:
            piece = swap(piece.astype(BF16), to_z(k)).astype(F32)
        out = piece if out is None else out + piece
    return out


def gather_pair(block):
    mine = [block, swap(block, Z_SWAP)]
    return mine + [swap(v, CORE_SWAP) for v in mine]


def scatter_pair(mine, part, later=()):
    far = mine[128:] + swap(part[128:], CORE_SWAP).astype(F32)
    far, *later = lax.optimization_barrier((far.astype(BF16), *later))
    far = swap(far, Z_SWAP).astype(F32)
    return mine[:128] + swap(part[:128], CORE_SWAP).astype(F32) + far, later


def sum_group(rows):
    groups = rows.shape[0] // 8
    other = swap(rows, CORE_SWAP).reshape(groups, 2, 4, 128)
    pair = rows.reshape(groups, 2, 4, 128) + jnp.concatenate([other[:, 1:], other[:, :1]], axis=1)
    odd = lax.axis_index("seq") // 2 % 2 == 1
    got = swap(pair, Z_SWAP)
    up = jnp.concatenate([got[:, :, 3:], got[:, :, :3]], axis=2)
    down = jnp.concatenate([got[:, :, 1:], got[:, :, :1]], axis=2)
    pair = pair + jnp.where(odd, down, up)
    got = swap(pair, FAR_SWAP)
    pair = pair + jnp.concatenate([got[:, :, 2:], got[:, :, :2]], axis=2)
    return pair.reshape(rows.shape)


def column(row):
    return jnp.transpose(jnp.broadcast_to(row, (128, 128)))


def row_sums(values):
    return jnp.sum(jnp.transpose(values), axis=0, keepdims=True)


def shaped(shape, dtype):
    return jax.ShapeDtypeStruct(shape, dtype)


class Kept:
    def __init__(self, value):
        self.value = value


def in_hbm(*values):
    return [Kept(v) for v in values]


def kernel_call(body, outs, inputs, scratch=(), flops=0, nbytes=0):
    hbm_outs = [isinstance(o, Kept) for o in outs]
    hbm_ins = [isinstance(x, Kept) for x in inputs]
    outs = [o.value if isinstance(o, Kept) else o for o in outs]
    inputs = [x.value if isinstance(x, Kept) else x for x in inputs]
    groups = [x if isinstance(x, list) else [x] for x in inputs]
    flat = [a for group in groups for a in group]
    joined = [
        shaped((sum(a.shape[0] for a in group),) + group[0].shape[1:], group[0].dtype)
        for group in groups
    ]

    def large(s):
        return math.prod(s.shape) * s.dtype.itemsize >= SMALL

    def where(s):
        return ANY if large(s) else SMEM if s.dtype == jnp.int32 else VMEM

    out_shapes = [joined[o] if isinstance(o, int) else o for o in outs]
    in_buffers = [pltpu.VMEM(s.shape, s.dtype) for s in joined if large(s)]
    out_buffers = [
        pltpu.VMEM(o.shape, o.dtype) for o in outs if not isinstance(o, int) and large(o)
    ]

    def whole(*refs):
        refs = list(refs)

        def pull(count):
            taken = refs[:count]
            del refs[:count]
            return taken

        in_refs, out_refs = pull(len(flat)), pull(len(outs))
        in_space, out_space = pull(len(in_buffers)), pull(len(out_buffers))
        own, (in_sem, out_sem) = pull(len(scratch)), refs
        loads, ins, at = {}, [], 0
        for group, s in zip(groups, joined):
            if not large(s):
                ins.append(in_refs[at])
                at += 1
                continue
            space, row = in_space.pop(0), 0
            loads[id(space)] = []
            for a in group:
                copy = pltpu.make_async_copy(
                    in_refs[at], space.at[pl.ds(row, a.shape[0])], in_sem.at[at]
                )
                copy.start()
                loads[id(space)].append(copy)
                row, at = row + a.shape[0], at + 1
            ins.append(space)
        made, stores = [], {}
        for k, (o, s, ref) in enumerate(zip(outs, out_shapes, out_refs)):
            if not large(s):
                made.append(ref)
                continue
            space = ins[o] if isinstance(o, int) else out_space.pop(0)
            stores[id(space)] = pltpu.make_async_copy(space, ref, out_sem.at[k])
            if not isinstance(o, int):
                made.append(space)
        started = []

        def ready(*spaces):
            for space in spaces:
                for copy in loads.pop(id(space), ()):
                    copy.wait()

        def done(*spaces):
            for space in spaces:
                copy = stores.pop(id(space))
                copy.start()
                started.append(copy)

        body(ready, done, *ins, *made, *own)
        for key in list(stores):
            copy = stores.pop(key)
            copy.start()
            started.append(copy)
        for copy in started:
            copy.wait()

    shapes = [pltpu.HBM(s.shape, s.dtype) if hbm else s for s, hbm in zip(out_shapes, hbm_outs)]
    return pl.pallas_call(
        whole,
        out_shape=tuple(shapes),
        in_specs=[where(s) for group, s in zip(groups, joined) for _ in group],
        out_specs=tuple(where(s) for s in out_shapes),
        scratch_shapes=[
            *in_buffers, *out_buffers, *scratch,
            pltpu.SemaphoreType.DMA((len(flat),)), pltpu.SemaphoreType.DMA((len(outs),)),
        ],
        compiler_params=pltpu.CompilerParams(vmem_limit_bytes=VMEM_BYTES),
        cost_estimate=pl.CostEstimate(flops=flops, bytes_accessed=nbytes, transcendentals=0),
    )(
        *[
            pltpu.with_memory_space_constraint(a, pltpu.HBM) if hbm else a
            for group, hbm in zip(groups, hbm_ins)
            for a in group
        ],
    )


def root(total, width):
    return lax.rsqrt(total * (1.0 / width) + EPS)


def project_body(
    ready, done, x_all, weight, gain_q, gain_k, cos, sin,
    q_raw, k_raw, q_rot, kv_rot, squares,
):
    ready(x_all, weight, cos, sin)
    done(x_all)

    def step(t, carry):
        at = pl.multiple_of(t * 256, 256)
        made = jnp.dot(x_all[pl.ds(at, 256), :], weight[...], preferred_element_type=F32)
        for part in range(2):
            rows = pl.ds(at + part * 128, 128)
            block = t * 2 + part
            here = made[part * 128 : part * 128 + 128]
            q, k = here[:, :256], here[:, 256:384]
            kv_rot[rows, 128:] = here[:, 384:].astype(BF16)
            q_raw[rows, :] = q
            k_raw[rows, :] = k
            squares[pl.ds(block, 1), :] = row_sums(
                q[:, :128] * q[:, :128] + q[:, 128:] * q[:, 128:]
            )
            squares[pl.ds(block + 8, 1), :] = row_sums(k * k)
            cosine, sine = cos[rows, :], sin[rows, :]
            for head in range(2):
                lanes = slice(head * 128, head * 128 + 128)
                turn = q[:, lanes] * gain_q[:, lanes]
                q_rot[rows, lanes] = (turn * cosine + pltpu.roll(turn, 64, 1) * sine).astype(BF16)
            turn = k * gain_k[...]
            kv_rot[rows, :128] = (turn * cosine + pltpu.roll(turn, 64, 1) * sine).astype(BF16)
        return carry

    lax.fori_loop(0, 4, step, 0)


def spot(place, block):
    z = lax.rem(place[1] + block % 4, 4)
    c = place[2] if block < 4 else 1 - place[2]
    return z, c


def attend_body(
    ready, done, place, q_rot, kv_rot, kv_low, squares, squares_low,
    out_raw, out_low, out_turned, q_tiles, keys, vals, logs, vals_t,
):
    ready(q_rot, kv_rot, kv_low)
    for b in range(8):
        rows = slice(b * 128, b * 128 + 128)
        z, c = spot(place, b)
        r = column(root(squares[b : b + 1, :], 2048.0)) * QUERY_SCALE
        inner = pl.ds(pl.multiple_of(c * 128, 128), 128)
        for head in range(2):
            q = q_rot[rows, head * 128 : head * 128 + 128].astype(F32)
            q_tiles[z * 2 + head, inner, :] = (q * r).astype(BF16)
        at = pl.ds(pl.multiple_of(1024 + z * 256 + c * 128, 128), 128)
        r = column(root(squares[8 + b : 9 + b, :], 1024.0))
        keys[at, :] = (kv_rot[rows, :128].astype(F32) * r).astype(BF16)
        vals[at, :] = kv_rot[rows, 128:]
        r = column(root(squares_low[b : b + 1, :], 1024.0))
        keys[rows, :] = (kv_low[rows, :128].astype(F32) * r).astype(BF16)
        vals[rows, :] = kv_low[rows, 128:]
    done(q_tiles, keys, vals)
    vals_t[...] = jnp.transpose(vals[...].astype(F32)).astype(BF16)
    allowed = lax.broadcasted_iota(jnp.int32, (256, 256), 0) <= lax.broadcasted_iota(
        jnp.int32, (256, 256), 1
    )

    def queries(first, i):
        at_diagonal = 1024 + i * 256
        ranges = [(first, at_diagonal)] if at_diagonal > first else []
        for head in range(2):
            q = q_tiles[i * 2 + head]
            scores = [
                lax.dot_general(keys[lo:hi, :], q, NT, preferred_element_type=F32)
                for lo, hi in ranges + [(at_diagonal, at_diagonal + 256)]
            ]
            scores[-1] = jnp.where(allowed, scores[-1], MASKED)
            tops = [jnp.max(s, axis=0, keepdims=True) for s in scores]
            top = functools.reduce(jnp.maximum, tops)
            total, acc = 0.0, 0.0
            for s, (lo, hi) in zip(scores, ranges + [(at_diagonal, at_diagonal + 256)]):
                p = jnp.exp2(s - top)
                total = total + jnp.sum(p, axis=0, keepdims=True)
                acc = acc + jnp.dot(
                    vals_t[:, lo:hi], p.astype(BF16), preferred_element_type=F32
                )
            turned = acc / total
            out = jnp.transpose(turned)
            turned = turned.astype(BF16)
            logs[i * 2 + head : i * 2 + head + 1, :] = top + jnp.log2(total)
            for c in range(2):
                block = lax.rem(i - place[1] + 4, 4) + 4 * jnp.abs(c - place[2])
                at = pl.ds(pl.multiple_of(block * 128, 128), 128)
                lanes = slice(head * 128, head * 128 + 128)
                out_raw[at, lanes] = out[c * 128 : c * 128 + 128, :]
                out_low[at, lanes] = out[c * 128 : c * 128 + 128, :].astype(BF16)
                out_turned[lanes, at] = turned[:, c * 128 : c * 128 + 128]

    @pl.when(place[0] == 1)
    def _():
        for i in range(4):
            queries(0, i)

    @pl.when(place[0] == 0)
    def _():
        for i in range(4):
            queries(1024, i)

    done(out_raw, out_low, out_turned)


def output_body(ready, done, mixed, w_out, a_mine, a_part):
    ready(mixed, w_out)

    def project(t, carry):
        at = pl.ds(pl.multiple_of(t * 256, 256), 256)
        far = pl.ds(pl.multiple_of(512 + t * 256, 256), 256)
        a_part[at, :] = jnp.dot(mixed[far, :], w_out[...], preferred_element_type=F32).astype(BF16)
        a_mine[at, :] = jnp.dot(mixed[at, :], w_out[...], preferred_element_type=F32)
        return carry

    lax.fori_loop(0, 2, project, 0)


def output_back_body(
    ready, done, place, out_raw, w_out, da_all, mixed_turned, d_tiles, deltas, grad_out
):
    ready(out_raw, w_out, da_all)
    for b in range(8):
        rows = slice(b * 128, b * 128 + 128)
        z, c = spot(place, b)
        inner = pl.ds(pl.multiple_of(c * 128, 128), 128)
        d_out = lax.dot_general(
            da_all[rows, :], w_out[...], NT, preferred_element_type=F32
        ).astype(BF16)
        for head in range(2):
            lanes = slice(head * 128, head * 128 + 128)
            grad = d_out[:, lanes]
            d_tiles[z * 2 + head, inner, :] = grad
            deltas[z * 2 + head, pl.ds(c, 1), :] = row_sums(grad.astype(F32) * out_raw[rows, lanes])
    done(d_tiles)
    ready(mixed_turned)
    for m in range(4):
        lanes = slice(m * 256, m * 256 + 256)
        made = jnp.dot(mixed_turned[...], da_all[:, lanes], preferred_element_type=F32).astype(BF16)
        for j in range(2):
            for f in range(8):
                to, at = f * 32 + j * 16, j * 128 + f * 16
                grad_out[to : to + 16, lanes] = made[at : at + 16]


def attend_back_body(
    ready, done, place, q_tiles, keys, vals, logs, d_tiles, deltas,
    dq, dk, dv, d_low, dots, keys_t, dk_acc, dv_acc,
):
    ready(keys)
    keys_t[...] = jnp.transpose(keys[...].astype(F32)).astype(BF16)
    ready(q_tiles, vals, d_tiles)
    dk_acc[...] = jnp.zeros_like(dk_acc)
    dv_acc[...] = jnp.zeros_like(dv_acc)
    allowed = lax.broadcasted_iota(jnp.int32, (256, 256), 0) <= lax.broadcasted_iota(
        jnp.int32, (256, 256), 1
    )

    def queries(first, i):
        at_diagonal = 1024 + i * 256
        q = [q_tiles[i * 2 + head] for head in range(2)]
        grad = [d_tiles[i * 2 + head] for head in range(2)]
        log = [logs[i * 2 + head : i * 2 + head + 1, :] for head in range(2)]
        delta = [
            jnp.concatenate([deltas[i * 2 + head, 0:1, :], deltas[i * 2 + head, 1:2, :]], axis=1)
            for head in range(2)
        ]
        total = [0.0, 0.0]
        for lo in range(first, at_diagonal + 256, 256):
            at = slice(lo, lo + 256)
            k, v = keys[at, :], vals[at, :]
            dk_tile, dv_tile = dk_acc[at, :], dv_acc[at, :]
            for head in range(2):
                s = lax.dot_general(k, q[head], NT, preferred_element_type=F32)
                p = jnp.exp2(s - log[head])
                if lo == at_diagonal:
                    p = jnp.where(allowed, p, 0.0)
                dp = lax.dot_general(v, grad[head], NT, preferred_element_type=F32)
                ds = (p * (dp - delta[head])).astype(BF16)
                dv_tile += jnp.dot(p.astype(BF16), grad[head], preferred_element_type=F32)
                dk_tile += jnp.dot(ds, q[head], preferred_element_type=F32)
                total[head] = total[head] + jnp.dot(
                    keys_t[:, at], ds, preferred_element_type=F32
                )
            dk_acc[at, :] = dk_tile
            dv_acc[at, :] = dv_tile
        dot = jnp.zeros((1, 256), F32)
        for head in range(2):
            out = jnp.transpose(total[head]) * DH ** (-0.5)
            dot += jnp.sum(total[head] * jnp.transpose(q[head].astype(F32)), axis=0, keepdims=True)
            for c in range(2):
                block = lax.rem(i - place[1] + 4, 4) + 4 * jnp.abs(c - place[2])
                at = pl.ds(pl.multiple_of(block * 128, 128), 128)
                dq[at, head * 128 : head * 128 + 128] = out[c * 128 : c * 128 + 128, :].astype(BF16)
        for c in range(2):
            block = lax.rem(i - place[1] + 4, 4) + 4 * jnp.abs(c - place[2])
            dots[pl.ds(block, 1), :] = dot[:, c * 128 : c * 128 + 128] * (1.0 / LOG2E)

    @pl.when(place[0] == 1)
    def _():
        for i in range(4):
            queries(0, i)

    @pl.when(place[0] == 0)
    def _():
        for i in range(4):
            queries(1024, i)

    for b in range(8):
        rows = slice(b * 128, b * 128 + 128)
        z, c = spot(place, b)
        at = pl.ds(pl.multiple_of(1024 + z * 256 + c * 128, 128), 128)
        key_grad = dk_acc[at, :] * (1.0 / LOG2E)
        dk[rows, :] = key_grad
        dv[rows, :] = dv_acc[at, :]
        dots[8 + b : 9 + b, :] = row_sums(key_grad * keys[at, :].astype(F32))
        key_grad = dk_acc[rows, :] * (1.0 / LOG2E)
        d_low[rows, :128] = key_grad.astype(BF16)
        d_low[rows, 128:] = dv_acc[rows, :].astype(BF16)
        dots[16 + b : 17 + b, :] = row_sums(key_grad * keys[rows, :].astype(F32))


def unproject_body(
    ready, done, place, dq, dk, dv, d_got, q_raw, k_raw, squares, dots, dots_got, cos, sin,
    gain_q, gain_k, x_turned, gains, d_made, sent, sums,
):
    sums[...] = jnp.zeros_like(sums)
    ready(dq, dk, dv, d_got, q_raw, k_raw, cos, sin)

    def step(b, carry):
        rows = pl.ds(pl.multiple_of(b * 128, 128), 128)
        cosine, sine = cos[rows, :], sin[rows, :]
        r = column(root(squares[pl.ds(b, 1), :], 2048.0))
        mean = column(dots[pl.ds(b, 1), :]) * (1.0 / 2048.0)
        for head in range(2):
            lanes = slice(head * 128, head * 128 + 128)
            turn = dq[rows, lanes].astype(F32)
            d_norm = turn * cosine - pltpu.roll(turn, 64, 1) * sine
            hat = q_raw[rows, lanes] * r
            sums[0:1, lanes] += jnp.sum(d_norm * hat, axis=0, keepdims=True)
            d_made[rows, lanes] = (r * (d_norm * gain_q[:, lanes] - hat * mean)).astype(BF16)
        r = column(root(squares[pl.ds(b + 8, 1), :], 1024.0))
        mean = column(dots[pl.ds(b + 8, 1), :] + dots_got[pl.ds(b, 1), :]) * (1.0 / 1024.0)
        turn = dk[rows, :] + d_got[rows, :128].astype(F32)
        d_norm = turn * cosine - pltpu.roll(turn, 64, 1) * sine
        hat = k_raw[rows, :] * r
        sums[0:1, 256:] += jnp.sum(d_norm * hat, axis=0, keepdims=True)
        d_made[rows, 256:384] = (r * (d_norm * gain_k[...] - hat * mean)).astype(BF16)
        d_made[rows, 384:] = (dv[rows, :] + d_got[rows, 128:].astype(F32)).astype(BF16)
        return carry

    lax.fori_loop(0, 8, step, 0)
    done(d_made)
    ready(x_turned, gains)

    def grad(t, carry):
        rows = pl.ds(pl.multiple_of(t * 256, 256), 256)
        sent[rows, :512] = jnp.dot(
            x_turned[rows, :], d_made[...], preferred_element_type=F32
        ).astype(BF16)
        sent[rows, 512:] = gains[rows, :]
        return carry

    lax.fori_loop(0, 4, grad, 0)
    extra = 0.0
    for lo, width, each, first in ((0, 256, 16, 0), (256, 128, 8, 16)):
        row = lax.broadcasted_iota(jnp.int32, (128, width), 0) // 8
        lane = lax.broadcasted_iota(jnp.int32, (128, width), 1) // each
        spread = jnp.where(row == lane, sums[0:1, lo : lo + width], 0.0).astype(BF16)
        lane = lax.broadcasted_iota(jnp.int32, (width, 128), 0) % each + first
        pick = jnp.where(lane == lax.broadcasted_iota(jnp.int32, (width, 128), 1), 1.0, 0.0)
        extra = extra + jnp.dot(spread, pick.astype(BF16), preferred_element_type=F32)
    rows = pl.ds(pl.multiple_of((place[1] * 2 + place[2]) * 128, 128), 128)
    sent[rows, 512:] = (gains[rows, :].astype(F32) + extra).astype(BF16)


def input_body(ready, done, d_made, weight, dx_mine, dx_part):
    ready(d_made, weight)

    def step(t, carry):
        at = pl.ds(pl.multiple_of(t * 256, 256), 256)
        far = pl.ds(pl.multiple_of(512 + t * 256, 256), 256)
        dx_part[at, :] = lax.dot_general(
            d_made[far, :], weight[...], NT, preferred_element_type=F32
        ).astype(BF16)
        dx_mine[at, :] = lax.dot_general(
            d_made[at, :], weight[...], NT, preferred_element_type=F32
        )
        return carry

    lax.fori_loop(0, 2, step, 0)


def expand_body(ready, done, h_all, weight, gate, up, expanded, m_mine, m_part, down):
    ready(weight)
    for f in range(8):
        down[f * 96 : f * 96 + 96, :768] = weight[f * 128 : f * 128 + 96, 1536:]
        for m in range(3):
            down[f * 96 + m * 32 : f * 96 + m * 32 + 32, 768:] = weight[
                f * 128 + 96 : f * 128 + 128, 1536 + m * 256 : 1792 + m * 256
            ]

    done(down)
    ready(h_all)
    done(h_all)

    def widen(n, carry):
        lanes = pl.ds(pl.multiple_of(n * 256, 256), 256)
        upper = pl.ds(pl.multiple_of(768 + n * 256, 256), 256)
        g = jnp.dot(h_all[...], weight[:, lanes], preferred_element_type=F32)
        u = jnp.dot(h_all[...], weight[:, upper], preferred_element_type=F32)
        gate[:, lanes] = g
        up[:, lanes] = u
        expanded[:, lanes] = (g * jax.nn.sigmoid(g) * u).astype(BF16)
        return carry

    lax.fori_loop(0, 3, widen, 0)
    done(gate, up, expanded)

    def narrow(n, carry):
        lanes = pl.ds(pl.multiple_of(n * 256, 256), 256)
        m = jnp.dot(expanded[...], down[:, lanes], preferred_element_type=F32)
        m_mine[:, lanes] = m[:256]
        m_part[:, lanes] = m[256:].astype(BF16)
        return carry

    lax.fori_loop(0, 4, narrow, 0)


def expand_back_body(ready, done, dm_all, gate, up, weight, down, d_gu, dh_mine, dh_part):
    ready(dm_all, gate, up, down)
    done(dm_all)

    def widen(n, carry):
        lanes = pl.ds(pl.multiple_of(n * 256, 256), 256)
        upper = pl.ds(pl.multiple_of(768 + n * 256, 256), 256)
        de = lax.dot_general(dm_all[...], down[lanes, :], NT, preferred_element_type=F32)
        g = gate[:, lanes]
        sig = jax.nn.sigmoid(g)
        d_gu[:, lanes] = (de * up[:, lanes] * sig * (1.0 + g * (1.0 - sig))).astype(BF16)
        d_gu[:, upper] = (de * (g * sig)).astype(BF16)
        return carry

    lax.fori_loop(0, 3, widen, 0)
    done(d_gu)
    ready(weight)

    def narrow(n, carry):
        lanes = pl.ds(pl.multiple_of(n * 256, 256), 256)
        dh = lax.dot_general(d_gu[...], weight[lanes, :1536], NT, preferred_element_type=F32)
        dh_mine[:, lanes] = dh[:256]
        dh_part[:, lanes] = dh[256:].astype(BF16)
        return carry

    lax.fori_loop(0, 4, narrow, 0)


def expand_grad_body(ready, done, h_turned, d_gu, expanded, dm_all, out, expanded_t):
    ready(expanded)
    expanded_t[...] = jnp.transpose(expanded[...].astype(F32)).astype(BF16)

    ready(h_turned, d_gu, dm_all)

    def widen(n, carry):
        lanes = pl.ds(pl.multiple_of(n * 256, 256), 256)
        out[:, lanes] = jnp.dot(
            h_turned[...], d_gu[:, lanes], preferred_element_type=F32
        ).astype(BF16)
        return carry

    lax.fori_loop(0, 6, widen, 0)
    for n in range(4):
        made = jnp.dot(
            expanded_t[...], dm_all[:, n * 256 : n * 256 + 256], preferred_element_type=F32
        ).astype(BF16)
        for f in range(16):
            if n < 3:
                out[f * 64 : f * 64 + 48, 1536 + n * 256 : 1792 + n * 256] = made[
                    f * 48 : f * 48 + 48
                ]
                continue
            for m in range(3):
                out[f * 64 + 48 : f * 64 + 64, 1536 + m * 256 : 1792 + m * 256] = made[
                    f * 48 + m * 16 : f * 48 + m * 16 + 16
                ]


def norm_scale(values):
    return lax.rsqrt(jnp.mean(values * values, axis=-1, keepdims=True) + EPS)


def norm_back(upstream, normed, scaling):
    return scaling * (upstream - normed * jnp.mean(upstream * normed, axis=-1, keepdims=True))


def rotary_tables(first, z, c):
    half = DH // 2
    k = jnp.arange(4, dtype=jnp.int32)
    starts = jnp.concatenate([((z + k) % 4) * 256 + c * 128, ((z + k) % 4) * 256 + (1 - c) * 128])
    places = (first + starts[:, None] + jnp.arange(128, dtype=jnp.int32)[None, :]).reshape(1024)
    inverse = THETA ** (-(jnp.arange(half, dtype=F32) * (2.0 / DH)))
    angles = places.astype(F32)[:, None] * inverse[None, :]
    cosine, sine = jnp.cos(angles), jnp.sin(angles)
    return (
        jnp.concatenate([cosine, cosine], axis=-1),
        jnp.concatenate([-sine, sine], axis=-1),
    )


def dot(a, b):
    return jnp.dot(a, b, preferred_element_type=F32)


def dot_nt(a, b):
    return lax.dot_general(a, b, NT, preferred_element_type=F32)


def dot_tn(a, b):
    return lax.dot_general(a, b, (((0,), (0,)), ((), ())), preferred_element_type=F32)


def on_device(
    tokens, out_grad, w_query, w_key, w_value, w_out, w_gate, w_up, w_down,
    gain_query, gain_key, gain_attn, gain_mlp,
):
    seq = lax.axis_index("seq")
    xh, zc = seq // 8, seq % 8
    z, c = zc // 2, zc % 2
    quarter = (z % 2) * 2 + c
    place = jnp.stack([xh, z, c]).astype(jnp.int32)
    inputs = tokens[0]

    def columns(weight, width):
        return lax.dynamic_slice_in_dim(weight, zc * width, width, 1)

    def spread(block):
        return lax.all_to_all(
            jnp.broadcast_to(block[None], (8,) + block.shape),
            "fsdp", split_axis=0, concat_axis=0, tiled=True,
        ).reshape(8 * block.shape[0], block.shape[1])

    x_blocks = gather_group(inputs)
    weight = spread(
        jnp.concatenate(
            [columns(w_query, 256), columns(w_key, 128), columns(w_value, 128)], axis=1
        )
    )
    w_out_rows = lax.ppermute(
        after(lax.dynamic_slice_in_dim(w_out, zc * 32, 32, 0), *x_blocks[1:4]),
        ("seq", "fsdp"),
        TURN,
    )

    def quarters(weight):
        part = lax.dynamic_slice_in_dim(weight.reshape(128, 8, 384), quarter * 96, 96, 2)
        return part.reshape(128, 768)

    down = lax.dynamic_slice_in_dim(w_down, quarter * 96, 96, 0)
    packed = jnp.concatenate(
        [
            down[:, :768],
            jnp.concatenate([down[m * 32 : m * 32 + 32, 768:] for m in range(3)], axis=1),
        ],
        axis=0,
    )
    w_mlp = jnp.concatenate([quarters(w_gate), quarters(w_up), packed], axis=1)
    weight, w_mlp, w_out_rows = lax.optimization_barrier((weight, w_mlp, w_out_rows))

    cosine, sine = rotary_tables(xh * 1024, z, c)
    gain_q = lax.dynamic_slice_in_dim(gain_query, zc * 256, 256, 0)[None]
    gain_k = lax.dynamic_slice_in_dim(gain_key, zc * 128, 128, 0)[None]
    x_all, q_raw, k_raw, q_rot, kv_rot, squares = kernel_call(
        project_body,
        [
            *in_hbm(
                0, shaped((1024, 256), F32), shaped((1024, 128), F32),
                shaped((1024, 256), BF16), shaped((1024, 256), BF16),
            ),
            shaped((16, 128), F32),
        ],
        [x_blocks, weight, gain_q, gain_k, cosine, sine],
        flops=2 * 1024 * 1024 * 512, nbytes=9 << 20,
    )

    kv_low = swap(kv_rot, LOW_TO_HIGH)
    w_mlp = lax.all_gather(after(w_mlp, squares), "fsdp", axis=0, tiled=True)
    squares = sum_group(squares)
    squares_low = swap(squares[8:], LOW_TO_HIGH)
    w_out_rows = spread(after(w_out_rows, squares_low))
    out_raw, mixed, mixed_turned, q_tiles, keys, vals, logs = kernel_call(
        attend_body,
        [
            *in_hbm(
                shaped((1024, 256), F32), shaped((1024, 256), BF16), shaped((256, 1024), BF16),
                shaped((8, 256, 128), BF16), shaped((2048, 128), BF16), shaped((2048, 128), BF16),
            ),
            shaped((8, 256), F32),
        ],
        [place, *in_hbm(q_rot, kv_rot), kv_low, squares, squares_low],
        [pltpu.VMEM((128, 2048), BF16)],
        flops=4 * 1024 * 2048 * 256, nbytes=9 << 20,
    )
    a_mine, a_part = kernel_call(
        output_body,
        [shaped((512, 1024), F32), shaped((512, 1024), BF16)],
        [*in_hbm(mixed), w_out_rows],
        flops=2 * 1024 * 1024 * 256, nbytes=5 << 20,
    )
    x_turned = x_all.T

    attended = scatter_group(a_mine, a_part)
    attended, x_turned = lax.optimization_barrier((attended, x_turned))
    attn_scale = norm_scale(attended)
    attn_hat = attended * attn_scale
    hidden_state = inputs.astype(F32) + attn_hat * gain_attn
    h_all, gate, up, expanded, m_mine, m_part, w_down_rows = kernel_call(
        expand_body,
        [
            0, shaped((512, 768), F32), shaped((512, 768), F32), shaped((512, 768), BF16),
            shaped((256, 1024), F32), shaped((256, 1024), BF16), shaped((768, 1024), BF16),
        ],
        [
            gather_pair(hidden_state.astype(BF16)), *in_hbm(w_mlp),
        ],
        flops=2 * 512 * 2304 * 1024, nbytes=12 << 20,
    )
    projected, _ = scatter_pair(m_mine, m_part)
    mlp_scale = norm_scale(projected)
    mlp_hat = projected * mlp_scale
    output = (hidden_state + mlp_hat * gain_mlp).astype(BF16)[None]

    upstream = out_grad[0].astype(F32)
    grad_gain_mlp = jnp.sum(upstream * mlp_hat, axis=0)
    d_projected = norm_back(upstream * gain_mlp, mlp_hat, mlp_scale).astype(BF16)
    n = jnp.arange(1024, dtype=jnp.int32)
    source = ((n // 8) % 16) * 64 + (n // 128) * 8 + n % 8
    order = (n[None, :] == source[:, None]).astype(BF16)
    h_turned = dot_nt(order, h_all).astype(BF16)
    d_blocks = gather_pair(d_projected)
    d_blocks[3], h_turned = lax.optimization_barrier((d_blocks[3], h_turned))
    dm_all, d_gu, dh_mine, dh_part = kernel_call(
        expand_back_body,
        [
            0, shaped((512, 1536), BF16), shaped((256, 1024), F32), shaped((256, 1024), BF16),
        ],
        [d_blocks, gate, up, w_mlp, w_down_rows],
        flops=2 * 512 * 2304 * 1024, nbytes=12 << 20,
    )

    far = dh_mine[128:] + swap(dh_part[128:], CORE_SWAP).astype(F32)
    far, d_gu, dm_all = lax.optimization_barrier((far.astype(BF16), d_gu, dm_all))
    far = swap(far, Z_SWAP)
    (grad_mlp,) = kernel_call(
        expand_grad_body,
        in_hbm(shaped((1024, 2304), BF16)),
        [h_turned, d_gu, expanded, dm_all],
        [pltpu.VMEM((768, 512), BF16)],
        flops=2 * 512 * 2304 * 1024, nbytes=9 << 20,
    )
    far, grad_mlp = lax.optimization_barrier((far, grad_mlp))
    grad_mlp = lax.psum_scatter(grad_mlp, "fsdp", scatter_dimension=0, tiled=True)
    d_hidden = upstream + dh_mine[:128] + swap(dh_part[:128], CORE_SWAP).astype(F32)
    d_hidden = d_hidden + far.astype(F32)

    grad_gain_attn = jnp.sum(d_hidden * attn_hat, axis=0)
    d_attended = norm_back(d_hidden * gain_attn, attn_hat, attn_scale).astype(BF16)
    d_tiles, deltas, grad_out = kernel_call(
        output_back_body,
        [shaped((8, 256, 128), BF16), shaped((8, 2, 128), F32), shaped((256, 1024), BF16)],
        [place, *in_hbm(out_raw, w_out_rows, gather_group(d_attended), mixed_turned)],
        flops=4 * 1024 * 1024 * 256, nbytes=6 << 20,
    )
    dq, dk, dv, d_low, dots = kernel_call(
        attend_back_body,
        [
            *in_hbm(
                shaped((1024, 256), BF16), shaped((1024, 128), F32), shaped((1024, 128), F32),
                shaped((1024, 256), BF16),
            ),
            shaped((24, 128), F32),
        ],
        [place, *in_hbm(q_tiles, keys, vals), logs, d_tiles, deltas],
        [
            pltpu.VMEM((128, 2048), BF16), pltpu.VMEM((2048, 128), F32),
            pltpu.VMEM((2048, 128), F32),
        ],
        flops=10 * 1024 * 2048 * 256, nbytes=8 << 20,
    )
    fsdp = lax.axis_index("fsdp")
    def halve(value, rows, bit, axis, pairs):
        parts = value.reshape(-1, 2, rows, 1024)
        given = jnp.where(bit == 1, parts[:, 0], parts[:, 1])
        mine = jnp.where(bit == 1, parts[:, 1], parts[:, 0]).astype(F32)
        return (mine + lax.ppermute(given, axis, pairs).astype(F32)).astype(BF16)

    grad_out = halve(grad_out, 32, fsdp % 2, "fsdp", [(i, i ^ 1) for i in range(8)])
    d_got = swap(d_low, HIGH_TO_LOW)
    dots = sum_group(dots)
    dots_got = swap(dots[16:], HIGH_TO_LOW)

    gains = jnp.concatenate([grad_gain_attn.reshape(128, 8), grad_gain_mlp.reshape(128, 8)], axis=1)
    gains = jnp.broadcast_to(
        jnp.pad(gains.astype(BF16), ((0, 0), (24, 88)))[:, None, :], (128, 8, 128)
    ).reshape(1024, 128)
    d_made, sent = kernel_call(
        unproject_body,
        [shaped((1024, 512), BF16), shaped((1024, 640), BF16)],
        [
            place, *in_hbm(dq, dk, dv), d_got, *in_hbm(q_raw, k_raw), squares, dots, dots_got, cosine, sine,
            gain_q, gain_k, *in_hbm(x_turned), gains,
        ],
        [pltpu.VMEM((8, 384), F32)],
        flops=2 * 1024 * 1024 * 512, nbytes=9 << 20,
    )

    def halves(value, upper):
        low, high = value[: value.shape[0] // 2], value[value.shape[0] // 2 :]
        return jnp.where(upper, high, low), jnp.where(upper, low, high)

    mine, given = halves(grad_mlp, xh == 1)
    mine = mine.astype(F32) + swap(given, X_SWAP).astype(F32)
    grad_out = after(grad_out, sent)
    grad_out = halve(grad_out, 32, fsdp // 2 % 2, "fsdp", [(i, i ^ 2) for i in range(8)])
    grad_out = halve(grad_out, 32, fsdp // 4, "fsdp", [(i, i ^ 4) for i in range(8)])
    got_made = lax.all_to_all(
        sent.reshape(128, 8, 640), ("seq", "fsdp"), split_axis=0, concat_axis=0, tiled=True
    )
    dx_mine, dx_part = kernel_call(
        input_body,
        [shaped((512, 1024), F32), shaped((512, 1024), BF16)],
        [after(d_made, sent), weight],
        flops=2 * 1024 * 1024 * 512, nbytes=5 << 20,
    )
    rows = [slice(k * 128, k * 128 + 128) for k in range(4)]
    pieces = [dx_mine[r] + swap(dx_part[r], CORE_SWAP).astype(F32) for r in rows]
    far = [piece.astype(BF16) for piece in pieces[1:]]
    d_inputs = pieces[0] + sum(
        swap(piece, to_z(k)).astype(F32) for k, piece in enumerate(far, 1)
    )
    grad_down = jnp.concatenate(
        [
            mine[:48, 1536:2304],
            jnp.concatenate([mine[48:, 1536 + m * 256 : 1792 + m * 256] for m in range(3)], axis=0),
        ],
        axis=1,
    )
    grad_down, given_down = halves(grad_down, z >= 2)
    mine, given = halves(mine[:, :1536], z >= 2)
    given = swap(
        jnp.concatenate([given.reshape(48, 1024), given_down], axis=0).astype(BF16), FAR_SWAP
    ).astype(F32)
    mine = (mine + given[:48].reshape(32, 1536)).astype(BF16)
    grad_down = (grad_down + given[48:]).astype(BF16)

    got_made, mine, grad_down, grad_out, d_inputs = lax.optimization_barrier(
        (got_made, mine, grad_down, grad_out, d_inputs)
    )
    grad_out = halve(grad_out, 16, xh, "seq", X_SWAP)
    grad_out = swap(grad_out.reshape(16, 1024), OUT_HOME)
    grad_down = lax.ppermute(grad_down, ("seq", "fsdp"), DOWN_HOME)
    mine, given = halves(mine, z % 2 == 1)
    got = swap(given, Z_SWAP)
    mine = jnp.stack([jnp.where(z % 2 == 1, got, mine), jnp.where(z % 2 == 1, mine, got)])
    mine = mine.reshape(2, 2, 8, 1536)
    given = jnp.where(c == 1, mine[:, 0], mine[:, 1])
    mine = jnp.where(c == 1, mine[:, 1], mine[:, 0])
    got = swap(given, CORE_SWAP)
    got_wide = jnp.stack([jnp.where(c == 1, got, mine), jnp.where(c == 1, mine, got)], axis=1)
    summed = jnp.sum(got_made.reshape(2, 8, 8, 8, 640).astype(F32), axis=(0, 2))
    gains = jnp.sum(summed[:, 0, 512:], axis=0)

    def take(first, width):
        return summed[:, :, first : first + width].swapaxes(0, 1).reshape(8, 8 * width)

    wide = got_wide.astype(F32).reshape(4, 8, 2, 8, 96)
    wide = wide.transpose(2, 1, 3, 0, 4).reshape(2, 8, 3072)
    return (
        output,
        (d_hidden + d_inputs).astype(BF16)[None],
        take(0, 256),
        take(256, 128),
        take(384, 128),
        grad_out.astype(F32),
        wide[0],
        wide[1],
        grad_down.astype(F32),
        gains[:16],
        gains[16:24],
        gains[24:32],
        gains[32:40],
    )


def solution(mesh):
    rows = P("fsdp", "seq", None)
    weight = P("fsdp", None)
    grad = P(("seq", "fsdp"), None)
    gain = P(("seq", "fsdp"))
    return jax.shard_map(
        on_device,
        mesh=mesh,
        in_specs=(rows,) * 2 + (weight,) * 7 + (P(),) * 4,
        out_specs=(rows,) * 2 + (grad,) * 7 + (gain,) * 4,
        check_vma=False,
    )
```

```python
import functools
import math

import jax
import jax.numpy as jnp
from jax import lax
from jax.experimental import pallas as pl
from jax.experimental.pallas import tpu as pltpu
from jax.sharding import PartitionSpec as P

BF16 = jnp.bfloat16
F32 = jnp.float32
DH = 128
EPS = 1e-06
THETA = 1000000.0
MASKED = -1e30
LOG2E = math.log2(math.e)
QUERY_SCALE = DH ** (-0.5) * LOG2E
VMEM_BYTES = 20 * 1024 * 1024
VMEM = pl.BlockSpec(memory_space=pltpu.VMEM)
SMEM = pl.BlockSpec(memory_space=pltpu.SMEM)
ANY = pl.BlockSpec(memory_space=pl.ANY)
SMALL = 64 * 1024
NT = (((1,), (1,)), ((), ()))

SEQ_PLACES = [(xh, z, c) for xh in range(2) for z in range(4) for c in range(2)]


def seq_index(xh, z, c):
    return xh * 8 + (z % 4) * 2 + c


CORE_SWAP = [(i, i ^ 1) for i in range(16)]
LOW_TO_HIGH = [(i, i + 8) for i in range(8)]
HIGH_TO_LOW = [(i + 8, i) for i in range(8)]
X_SWAP = [(i, i ^ 8) for i in range(16)]


def from_z(k):
    return [(seq_index(xh, z + k, c), seq_index(xh, z, c)) for xh, z, c in SEQ_PLACES]


def to_z(k):
    return [(seq_index(xh, z, c), seq_index(xh, z + k, c)) for xh, z, c in SEQ_PLACES]


def across(pairs):
    return [(seq * 8 + f, to_seq * 8 + to_f) for seq, f, to_seq, to_f in pairs]


TURN = across(
    (xh * 8 + a, f, xh * 8 + f, a) for xh in range(2) for a in range(8) for f in range(8)
)
Z_SWAP = [(i, i ^ 2) for i in range(16)]
FAR_SWAP = [(i, i ^ 4) for i in range(16)]
OUT_HOME = [(xh * 8 + a, 2 * a + xh) for xh in range(2) for a in range(8)]


def down_home(other):
    return across(
        (seq_index(xh, 2 * zh + zl, c), f, 2 * f + zl, 4 * c + 2 * xh + (zh ^ other))
        for xh in range(2) for zh in range(2) for zl in range(2) for c in range(2) for f in range(8)
    )


def swap(value, pairs):
    return lax.ppermute(value, "seq", pairs)


def after(value, *others):
    return lax.optimization_barrier((value, *others))[0]


def gather_group(block):
    far = {k: swap(block, from_z(k)) for k in (2, 1, 3)}
    mine = [block, far[1], far[2], far[3]]
    return mine + [swap(v, CORE_SWAP) for v in mine]


def scatter_group(mine, part):
    rows = [slice(k * 128, k * 128 + 128) for k in range(4)]
    out = None
    for k in (2, 1, 3, 0):
        piece = mine[rows[k]] + swap(part[rows[k]], CORE_SWAP).astype(F32)
        if k:
            piece = swap(piece.astype(BF16), to_z(k)).astype(F32)
        out = piece if out is None else out + piece
    return out


def gather_pair(block):
    mine = [block, swap(block, Z_SWAP)]
    return mine + [swap(v, CORE_SWAP) for v in mine]


def scatter_pair(mine, part, later=()):
    far = mine[128:] + swap(part[128:], CORE_SWAP).astype(F32)
    far, *later = lax.optimization_barrier((far.astype(BF16), *later))
    far = swap(far, Z_SWAP).astype(F32)
    return mine[:128] + swap(part[:128], CORE_SWAP).astype(F32) + far, later


def sum_group(rows):
    groups = rows.shape[0] // 8
    other = swap(rows, CORE_SWAP).reshape(groups, 2, 4, 128)
    pair = rows.reshape(groups, 2, 4, 128) + jnp.concatenate([other[:, 1:], other[:, :1]], axis=1)
    odd = lax.axis_index("seq") // 2 % 2 == 1
    got = swap(pair, Z_SWAP)
    up = jnp.concatenate([got[:, :, 3:], got[:, :, :3]], axis=2)
    down = jnp.concatenate([got[:, :, 1:], got[:, :, :1]], axis=2)
    pair = pair + jnp.where(odd, down, up)
    got = swap(pair, FAR_SWAP)
    pair = pair + jnp.concatenate([got[:, :, 2:], got[:, :, :2]], axis=2)
    return pair.reshape(rows.shape)


def column(row):
    return jnp.transpose(jnp.broadcast_to(row, (128, 128)))


def row_sums(values):
    return jnp.sum(jnp.transpose(values), axis=0, keepdims=True)


def shaped(shape, dtype):
    return jax.ShapeDtypeStruct(shape, dtype)


class Kept:
    def __init__(self, value):
        self.value = value


def in_hbm(*values):
    return [Kept(v) for v in values]


def kernel_call(body, outs, inputs, scratch=(), flops=0, nbytes=0):
    hbm_outs = [isinstance(o, Kept) for o in outs]
    hbm_ins = [isinstance(x, Kept) for x in inputs]
    outs = [o.value if isinstance(o, Kept) else o for o in outs]
    inputs = [x.value if isinstance(x, Kept) else x for x in inputs]
    groups = [x if isinstance(x, list) else [x] for x in inputs]
    flat = [a for group in groups for a in group]
    joined = [
        shaped((sum(a.shape[0] for a in group),) + group[0].shape[1:], group[0].dtype)
        for group in groups
    ]

    def large(s):
        return math.prod(s.shape) * s.dtype.itemsize >= SMALL

    def where(s):
        return ANY if large(s) else SMEM if s.dtype == jnp.int32 else VMEM

    out_shapes = [joined[o] if isinstance(o, int) else o for o in outs]
    in_buffers = [pltpu.VMEM(s.shape, s.dtype) for s in joined if large(s)]
    out_buffers = [
        pltpu.VMEM(o.shape, o.dtype) for o in outs if not isinstance(o, int) and large(o)
    ]

    def whole(*refs):
        refs = list(refs)

        def pull(count):
            taken = refs[:count]
            del refs[:count]
            return taken

        in_refs, out_refs = pull(len(flat)), pull(len(outs))
        in_space, out_space = pull(len(in_buffers)), pull(len(out_buffers))
        own, (in_sem, out_sem) = pull(len(scratch)), refs
        loads, ins, at = {}, [], 0
        for group, s in zip(groups, joined):
            if not large(s):
                ins.append(in_refs[at])
                at += 1
                continue
            space, row = in_space.pop(0), 0
            loads[id(space)] = []
            for a in group:
                copy = pltpu.make_async_copy(
                    in_refs[at], space.at[pl.ds(row, a.shape[0])], in_sem.at[at]
                )
                copy.start()
                loads[id(space)].append(copy)
                row, at = row + a.shape[0], at + 1
            ins.append(space)
        made, stores = [], {}
        for k, (o, s, ref) in enumerate(zip(outs, out_shapes, out_refs)):
            if not large(s):
                made.append(ref)
                continue
            space = ins[o] if isinstance(o, int) else out_space.pop(0)
            stores[id(space)] = pltpu.make_async_copy(space, ref, out_sem.at[k])
            if not isinstance(o, int):
                made.append(space)
        started = []

        def ready(*spaces):
            for space in spaces:
                for copy in loads.pop(id(space), ()):
                    copy.wait()

        def done(*spaces):
            for space in spaces:
                copy = stores.pop(id(space))
                copy.start()
                started.append(copy)

        body(ready, done, *ins, *made, *own)
        for key in list(stores):
            copy = stores.pop(key)
            copy.start()
            started.append(copy)
        for copy in started:
            copy.wait()

    shapes = [pltpu.HBM(s.shape, s.dtype) if hbm else s for s, hbm in zip(out_shapes, hbm_outs)]
    return pl.pallas_call(
        whole,
        out_shape=tuple(shapes),
        in_specs=[where(s) for group, s in zip(groups, joined) for _ in group],
        out_specs=tuple(where(s) for s in out_shapes),
        scratch_shapes=[
            *in_buffers, *out_buffers, *scratch,
            pltpu.SemaphoreType.DMA((len(flat),)), pltpu.SemaphoreType.DMA((len(outs),)),
        ],
        compiler_params=pltpu.CompilerParams(vmem_limit_bytes=VMEM_BYTES),
        cost_estimate=pl.CostEstimate(flops=flops, bytes_accessed=nbytes, transcendentals=0),
    )(
        *[
            pltpu.with_memory_space_constraint(a, pltpu.HBM) if hbm else a
            for group, hbm in zip(groups, hbm_ins)
            for a in group
        ],
    )


def root(total, width):
    return lax.rsqrt(total * (1.0 / width) + EPS)


def project_body(
    ready, done, x_all, weight, gain_q, gain_k, cos, sin,
    q_raw, k_raw, q_rot, kv_rot, squares,
):
    ready(x_all, weight, cos, sin)
    done(x_all)

    def step(t, carry):
        at = pl.multiple_of(t * 256, 256)
        made = jnp.dot(x_all[pl.ds(at, 256), :], weight[...], preferred_element_type=F32)
        for part in range(2):
            rows = pl.ds(at + part * 128, 128)
            block = t * 2 + part
            here = made[part * 128 : part * 128 + 128]
            q, k = here[:, :256], here[:, 256:384]
            kv_rot[rows, 128:] = here[:, 384:].astype(BF16)
            q_raw[rows, :] = q
            k_raw[rows, :] = k
            squares[pl.ds(block, 1), :] = row_sums(
                q[:, :128] * q[:, :128] + q[:, 128:] * q[:, 128:]
            )
            squares[pl.ds(block + 8, 1), :] = row_sums(k * k)
            cosine, sine = cos[rows, :], sin[rows, :]
            for head in range(2):
                lanes = slice(head * 128, head * 128 + 128)
                turn = q[:, lanes] * gain_q[:, lanes]
                q_rot[rows, lanes] = (turn * cosine + pltpu.roll(turn, 64, 1) * sine).astype(BF16)
            turn = k * gain_k[...]
            kv_rot[rows, :128] = (turn * cosine + pltpu.roll(turn, 64, 1) * sine).astype(BF16)
        return carry

    lax.fori_loop(0, 4, step, 0)


def spot(place, block):
    z = lax.rem(place[1] + block % 4, 4)
    c = place[2] if block < 4 else 1 - place[2]
    return z, c


def attend_body(
    ready, done, place, q_rot, kv_rot, kv_low, squares, squares_low,
    out_raw, out_low, out_turned, q_tiles, keys, vals, logs, vals_t,
):
    ready(q_rot, kv_rot, kv_low)
    for b in range(8):
        rows = slice(b * 128, b * 128 + 128)
        z, c = spot(place, b)
        r = column(root(squares[b : b + 1, :], 2048.0)) * QUERY_SCALE
        inner = pl.ds(pl.multiple_of(c * 128, 128), 128)
        for head in range(2):
            q = q_rot[rows, head * 128 : head * 128 + 128].astype(F32)
            q_tiles[z * 2 + head, inner, :] = (q * r).astype(BF16)
        at = pl.ds(pl.multiple_of(1024 + z * 256 + c * 128, 128), 128)
        r = column(root(squares[8 + b : 9 + b, :], 1024.0))
        keys[at, :] = (kv_rot[rows, :128].astype(F32) * r).astype(BF16)
        vals[at, :] = kv_rot[rows, 128:]
        r = column(root(squares_low[b : b + 1, :], 1024.0))
        keys[rows, :] = (kv_low[rows, :128].astype(F32) * r).astype(BF16)
        vals[rows, :] = kv_low[rows, 128:]
    done(q_tiles, keys, vals)
    vals_t[...] = jnp.transpose(vals[...].astype(F32)).astype(BF16)
    allowed = lax.broadcasted_iota(jnp.int32, (256, 256), 0) <= lax.broadcasted_iota(
        jnp.int32, (256, 256), 1
    )

    def queries(first, i):
        at_diagonal = 1024 + i * 256
        ranges = [(first, at_diagonal)] if at_diagonal > first else []
        for head in range(2):
            q = q_tiles[i * 2 + head]
            scores = [
                lax.dot_general(keys[lo:hi, :], q, NT, preferred_element_type=F32)
                for lo, hi in ranges + [(at_diagonal, at_diagonal + 256)]
            ]
            scores[-1] = jnp.where(allowed, scores[-1], MASKED)
            tops = [jnp.max(s, axis=0, keepdims=True) for s in scores]
            top = functools.reduce(jnp.maximum, tops)
            total, acc = 0.0, 0.0
            for s, (lo, hi) in zip(scores, ranges + [(at_diagonal, at_diagonal + 256)]):
                p = jnp.exp2(s - top)
                total = total + jnp.sum(p, axis=0, keepdims=True)
                acc = acc + jnp.dot(
                    vals_t[:, lo:hi], p.astype(BF16), preferred_element_type=F32
                )
            turned = acc / total
            out = jnp.transpose(turned)
            turned = turned.astype(BF16)
            logs[i * 2 + head : i * 2 + head + 1, :] = top + jnp.log2(total)
            for c in range(2):
                block = lax.rem(i - place[1] + 4, 4) + 4 * jnp.abs(c - place[2])
                at = pl.ds(pl.multiple_of(block * 128, 128), 128)
                lanes = slice(head * 128, head * 128 + 128)
                out_raw[at, lanes] = out[c * 128 : c * 128 + 128, :]
                out_low[at, lanes] = out[c * 128 : c * 128 + 128, :].astype(BF16)
                out_turned[lanes, at] = turned[:, c * 128 : c * 128 + 128]

    @pl.when(place[0] == 1)
    def _():
        for i in range(4):
            queries(0, i)

    @pl.when(place[0] == 0)
    def _():
        for i in range(4):
            queries(1024, i)

    done(out_raw, out_low, out_turned)


def output_body(ready, done, mixed, w_out, a_mine, a_part):
    ready(mixed, w_out)

    def project(t, carry):
        at = pl.ds(pl.multiple_of(t * 256, 256), 256)
        far = pl.ds(pl.multiple_of(512 + t * 256, 256), 256)
        a_part[at, :] = jnp.dot(mixed[far, :], w_out[...], preferred_element_type=F32).astype(BF16)
        a_mine[at, :] = jnp.dot(mixed[at, :], w_out[...], preferred_element_type=F32)
        return carry

    lax.fori_loop(0, 2, project, 0)


def output_back_body(
    ready, done, place, out_raw, w_out, da_all, mixed_turned, d_tiles, deltas, grad_out
):
    ready(out_raw, w_out, da_all)
    for b in range(8):
        rows = slice(b * 128, b * 128 + 128)
        z, c = spot(place, b)
        inner = pl.ds(pl.multiple_of(c * 128, 128), 128)
        d_out = lax.dot_general(
            da_all[rows, :], w_out[...], NT, preferred_element_type=F32
        ).astype(BF16)
        for head in range(2):
            lanes = slice(head * 128, head * 128 + 128)
            grad = d_out[:, lanes]
            d_tiles[z * 2 + head, inner, :] = grad
            deltas[z * 2 + head, pl.ds(c, 1), :] = row_sums(grad.astype(F32) * out_raw[rows, lanes])
    done(d_tiles)
    ready(mixed_turned)
    for m in range(4):
        lanes = slice(m * 256, m * 256 + 256)
        made = jnp.dot(mixed_turned[...], da_all[:, lanes], preferred_element_type=F32).astype(BF16)
        for j in range(2):
            for f in range(8):
                to, at = f * 32 + j * 16, j * 128 + f * 16
                grad_out[to : to + 16, lanes] = made[at : at + 16]


def back_tiles(places, first, i, total, q_tiles, d_tiles, logs, deltas, keys, vals, keys_t, dk, dv):
    q = [q_tiles[i * 2 + head] for head in range(2)]
    grad = [d_tiles[i * 2 + head] for head in range(2)]
    log = [logs[i * 2 + head : i * 2 + head + 1, :] for head in range(2)]
    delta = [
        jnp.concatenate([deltas[i * 2 + head, 0:1, :], deltas[i * 2 + head, 1:2, :]], axis=1)
        for head in range(2)
    ]
    for lo, diagonal in places:
        at = slice(lo, lo + 256)
        here = slice(lo - first, lo - first + 256)
        k, v = keys[at, :], vals[at, :]
        dk_tile, dv_tile = dk[here, :], dv[here, :]
        for head in range(2):
            s = lax.dot_general(k, q[head], NT, preferred_element_type=F32)
            p = jnp.exp2(s - log[head])
            if diagonal:
                row = lax.broadcasted_iota(jnp.int32, (256, 256), 0)
                p = jnp.where(row <= lax.broadcasted_iota(jnp.int32, (256, 256), 1), p, 0.0)
            dp = lax.dot_general(v, grad[head], NT, preferred_element_type=F32)
            ds = (p * (dp - delta[head])).astype(BF16)
            dv_tile += jnp.dot(p.astype(BF16), grad[head], preferred_element_type=F32)
            dk_tile += jnp.dot(ds, q[head], preferred_element_type=F32)
            total[head] = total[head] + jnp.dot(keys_t[:, here], ds, preferred_element_type=F32)
        dk[here, :] = dk_tile
        dv[here, :] = dv_tile
    return total


def low_back_body(
    ready, done, place, q_tiles, keys, vals, logs, d_tiles, deltas,
    dq, d_low, dots, keys_t, dk_acc, dv_acc,
):
    ready(q_tiles, keys, vals, d_tiles)

    @pl.when(place[0] == 1)
    def _():
        keys_t[...] = jnp.transpose(keys[:1024, :].astype(F32)).astype(BF16)
        dk_acc[...] = jnp.zeros_like(dk_acc)
        dv_acc[...] = jnp.zeros_like(dv_acc)
        for i in range(4):
            total = back_tiles(
                [(lo, False) for lo in range(0, 1024, 256)], 0, i, [0.0, 0.0],
                q_tiles, d_tiles, logs, deltas, keys, vals, keys_t, dk_acc, dv_acc,
            )
            for head in range(2):
                dq[i * 2 + head] = total[head]
        for b in range(8):
            rows = slice(b * 128, b * 128 + 128)
            key_grad = dk_acc[rows, :] * (1.0 / LOG2E)
            d_low[rows, :128] = key_grad.astype(BF16)
            d_low[rows, 128:] = dv_acc[rows, :].astype(BF16)
            dots[b : b + 1, :] = row_sums(key_grad * keys[rows, :].astype(F32))

    @pl.when(place[0] == 0)
    def _():
        dq[...] = jnp.zeros_like(dq)
        d_low[...] = jnp.zeros_like(d_low)
        dots[...] = jnp.zeros_like(dots)


def own_back_body(
    ready, done, place, q_tiles, keys, vals, logs, d_tiles, deltas, dq_low, dots_low,
    dq, dk, dv, dots, keys_t, dk_acc, dv_acc,
):
    ready(keys)
    keys_t[...] = jnp.transpose(keys[1024:, :].astype(F32)).astype(BF16)
    dk_acc[...] = jnp.zeros_like(dk_acc)
    dv_acc[...] = jnp.zeros_like(dv_acc)
    ready(q_tiles, vals, d_tiles, dq_low)
    for i in range(4):
        total = back_tiles(
            [(1024 + j * 256, j == i) for j in range(i + 1)], 1024, i,
            [dq_low[i * 2 + head] for head in range(2)],
            q_tiles, d_tiles, logs, deltas, keys, vals, keys_t, dk_acc, dv_acc,
        )
        dot = jnp.zeros((1, 256), F32)
        for head in range(2):
            out = jnp.transpose(total[head]) * DH ** (-0.5)
            dot += jnp.sum(
                total[head] * jnp.transpose(q_tiles[i * 2 + head].astype(F32)), axis=0, keepdims=True
            )
            for c in range(2):
                block = lax.rem(i - place[1] + 4, 4) + 4 * jnp.abs(c - place[2])
                at = pl.ds(pl.multiple_of(block * 128, 128), 128)
                dq[at, head * 128 : head * 128 + 128] = out[c * 128 : c * 128 + 128, :].astype(BF16)
        for c in range(2):
            block = lax.rem(i - place[1] + 4, 4) + 4 * jnp.abs(c - place[2])
            dots[pl.ds(block, 1), :] = dot[:, c * 128 : c * 128 + 128] * (1.0 / LOG2E)
    done(dq)
    for b in range(8):
        rows = slice(b * 128, b * 128 + 128)
        z, c = spot(place, b)
        at = pl.multiple_of(z * 256 + c * 128, 128)
        key_grad = dk_acc[pl.ds(at, 128), :] * (1.0 / LOG2E)
        dk[rows, :] = key_grad
        dv[rows, :] = dv_acc[pl.ds(at, 128), :]
        dots[8 + b : 9 + b, :] = row_sums(key_grad * keys[pl.ds(1024 + at, 128), :].astype(F32))
    dots[16:24, :] = dots_low[...]


def unproject_body(
    ready, done, place, dq, dk, dv, d_got, q_raw, k_raw, squares, dots, dots_got, cos, sin,
    gain_q, gain_k, x_turned, gains, d_made, sent, sums,
):
    sums[...] = jnp.zeros_like(sums)
    ready(dq, dk, dv, d_got, q_raw, k_raw, cos, sin)

    def step(b, carry):
        rows = pl.ds(pl.multiple_of(b * 128, 128), 128)
        cosine, sine = cos[rows, :], sin[rows, :]
        r = column(root(squares[pl.ds(b, 1), :], 2048.0))
        mean = column(dots[pl.ds(b, 1), :]) * (1.0 / 2048.0)
        for head in range(2):
            lanes = slice(head * 128, head * 128 + 128)
            turn = dq[rows, lanes].astype(F32)
            d_norm = turn * cosine - pltpu.roll(turn, 64, 1) * sine
            hat = q_raw[rows, lanes] * r
            sums[0:1, lanes] += jnp.sum(d_norm * hat, axis=0, keepdims=True)
            d_made[rows, lanes] = (r * (d_norm * gain_q[:, lanes] - hat * mean)).astype(BF16)
        r = column(root(squares[pl.ds(b + 8, 1), :], 1024.0))
        mean = column(dots[pl.ds(b + 8, 1), :] + dots_got[pl.ds(b, 1), :]) * (1.0 / 1024.0)
        turn = dk[rows, :] + d_got[rows, :128].astype(F32)
        d_norm = turn * cosine - pltpu.roll(turn, 64, 1) * sine
        hat = k_raw[rows, :] * r
        sums[0:1, 256:] += jnp.sum(d_norm * hat, axis=0, keepdims=True)
        d_made[rows, 256:384] = (r * (d_norm * gain_k[...] - hat * mean)).astype(BF16)
        d_made[rows, 384:] = (dv[rows, :] + d_got[rows, 128:].astype(F32)).astype(BF16)
        return carry

    lax.fori_loop(0, 8, step, 0)
    done(d_made)
    ready(x_turned, gains)

    def grad(t, carry):
        rows = pl.ds(pl.multiple_of(t * 256, 256), 256)
        sent[rows, :512] = jnp.dot(
            x_turned[rows, :], d_made[...], preferred_element_type=F32
        ).astype(BF16)
        sent[rows, 512:] = gains[rows, :]
        return carry

    lax.fori_loop(0, 4, grad, 0)
    extra = 0.0
    for lo, width, each, first in ((0, 256, 16, 0), (256, 128, 8, 16)):
        row = lax.broadcasted_iota(jnp.int32, (128, width), 0) // 8
        lane = lax.broadcasted_iota(jnp.int32, (128, width), 1) // each
        spread = jnp.where(row == lane, sums[0:1, lo : lo + width], 0.0).astype(BF16)
        lane = lax.broadcasted_iota(jnp.int32, (width, 128), 0) % each + first
        pick = jnp.where(lane == lax.broadcasted_iota(jnp.int32, (width, 128), 1), 1.0, 0.0)
        extra = extra + jnp.dot(spread, pick.astype(BF16), preferred_element_type=F32)
    rows = pl.ds(pl.multiple_of((place[1] * 2 + place[2]) * 128, 128), 128)
    sent[rows, 512:] = (gains[rows, :].astype(F32) + extra).astype(BF16)


def input_body(ready, done, d_made, weight, dx_mine, dx_part):
    ready(d_made, weight)

    def step(t, carry):
        at = pl.ds(pl.multiple_of(t * 256, 256), 256)
        far = pl.ds(pl.multiple_of(512 + t * 256, 256), 256)
        dx_part[at, :] = lax.dot_general(
            d_made[far, :], weight[...], NT, preferred_element_type=F32
        ).astype(BF16)
        dx_mine[at, :] = lax.dot_general(
            d_made[at, :], weight[...], NT, preferred_element_type=F32
        )
        return carry

    lax.fori_loop(0, 2, step, 0)


def expand_body(ready, done, h_all, weight, packed, gate, up, expanded, m_mine, m_part, down):
    ready(packed)
    for f in range(8):
        down[f * 96 : f * 96 + 96, :768] = packed[f * 128 : f * 128 + 96, :]
        for m in range(3):
            down[f * 96 + m * 32 : f * 96 + m * 32 + 32, 768:] = packed[
                f * 128 + 96 : f * 128 + 128, m * 256 : m * 256 + 256
            ]

    done(down)
    ready(h_all, weight)
    done(h_all)

    def widen(n, carry):
        lanes = pl.ds(pl.multiple_of(n * 256, 256), 256)
        upper = pl.ds(pl.multiple_of(768 + n * 256, 256), 256)
        g = jnp.dot(h_all[...], weight[:, lanes], preferred_element_type=F32)
        u = jnp.dot(h_all[...], weight[:, upper], preferred_element_type=F32)
        gate[:, lanes] = g
        up[:, lanes] = u
        expanded[:, lanes] = (g * jax.nn.sigmoid(g) * u).astype(BF16)
        return carry

    lax.fori_loop(0, 3, widen, 0)
    done(gate, up, expanded)

    def narrow(n, carry):
        lanes = pl.ds(pl.multiple_of(n * 256, 256), 256)
        m = jnp.dot(expanded[...], down[:, lanes], preferred_element_type=F32)
        m_mine[:, lanes] = m[:256]
        m_part[:, lanes] = m[256:].astype(BF16)
        return carry

    lax.fori_loop(0, 4, narrow, 0)


def expand_back_body(ready, done, dm_all, gate, up, weight, down, d_gu, dh_mine, dh_part):
    ready(dm_all, gate, up, down)
    done(dm_all)

    def widen(n, carry):
        lanes = pl.ds(pl.multiple_of(n * 256, 256), 256)
        upper = pl.ds(pl.multiple_of(768 + n * 256, 256), 256)
        de = lax.dot_general(dm_all[...], down[lanes, :], NT, preferred_element_type=F32)
        g = gate[:, lanes]
        sig = jax.nn.sigmoid(g)
        d_gu[:, lanes] = (de * up[:, lanes] * sig * (1.0 + g * (1.0 - sig))).astype(BF16)
        d_gu[:, upper] = (de * (g * sig)).astype(BF16)
        return carry

    lax.fori_loop(0, 3, widen, 0)
    done(d_gu)
    ready(weight)

    def narrow(n, carry):
        lanes = pl.ds(pl.multiple_of(n * 256, 256), 256)
        dh = lax.dot_general(d_gu[...], weight[lanes, :], NT, preferred_element_type=F32)
        dh_mine[:, lanes] = dh[:256]
        dh_part[:, lanes] = dh[256:].astype(BF16)
        return carry

    lax.fori_loop(0, 4, narrow, 0)


def expand_grad_body(ready, done, h_turned, d_gu, expanded, dm_all, out, expanded_t):
    ready(expanded)
    expanded_t[...] = jnp.transpose(expanded[...].astype(F32)).astype(BF16)

    ready(h_turned, d_gu, dm_all)

    def widen(n, carry):
        lanes = pl.ds(pl.multiple_of(n * 256, 256), 256)
        out[:, lanes] = jnp.dot(
            h_turned[...], d_gu[:, lanes], preferred_element_type=F32
        ).astype(BF16)
        return carry

    lax.fori_loop(0, 6, widen, 0)
    for n in range(4):
        made = jnp.dot(
            expanded_t[...], dm_all[:, n * 256 : n * 256 + 256], preferred_element_type=F32
        ).astype(BF16)
        for f in range(16):
            if n < 3:
                out[f * 64 : f * 64 + 48, 1536 + n * 256 : 1792 + n * 256] = made[
                    f * 48 : f * 48 + 48
                ]
                continue
            for m in range(3):
                out[f * 64 + 48 : f * 64 + 64, 1536 + m * 256 : 1792 + m * 256] = made[
                    f * 48 + m * 16 : f * 48 + m * 16 + 16
                ]


def norm_scale(values):
    return lax.rsqrt(jnp.mean(values * values, axis=-1, keepdims=True) + EPS)


def norm_back(upstream, normed, scaling):
    return scaling * (upstream - normed * jnp.mean(upstream * normed, axis=-1, keepdims=True))


def rotary_tables(first, z, c):
    half = DH // 2
    k = jnp.arange(4, dtype=jnp.int32)
    starts = jnp.concatenate([((z + k) % 4) * 256 + c * 128, ((z + k) % 4) * 256 + (1 - c) * 128])
    places = (first + starts[:, None] + jnp.arange(128, dtype=jnp.int32)[None, :]).reshape(1024)
    inverse = THETA ** (-(jnp.arange(half, dtype=F32) * (2.0 / DH)))
    angles = places.astype(F32)[:, None] * inverse[None, :]
    cosine, sine = jnp.cos(angles), jnp.sin(angles)
    return (
        jnp.concatenate([cosine, cosine], axis=-1),
        jnp.concatenate([-sine, sine], axis=-1),
    )


def dot(a, b):
    return jnp.dot(a, b, preferred_element_type=F32)


def dot_nt(a, b):
    return lax.dot_general(a, b, NT, preferred_element_type=F32)


def dot_tn(a, b):
    return lax.dot_general(a, b, (((0,), (0,)), ((), ())), preferred_element_type=F32)


def on_device(
    tokens, out_grad, w_query, w_key, w_value, w_out, w_gate, w_up, w_down,
    gain_query, gain_key, gain_attn, gain_mlp,
):
    seq = lax.axis_index("seq")
    xh, zc = seq // 8, seq % 8
    z, c = zc // 2, zc % 2
    quarter = (z % 2) * 2 + c
    place = jnp.stack([xh, z, c]).astype(jnp.int32)
    inputs = tokens[0]

    def columns(weight, width):
        return lax.dynamic_slice_in_dim(weight, zc * width, width, 1)

    def spread(block):
        return lax.all_to_all(
            jnp.broadcast_to(block[None], (8,) + block.shape),
            "fsdp", split_axis=0, concat_axis=0, tiled=True,
        ).reshape(8 * block.shape[0], block.shape[1])

    x_blocks = gather_group(inputs)
    weight = spread(
        jnp.concatenate(
            [columns(w_query, 256), columns(w_key, 128), columns(w_value, 128)], axis=1
        )
    )
    w_out_rows = lax.ppermute(
        after(lax.dynamic_slice_in_dim(w_out, zc * 32, 32, 0), *x_blocks[1:4]),
        ("seq", "fsdp"),
        TURN,
    )

    def quarters(weight):
        part = lax.dynamic_slice_in_dim(weight.reshape(128, 8, 384), quarter * 96, 96, 2)
        return part.reshape(128, 768)

    down = lax.dynamic_slice_in_dim(w_down, quarter * 96, 96, 0)
    packed = jnp.concatenate(
        [
            down[:, :768],
            jnp.concatenate([down[m * 32 : m * 32 + 32, 768:] for m in range(3)], axis=1),
        ],
        axis=0,
    )
    w_narrow = lax.all_gather(packed, "fsdp", axis=0, tiled=True)
    w_wide = jnp.concatenate([quarters(w_gate), quarters(w_up)], axis=1)
    weight, w_wide, w_out_rows = lax.optimization_barrier((weight, w_wide, w_out_rows))

    cosine, sine = rotary_tables(xh * 1024, z, c)
    gain_q = lax.dynamic_slice_in_dim(gain_query, zc * 256, 256, 0)[None]
    gain_k = lax.dynamic_slice_in_dim(gain_key, zc * 128, 128, 0)[None]
    x_all, q_raw, k_raw, q_rot, kv_rot, squares = kernel_call(
        project_body,
        [
            *in_hbm(
                0, shaped((1024, 256), F32), shaped((1024, 128), F32),
                shaped((1024, 256), BF16), shaped((1024, 256), BF16),
            ),
            shaped((16, 128), F32),
        ],
        [x_blocks, weight, gain_q, gain_k, cosine, sine],
        flops=2 * 1024 * 1024 * 512, nbytes=9 << 20,
    )

    kv_low = swap(kv_rot, LOW_TO_HIGH)
    squares = sum_group(squares)
    squares_low = swap(squares[8:], LOW_TO_HIGH)
    kv_low, squares, squares_low, w_wide, w_narrow, w_out_rows = lax.optimization_barrier(
        (kv_low, squares, squares_low, w_wide, w_narrow, w_out_rows)
    )
    w_wide = lax.all_gather(w_wide, "fsdp", axis=0, tiled=True)
    w_out_rows = spread(w_out_rows)
    out_raw, mixed, mixed_turned, q_tiles, keys, vals, logs = kernel_call(
        attend_body,
        [
            *in_hbm(
                shaped((1024, 256), F32), shaped((1024, 256), BF16), shaped((256, 1024), BF16),
                shaped((8, 256, 128), BF16), shaped((2048, 128), BF16), shaped((2048, 128), BF16),
            ),
            shaped((8, 256), F32),
        ],
        [place, *in_hbm(q_rot, kv_rot), kv_low, squares, squares_low],
        [pltpu.VMEM((128, 2048), BF16)],
        flops=4 * 1024 * 2048 * 256, nbytes=9 << 20,
    )
    a_mine, a_part = kernel_call(
        output_body,
        [shaped((512, 1024), F32), shaped((512, 1024), BF16)],
        [*in_hbm(mixed), w_out_rows],
        flops=2 * 1024 * 1024 * 256, nbytes=5 << 20,
    )
    x_turned = x_all.T

    attended = scatter_group(a_mine, a_part)
    attended, x_turned = lax.optimization_barrier((attended, x_turned))
    attn_scale = norm_scale(attended)
    attn_hat = attended * attn_scale
    hidden_state = inputs.astype(F32) + attn_hat * gain_attn
    h_all, gate, up, expanded, m_mine, m_part, w_down_rows = kernel_call(
        expand_body,
        [
            0, shaped((512, 768), F32), shaped((512, 768), F32), shaped((512, 768), BF16),
            shaped((256, 1024), F32), shaped((256, 1024), BF16), shaped((768, 1024), BF16),
        ],
        [
            gather_pair(hidden_state.astype(BF16)), *in_hbm(w_wide, w_narrow),
        ],
        flops=2 * 512 * 2304 * 1024, nbytes=12 << 20,
    )
    projected, _ = scatter_pair(m_mine, m_part)
    mlp_scale = norm_scale(projected)
    mlp_hat = projected * mlp_scale
    output = (hidden_state + mlp_hat * gain_mlp).astype(BF16)[None]

    upstream = out_grad[0].astype(F32)
    grad_gain_mlp = jnp.sum(upstream * mlp_hat, axis=0)
    d_projected = norm_back(upstream * gain_mlp, mlp_hat, mlp_scale).astype(BF16)
    n = jnp.arange(1024, dtype=jnp.int32)
    source = ((n // 8) % 16) * 64 + (n // 128) * 8 + n % 8
    order = (n[None, :] == source[:, None]).astype(BF16)
    h_turned = dot_nt(order, h_all).astype(BF16)
    d_blocks = gather_pair(d_projected)
    d_blocks[3], h_turned = lax.optimization_barrier((d_blocks[3], h_turned))
    dm_all, d_gu, dh_mine, dh_part = kernel_call(
        expand_back_body,
        [
            0, shaped((512, 1536), BF16), shaped((256, 1024), F32), shaped((256, 1024), BF16),
        ],
        [d_blocks, gate, up, w_wide, w_down_rows],
        flops=2 * 512 * 2304 * 1024, nbytes=12 << 20,
    )

    far = dh_mine[128:] + swap(dh_part[128:], CORE_SWAP).astype(F32)
    far, d_gu, dm_all = lax.optimization_barrier((far.astype(BF16), d_gu, dm_all))
    far = swap(far, Z_SWAP)
    (grad_mlp,) = kernel_call(
        expand_grad_body,
        in_hbm(shaped((1024, 2304), BF16)),
        [h_turned, d_gu, expanded, dm_all],
        [pltpu.VMEM((768, 512), BF16)],
        flops=2 * 512 * 2304 * 1024, nbytes=9 << 20,
    )
    far, grad_mlp = lax.optimization_barrier((far, grad_mlp))
    grad_mlp = lax.psum_scatter(grad_mlp, "fsdp", scatter_dimension=0, tiled=True)
    d_hidden = upstream + dh_mine[:128] + swap(dh_part[:128], CORE_SWAP).astype(F32)
    d_hidden = d_hidden + far.astype(F32)

    grad_gain_attn = jnp.sum(d_hidden * attn_hat, axis=0)
    d_attended = norm_back(d_hidden * gain_attn, attn_hat, attn_scale).astype(BF16)
    d_tiles, deltas, grad_out = kernel_call(
        output_back_body,
        [shaped((8, 256, 128), BF16), shaped((8, 2, 128), F32), shaped((256, 1024), BF16)],
        [place, *in_hbm(out_raw, w_out_rows, gather_group(d_attended), mixed_turned)],
        flops=4 * 1024 * 1024 * 256, nbytes=6 << 20,
    )
    fsdp = lax.axis_index("fsdp")

    def halve(value, rows, bit, axis, pairs):
        parts = value.reshape(-1, 2, rows, 1024)
        given = jnp.where(bit == 1, parts[:, 0], parts[:, 1])
        mine = jnp.where(bit == 1, parts[:, 1], parts[:, 0]).astype(F32)
        return (mine + lax.ppermute(given, axis, pairs).astype(F32)).astype(BF16)

    grad_out = halve(grad_out, 32, fsdp % 2, "fsdp", [(i, i ^ 1) for i in range(8)])
    scratch = [
        pltpu.VMEM((128, 1024), BF16), pltpu.VMEM((1024, 128), F32), pltpu.VMEM((1024, 128), F32),
    ]
    shared = [place, *in_hbm(q_tiles, keys, vals), logs, d_tiles, deltas]
    dq_low, d_low, dots_low = kernel_call(
        low_back_body,
        [
            shaped((8, 128, 256), F32), *in_hbm(shaped((1024, 256), BF16)), shaped((8, 128), F32),
        ],
        shared,
        scratch,
        flops=10 * 1024 * 1024 * 256, nbytes=4 << 20,
    )
    dq_low, grad_out = lax.optimization_barrier((dq_low, grad_out))
    grad_out = halve(grad_out, 32, fsdp // 2 % 2, "fsdp", [(i, i ^ 2) for i in range(8)])
    dq, dk, dv, dots = kernel_call(
        own_back_body,
        [
            *in_hbm(
                shaped((1024, 256), BF16), shaped((1024, 128), F32), shaped((1024, 128), F32),
            ),
            shaped((24, 128), F32),
        ],
        [*shared, dq_low, dots_low],
        scratch,
        flops=10 * 1024 * 640 * 256, nbytes=5 << 20,
    )
    dots, grad_out = lax.optimization_barrier((dots, grad_out))
    grad_out = halve(grad_out, 32, fsdp // 4, "fsdp", [(i, i ^ 4) for i in range(8)])
    d_got = swap(d_low, HIGH_TO_LOW)
    dots = sum_group(dots)
    dots_got = swap(dots[16:], HIGH_TO_LOW)

    gains = jnp.concatenate([grad_gain_attn.reshape(128, 8), grad_gain_mlp.reshape(128, 8)], axis=1)
    gains = jnp.broadcast_to(
        jnp.pad(gains.astype(BF16), ((0, 0), (24, 88)))[:, None, :], (128, 8, 128)
    ).reshape(1024, 128)
    d_made, sent = kernel_call(
        unproject_body,
        [shaped((1024, 512), BF16), shaped((1024, 640), BF16)],
        [
            place, *in_hbm(dq, dk, dv), d_got, *in_hbm(q_raw, k_raw), squares, dots, dots_got, cosine, sine,
            gain_q, gain_k, *in_hbm(x_turned), gains,
        ],
        [pltpu.VMEM((8, 384), F32)],
        flops=2 * 1024 * 1024 * 512, nbytes=9 << 20,
    )

    def halves(value, upper):
        low, high = value[: value.shape[0] // 2], value[value.shape[0] // 2 :]
        return jnp.where(upper, high, low), jnp.where(upper, low, high)

    mine, given = halves(grad_mlp, xh == 1)
    mine = mine.astype(F32) + swap(given, X_SWAP).astype(F32)
    sent, grad_out = lax.optimization_barrier((sent, grad_out))
    grad_out = halve(grad_out, 16, xh, "seq", X_SWAP)
    got_made = lax.all_to_all(
        sent.reshape(128, 8, 640), ("seq", "fsdp"), split_axis=0, concat_axis=0, tiled=True
    )
    dx_mine, dx_part = kernel_call(
        input_body,
        in_hbm(shaped((512, 1024), F32), shaped((512, 1024), BF16)),
        [after(d_made, sent), weight],
        flops=2 * 1024 * 1024 * 512, nbytes=5 << 20,
    )
    rows = [slice(k * 128, k * 128 + 128) for k in range(4)]
    pieces = [dx_mine[r] + swap(dx_part[r], CORE_SWAP).astype(F32) for r in rows]
    far = [piece.astype(BF16) for piece in pieces[1:]]
    d_inputs = pieces[0] + sum(
        swap(piece, to_z(k)).astype(F32) for k, piece in enumerate(far, 1)
    )
    got_made, mine, grad_out, d_inputs = lax.optimization_barrier(
        (got_made, mine, grad_out, d_inputs)
    )
    grad_out = swap(grad_out.reshape(16, 1024), OUT_HOME)
    mine = mine.astype(BF16)
    grad_down = jnp.concatenate(
        [
            mine[:48, 1536:],
            jnp.concatenate([mine[48:, 1536 + m * 256 : 1792 + m * 256] for m in range(3)], axis=0),
        ],
        axis=1,
    )
    grad_down = sum(
        lax.ppermute(
            jnp.where((z >= 2) != other, grad_down[24:], grad_down[:24]),
            ("seq", "fsdp"),
            down_home(other),
        ).astype(F32)
        for other in (False, True)
    )
    mine = mine[:, :1536].reshape(4, 16, 1536)
    terms = []
    for k in range(4):
        piece = lax.dynamic_index_in_dim(mine, (z + k) % 4, 0, keepdims=False)
        terms.append(swap(piece, to_z(k)) if k else piece)
    near = (terms[0].astype(F32) + terms[2].astype(F32)).astype(BF16).reshape(2, 8, 1536)
    off = (terms[1].astype(F32) + terms[3].astype(F32)).astype(BF16).reshape(2, 8, 1536)
    mine = jnp.stack([jnp.where(z % 2 == 1, off, near), jnp.where(z % 2 == 1, near, off)])
    given = jnp.where(c == 1, mine[:, 0], mine[:, 1])
    mine = jnp.where(c == 1, mine[:, 1], mine[:, 0])
    got = swap(given, CORE_SWAP)
    got_wide = jnp.stack([jnp.where(c == 1, got, mine), jnp.where(c == 1, mine, got)], axis=1)
    summed = jnp.sum(got_made.reshape(2, 8, 8, 8, 640).astype(F32), axis=(0, 2))
    gains = jnp.sum(summed[:, 0, 512:], axis=0)

    def take(first, width):
        return summed[:, :, first : first + width].swapaxes(0, 1).reshape(8, 8 * width)

    wide = got_wide.astype(F32).reshape(4, 8, 2, 8, 96)
    wide = wide.transpose(2, 1, 3, 0, 4).reshape(2, 8, 3072)
    return (
        output,
        (d_hidden + d_inputs).astype(BF16)[None],
        take(0, 256),
        take(256, 128),
        take(384, 128),
        grad_out.astype(F32),
        wide[0],
        wide[1],
        grad_down.astype(F32),
        gains[:16],
        gains[16:24],
        gains[24:32],
        gains[32:40],
    )


def solution(mesh):
    rows = P("fsdp", "seq", None)
    weight = P("fsdp", None)
    grad = P(("seq", "fsdp"), None)
    gain = P(("seq", "fsdp"))
    return jax.shard_map(
        on_device,
        mesh=mesh,
        in_specs=(rows,) * 2 + (weight,) * 7 + (P(),) * 4,
        out_specs=(rows,) * 2 + (grad,) * 7 + (gain,) * 4,
        check_vma=False,
    )
```

```python
import functools
import math

import jax
import jax.numpy as jnp
from jax import lax
from jax.experimental import pallas as pl
from jax.experimental.pallas import tpu as pltpu
from jax.sharding import PartitionSpec as P

BF16 = jnp.bfloat16
F32 = jnp.float32
DH = 128
EPS = 1e-06
THETA = 1000000.0
MASKED = -1e30
LOG2E = math.log2(math.e)
QUERY_SCALE = DH ** (-0.5) * LOG2E
VMEM_BYTES = 20 * 1024 * 1024
VMEM = pl.BlockSpec(memory_space=pltpu.VMEM)
SMEM = pl.BlockSpec(memory_space=pltpu.SMEM)
ANY = pl.BlockSpec(memory_space=pl.ANY)
SMALL = 64 * 1024
NT = (((1,), (1,)), ((), ()))

SEQ_PLACES = [(xh, z, c) for xh in range(2) for z in range(4) for c in range(2)]


def seq_index(xh, z, c):
    return xh * 8 + (z % 4) * 2 + c


CORE_SWAP = [(i, i ^ 1) for i in range(16)]
LOW_TO_HIGH = [(i, i + 8) for i in range(8)]
HIGH_TO_LOW = [(i + 8, i) for i in range(8)]
X_SWAP = [(i, i ^ 8) for i in range(16)]


def from_z(k):
    return [(seq_index(xh, z + k, c), seq_index(xh, z, c)) for xh, z, c in SEQ_PLACES]


def to_z(k):
    return [(seq_index(xh, z, c), seq_index(xh, z + k, c)) for xh, z, c in SEQ_PLACES]


def across(pairs):
    return [(seq * 8 + f, to_seq * 8 + to_f) for seq, f, to_seq, to_f in pairs]


TURN = across(
    (xh * 8 + a, f, xh * 8 + f, a) for xh in range(2) for a in range(8) for f in range(8)
)
Z_SWAP = [(i, i ^ 2) for i in range(16)]
FAR_SWAP = [(i, i ^ 4) for i in range(16)]


def out_home(other):
    return [(xh * 8 + a, 2 * a + (xh ^ other)) for xh in range(2) for a in range(8)]


def down_home(other):
    return across(
        (seq_index(own // 2, 2 * (own % 2) + zl, c), f, 2 * f + zl, 4 * c + (own ^ other))
        for own in range(4) for zl in range(2) for c in range(2) for f in range(8)
    )


def swap(value, pairs):
    return lax.ppermute(value, "seq", pairs)


def after(value, *others):
    return lax.optimization_barrier((value, *others))[0]


def gather_group(block):
    far = {k: swap(block, from_z(k)) for k in (2, 1, 3)}
    mine = [block, far[1], far[2], far[3]]
    return mine + [swap(v, CORE_SWAP) for v in mine]


def scatter_group(mine, part):
    rows = [slice(k * 128, k * 128 + 128) for k in range(4)]
    out = None
    for k in (2, 1, 3, 0):
        piece = mine[rows[k]] + swap(part[rows[k]], CORE_SWAP).astype(F32)
        if k:
            piece = swap(piece.astype(BF16), to_z(k)).astype(F32)
        out = piece if out is None else out + piece
    return out


def gather_pair(block):
    mine = [block, swap(block, Z_SWAP)]
    return mine + [swap(v, CORE_SWAP) for v in mine]


def scatter_pair(mine, part, later=()):
    far = mine[128:] + swap(part[128:], CORE_SWAP).astype(F32)
    far, *later = lax.optimization_barrier((far.astype(BF16), *later))
    far = swap(far, Z_SWAP).astype(F32)
    return mine[:128] + swap(part[:128], CORE_SWAP).astype(F32) + far, later


def sum_group(rows):
    groups = rows.shape[0] // 8
    other = swap(rows, CORE_SWAP).reshape(groups, 2, 4, 128)
    pair = rows.reshape(groups, 2, 4, 128) + jnp.concatenate([other[:, 1:], other[:, :1]], axis=1)
    odd = lax.axis_index("seq") // 2 % 2 == 1
    got = swap(pair, Z_SWAP)
    up = jnp.concatenate([got[:, :, 3:], got[:, :, :3]], axis=2)
    down = jnp.concatenate([got[:, :, 1:], got[:, :, :1]], axis=2)
    pair = pair + jnp.where(odd, down, up)
    got = swap(pair, FAR_SWAP)
    pair = pair + jnp.concatenate([got[:, :, 2:], got[:, :, :2]], axis=2)
    return pair.reshape(rows.shape)


def column(row):
    return jnp.transpose(jnp.broadcast_to(row, (128, 128)))


def row_sums(values):
    return jnp.sum(jnp.transpose(values), axis=0, keepdims=True)


def shaped(shape, dtype):
    return jax.ShapeDtypeStruct(shape, dtype)


class Kept:
    def __init__(self, value):
        self.value = value


def in_hbm(*values):
    return [Kept(v) for v in values]


def kernel_call(body, outs, inputs, scratch=(), flops=0, nbytes=0):
    hbm_outs = [isinstance(o, Kept) for o in outs]
    hbm_ins = [isinstance(x, Kept) for x in inputs]
    outs = [o.value if isinstance(o, Kept) else o for o in outs]
    inputs = [x.value if isinstance(x, Kept) else x for x in inputs]
    groups = [x if isinstance(x, list) else [x] for x in inputs]
    flat = [a for group in groups for a in group]
    joined = [
        shaped((sum(a.shape[0] for a in group),) + group[0].shape[1:], group[0].dtype)
        for group in groups
    ]

    def large(s):
        return math.prod(s.shape) * s.dtype.itemsize >= SMALL

    def where(s):
        return ANY if large(s) else SMEM if s.dtype == jnp.int32 else VMEM

    out_shapes = [joined[o] if isinstance(o, int) else o for o in outs]
    in_buffers = [pltpu.VMEM(s.shape, s.dtype) for s in joined if large(s)]
    out_buffers = [
        pltpu.VMEM(o.shape, o.dtype) for o in outs if not isinstance(o, int) and large(o)
    ]

    def whole(*refs):
        refs = list(refs)

        def pull(count):
            taken = refs[:count]
            del refs[:count]
            return taken

        in_refs, out_refs = pull(len(flat)), pull(len(outs))
        in_space, out_space = pull(len(in_buffers)), pull(len(out_buffers))
        own, (in_sem, out_sem) = pull(len(scratch)), refs
        loads, ins, at = {}, [], 0
        for group, s in zip(groups, joined):
            if not large(s):
                ins.append(in_refs[at])
                at += 1
                continue
            space, row = in_space.pop(0), 0
            loads[id(space)] = []
            for a in group:
                copy = pltpu.make_async_copy(
                    in_refs[at], space.at[pl.ds(row, a.shape[0])], in_sem.at[at]
                )
                copy.start()
                loads[id(space)].append(copy)
                row, at = row + a.shape[0], at + 1
            ins.append(space)
        made, stores = [], {}
        for k, (o, s, ref) in enumerate(zip(outs, out_shapes, out_refs)):
            if not large(s):
                made.append(ref)
                continue
            space = ins[o] if isinstance(o, int) else out_space.pop(0)
            stores[id(space)] = pltpu.make_async_copy(space, ref, out_sem.at[k])
            if not isinstance(o, int):
                made.append(space)
        started = []

        def ready(*spaces):
            for space in spaces:
                for copy in loads.pop(id(space), ()):
                    copy.wait()

        def done(*spaces):
            for space in spaces:
                copy = stores.pop(id(space))
                copy.start()
                started.append(copy)

        body(ready, done, *ins, *made, *own)
        for key in list(stores):
            copy = stores.pop(key)
            copy.start()
            started.append(copy)
        for copy in started:
            copy.wait()

    shapes = [pltpu.HBM(s.shape, s.dtype) if hbm else s for s, hbm in zip(out_shapes, hbm_outs)]
    return pl.pallas_call(
        whole,
        out_shape=tuple(shapes),
        in_specs=[where(s) for group, s in zip(groups, joined) for _ in group],
        out_specs=tuple(where(s) for s in out_shapes),
        scratch_shapes=[
            *in_buffers, *out_buffers, *scratch,
            pltpu.SemaphoreType.DMA((len(flat),)), pltpu.SemaphoreType.DMA((len(outs),)),
        ],
        compiler_params=pltpu.CompilerParams(vmem_limit_bytes=VMEM_BYTES),
        cost_estimate=pl.CostEstimate(flops=flops, bytes_accessed=nbytes, transcendentals=0),
    )(
        *[
            pltpu.with_memory_space_constraint(a, pltpu.HBM) if hbm else a
            for group, hbm in zip(groups, hbm_ins)
            for a in group
        ],
    )


def root(total, width):
    return lax.rsqrt(total * (1.0 / width) + EPS)


def project_body(
    ready, done, x_all, weight, gain_q, gain_k, cos, sin,
    q_raw, k_raw, q_rot, kv_rot, squares,
):
    ready(x_all, weight, cos, sin)
    done(x_all)

    def step(t, carry):
        at = pl.multiple_of(t * 256, 256)
        made = jnp.dot(x_all[pl.ds(at, 256), :], weight[...], preferred_element_type=F32)
        for part in range(2):
            rows = pl.ds(at + part * 128, 128)
            block = t * 2 + part
            here = made[part * 128 : part * 128 + 128]
            q, k = here[:, :256], here[:, 256:384]
            kv_rot[rows, 128:] = here[:, 384:].astype(BF16)
            q_raw[rows, :] = q
            k_raw[rows, :] = k
            squares[pl.ds(block, 1), :] = row_sums(
                q[:, :128] * q[:, :128] + q[:, 128:] * q[:, 128:]
            )
            squares[pl.ds(block + 8, 1), :] = row_sums(k * k)
            cosine, sine = cos[rows, :], sin[rows, :]
            for head in range(2):
                lanes = slice(head * 128, head * 128 + 128)
                turn = q[:, lanes] * gain_q[:, lanes]
                q_rot[rows, lanes] = (turn * cosine + pltpu.roll(turn, 64, 1) * sine).astype(BF16)
            turn = k * gain_k[...]
            kv_rot[rows, :128] = (turn * cosine + pltpu.roll(turn, 64, 1) * sine).astype(BF16)
        return carry

    lax.fori_loop(0, 4, step, 0)


def spot(place, block):
    z = lax.rem(place[1] + block % 4, 4)
    c = place[2] if block < 4 else 1 - place[2]
    return z, c


def attend_body(
    ready, done, place, q_rot, kv_rot, kv_low, squares, squares_low,
    out_raw, out_low, out_turned, q_tiles, keys, vals, logs, vals_t,
):
    ready(q_rot, kv_rot, kv_low)
    for b in range(8):
        rows = slice(b * 128, b * 128 + 128)
        z, c = spot(place, b)
        r = column(root(squares[b : b + 1, :], 2048.0)) * QUERY_SCALE
        inner = pl.ds(pl.multiple_of(c * 128, 128), 128)
        for head in range(2):
            q = q_rot[rows, head * 128 : head * 128 + 128].astype(F32)
            q_tiles[z * 2 + head, inner, :] = (q * r).astype(BF16)
        at = pl.ds(pl.multiple_of(1024 + z * 256 + c * 128, 128), 128)
        r = column(root(squares[8 + b : 9 + b, :], 1024.0))
        keys[at, :] = (kv_rot[rows, :128].astype(F32) * r).astype(BF16)
        vals[at, :] = kv_rot[rows, 128:]
        r = column(root(squares_low[b : b + 1, :], 1024.0))
        keys[rows, :] = (kv_low[rows, :128].astype(F32) * r).astype(BF16)
        vals[rows, :] = kv_low[rows, 128:]
    done(q_tiles, keys, vals)
    vals_t[...] = jnp.transpose(vals[...].astype(F32)).astype(BF16)
    allowed = lax.broadcasted_iota(jnp.int32, (256, 256), 0) <= lax.broadcasted_iota(
        jnp.int32, (256, 256), 1
    )

    def queries(first, i):
        at_diagonal = 1024 + i * 256
        ranges = [(first, at_diagonal)] if at_diagonal > first else []
        for head in range(2):
            q = q_tiles[i * 2 + head]
            scores = [
                lax.dot_general(keys[lo:hi, :], q, NT, preferred_element_type=F32)
                for lo, hi in ranges + [(at_diagonal, at_diagonal + 256)]
            ]
            scores[-1] = jnp.where(allowed, scores[-1], MASKED)
            tops = [jnp.max(s, axis=0, keepdims=True) for s in scores]
            top = functools.reduce(jnp.maximum, tops)
            total, acc = 0.0, 0.0
            for s, (lo, hi) in zip(scores, ranges + [(at_diagonal, at_diagonal + 256)]):
                p = jnp.exp2(s - top)
                total = total + jnp.sum(p, axis=0, keepdims=True)
                acc = acc + jnp.dot(
                    vals_t[:, lo:hi], p.astype(BF16), preferred_element_type=F32
                )
            turned = acc / total
            out = jnp.transpose(turned)
            turned = turned.astype(BF16)
            logs[i * 2 + head : i * 2 + head + 1, :] = top + jnp.log2(total)
            for c in range(2):
                block = lax.rem(i - place[1] + 4, 4) + 4 * jnp.abs(c - place[2])
                at = pl.ds(pl.multiple_of(block * 128, 128), 128)
                lanes = slice(head * 128, head * 128 + 128)
                out_raw[at, lanes] = out[c * 128 : c * 128 + 128, :]
                out_low[at, lanes] = out[c * 128 : c * 128 + 128, :].astype(BF16)
                out_turned[lanes, at] = turned[:, c * 128 : c * 128 + 128]

    @pl.when(place[0] == 1)
    def _():
        for i in range(4):
            queries(0, i)

    @pl.when(place[0] == 0)
    def _():
        for i in range(4):
            queries(1024, i)

    done(out_raw, out_low, out_turned)


def output_body(ready, done, mixed, w_out, a_mine, a_part):
    ready(mixed, w_out)

    def project(t, carry):
        at = pl.ds(pl.multiple_of(t * 256, 256), 256)
        far = pl.ds(pl.multiple_of(512 + t * 256, 256), 256)
        a_part[at, :] = jnp.dot(mixed[far, :], w_out[...], preferred_element_type=F32).astype(BF16)
        a_mine[at, :] = jnp.dot(mixed[at, :], w_out[...], preferred_element_type=F32)
        return carry

    lax.fori_loop(0, 2, project, 0)


def output_back_body(
    ready, done, place, out_raw, w_out, da_all, mixed_turned, d_tiles, deltas, grad_out
):
    ready(out_raw, w_out, da_all)
    for b in range(8):
        rows = slice(b * 128, b * 128 + 128)
        z, c = spot(place, b)
        inner = pl.ds(pl.multiple_of(c * 128, 128), 128)
        d_out = lax.dot_general(
            da_all[rows, :], w_out[...], NT, preferred_element_type=F32
        ).astype(BF16)
        for head in range(2):
            lanes = slice(head * 128, head * 128 + 128)
            grad = d_out[:, lanes]
            d_tiles[z * 2 + head, inner, :] = grad
            deltas[z * 2 + head, pl.ds(c, 1), :] = row_sums(grad.astype(F32) * out_raw[rows, lanes])
    done(d_tiles)
    ready(mixed_turned)
    for m in range(4):
        lanes = slice(m * 256, m * 256 + 256)
        made = jnp.dot(mixed_turned[...], da_all[:, lanes], preferred_element_type=F32).astype(BF16)
        for j in range(2):
            for f in range(8):
                to, at = f * 32 + j * 16, j * 128 + f * 16
                grad_out[to : to + 16, lanes] = made[at : at + 16]


def back_tiles(places, first, i, total, q_tiles, d_tiles, logs, deltas, keys, vals, keys_t, dk, dv):
    q = [q_tiles[i * 2 + head] for head in range(2)]
    grad = [d_tiles[i * 2 + head] for head in range(2)]
    log = [logs[i * 2 + head : i * 2 + head + 1, :] for head in range(2)]
    delta = [
        jnp.concatenate([deltas[i * 2 + head, 0:1, :], deltas[i * 2 + head, 1:2, :]], axis=1)
        for head in range(2)
    ]
    for lo, diagonal in places:
        at = slice(lo, lo + 256)
        here = slice(lo - first, lo - first + 256)
        k, v = keys[at, :], vals[at, :]
        dk_tile, dv_tile = dk[here, :], dv[here, :]
        for head in range(2):
            s = lax.dot_general(k, q[head], NT, preferred_element_type=F32)
            p = jnp.exp2(s - log[head])
            if diagonal:
                row = lax.broadcasted_iota(jnp.int32, (256, 256), 0)
                p = jnp.where(row <= lax.broadcasted_iota(jnp.int32, (256, 256), 1), p, 0.0)
            dp = lax.dot_general(v, grad[head], NT, preferred_element_type=F32)
            ds = (p * (dp - delta[head])).astype(BF16)
            dv_tile += jnp.dot(p.astype(BF16), grad[head], preferred_element_type=F32)
            dk_tile += jnp.dot(ds, q[head], preferred_element_type=F32)
            total[head] = total[head] + jnp.dot(keys_t[:, here], ds, preferred_element_type=F32)
        dk[here, :] = dk_tile
        dv[here, :] = dv_tile
    return total


def low_back_body(
    ready, done, place, q_tiles, keys, vals, logs, d_tiles, deltas,
    dq, d_low, dots, keys_t, dk_acc, dv_acc,
):
    ready(q_tiles, keys, vals, d_tiles)

    @pl.when(place[0] == 1)
    def _():
        keys_t[...] = jnp.transpose(keys[:1024, :].astype(F32)).astype(BF16)
        dk_acc[...] = jnp.zeros_like(dk_acc)
        dv_acc[...] = jnp.zeros_like(dv_acc)
        for i in range(4):
            total = back_tiles(
                [(lo, False) for lo in range(0, 1024, 256)], 0, i, [0.0, 0.0],
                q_tiles, d_tiles, logs, deltas, keys, vals, keys_t, dk_acc, dv_acc,
            )
            for head in range(2):
                dq[i * 2 + head] = total[head]
        for b in range(8):
            rows = slice(b * 128, b * 128 + 128)
            key_grad = dk_acc[rows, :] * (1.0 / LOG2E)
            d_low[rows, :128] = key_grad.astype(BF16)
            d_low[rows, 128:] = dv_acc[rows, :].astype(BF16)
            dots[b : b + 1, :] = row_sums(key_grad * keys[rows, :].astype(F32))

    @pl.when(place[0] == 0)
    def _():
        dq[...] = jnp.zeros_like(dq)
        d_low[...] = jnp.zeros_like(d_low)
        dots[...] = jnp.zeros_like(dots)


def own_back_body(
    ready, done, place, q_tiles, keys, vals, logs, d_tiles, deltas, dq_low, dots_low,
    dq, dk, dv, dots, keys_t, dk_acc, dv_acc,
):
    ready(keys)
    keys_t[...] = jnp.transpose(keys[1024:, :].astype(F32)).astype(BF16)
    dk_acc[...] = jnp.zeros_like(dk_acc)
    dv_acc[...] = jnp.zeros_like(dv_acc)
    ready(q_tiles, vals, d_tiles, dq_low)
    for i in range(4):
        total = back_tiles(
            [(1024 + j * 256, j == i) for j in range(i + 1)], 1024, i,
            [dq_low[i * 2 + head] for head in range(2)],
            q_tiles, d_tiles, logs, deltas, keys, vals, keys_t, dk_acc, dv_acc,
        )
        dot = jnp.zeros((1, 256), F32)
        for head in range(2):
            out = jnp.transpose(total[head]) * DH ** (-0.5)
            dot += jnp.sum(
                total[head] * jnp.transpose(q_tiles[i * 2 + head].astype(F32)), axis=0, keepdims=True
            )
            for c in range(2):
                block = lax.rem(i - place[1] + 4, 4) + 4 * jnp.abs(c - place[2])
                at = pl.ds(pl.multiple_of(block * 128, 128), 128)
                dq[at, head * 128 : head * 128 + 128] = out[c * 128 : c * 128 + 128, :].astype(BF16)
        for c in range(2):
            block = lax.rem(i - place[1] + 4, 4) + 4 * jnp.abs(c - place[2])
            dots[pl.ds(block, 1), :] = dot[:, c * 128 : c * 128 + 128] * (1.0 / LOG2E)
    done(dq)
    for b in range(8):
        rows = slice(b * 128, b * 128 + 128)
        z, c = spot(place, b)
        at = pl.multiple_of(z * 256 + c * 128, 128)
        key_grad = dk_acc[pl.ds(at, 128), :] * (1.0 / LOG2E)
        dk[rows, :] = key_grad
        dv[rows, :] = dv_acc[pl.ds(at, 128), :]
        dots[8 + b : 9 + b, :] = row_sums(key_grad * keys[pl.ds(1024 + at, 128), :].astype(F32))
    dots[16:24, :] = dots_low[...]


def unproject_body(
    ready, done, place, dq, dk, dv, d_got, q_raw, k_raw, squares, dots, dots_got, cos, sin,
    gain_q, gain_k, x_turned, gains, d_made, sent, sums,
):
    sums[...] = jnp.zeros_like(sums)
    ready(dq, dk, dv, d_got, q_raw, k_raw, cos, sin)

    def step(b, carry):
        rows = pl.ds(pl.multiple_of(b * 128, 128), 128)
        cosine, sine = cos[rows, :], sin[rows, :]
        r = column(root(squares[pl.ds(b, 1), :], 2048.0))
        mean = column(dots[pl.ds(b, 1), :]) * (1.0 / 2048.0)
        for head in range(2):
            lanes = slice(head * 128, head * 128 + 128)
            turn = dq[rows, lanes].astype(F32)
            d_norm = turn * cosine - pltpu.roll(turn, 64, 1) * sine
            hat = q_raw[rows, lanes] * r
            sums[0:1, lanes] += jnp.sum(d_norm * hat, axis=0, keepdims=True)
            d_made[rows, lanes] = (r * (d_norm * gain_q[:, lanes] - hat * mean)).astype(BF16)
        r = column(root(squares[pl.ds(b + 8, 1), :], 1024.0))
        mean = column(dots[pl.ds(b + 8, 1), :] + dots_got[pl.ds(b, 1), :]) * (1.0 / 1024.0)
        turn = dk[rows, :] + d_got[rows, :128].astype(F32)
        d_norm = turn * cosine - pltpu.roll(turn, 64, 1) * sine
        hat = k_raw[rows, :] * r
        sums[0:1, 256:] += jnp.sum(d_norm * hat, axis=0, keepdims=True)
        d_made[rows, 256:384] = (r * (d_norm * gain_k[...] - hat * mean)).astype(BF16)
        d_made[rows, 384:] = (dv[rows, :] + d_got[rows, 128:].astype(F32)).astype(BF16)
        return carry

    lax.fori_loop(0, 8, step, 0)
    done(d_made)
    ready(x_turned, gains)

    def grad(t, carry):
        rows = pl.ds(pl.multiple_of(t * 256, 256), 256)
        sent[rows, :512] = jnp.dot(
            x_turned[rows, :], d_made[...], preferred_element_type=F32
        ).astype(BF16)
        sent[rows, 512:] = gains[rows, :]
        return carry

    lax.fori_loop(0, 4, grad, 0)
    extra = 0.0
    for lo, width, each, first in ((0, 256, 16, 0), (256, 128, 8, 16)):
        row = lax.broadcasted_iota(jnp.int32, (128, width), 0) // 8
        lane = lax.broadcasted_iota(jnp.int32, (128, width), 1) // each
        spread = jnp.where(row == lane, sums[0:1, lo : lo + width], 0.0).astype(BF16)
        lane = lax.broadcasted_iota(jnp.int32, (width, 128), 0) % each + first
        pick = jnp.where(lane == lax.broadcasted_iota(jnp.int32, (width, 128), 1), 1.0, 0.0)
        extra = extra + jnp.dot(spread, pick.astype(BF16), preferred_element_type=F32)
    rows = pl.ds(pl.multiple_of((place[1] * 2 + place[2]) * 128, 128), 128)
    sent[rows, 512:] = (gains[rows, :].astype(F32) + extra).astype(BF16)


def input_body(ready, done, d_made, weight, dx_mine, dx_part):
    ready(d_made, weight)

    def step(t, carry):
        at = pl.ds(pl.multiple_of(t * 256, 256), 256)
        far = pl.ds(pl.multiple_of(512 + t * 256, 256), 256)
        dx_part[at, :] = lax.dot_general(
            d_made[far, :], weight[...], NT, preferred_element_type=F32
        ).astype(BF16)
        dx_mine[at, :] = lax.dot_general(
            d_made[at, :], weight[...], NT, preferred_element_type=F32
        )
        return carry

    lax.fori_loop(0, 2, step, 0)


def expand_body(ready, done, h_all, weight, packed, gate, up, expanded, m_mine, m_part, down):
    ready(packed)
    for f in range(8):
        down[f * 96 : f * 96 + 96, :768] = packed[f * 128 : f * 128 + 96, :]
        for m in range(3):
            down[f * 96 + m * 32 : f * 96 + m * 32 + 32, 768:] = packed[
                f * 128 + 96 : f * 128 + 128, m * 256 : m * 256 + 256
            ]

    done(down)
    ready(h_all, weight)
    done(h_all)

    def widen(n, carry):
        lanes = pl.ds(pl.multiple_of(n * 256, 256), 256)
        upper = pl.ds(pl.multiple_of(768 + n * 256, 256), 256)
        g = jnp.dot(h_all[...], weight[:, lanes], preferred_element_type=F32)
        u = jnp.dot(h_all[...], weight[:, upper], preferred_element_type=F32)
        gate[:, lanes] = g
        up[:, lanes] = u
        expanded[:, lanes] = (g * jax.nn.sigmoid(g) * u).astype(BF16)
        return carry

    lax.fori_loop(0, 3, widen, 0)
    done(gate, up, expanded)

    def narrow(n, carry):
        lanes = pl.ds(pl.multiple_of(n * 256, 256), 256)
        m = jnp.dot(expanded[...], down[:, lanes], preferred_element_type=F32)
        m_mine[:, lanes] = m[:256]
        m_part[:, lanes] = m[256:].astype(BF16)
        return carry

    lax.fori_loop(0, 4, narrow, 0)


def expand_back_body(ready, done, dm_all, gate, up, weight, down, d_gu, dh_mine, dh_part):
    ready(dm_all, gate, up, down)
    done(dm_all)

    def widen(n, carry):
        lanes = pl.ds(pl.multiple_of(n * 256, 256), 256)
        upper = pl.ds(pl.multiple_of(768 + n * 256, 256), 256)
        de = lax.dot_general(dm_all[...], down[lanes, :], NT, preferred_element_type=F32)
        g = gate[:, lanes]
        sig = jax.nn.sigmoid(g)
        d_gu[:, lanes] = (de * up[:, lanes] * sig * (1.0 + g * (1.0 - sig))).astype(BF16)
        d_gu[:, upper] = (de * (g * sig)).astype(BF16)
        return carry

    lax.fori_loop(0, 3, widen, 0)
    done(d_gu)
    ready(weight)

    def narrow(n, carry):
        lanes = pl.ds(pl.multiple_of(n * 256, 256), 256)
        dh = lax.dot_general(d_gu[...], weight[lanes, :], NT, preferred_element_type=F32)
        dh_mine[:, lanes] = dh[:256]
        dh_part[:, lanes] = dh[256:].astype(BF16)
        return carry

    lax.fori_loop(0, 4, narrow, 0)


def expand_grad_body(ready, done, h_turned, d_gu, expanded, dm_all, out, expanded_t):
    ready(expanded)
    expanded_t[...] = jnp.transpose(expanded[...].astype(F32)).astype(BF16)

    ready(h_turned, d_gu, dm_all)

    def widen(n, carry):
        lanes = pl.ds(pl.multiple_of(n * 256, 256), 256)
        out[:, lanes] = jnp.dot(
            h_turned[...], d_gu[:, lanes], preferred_element_type=F32
        ).astype(BF16)
        return carry

    lax.fori_loop(0, 6, widen, 0)
    for n in range(4):
        made = jnp.dot(
            expanded_t[...], dm_all[:, n * 256 : n * 256 + 256], preferred_element_type=F32
        ).astype(BF16)
        for f in range(16):
            if n < 3:
                out[f * 64 : f * 64 + 48, 1536 + n * 256 : 1792 + n * 256] = made[
                    f * 48 : f * 48 + 48
                ]
                continue
            for m in range(3):
                out[f * 64 + 48 : f * 64 + 64, 1536 + m * 256 : 1792 + m * 256] = made[
                    f * 48 + m * 16 : f * 48 + m * 16 + 16
                ]


def norm_scale(values):
    return lax.rsqrt(jnp.mean(values * values, axis=-1, keepdims=True) + EPS)


def norm_back(upstream, normed, scaling):
    return scaling * (upstream - normed * jnp.mean(upstream * normed, axis=-1, keepdims=True))


def rotary_tables(first, z, c):
    half = DH // 2
    k = jnp.arange(4, dtype=jnp.int32)
    starts = jnp.concatenate([((z + k) % 4) * 256 + c * 128, ((z + k) % 4) * 256 + (1 - c) * 128])
    places = (first + starts[:, None] + jnp.arange(128, dtype=jnp.int32)[None, :]).reshape(1024)
    inverse = THETA ** (-(jnp.arange(half, dtype=F32) * (2.0 / DH)))
    angles = places.astype(F32)[:, None] * inverse[None, :]
    cosine, sine = jnp.cos(angles), jnp.sin(angles)
    return (
        jnp.concatenate([cosine, cosine], axis=-1),
        jnp.concatenate([-sine, sine], axis=-1),
    )


def dot(a, b):
    return jnp.dot(a, b, preferred_element_type=F32)


def dot_nt(a, b):
    return lax.dot_general(a, b, NT, preferred_element_type=F32)


def dot_tn(a, b):
    return lax.dot_general(a, b, (((0,), (0,)), ((), ())), preferred_element_type=F32)


def on_device(
    tokens, out_grad, w_query, w_key, w_value, w_out, w_gate, w_up, w_down,
    gain_query, gain_key, gain_attn, gain_mlp,
):
    seq = lax.axis_index("seq")
    xh, zc = seq // 8, seq % 8
    z, c = zc // 2, zc % 2
    quarter = (z % 2) * 2 + c
    place = jnp.stack([xh, z, c]).astype(jnp.int32)
    inputs = tokens[0]

    def columns(weight, width):
        return lax.dynamic_slice_in_dim(weight, zc * width, width, 1)

    def spread(block):
        return lax.all_to_all(
            jnp.broadcast_to(block[None], (8,) + block.shape),
            "fsdp", split_axis=0, concat_axis=0, tiled=True,
        ).reshape(8 * block.shape[0], block.shape[1])

    x_blocks = gather_group(inputs)
    weight = spread(
        jnp.concatenate(
            [columns(w_query, 256), columns(w_key, 128), columns(w_value, 128)], axis=1
        )
    )
    w_out_rows = lax.ppermute(
        after(lax.dynamic_slice_in_dim(w_out, zc * 32, 32, 0), weight),
        ("seq", "fsdp"),
        TURN,
    )

    def quarters(weight):
        part = lax.dynamic_slice_in_dim(weight.reshape(128, 8, 384), quarter * 96, 96, 2)
        return part.reshape(128, 768)

    down = lax.dynamic_slice_in_dim(w_down, quarter * 96, 96, 0)
    packed = jnp.concatenate(
        [
            down[:, :768],
            jnp.concatenate([down[m * 32 : m * 32 + 32, 768:] for m in range(3)], axis=1),
        ],
        axis=0,
    )
    w_narrow = lax.all_gather(packed, "fsdp", axis=0, tiled=True)
    w_wide = jnp.concatenate([quarters(w_gate), quarters(w_up)], axis=1)
    weight, w_wide = lax.optimization_barrier((weight, w_wide))

    cosine, sine = rotary_tables(xh * 1024, z, c)
    gain_q = lax.dynamic_slice_in_dim(gain_query, zc * 256, 256, 0)[None]
    gain_k = lax.dynamic_slice_in_dim(gain_key, zc * 128, 128, 0)[None]
    x_all, q_raw, k_raw, q_rot, kv_rot, squares = kernel_call(
        project_body,
        [
            *in_hbm(
                0, shaped((1024, 256), F32), shaped((1024, 128), F32),
                shaped((1024, 256), BF16), shaped((1024, 256), BF16),
            ),
            shaped((16, 128), F32),
        ],
        [x_blocks, weight, gain_q, gain_k, cosine, sine],
        flops=2 * 1024 * 1024 * 512, nbytes=9 << 20,
    )

    kv_low = swap(kv_rot, LOW_TO_HIGH)
    squares = sum_group(squares)
    squares_low = swap(squares[8:], LOW_TO_HIGH)
    kv_low, squares, squares_low, w_wide, w_narrow, w_out_rows = lax.optimization_barrier(
        (kv_low, squares, squares_low, w_wide, w_narrow, w_out_rows)
    )
    w_wide = lax.all_gather(w_wide, "fsdp", axis=0, tiled=True)
    w_out_rows = spread(w_out_rows)
    out_raw, mixed, mixed_turned, q_tiles, keys, vals, logs = kernel_call(
        attend_body,
        [
            *in_hbm(
                shaped((1024, 256), F32), shaped((1024, 256), BF16), shaped((256, 1024), BF16),
                shaped((8, 256, 128), BF16), shaped((2048, 128), BF16), shaped((2048, 128), BF16),
            ),
            shaped((8, 256), F32),
        ],
        [place, *in_hbm(q_rot, kv_rot), kv_low, squares, squares_low],
        [pltpu.VMEM((128, 2048), BF16)],
        flops=4 * 1024 * 2048 * 256, nbytes=9 << 20,
    )
    a_mine, a_part = kernel_call(
        output_body,
        [shaped((512, 1024), F32), shaped((512, 1024), BF16)],
        [*in_hbm(mixed), w_out_rows],
        flops=2 * 1024 * 1024 * 256, nbytes=5 << 20,
    )
    x_turned = x_all.T

    attended = scatter_group(a_mine, a_part)
    attended, x_turned = lax.optimization_barrier((attended, x_turned))
    attn_scale = norm_scale(attended)
    attn_hat = attended * attn_scale
    hidden_state = inputs.astype(F32) + attn_hat * gain_attn
    h_all, gate, up, expanded, m_mine, m_part, w_down_rows = kernel_call(
        expand_body,
        [
            0, shaped((512, 768), F32), shaped((512, 768), F32), shaped((512, 768), BF16),
            shaped((256, 1024), F32), shaped((256, 1024), BF16), shaped((768, 1024), BF16),
        ],
        [
            gather_pair(hidden_state.astype(BF16)), *in_hbm(w_wide, w_narrow),
        ],
        flops=2 * 512 * 2304 * 1024, nbytes=12 << 20,
    )
    projected, _ = scatter_pair(m_mine, m_part)
    mlp_scale = norm_scale(projected)
    mlp_hat = projected * mlp_scale
    output = (hidden_state + mlp_hat * gain_mlp).astype(BF16)[None]

    upstream = out_grad[0].astype(F32)
    grad_gain_mlp = jnp.sum(upstream * mlp_hat, axis=0)
    d_projected = norm_back(upstream * gain_mlp, mlp_hat, mlp_scale).astype(BF16)
    n = jnp.arange(1024, dtype=jnp.int32)
    source = ((n // 8) % 16) * 64 + (n // 128) * 8 + n % 8
    order = (n[None, :] == source[:, None]).astype(BF16)
    h_turned = dot_nt(order, h_all).astype(BF16)
    d_blocks = gather_pair(d_projected)
    d_blocks[3], h_turned = lax.optimization_barrier((d_blocks[3], h_turned))
    dm_all, d_gu, dh_mine, dh_part = kernel_call(
        expand_back_body,
        [
            0, shaped((512, 1536), BF16), shaped((256, 1024), F32), shaped((256, 1024), BF16),
        ],
        [d_blocks, gate, up, w_wide, w_down_rows],
        flops=2 * 512 * 2304 * 1024, nbytes=12 << 20,
    )

    far = dh_mine[128:] + swap(dh_part[128:], CORE_SWAP).astype(F32)
    far, d_gu, dm_all = lax.optimization_barrier((far.astype(BF16), d_gu, dm_all))
    far = swap(far, Z_SWAP)
    (grad_mlp,) = kernel_call(
        expand_grad_body,
        in_hbm(shaped((1024, 2304), BF16)),
        [h_turned, d_gu, expanded, dm_all],
        [pltpu.VMEM((768, 512), BF16)],
        flops=2 * 512 * 2304 * 1024, nbytes=9 << 20,
    )
    far, grad_mlp = lax.optimization_barrier((far, grad_mlp))
    grad_mlp = lax.psum_scatter(grad_mlp, "fsdp", scatter_dimension=0, tiled=True)
    d_hidden = upstream + dh_mine[:128] + swap(dh_part[:128], CORE_SWAP).astype(F32)
    d_hidden = d_hidden + far.astype(F32)

    grad_gain_attn = jnp.sum(d_hidden * attn_hat, axis=0)
    d_attended = norm_back(d_hidden * gain_attn, attn_hat, attn_scale).astype(BF16)
    d_tiles, deltas, grad_out = kernel_call(
        output_back_body,
        [shaped((8, 256, 128), BF16), shaped((8, 2, 128), F32), shaped((256, 1024), BF16)],
        [place, *in_hbm(out_raw, w_out_rows, gather_group(d_attended), mixed_turned)],
        flops=4 * 1024 * 1024 * 256, nbytes=6 << 20,
    )
    fsdp = lax.axis_index("fsdp")

    def halve(value, rows, bit, axis, pairs):
        parts = value.reshape(-1, 2, rows, 1024)
        given = jnp.where(bit == 1, parts[:, 0], parts[:, 1])
        mine = jnp.where(bit == 1, parts[:, 1], parts[:, 0]).astype(F32)
        return (mine + lax.ppermute(given, axis, pairs).astype(F32)).astype(BF16)

    grad_out = halve(grad_out, 32, fsdp % 2, "fsdp", [(i, i ^ 1) for i in range(8)])
    scratch = [
        pltpu.VMEM((128, 1024), BF16), pltpu.VMEM((1024, 128), F32), pltpu.VMEM((1024, 128), F32),
    ]
    shared = [place, *in_hbm(q_tiles, keys, vals), logs, d_tiles, deltas]
    dq_low, d_low, dots_low = kernel_call(
        low_back_body,
        [
            shaped((8, 128, 256), F32), *in_hbm(shaped((1024, 256), BF16)), shaped((8, 128), F32),
        ],
        shared,
        scratch,
        flops=10 * 1024 * 1024 * 256, nbytes=4 << 20,
    )
    dq_low, grad_out = lax.optimization_barrier((dq_low, grad_out))
    grad_out = halve(grad_out, 32, fsdp // 2 % 2, "fsdp", [(i, i ^ 2) for i in range(8)])
    dq, dk, dv, dots = kernel_call(
        own_back_body,
        [
            *in_hbm(
                shaped((1024, 256), BF16), shaped((1024, 128), F32), shaped((1024, 128), F32),
            ),
            shaped((24, 128), F32),
        ],
        [*shared, dq_low, dots_low],
        scratch,
        flops=10 * 1024 * 640 * 256, nbytes=5 << 20,
    )
    dots, grad_out = lax.optimization_barrier((dots, grad_out))
    grad_out = halve(grad_out, 32, fsdp // 4, "fsdp", [(i, i ^ 4) for i in range(8)])
    d_got = swap(d_low, HIGH_TO_LOW)
    dots = sum_group(dots)
    dots_got = swap(dots[16:], HIGH_TO_LOW)

    gains = jnp.concatenate([grad_gain_attn.reshape(128, 8), grad_gain_mlp.reshape(128, 8)], axis=1)
    gains = jnp.broadcast_to(
        jnp.pad(gains.astype(BF16), ((0, 0), (24, 88)))[:, None, :], (128, 8, 128)
    ).reshape(1024, 128)
    d_made, sent = kernel_call(
        unproject_body,
        [shaped((1024, 512), BF16), shaped((1024, 640), BF16)],
        [
            place, *in_hbm(dq, dk, dv), d_got, *in_hbm(q_raw, k_raw), squares, dots, dots_got, cosine, sine,
            gain_q, gain_k, *in_hbm(x_turned), gains,
        ],
        [pltpu.VMEM((8, 384), F32)],
        flops=2 * 1024 * 1024 * 512, nbytes=9 << 20,
    )

    def halves(value, upper):
        low, high = value[: value.shape[0] // 2], value[value.shape[0] // 2 :]
        return jnp.where(upper, high, low), jnp.where(upper, low, high)

    mine, given = halves(grad_mlp, xh == 1)
    mine = mine.astype(F32) + swap(given, X_SWAP).astype(F32)
    got_wide = lax.all_to_all(
        grad_mlp[:, :1536].reshape(16, 8, 1536), "seq", split_axis=0, concat_axis=0, tiled=True
    )
    sent, got_wide, grad_mlp, grad_out = lax.optimization_barrier(
        (sent, got_wide, grad_mlp, grad_out)
    )
    grad_down = jnp.concatenate(
        [
            piece
            for h in (0, 64)
            for piece in [
                jnp.concatenate(
                    [
                        grad_mlp[h : h + 48, 1536:],
                        jnp.concatenate(
                            [
                                grad_mlp[h + 48 : h + 64, 1536 + m * 256 : 1792 + m * 256]
                                for m in range(3)
                            ],
                            axis=0,
                        ),
                    ],
                    axis=1,
                )
            ]
        ],
        axis=0,
    ).reshape(4, 24, 1024)
    grad_down = sum(
        lax.ppermute(
            lax.dynamic_index_in_dim(grad_down, (xh * 2 + z // 2) ^ other, 0, keepdims=False),
            ("seq", "fsdp"),
            down_home(other),
        ).astype(F32)
        for other in range(4)
    )
    grad_out = grad_out.reshape(2, 16, 1024)
    grad_out = sum(
        swap(jnp.where((xh == 1) != other, grad_out[1], grad_out[0]), out_home(other)).astype(F32)
        for other in (False, True)
    )
    got_made = lax.all_to_all(
        sent.reshape(128, 8, 640), ("seq", "fsdp"), split_axis=0, concat_axis=0, tiled=True
    )
    dx_mine, dx_part = kernel_call(
        input_body,
        in_hbm(shaped((512, 1024), F32), shaped((512, 1024), BF16)),
        [after(d_made, sent), weight],
        flops=2 * 1024 * 1024 * 512, nbytes=5 << 20,
    )
    rows = [slice(k * 128, k * 128 + 128) for k in range(4)]
    pieces = [dx_mine[r] + swap(dx_part[r], CORE_SWAP).astype(F32) for r in rows]
    far = [piece.astype(BF16) for piece in pieces[1:]]
    d_inputs = pieces[0] + sum(
        swap(piece, to_z(k)).astype(F32) for k, piece in enumerate(far, 1)
    )
    got_made, grad_down, grad_out, d_inputs = lax.optimization_barrier(
        (got_made, grad_down, grad_out, d_inputs)
    )
    summed = jnp.sum(got_made.reshape(2, 8, 8, 8, 640).astype(F32), axis=(0, 2))
    gains = jnp.sum(summed[:, 0, 512:], axis=0)

    def take(first, width):
        return summed[:, :, first : first + width].swapaxes(0, 1).reshape(8, 8 * width)

    wide = jnp.sum(got_wide.reshape(2, 2, 4, 8, 2, 8, 96).astype(F32), axis=(0, 1))
    wide = wide.transpose(2, 1, 3, 0, 4).reshape(2, 8, 3072)
    return (
        output,
        (d_hidden + d_inputs).astype(BF16)[None],
        take(0, 256),
        take(256, 128),
        take(384, 128),
        grad_out.astype(F32),
        wide[0],
        wide[1],
        grad_down.astype(F32),
        gains[:16],
        gains[16:24],
        gains[24:32],
        gains[32:40],
    )


def solution(mesh):
    rows = P("fsdp", "seq", None)
    weight = P("fsdp", None)
    grad = P(("seq", "fsdp"), None)
    gain = P(("seq", "fsdp"))
    return jax.shard_map(
        on_device,
        mesh=mesh,
        in_specs=(rows,) * 2 + (weight,) * 7 + (P(),) * 4,
        out_specs=(rows,) * 2 + (grad,) * 7 + (gain,) * 4,
        check_vma=False,
    )
```

```python
import functools
import math

import jax
import jax.numpy as jnp
from jax import lax
from jax.experimental import pallas as pl
from jax.experimental.pallas import tpu as pltpu
from jax.sharding import PartitionSpec as P

BF16 = jnp.bfloat16
F32 = jnp.float32
DH = 128
EPS = 1e-06
THETA = 1000000.0
MASKED = -1e30
LOG2E = math.log2(math.e)
QUERY_SCALE = DH ** (-0.5) * LOG2E
VMEM_BYTES = 20 * 1024 * 1024
VMEM = pl.BlockSpec(memory_space=pltpu.VMEM)
SMEM = pl.BlockSpec(memory_space=pltpu.SMEM)
ANY = pl.BlockSpec(memory_space=pl.ANY)
SMALL = 64 * 1024
NT = (((1,), (1,)), ((), ()))

SEQ_PLACES = [(xh, z, c) for xh in range(2) for z in range(4) for c in range(2)]


def seq_index(xh, z, c):
    return xh * 8 + (z % 4) * 2 + c


CORE_SWAP = [(i, i ^ 1) for i in range(16)]
LOW_TO_HIGH = [(i, i + 8) for i in range(8)]
HIGH_TO_LOW = [(i + 8, i) for i in range(8)]
X_SWAP = [(i, i ^ 8) for i in range(16)]


def from_z(k):
    return [(seq_index(xh, z + k, c), seq_index(xh, z, c)) for xh, z, c in SEQ_PLACES]


def to_z(k):
    return [(seq_index(xh, z, c), seq_index(xh, z + k, c)) for xh, z, c in SEQ_PLACES]


def across(pairs):
    return [(seq * 8 + f, to_seq * 8 + to_f) for seq, f, to_seq, to_f in pairs]


TURN = across(
    (xh * 8 + a, f, xh * 8 + f, a) for xh in range(2) for a in range(8) for f in range(8)
)
Z_SWAP = [(i, i ^ 2) for i in range(16)]
FAR_SWAP = [(i, i ^ 4) for i in range(16)]


def out_home(other):
    return [(xh * 8 + a, 2 * a + (xh ^ other)) for xh in range(2) for a in range(8)]


def down_home(other):
    return across(
        (seq_index(own // 2, 2 * (own % 2) + zl, c), f, 2 * f + zl, 4 * c + (own ^ other))
        for own in range(4) for zl in range(2) for c in range(2) for f in range(8)
    )


def swap(value, pairs):
    return lax.ppermute(value, "seq", pairs)


def after(value, *others):
    return lax.optimization_barrier((value, *others))[0]


def gather_group(block):
    far = {k: swap(block, from_z(k)) for k in (2, 1, 3)}
    mine = [block, far[1], far[2], far[3]]
    return mine + [swap(v, CORE_SWAP) for v in mine]


def scatter_group(mine, part):
    rows = [slice(k * 128, k * 128 + 128) for k in range(4)]
    out = None
    for k in (2, 1, 3, 0):
        piece = mine[rows[k]] + swap(part[rows[k]], CORE_SWAP).astype(F32)
        if k:
            piece = swap(piece.astype(BF16), to_z(k)).astype(F32)
        out = piece if out is None else out + piece
    return out


def gather_pair(block):
    mine = [block, swap(block, Z_SWAP)]
    return mine + [swap(v, CORE_SWAP) for v in mine]


def scatter_pair(mine, part, later=()):
    far = mine[128:] + swap(part[128:], CORE_SWAP).astype(F32)
    far, *later = lax.optimization_barrier((far.astype(BF16), *later))
    far = swap(far, Z_SWAP).astype(F32)
    return mine[:128] + swap(part[:128], CORE_SWAP).astype(F32) + far, later


def sum_group(rows):
    groups = rows.shape[0] // 8
    other = swap(rows, CORE_SWAP).reshape(groups, 2, 4, 128)
    pair = rows.reshape(groups, 2, 4, 128) + jnp.concatenate([other[:, 1:], other[:, :1]], axis=1)
    odd = lax.axis_index("seq") // 2 % 2 == 1
    got = swap(pair, Z_SWAP)
    up = jnp.concatenate([got[:, :, 3:], got[:, :, :3]], axis=2)
    down = jnp.concatenate([got[:, :, 1:], got[:, :, :1]], axis=2)
    pair = pair + jnp.where(odd, down, up)
    got = swap(pair, FAR_SWAP)
    pair = pair + jnp.concatenate([got[:, :, 2:], got[:, :, :2]], axis=2)
    return pair.reshape(rows.shape)


def column(row):
    return jnp.transpose(jnp.broadcast_to(row, (128, 128)))


def row_sums(values):
    return jnp.sum(jnp.transpose(values), axis=0, keepdims=True)


def shaped(shape, dtype):
    return jax.ShapeDtypeStruct(shape, dtype)


class Kept:
    def __init__(self, value):
        self.value = value


def in_hbm(*values):
    return [Kept(v) for v in values]


def kernel_call(body, outs, inputs, scratch=(), flops=0, nbytes=0):
    hbm_outs = [isinstance(o, Kept) for o in outs]
    hbm_ins = [isinstance(x, Kept) for x in inputs]
    outs = [o.value if isinstance(o, Kept) else o for o in outs]
    inputs = [x.value if isinstance(x, Kept) else x for x in inputs]
    groups = [x if isinstance(x, list) else [x] for x in inputs]
    flat = [a for group in groups for a in group]
    joined = [
        shaped((sum(a.shape[0] for a in group),) + group[0].shape[1:], group[0].dtype)
        for group in groups
    ]

    def large(s):
        return math.prod(s.shape) * s.dtype.itemsize >= SMALL

    def where(s):
        return ANY if large(s) else SMEM if s.dtype == jnp.int32 else VMEM

    out_shapes = [joined[o] if isinstance(o, int) else o for o in outs]
    in_buffers = [pltpu.VMEM(s.shape, s.dtype) for s in joined if large(s)]
    out_buffers = [
        pltpu.VMEM(o.shape, o.dtype) for o in outs if not isinstance(o, int) and large(o)
    ]

    def whole(*refs):
        refs = list(refs)

        def pull(count):
            taken = refs[:count]
            del refs[:count]
            return taken

        in_refs, out_refs = pull(len(flat)), pull(len(outs))
        in_space, out_space = pull(len(in_buffers)), pull(len(out_buffers))
        own, (in_sem, out_sem) = pull(len(scratch)), refs
        loads, ins, at = {}, [], 0
        for group, s in zip(groups, joined):
            if not large(s):
                ins.append(in_refs[at])
                at += 1
                continue
            space, row = in_space.pop(0), 0
            loads[id(space)] = []
            for a in group:
                copy = pltpu.make_async_copy(
                    in_refs[at], space.at[pl.ds(row, a.shape[0])], in_sem.at[at]
                )
                copy.start()
                loads[id(space)].append(copy)
                row, at = row + a.shape[0], at + 1
            ins.append(space)
        made, stores = [], {}
        for k, (o, s, ref) in enumerate(zip(outs, out_shapes, out_refs)):
            if not large(s):
                made.append(ref)
                continue
            space = ins[o] if isinstance(o, int) else out_space.pop(0)
            stores[id(space)] = pltpu.make_async_copy(space, ref, out_sem.at[k])
            if not isinstance(o, int):
                made.append(space)
        started = []

        def ready(*spaces):
            for space in spaces:
                for copy in loads.pop(id(space), ()):
                    copy.wait()

        def done(*spaces):
            for space in spaces:
                copy = stores.pop(id(space))
                copy.start()
                started.append(copy)

        body(ready, done, *ins, *made, *own)
        for key in list(stores):
            copy = stores.pop(key)
            copy.start()
            started.append(copy)
        for copy in started:
            copy.wait()

    shapes = [pltpu.HBM(s.shape, s.dtype) if hbm else s for s, hbm in zip(out_shapes, hbm_outs)]
    return pl.pallas_call(
        whole,
        out_shape=tuple(shapes),
        in_specs=[where(s) for group, s in zip(groups, joined) for _ in group],
        out_specs=tuple(where(s) for s in out_shapes),
        scratch_shapes=[
            *in_buffers, *out_buffers, *scratch,
            pltpu.SemaphoreType.DMA((len(flat),)), pltpu.SemaphoreType.DMA((len(outs),)),
        ],
        compiler_params=pltpu.CompilerParams(vmem_limit_bytes=VMEM_BYTES),
        cost_estimate=pl.CostEstimate(flops=flops, bytes_accessed=nbytes, transcendentals=0),
    )(
        *[
            pltpu.with_memory_space_constraint(a, pltpu.HBM) if hbm else a
            for group, hbm in zip(groups, hbm_ins)
            for a in group
        ],
    )


def root(total, width):
    return lax.rsqrt(total * (1.0 / width) + EPS)


def project_body(
    ready, done, x_all, weight, gain_q, gain_k, cos, sin,
    q_raw, k_raw, q_rot, kv_rot, squares,
):
    ready(x_all, weight, cos, sin)
    done(x_all)

    def step(t, carry):
        at = pl.multiple_of(t * 256, 256)
        made = jnp.dot(x_all[pl.ds(at, 256), :], weight[...], preferred_element_type=F32)
        for part in range(2):
            rows = pl.ds(at + part * 128, 128)
            block = t * 2 + part
            here = made[part * 128 : part * 128 + 128]
            q, k = here[:, :256], here[:, 256:384]
            kv_rot[rows, 128:] = here[:, 384:].astype(BF16)
            q_raw[rows, :] = q
            k_raw[rows, :] = k
            squares[pl.ds(block, 1), :] = row_sums(
                q[:, :128] * q[:, :128] + q[:, 128:] * q[:, 128:]
            )
            squares[pl.ds(block + 8, 1), :] = row_sums(k * k)
            cosine, sine = cos[rows, :], sin[rows, :]
            for head in range(2):
                lanes = slice(head * 128, head * 128 + 128)
                turn = q[:, lanes] * gain_q[:, lanes]
                q_rot[rows, lanes] = (turn * cosine + pltpu.roll(turn, 64, 1) * sine).astype(BF16)
            turn = k * gain_k[...]
            kv_rot[rows, :128] = (turn * cosine + pltpu.roll(turn, 64, 1) * sine).astype(BF16)
        return carry

    lax.fori_loop(0, 4, step, 0)


def spot(place, block):
    z = lax.rem(place[1] + block % 4, 4)
    c = place[2] if block < 4 else 1 - place[2]
    return z, c


def attend_body(
    ready, done, place, q_rot, kv_rot, kv_low, squares, squares_low,
    out_raw, out_low, out_turned, q_tiles, keys, vals, logs, vals_t,
):
    ready(q_rot, kv_rot, kv_low)
    for b in range(8):
        rows = slice(b * 128, b * 128 + 128)
        z, c = spot(place, b)
        r = column(root(squares[b : b + 1, :], 2048.0)) * QUERY_SCALE
        inner = pl.ds(pl.multiple_of(c * 128, 128), 128)
        for head in range(2):
            q = q_rot[rows, head * 128 : head * 128 + 128].astype(F32)
            q_tiles[z * 2 + head, inner, :] = (q * r).astype(BF16)
        at = pl.ds(pl.multiple_of(1024 + z * 256 + c * 128, 128), 128)
        r = column(root(squares[8 + b : 9 + b, :], 1024.0))
        keys[at, :] = (kv_rot[rows, :128].astype(F32) * r).astype(BF16)
        vals[at, :] = kv_rot[rows, 128:]
        r = column(root(squares_low[b : b + 1, :], 1024.0))
        keys[rows, :] = (kv_low[rows, :128].astype(F32) * r).astype(BF16)
        vals[rows, :] = kv_low[rows, 128:]
    done(q_tiles, keys, vals)
    vals_t[...] = jnp.transpose(vals[...].astype(F32)).astype(BF16)
    allowed = lax.broadcasted_iota(jnp.int32, (256, 256), 0) <= lax.broadcasted_iota(
        jnp.int32, (256, 256), 1
    )

    def queries(first, i):
        at_diagonal = 1024 + i * 256
        ranges = [(first, at_diagonal)] if at_diagonal > first else []
        for head in range(2):
            q = q_tiles[i * 2 + head]
            scores = [
                lax.dot_general(keys[lo:hi, :], q, NT, preferred_element_type=F32)
                for lo, hi in ranges + [(at_diagonal, at_diagonal + 256)]
            ]
            scores[-1] = jnp.where(allowed, scores[-1], MASKED)
            tops = [jnp.max(s, axis=0, keepdims=True) for s in scores]
            top = functools.reduce(jnp.maximum, tops)
            total, acc = 0.0, 0.0
            for s, (lo, hi) in zip(scores, ranges + [(at_diagonal, at_diagonal + 256)]):
                p = jnp.exp2(s - top)
                total = total + jnp.sum(p, axis=0, keepdims=True)
                acc = acc + jnp.dot(
                    vals_t[:, lo:hi], p.astype(BF16), preferred_element_type=F32
                )
            turned = acc / total
            out = jnp.transpose(turned)
            turned = turned.astype(BF16)
            logs[i * 2 + head : i * 2 + head + 1, :] = top + jnp.log2(total)
            for c in range(2):
                block = lax.rem(i - place[1] + 4, 4) + 4 * jnp.abs(c - place[2])
                at = pl.ds(pl.multiple_of(block * 128, 128), 128)
                lanes = slice(head * 128, head * 128 + 128)
                out_raw[at, lanes] = out[c * 128 : c * 128 + 128, :]
                out_low[at, lanes] = out[c * 128 : c * 128 + 128, :].astype(BF16)
                out_turned[lanes, at] = turned[:, c * 128 : c * 128 + 128]

    @pl.when(place[0] == 1)
    def _():
        for i in range(4):
            queries(0, i)

    @pl.when(place[0] == 0)
    def _():
        for i in range(4):
            queries(1024, i)

    done(out_raw, out_low, out_turned)


def output_body(ready, done, mixed, w_out, a_mine, a_part):
    ready(mixed, w_out)

    def project(t, carry):
        at = pl.ds(pl.multiple_of(t * 256, 256), 256)
        far = pl.ds(pl.multiple_of(512 + t * 256, 256), 256)
        a_part[at, :] = jnp.dot(mixed[far, :], w_out[...], preferred_element_type=F32).astype(BF16)
        a_mine[at, :] = jnp.dot(mixed[at, :], w_out[...], preferred_element_type=F32)
        return carry

    lax.fori_loop(0, 2, project, 0)


def output_back_body(
    ready, done, place, out_raw, w_out, da_all, mixed_turned, d_tiles, deltas, grad_out
):
    ready(out_raw, w_out, da_all)
    for b in range(8):
        rows = slice(b * 128, b * 128 + 128)
        z, c = spot(place, b)
        inner = pl.ds(pl.multiple_of(c * 128, 128), 128)
        d_out = lax.dot_general(
            da_all[rows, :], w_out[...], NT, preferred_element_type=F32
        ).astype(BF16)
        for head in range(2):
            lanes = slice(head * 128, head * 128 + 128)
            grad = d_out[:, lanes]
            d_tiles[z * 2 + head, inner, :] = grad
            deltas[z * 2 + head, pl.ds(c, 1), :] = row_sums(grad.astype(F32) * out_raw[rows, lanes])
    done(d_tiles)
    ready(mixed_turned)
    for m in range(4):
        lanes = slice(m * 256, m * 256 + 256)
        made = jnp.dot(mixed_turned[...], da_all[:, lanes], preferred_element_type=F32).astype(BF16)
        for j in range(2):
            for f in range(8):
                to, at = f * 32 + j * 16, j * 128 + f * 16
                grad_out[to : to + 16, lanes] = made[at : at + 16]


def back_tiles(places, i, total, q_tiles, d_tiles, logs, deltas, keys, vals, keys_t, dk, dv):
    q = [q_tiles[i * 2 + head] for head in range(2)]
    grad = [d_tiles[i * 2 + head] for head in range(2)]
    log = [logs[i * 2 + head : i * 2 + head + 1, :] for head in range(2)]
    delta = [
        jnp.concatenate([deltas[i * 2 + head, 0:1, :], deltas[i * 2 + head, 1:2, :]], axis=1)
        for head in range(2)
    ]
    for lo, diagonal in places:
        at = slice(lo, lo + 256)
        k, v = keys[at, :], vals[at, :]
        dk_tile, dv_tile = dk[at, :], dv[at, :]
        for head in range(2):
            s = lax.dot_general(k, q[head], NT, preferred_element_type=F32)
            p = jnp.exp2(s - log[head])
            if diagonal:
                row = lax.broadcasted_iota(jnp.int32, (256, 256), 0)
                p = jnp.where(row <= lax.broadcasted_iota(jnp.int32, (256, 256), 1), p, 0.0)
            dp = lax.dot_general(v, grad[head], NT, preferred_element_type=F32)
            ds = (p * (dp - delta[head])).astype(BF16)
            dv_tile += jnp.dot(p.astype(BF16), grad[head], preferred_element_type=F32)
            dk_tile += jnp.dot(ds, q[head], preferred_element_type=F32)
            total[head] = total[head] + jnp.dot(keys_t[:, at], ds, preferred_element_type=F32)
        dk[at, :] = dk_tile
        dv[at, :] = dv_tile
    return total


def attend_back_body(
    ready, done, place, q_tiles, keys, vals, logs, d_tiles, deltas,
    dq, dk, dv, d_low, dots, keys_t, dk_acc, dv_acc,
):
    ready(keys)
    keys_t[...] = jnp.transpose(keys[...].astype(F32)).astype(BF16)
    dk_acc[...] = jnp.zeros_like(dk_acc)
    dv_acc[...] = jnp.zeros_like(dv_acc)
    ready(q_tiles, vals, d_tiles)

    def queries(first, i):
        total = back_tiles(
            [(lo, lo == 1024 + i * 256) for lo in range(first, 1280 + i * 256, 256)], i, [0.0, 0.0],
            q_tiles, d_tiles, logs, deltas, keys, vals, keys_t, dk_acc, dv_acc,
        )
        dot = jnp.zeros((1, 256), F32)
        for head in range(2):
            out = jnp.transpose(total[head]) * DH ** (-0.5)
            dot += jnp.sum(
                total[head] * jnp.transpose(q_tiles[i * 2 + head].astype(F32)), axis=0, keepdims=True
            )
            for c in range(2):
                block = lax.rem(i - place[1] + 4, 4) + 4 * jnp.abs(c - place[2])
                at = pl.ds(pl.multiple_of(block * 128, 128), 128)
                dq[at, head * 128 : head * 128 + 128] = out[c * 128 : c * 128 + 128, :].astype(BF16)
        for c in range(2):
            block = lax.rem(i - place[1] + 4, 4) + 4 * jnp.abs(c - place[2])
            dots[pl.ds(block, 1), :] = dot[:, c * 128 : c * 128 + 128] * (1.0 / LOG2E)

    @pl.when(place[0] == 1)
    def _():
        for i in range(4):
            queries(0, i)

    @pl.when(place[0] == 0)
    def _():
        for i in range(4):
            queries(1024, i)

    done(dq)
    for b in range(8):
        rows = slice(b * 128, b * 128 + 128)
        z, c = spot(place, b)
        at = pl.ds(pl.multiple_of(1024 + z * 256 + c * 128, 128), 128)
        key_grad = dk_acc[at, :] * (1.0 / LOG2E)
        dk[rows, :] = key_grad
        dv[rows, :] = dv_acc[at, :]
        dots[8 + b : 9 + b, :] = row_sums(key_grad * keys[at, :].astype(F32))
        key_grad = dk_acc[rows, :] * (1.0 / LOG2E)
        d_low[rows, :128] = key_grad.astype(BF16)
        d_low[rows, 128:] = dv_acc[rows, :].astype(BF16)
        dots[16 + b : 17 + b, :] = row_sums(key_grad * keys[rows, :].astype(F32))


def unproject_body(
    ready, done, place, dq, dk, dv, d_got, q_raw, k_raw, squares, dots, dots_got, cos, sin,
    gain_q, gain_k, x_turned, gains, d_made, sent, sums,
):
    sums[...] = jnp.zeros_like(sums)
    ready(dq, dk, dv, d_got, q_raw, k_raw, cos, sin)

    def step(b, carry):
        rows = pl.ds(pl.multiple_of(b * 128, 128), 128)
        cosine, sine = cos[rows, :], sin[rows, :]
        r = column(root(squares[pl.ds(b, 1), :], 2048.0))
        mean = column(dots[pl.ds(b, 1), :]) * (1.0 / 2048.0)
        for head in range(2):
            lanes = slice(head * 128, head * 128 + 128)
            turn = dq[rows, lanes].astype(F32)
            d_norm = turn * cosine - pltpu.roll(turn, 64, 1) * sine
            hat = q_raw[rows, lanes] * r
            sums[0:1, lanes] += jnp.sum(d_norm * hat, axis=0, keepdims=True)
            d_made[rows, lanes] = (r * (d_norm * gain_q[:, lanes] - hat * mean)).astype(BF16)
        r = column(root(squares[pl.ds(b + 8, 1), :], 1024.0))
        mean = column(dots[pl.ds(b + 8, 1), :] + dots_got[pl.ds(b, 1), :]) * (1.0 / 1024.0)
        turn = dk[rows, :] + d_got[rows, :128].astype(F32)
        d_norm = turn * cosine - pltpu.roll(turn, 64, 1) * sine
        hat = k_raw[rows, :] * r
        sums[0:1, 256:] += jnp.sum(d_norm * hat, axis=0, keepdims=True)
        d_made[rows, 256:384] = (r * (d_norm * gain_k[...] - hat * mean)).astype(BF16)
        d_made[rows, 384:] = (dv[rows, :] + d_got[rows, 128:].astype(F32)).astype(BF16)
        return carry

    lax.fori_loop(0, 8, step, 0)
    done(d_made)
    ready(x_turned, gains)

    def grad(t, carry):
        rows = pl.ds(pl.multiple_of(t * 256, 256), 256)
        sent[rows, :512] = jnp.dot(
            x_turned[rows, :], d_made[...], preferred_element_type=F32
        ).astype(BF16)
        sent[rows, 512:] = gains[rows, :]
        return carry

    lax.fori_loop(0, 4, grad, 0)
    extra = 0.0
    for lo, width, each, first in ((0, 256, 16, 0), (256, 128, 8, 16)):
        row = lax.broadcasted_iota(jnp.int32, (128, width), 0) // 8
        lane = lax.broadcasted_iota(jnp.int32, (128, width), 1) // each
        spread = jnp.where(row == lane, sums[0:1, lo : lo + width], 0.0).astype(BF16)
        lane = lax.broadcasted_iota(jnp.int32, (width, 128), 0) % each + first
        pick = jnp.where(lane == lax.broadcasted_iota(jnp.int32, (width, 128), 1), 1.0, 0.0)
        extra = extra + jnp.dot(spread, pick.astype(BF16), preferred_element_type=F32)
    rows = pl.ds(pl.multiple_of((place[1] * 2 + place[2]) * 128, 128), 128)
    sent[rows, 512:] = (gains[rows, :].astype(F32) + extra).astype(BF16)


def input_body(ready, done, d_made, weight, dx_mine, dx_part):
    ready(d_made, weight)

    def step(t, carry):
        at = pl.ds(pl.multiple_of(t * 256, 256), 256)
        far = pl.ds(pl.multiple_of(512 + t * 256, 256), 256)
        dx_part[at, :] = lax.dot_general(
            d_made[far, :], weight[...], NT, preferred_element_type=F32
        ).astype(BF16)
        dx_mine[at, :] = lax.dot_general(
            d_made[at, :], weight[...], NT, preferred_element_type=F32
        )
        return carry

    lax.fori_loop(0, 2, step, 0)


def expand_body(ready, done, h_all, weight, packed, gate, up, expanded, m_mine, m_part, down):
    ready(packed)
    for f in range(8):
        down[f * 96 : f * 96 + 96, :768] = packed[f * 128 : f * 128 + 96, :]
        for m in range(3):
            down[f * 96 + m * 32 : f * 96 + m * 32 + 32, 768:] = packed[
                f * 128 + 96 : f * 128 + 128, m * 256 : m * 256 + 256
            ]

    done(down)
    ready(h_all, weight)
    done(h_all)

    def widen(n, carry):
        lanes = pl.ds(pl.multiple_of(n * 256, 256), 256)
        upper = pl.ds(pl.multiple_of(768 + n * 256, 256), 256)
        g = jnp.dot(h_all[...], weight[:, lanes], preferred_element_type=F32)
        u = jnp.dot(h_all[...], weight[:, upper], preferred_element_type=F32)
        gate[:, lanes] = g
        up[:, lanes] = u
        expanded[:, lanes] = (g * jax.nn.sigmoid(g) * u).astype(BF16)
        return carry

    lax.fori_loop(0, 3, widen, 0)
    done(gate, up, expanded)

    def narrow(n, carry):
        lanes = pl.ds(pl.multiple_of(n * 256, 256), 256)
        m = jnp.dot(expanded[...], down[:, lanes], preferred_element_type=F32)
        m_mine[:, lanes] = m[:256]
        m_part[:, lanes] = m[256:].astype(BF16)
        return carry

    lax.fori_loop(0, 4, narrow, 0)


def expand_back_body(ready, done, dm_all, gate, up, weight, down, d_gu, dh_mine, dh_part):
    ready(dm_all, gate, up, down)
    done(dm_all)

    def widen(n, carry):
        lanes = pl.ds(pl.multiple_of(n * 256, 256), 256)
        upper = pl.ds(pl.multiple_of(768 + n * 256, 256), 256)
        de = lax.dot_general(dm_all[...], down[lanes, :], NT, preferred_element_type=F32)
        g = gate[:, lanes]
        sig = jax.nn.sigmoid(g)
        d_gu[:, lanes] = (de * up[:, lanes] * sig * (1.0 + g * (1.0 - sig))).astype(BF16)
        d_gu[:, upper] = (de * (g * sig)).astype(BF16)
        return carry

    lax.fori_loop(0, 3, widen, 0)
    done(d_gu)
    ready(weight)

    def narrow(n, carry):
        lanes = pl.ds(pl.multiple_of(n * 256, 256), 256)
        dh = lax.dot_general(d_gu[...], weight[lanes, :], NT, preferred_element_type=F32)
        dh_mine[:, lanes] = dh[:256]
        dh_part[:, lanes] = dh[256:].astype(BF16)
        return carry

    lax.fori_loop(0, 4, narrow, 0)


def expand_grad_body(ready, done, h_turned, d_gu, expanded, dm_all, out, expanded_t):
    ready(expanded)
    expanded_t[...] = jnp.transpose(expanded[...].astype(F32)).astype(BF16)

    ready(h_turned, d_gu, dm_all)

    def widen(n, carry):
        lanes = pl.ds(pl.multiple_of(n * 256, 256), 256)
        out[:, lanes] = jnp.dot(
            h_turned[...], d_gu[:, lanes], preferred_element_type=F32
        ).astype(BF16)
        return carry

    lax.fori_loop(0, 6, widen, 0)
    for n in range(4):
        made = jnp.dot(
            expanded_t[...], dm_all[:, n * 256 : n * 256 + 256], preferred_element_type=F32
        ).astype(BF16)
        for f in range(16):
            if n < 3:
                out[f * 64 : f * 64 + 48, 1536 + n * 256 : 1792 + n * 256] = made[
                    f * 48 : f * 48 + 48
                ]
                continue
            for m in range(3):
                out[f * 64 + 48 : f * 64 + 64, 1536 + m * 256 : 1792 + m * 256] = made[
                    f * 48 + m * 16 : f * 48 + m * 16 + 16
                ]


def norm_scale(values):
    return lax.rsqrt(jnp.mean(values * values, axis=-1, keepdims=True) + EPS)


def norm_back(upstream, normed, scaling):
    return scaling * (upstream - normed * jnp.mean(upstream * normed, axis=-1, keepdims=True))


def rotary_tables(first, z, c):
    half = DH // 2
    k = jnp.arange(4, dtype=jnp.int32)
    starts = jnp.concatenate([((z + k) % 4) * 256 + c * 128, ((z + k) % 4) * 256 + (1 - c) * 128])
    places = (first + starts[:, None] + jnp.arange(128, dtype=jnp.int32)[None, :]).reshape(1024)
    inverse = THETA ** (-(jnp.arange(half, dtype=F32) * (2.0 / DH)))
    angles = places.astype(F32)[:, None] * inverse[None, :]
    cosine, sine = jnp.cos(angles), jnp.sin(angles)
    return (
        jnp.concatenate([cosine, cosine], axis=-1),
        jnp.concatenate([-sine, sine], axis=-1),
    )


def dot(a, b):
    return jnp.dot(a, b, preferred_element_type=F32)


def dot_nt(a, b):
    return lax.dot_general(a, b, NT, preferred_element_type=F32)


def dot_tn(a, b):
    return lax.dot_general(a, b, (((0,), (0,)), ((), ())), preferred_element_type=F32)


def on_device(
    tokens, out_grad, w_query, w_key, w_value, w_out, w_gate, w_up, w_down,
    gain_query, gain_key, gain_attn, gain_mlp,
):
    seq = lax.axis_index("seq")
    xh, zc = seq // 8, seq % 8
    z, c = zc // 2, zc % 2
    quarter = (z % 2) * 2 + c
    place = jnp.stack([xh, z, c]).astype(jnp.int32)
    inputs = tokens[0]

    def columns(weight, width):
        return lax.dynamic_slice_in_dim(weight, zc * width, width, 1)

    def spread(block):
        return lax.all_to_all(
            jnp.broadcast_to(block[None], (8,) + block.shape),
            "fsdp", split_axis=0, concat_axis=0, tiled=True,
        ).reshape(8 * block.shape[0], block.shape[1])

    x_blocks = gather_group(inputs)
    weight = spread(
        jnp.concatenate(
            [columns(w_query, 256), columns(w_key, 128), columns(w_value, 128)], axis=1
        )
    )
    w_out_rows = lax.ppermute(
        after(lax.dynamic_slice_in_dim(w_out, zc * 32, 32, 0), weight),
        ("seq", "fsdp"),
        TURN,
    )

    def quarters(weight):
        part = lax.dynamic_slice_in_dim(weight.reshape(128, 8, 384), quarter * 96, 96, 2)
        return part.reshape(128, 768)

    down = lax.dynamic_slice_in_dim(w_down, quarter * 96, 96, 0)
    packed = jnp.concatenate(
        [
            down[:, :768],
            jnp.concatenate([down[m * 32 : m * 32 + 32, 768:] for m in range(3)], axis=1),
        ],
        axis=0,
    )
    w_narrow = lax.all_gather(packed, "fsdp", axis=0, tiled=True)
    w_wide = jnp.concatenate([quarters(w_gate), quarters(w_up)], axis=1)
    weight, w_wide = lax.optimization_barrier((weight, w_wide))

    cosine, sine = rotary_tables(xh * 1024, z, c)
    gain_q = lax.dynamic_slice_in_dim(gain_query, zc * 256, 256, 0)[None]
    gain_k = lax.dynamic_slice_in_dim(gain_key, zc * 128, 128, 0)[None]
    x_all, q_raw, k_raw, q_rot, kv_rot, squares = kernel_call(
        project_body,
        [
            *in_hbm(
                0, shaped((1024, 256), F32), shaped((1024, 128), F32),
                shaped((1024, 256), BF16), shaped((1024, 256), BF16),
            ),
            shaped((16, 128), F32),
        ],
        [x_blocks, weight, gain_q, gain_k, cosine, sine],
        flops=2 * 1024 * 1024 * 512, nbytes=9 << 20,
    )

    kv_low = swap(kv_rot, LOW_TO_HIGH)
    squares = sum_group(squares)
    squares_low = swap(squares[8:], LOW_TO_HIGH)
    kv_low, squares, squares_low, w_wide, w_narrow, w_out_rows = lax.optimization_barrier(
        (kv_low, squares, squares_low, w_wide, w_narrow, w_out_rows)
    )
    w_wide = lax.all_gather(w_wide, "fsdp", axis=0, tiled=True)
    w_out_rows = spread(w_out_rows)
    out_raw, mixed, mixed_turned, q_tiles, keys, vals, logs = kernel_call(
        attend_body,
        [
            *in_hbm(
                shaped((1024, 256), F32), shaped((1024, 256), BF16), shaped((256, 1024), BF16),
                shaped((8, 256, 128), BF16), shaped((2048, 128), BF16), shaped((2048, 128), BF16),
            ),
            shaped((8, 256), F32),
        ],
        [place, *in_hbm(q_rot, kv_rot), kv_low, squares, squares_low],
        [pltpu.VMEM((128, 2048), BF16)],
        flops=4 * 1024 * 2048 * 256, nbytes=9 << 20,
    )
    a_mine, a_part = kernel_call(
        output_body,
        [shaped((512, 1024), F32), shaped((512, 1024), BF16)],
        [*in_hbm(mixed), w_out_rows],
        flops=2 * 1024 * 1024 * 256, nbytes=5 << 20,
    )
    x_turned = x_all.T

    attended = scatter_group(a_mine, a_part)
    attended, x_turned = lax.optimization_barrier((attended, x_turned))
    attn_scale = norm_scale(attended)
    attn_hat = attended * attn_scale
    hidden_state = inputs.astype(F32) + attn_hat * gain_attn
    h_all, gate, up, expanded, m_mine, m_part, w_down_rows = kernel_call(
        expand_body,
        [
            0, shaped((512, 768), F32), shaped((512, 768), F32), shaped((512, 768), BF16),
            shaped((256, 1024), F32), shaped((256, 1024), BF16), shaped((768, 1024), BF16),
        ],
        [
            gather_pair(hidden_state.astype(BF16)), *in_hbm(w_wide, w_narrow),
        ],
        flops=2 * 512 * 2304 * 1024, nbytes=12 << 20,
    )
    projected, _ = scatter_pair(m_mine, m_part)
    mlp_scale = norm_scale(projected)
    mlp_hat = projected * mlp_scale
    output = (hidden_state + mlp_hat * gain_mlp).astype(BF16)[None]

    upstream = out_grad[0].astype(F32)
    grad_gain_mlp = jnp.sum(upstream * mlp_hat, axis=0)
    d_projected = norm_back(upstream * gain_mlp, mlp_hat, mlp_scale).astype(BF16)
    n = jnp.arange(1024, dtype=jnp.int32)
    source = ((n // 8) % 16) * 64 + (n // 128) * 8 + n % 8
    order = (n[None, :] == source[:, None]).astype(BF16)
    h_turned = dot_nt(order, h_all).astype(BF16)
    d_blocks = gather_pair(d_projected)
    d_blocks[3], h_turned = lax.optimization_barrier((d_blocks[3], h_turned))
    dm_all, d_gu, dh_mine, dh_part = kernel_call(
        expand_back_body,
        [
            0, shaped((512, 1536), BF16), shaped((256, 1024), F32), shaped((256, 1024), BF16),
        ],
        [d_blocks, gate, up, w_wide, w_down_rows],
        flops=2 * 512 * 2304 * 1024, nbytes=12 << 20,
    )

    far = dh_mine[128:] + swap(dh_part[128:], CORE_SWAP).astype(F32)
    far, d_gu, dm_all = lax.optimization_barrier((far.astype(BF16), d_gu, dm_all))
    far = swap(far, Z_SWAP)
    (grad_mlp,) = kernel_call(
        expand_grad_body,
        in_hbm(shaped((1024, 2304), BF16)),
        [h_turned, d_gu, expanded, dm_all],
        [pltpu.VMEM((768, 512), BF16)],
        flops=2 * 512 * 2304 * 1024, nbytes=9 << 20,
    )
    far, grad_mlp = lax.optimization_barrier((far, grad_mlp))
    grad_mlp = lax.psum_scatter(grad_mlp, "fsdp", scatter_dimension=0, tiled=True)
    d_hidden = upstream + dh_mine[:128] + swap(dh_part[:128], CORE_SWAP).astype(F32)
    d_hidden = d_hidden + far.astype(F32)

    grad_gain_attn = jnp.sum(d_hidden * attn_hat, axis=0)
    d_attended = norm_back(d_hidden * gain_attn, attn_hat, attn_scale).astype(BF16)
    d_tiles, deltas, grad_out = kernel_call(
        output_back_body,
        [shaped((8, 256, 128), BF16), shaped((8, 2, 128), F32), shaped((256, 1024), BF16)],
        [place, *in_hbm(out_raw, w_out_rows, gather_group(d_attended), mixed_turned)],
        flops=4 * 1024 * 1024 * 256, nbytes=6 << 20,
    )
    fsdp = lax.axis_index("fsdp")

    def halve(value, rows, bit, axis, pairs):
        parts = value.reshape(-1, 2, rows, 1024)
        given = jnp.where(bit == 1, parts[:, 0], parts[:, 1])
        mine = jnp.where(bit == 1, parts[:, 1], parts[:, 0]).astype(F32)
        return (mine + lax.ppermute(given, axis, pairs).astype(F32)).astype(BF16)

    grad_out = halve(grad_out, 32, fsdp % 2, "fsdp", [(i, i ^ 1) for i in range(8)])
    dq, dk, dv, d_low, dots = kernel_call(
        attend_back_body,
        [
            *in_hbm(
                shaped((1024, 256), BF16), shaped((1024, 128), F32), shaped((1024, 128), F32),
                shaped((1024, 256), BF16),
            ),
            shaped((24, 128), F32),
        ],
        [place, *in_hbm(q_tiles, keys, vals), logs, d_tiles, deltas],
        [
            pltpu.VMEM((128, 2048), BF16), pltpu.VMEM((2048, 128), F32),
            pltpu.VMEM((2048, 128), F32),
        ],
        flops=10 * 1024 * 2048 * 256, nbytes=8 << 20,
    )
    dots, grad_out = lax.optimization_barrier((dots, grad_out))
    grad_out = halve(grad_out, 32, fsdp // 2 % 2, "fsdp", [(i, i ^ 2) for i in range(8)])
    grad_out = halve(grad_out, 32, fsdp // 4, "fsdp", [(i, i ^ 4) for i in range(8)])
    d_got = swap(d_low, HIGH_TO_LOW)
    dots = sum_group(dots)
    dots_got = swap(dots[16:], HIGH_TO_LOW)

    gains = jnp.concatenate([grad_gain_attn.reshape(128, 8), grad_gain_mlp.reshape(128, 8)], axis=1)
    gains = jnp.broadcast_to(
        jnp.pad(gains.astype(BF16), ((0, 0), (24, 88)))[:, None, :], (128, 8, 128)
    ).reshape(1024, 128)
    d_made, sent = kernel_call(
        unproject_body,
        [*in_hbm(shaped((1024, 512), BF16)), shaped((1024, 640), BF16)],
        [
            place, *in_hbm(dq, dk, dv), d_got, *in_hbm(q_raw, k_raw), squares, dots, dots_got, cosine, sine,
            gain_q, gain_k, *in_hbm(x_turned), gains,
        ],
        [pltpu.VMEM((8, 384), F32)],
        flops=2 * 1024 * 1024 * 512, nbytes=9 << 20,
    )

    def halves(value, upper):
        low, high = value[: value.shape[0] // 2], value[value.shape[0] // 2 :]
        return jnp.where(upper, high, low), jnp.where(upper, low, high)

    mine, given = halves(grad_mlp, xh == 1)
    mine = mine.astype(F32) + swap(given, X_SWAP).astype(F32)
    got_wide = lax.all_to_all(
        grad_mlp[:, :1536].reshape(16, 8, 1536), "seq", split_axis=0, concat_axis=0, tiled=True
    )
    sent, got_wide, grad_mlp, grad_out = lax.optimization_barrier(
        (sent, got_wide, grad_mlp, grad_out)
    )
    grad_down = jnp.concatenate(
        [
            piece
            for h in (0, 64)
            for piece in [
                jnp.concatenate(
                    [
                        grad_mlp[h : h + 48, 1536:],
                        jnp.concatenate(
                            [
                                grad_mlp[h + 48 : h + 64, 1536 + m * 256 : 1792 + m * 256]
                                for m in range(3)
                            ],
                            axis=0,
                        ),
                    ],
                    axis=1,
                )
            ]
        ],
        axis=0,
    ).reshape(4, 24, 1024)
    grad_down = sum(
        lax.ppermute(
            lax.dynamic_index_in_dim(grad_down, (xh * 2 + z // 2) ^ other, 0, keepdims=False),
            ("seq", "fsdp"),
            down_home(other),
        ).astype(F32)
        for other in range(4)
    )
    got_made = lax.all_to_all(
        sent.reshape(128, 8, 640), ("seq", "fsdp"), split_axis=0, concat_axis=0, tiled=True
    )
    dx_mine, dx_part = kernel_call(
        input_body,
        in_hbm(shaped((512, 1024), F32), shaped((512, 1024), BF16)),
        [*in_hbm(after(d_made, sent)), weight],
        flops=2 * 1024 * 1024 * 512, nbytes=5 << 20,
    )
    rows = [slice(k * 128, k * 128 + 128) for k in range(4)]
    pieces = [dx_mine[r] + swap(dx_part[r], CORE_SWAP).astype(F32) for r in rows]
    far = [piece.astype(BF16) for piece in pieces[1:]]
    got_made, grad_down, grad_out, far = lax.optimization_barrier(
        (got_made, grad_down, grad_out, far)
    )
    grad_out = grad_out.reshape(2, 16, 1024)
    grad_out = sum(
        swap(jnp.where((xh == 1) != other, grad_out[1], grad_out[0]), out_home(other)).astype(F32)
        for other in (False, True)
    )
    d_inputs = pieces[0] + sum(
        swap(piece, to_z(k)).astype(F32) for k, piece in enumerate(far, 1)
    )
    summed = jnp.sum(got_made.reshape(2, 8, 8, 8, 640).astype(F32), axis=(0, 2))
    gains = jnp.sum(summed[:, 0, 512:], axis=0)

    def take(first, width):
        return summed[:, :, first : first + width].swapaxes(0, 1).reshape(8, 8 * width)

    wide = jnp.sum(got_wide.reshape(2, 2, 4, 8, 2, 8, 96).astype(F32), axis=(0, 1))
    wide = wide.transpose(2, 1, 3, 0, 4).reshape(2, 8, 3072)
    return (
        output,
        (d_hidden + d_inputs).astype(BF16)[None],
        take(0, 256),
        take(256, 128),
        take(384, 128),
        grad_out.astype(F32),
        wide[0],
        wide[1],
        grad_down.astype(F32),
        gains[:16],
        gains[16:24],
        gains[24:32],
        gains[32:40],
    )


def solution(mesh):
    rows = P("fsdp", "seq", None)
    weight = P("fsdp", None)
    grad = P(("seq", "fsdp"), None)
    gain = P(("seq", "fsdp"))
    return jax.shard_map(
        on_device,
        mesh=mesh,
        in_specs=(rows,) * 2 + (weight,) * 7 + (P(),) * 4,
        out_specs=(rows,) * 2 + (grad,) * 7 + (gain,) * 4,
        check_vma=False,
    )
```

```python
import functools
import math

import jax
import jax.numpy as jnp
from jax import lax
from jax.experimental import pallas as pl
from jax.experimental.pallas import tpu as pltpu
from jax.sharding import PartitionSpec as P

BF16 = jnp.bfloat16
F32 = jnp.float32
DH = 128
EPS = 1e-06
THETA = 1000000.0
MASKED = -1e30
LOG2E = math.log2(math.e)
QUERY_SCALE = DH ** (-0.5) * LOG2E
VMEM_BYTES = 20 * 1024 * 1024
VMEM = pl.BlockSpec(memory_space=pltpu.VMEM)
SMEM = pl.BlockSpec(memory_space=pltpu.SMEM)
ANY = pl.BlockSpec(memory_space=pl.ANY)
SMALL = 64 * 1024
NT = (((1,), (1,)), ((), ()))

SEQ_PLACES = [(xh, z, c) for xh in range(2) for z in range(4) for c in range(2)]


def seq_index(xh, z, c):
    return xh * 8 + (z % 4) * 2 + c


CORE_SWAP = [(i, i ^ 1) for i in range(16)]
LOW_TO_HIGH = [(i, i + 8) for i in range(8)]
HIGH_TO_LOW = [(i + 8, i) for i in range(8)]
X_SWAP = [(i, i ^ 8) for i in range(16)]


def from_z(k):
    return [(seq_index(xh, z + k, c), seq_index(xh, z, c)) for xh, z, c in SEQ_PLACES]


def to_z(k):
    return [(seq_index(xh, z, c), seq_index(xh, z + k, c)) for xh, z, c in SEQ_PLACES]


def across(pairs):
    return [(seq * 8 + f, to_seq * 8 + to_f) for seq, f, to_seq, to_f in pairs]


TURN = across(
    (xh * 8 + a, f, xh * 8 + f, a) for xh in range(2) for a in range(8) for f in range(8)
)
Z_SWAP = [(i, i ^ 2) for i in range(16)]
FAR_SWAP = [(i, i ^ 4) for i in range(16)]


def out_home(other):
    return [(xh * 8 + a, 2 * a + (xh ^ other)) for xh in range(2) for a in range(8)]


def down_home(other):
    return across(
        (seq_index(own // 2, 2 * (own % 2) + zl, c), f, 2 * f + zl, 4 * c + (own ^ other))
        for own in range(4) for zl in range(2) for c in range(2) for f in range(8)
    )


def swap(value, pairs):
    return lax.ppermute(value, "seq", pairs)


def after(value, *others):
    return lax.optimization_barrier((value, *others))[0]


def gather_group(block):
    far = {k: swap(block, from_z(k)) for k in (2, 1, 3)}
    mine = [block, far[1], far[2], far[3]]
    return mine + [swap(v, CORE_SWAP) for v in mine]


def scatter_group(mine, part):
    rows = [slice(k * 128, k * 128 + 128) for k in range(4)]
    out = None
    for k in (2, 1, 3, 0):
        piece = mine[rows[k]] + swap(part[rows[k]], CORE_SWAP).astype(F32)
        if k:
            piece = swap(piece.astype(BF16), to_z(k)).astype(F32)
        out = piece if out is None else out + piece
    return out


def gather_pair(block):
    mine = [block, swap(block, Z_SWAP)]
    return mine + [swap(v, CORE_SWAP) for v in mine]


def scatter_pair(mine, part, later=()):
    far = mine[128:] + swap(part[128:], CORE_SWAP).astype(F32)
    far, *later = lax.optimization_barrier((far.astype(BF16), *later))
    far = swap(far, Z_SWAP).astype(F32)
    return mine[:128] + swap(part[:128], CORE_SWAP).astype(F32) + far, later


def sum_group(rows):
    groups = rows.shape[0] // 8
    other = swap(rows, CORE_SWAP).reshape(groups, 2, 4, 128)
    pair = rows.reshape(groups, 2, 4, 128) + jnp.concatenate([other[:, 1:], other[:, :1]], axis=1)
    odd = lax.axis_index("seq") // 2 % 2 == 1
    got = swap(pair, Z_SWAP)
    up = jnp.concatenate([got[:, :, 3:], got[:, :, :3]], axis=2)
    down = jnp.concatenate([got[:, :, 1:], got[:, :, :1]], axis=2)
    pair = pair + jnp.where(odd, down, up)
    got = swap(pair, FAR_SWAP)
    pair = pair + jnp.concatenate([got[:, :, 2:], got[:, :, :2]], axis=2)
    return pair.reshape(rows.shape)


def column(row):
    return jnp.transpose(jnp.broadcast_to(row, (128, 128)))


def row_sums(values):
    return jnp.sum(jnp.transpose(values), axis=0, keepdims=True)


def shaped(shape, dtype):
    return jax.ShapeDtypeStruct(shape, dtype)


class Kept:
    def __init__(self, value):
        self.value = value


def in_hbm(*values):
    return [Kept(v) for v in values]


def kernel_call(body, outs, inputs, scratch=(), flops=0, nbytes=0):
    hbm_outs = [isinstance(o, Kept) for o in outs]
    hbm_ins = [isinstance(x, Kept) for x in inputs]
    outs = [o.value if isinstance(o, Kept) else o for o in outs]
    inputs = [x.value if isinstance(x, Kept) else x for x in inputs]
    groups = [x if isinstance(x, list) else [x] for x in inputs]
    flat = [a for group in groups for a in group]
    joined = [
        shaped((sum(a.shape[0] for a in group),) + group[0].shape[1:], group[0].dtype)
        for group in groups
    ]

    def large(s):
        return math.prod(s.shape) * s.dtype.itemsize >= SMALL

    def where(s):
        return ANY if large(s) else SMEM if s.dtype == jnp.int32 else VMEM

    out_shapes = [joined[o] if isinstance(o, int) else o for o in outs]
    in_buffers = [pltpu.VMEM(s.shape, s.dtype) for s in joined if large(s)]
    out_buffers = [
        pltpu.VMEM(o.shape, o.dtype) for o in outs if not isinstance(o, int) and large(o)
    ]

    def whole(*refs):
        refs = list(refs)

        def pull(count):
            taken = refs[:count]
            del refs[:count]
            return taken

        in_refs, out_refs = pull(len(flat)), pull(len(outs))
        in_space, out_space = pull(len(in_buffers)), pull(len(out_buffers))
        own, (in_sem, out_sem) = pull(len(scratch)), refs
        loads, ins, at = {}, [], 0
        for group, s in zip(groups, joined):
            if not large(s):
                ins.append(in_refs[at])
                at += 1
                continue
            space, row = in_space.pop(0), 0
            loads[id(space)] = []
            for a in group:
                copy = pltpu.make_async_copy(
                    in_refs[at], space.at[pl.ds(row, a.shape[0])], in_sem.at[at]
                )
                copy.start()
                loads[id(space)].append(copy)
                row, at = row + a.shape[0], at + 1
            ins.append(space)
        made, stores = [], {}
        for k, (o, s, ref) in enumerate(zip(outs, out_shapes, out_refs)):
            if not large(s):
                made.append(ref)
                continue
            space = ins[o] if isinstance(o, int) else out_space.pop(0)
            stores[id(space)] = pltpu.make_async_copy(space, ref, out_sem.at[k])
            if not isinstance(o, int):
                made.append(space)
        started = []

        def ready(*spaces):
            for space in spaces:
                for copy in loads.pop(id(space), ()):
                    copy.wait()

        def done(*spaces):
            for space in spaces:
                copy = stores.pop(id(space))
                copy.start()
                started.append(copy)

        body(ready, done, *ins, *made, *own)
        for key in list(stores):
            copy = stores.pop(key)
            copy.start()
            started.append(copy)
        for copy in started:
            copy.wait()

    shapes = [pltpu.HBM(s.shape, s.dtype) if hbm else s for s, hbm in zip(out_shapes, hbm_outs)]
    return pl.pallas_call(
        whole,
        out_shape=tuple(shapes),
        in_specs=[where(s) for group, s in zip(groups, joined) for _ in group],
        out_specs=tuple(where(s) for s in out_shapes),
        scratch_shapes=[
            *in_buffers, *out_buffers, *scratch,
            pltpu.SemaphoreType.DMA((len(flat),)), pltpu.SemaphoreType.DMA((len(outs),)),
        ],
        compiler_params=pltpu.CompilerParams(vmem_limit_bytes=VMEM_BYTES),
        cost_estimate=pl.CostEstimate(flops=flops, bytes_accessed=nbytes, transcendentals=0),
    )(
        *[
            pltpu.with_memory_space_constraint(a, pltpu.HBM) if hbm else a
            for group, hbm in zip(groups, hbm_ins)
            for a in group
        ],
    )


def root(total, width):
    return lax.rsqrt(total * (1.0 / width) + EPS)


def project_body(
    ready, done, x_all, weight, gain_q, gain_k, cos, sin,
    q_raw, k_raw, q_rot, kv_rot, squares,
):
    ready(x_all, weight, cos, sin)
    done(x_all)

    def step(t, carry):
        at = pl.multiple_of(t * 256, 256)
        made = jnp.dot(x_all[pl.ds(at, 256), :], weight[...], preferred_element_type=F32)
        for part in range(2):
            rows = pl.ds(at + part * 128, 128)
            block = t * 2 + part
            here = made[part * 128 : part * 128 + 128]
            q, k = here[:, :256], here[:, 256:384]
            kv_rot[rows, 128:] = here[:, 384:].astype(BF16)
            q_raw[rows, :] = q
            k_raw[rows, :] = k
            squares[pl.ds(block, 1), :] = row_sums(
                q[:, :128] * q[:, :128] + q[:, 128:] * q[:, 128:]
            )
            squares[pl.ds(block + 8, 1), :] = row_sums(k * k)
            cosine, sine = cos[rows, :], sin[rows, :]
            for head in range(2):
                lanes = slice(head * 128, head * 128 + 128)
                turn = q[:, lanes] * gain_q[:, lanes]
                q_rot[rows, lanes] = (turn * cosine + pltpu.roll(turn, 64, 1) * sine).astype(BF16)
            turn = k * gain_k[...]
            kv_rot[rows, :128] = (turn * cosine + pltpu.roll(turn, 64, 1) * sine).astype(BF16)
        return carry

    lax.fori_loop(0, 4, step, 0)


def spot(place, block):
    z = lax.rem(place[1] + block % 4, 4)
    c = place[2] if block < 4 else 1 - place[2]
    return z, c


def diagonal():
    query = lax.broadcasted_iota(jnp.int32, (256, 512), 1) % 256
    return lax.broadcasted_iota(jnp.int32, (256, 512), 0) <= query


def attend_body(
    ready, done, place, q_rot, kv_rot, kv_low, squares, squares_low,
    out_raw, out_low, out_turned, q_tiles, keys, vals, logs, vals_t,
):
    ready(q_rot, kv_rot, kv_low)
    for b in range(8):
        rows = slice(b * 128, b * 128 + 128)
        z, c = spot(place, b)
        r = column(root(squares[b : b + 1, :], 2048.0)) * QUERY_SCALE
        inner = pl.ds(pl.multiple_of(c * 128, 128), 128)
        for head in range(2):
            q = q_rot[rows, head * 128 : head * 128 + 128].astype(F32)
            q_tiles[z * 2 + head, inner, :] = (q * r).astype(BF16)
        at = pl.ds(pl.multiple_of(1024 + z * 256 + c * 128, 128), 128)
        r = column(root(squares[8 + b : 9 + b, :], 1024.0))
        keys[at, :] = (kv_rot[rows, :128].astype(F32) * r).astype(BF16)
        vals[at, :] = kv_rot[rows, 128:]
        r = column(root(squares_low[b : b + 1, :], 1024.0))
        keys[rows, :] = (kv_low[rows, :128].astype(F32) * r).astype(BF16)
        vals[rows, :] = kv_low[rows, 128:]
    done(q_tiles, keys, vals)
    vals_t[...] = jnp.transpose(vals[...].astype(F32)).astype(BF16)

    def queries(first, i):
        at_diagonal = 1024 + i * 256
        q = q_tiles[i * 2 : i * 2 + 2].reshape(512, 128)
        ranges = [(lo, lo + 256) for lo in range(first, at_diagonal + 256, 256)]
        scores = [
            lax.dot_general(keys[lo:hi, :], q, NT, preferred_element_type=F32) for lo, hi in ranges
        ]
        scores[-1] = jnp.where(diagonal(), scores[-1], MASKED)
        top = functools.reduce(jnp.maximum, [jnp.max(s, axis=0, keepdims=True) for s in scores])
        total, acc = 0.0, 0.0
        for s, (lo, hi) in zip(scores, ranges):
            p = jnp.exp2(s - top)
            total = total + jnp.sum(p, axis=0, keepdims=True)
            acc = acc + jnp.dot(vals_t[:, lo:hi], p.astype(BF16), preferred_element_type=F32)
        acc = acc / total
        log = top + jnp.log2(total)
        for head in range(2):
            turned = acc[:, head * 256 : head * 256 + 256]
            out = jnp.transpose(turned)
            turned = turned.astype(BF16)
            logs[i * 2 + head : i * 2 + head + 1, :] = log[:, head * 256 : head * 256 + 256]
            for c in range(2):
                block = lax.rem(i - place[1] + 4, 4) + 4 * jnp.abs(c - place[2])
                at = pl.ds(pl.multiple_of(block * 128, 128), 128)
                lanes = slice(head * 128, head * 128 + 128)
                out_raw[at, lanes] = out[c * 128 : c * 128 + 128, :]
                out_low[at, lanes] = out[c * 128 : c * 128 + 128, :].astype(BF16)
                out_turned[lanes, at] = turned[:, c * 128 : c * 128 + 128]

    @pl.when(place[0] == 1)
    def _():
        for i in range(4):
            queries(0, i)

    @pl.when(place[0] == 0)
    def _():
        for i in range(4):
            queries(1024, i)

    done(out_raw, out_low, out_turned)


def output_body(ready, done, mixed, w_out, a_mine, a_part):
    ready(mixed, w_out)

    def project(t, carry):
        at = pl.ds(pl.multiple_of(t * 256, 256), 256)
        far = pl.ds(pl.multiple_of(512 + t * 256, 256), 256)
        a_part[at, :] = jnp.dot(mixed[far, :], w_out[...], preferred_element_type=F32).astype(BF16)
        a_mine[at, :] = jnp.dot(mixed[at, :], w_out[...], preferred_element_type=F32)
        return carry

    lax.fori_loop(0, 2, project, 0)


def output_back_body(
    ready, done, place, out_raw, w_out, da_all, mixed_turned, d_tiles, deltas, grad_out
):
    ready(out_raw, w_out, da_all)
    for b in range(8):
        rows = slice(b * 128, b * 128 + 128)
        z, c = spot(place, b)
        inner = pl.ds(pl.multiple_of(c * 128, 128), 128)
        d_out = lax.dot_general(
            da_all[rows, :], w_out[...], NT, preferred_element_type=F32
        ).astype(BF16)
        for head in range(2):
            lanes = slice(head * 128, head * 128 + 128)
            grad = d_out[:, lanes]
            d_tiles[z * 2 + head, inner, :] = grad
            deltas[z * 2 + head, pl.ds(c, 1), :] = row_sums(grad.astype(F32) * out_raw[rows, lanes])
    done(d_tiles)
    ready(mixed_turned)
    for m in range(4):
        lanes = slice(m * 256, m * 256 + 256)
        made = jnp.dot(mixed_turned[...], da_all[:, lanes], preferred_element_type=F32).astype(BF16)
        for j in range(2):
            for f in range(8):
                to, at = f * 32 + j * 16, j * 128 + f * 16
                grad_out[to : to + 16, lanes] = made[at : at + 16]


def attend_back_body(
    ready, done, place, q_tiles, keys, vals, logs, d_tiles, deltas,
    dq, dk, dv, d_low, dots, keys_t, dk_acc, dv_acc,
):
    ready(keys)
    keys_t[...] = jnp.transpose(keys[...].astype(F32)).astype(BF16)
    dk_acc[...] = jnp.zeros_like(dk_acc)
    dv_acc[...] = jnp.zeros_like(dv_acc)
    ready(q_tiles, vals, d_tiles)

    def queries(first, i):
        at_diagonal = 1024 + i * 256
        q = q_tiles[i * 2 : i * 2 + 2].reshape(512, 128)
        grad = d_tiles[i * 2 : i * 2 + 2].reshape(512, 128)
        log = jnp.concatenate([logs[i * 2 : i * 2 + 1, :], logs[i * 2 + 1 : i * 2 + 2, :]], axis=1)
        delta = jnp.concatenate(
            [deltas[i * 2 + head, c : c + 1, :] for head in range(2) for c in range(2)], axis=1
        )
        total = 0.0
        for lo in range(first, at_diagonal + 256, 256):
            at = slice(lo, lo + 256)
            k, v = keys[at, :], vals[at, :]
            s = lax.dot_general(k, q, NT, preferred_element_type=F32)
            p = jnp.exp2(s - log)
            if lo == at_diagonal:
                p = jnp.where(diagonal(), p, 0.0)
            dp = lax.dot_general(v, grad, NT, preferred_element_type=F32)
            ds = (p * (dp - delta)).astype(BF16)
            dv_acc[at, :] += jnp.dot(p.astype(BF16), grad, preferred_element_type=F32)
            dk_acc[at, :] += jnp.dot(ds, q, preferred_element_type=F32)
            total = total + jnp.dot(keys_t[:, at], ds, preferred_element_type=F32)
        dot = total * jnp.transpose(q.astype(F32))
        dot = jnp.sum(dot[:, :256] + dot[:, 256:], axis=0, keepdims=True)
        for head in range(2):
            out = jnp.transpose(total[:, head * 256 : head * 256 + 256]) * DH ** (-0.5)
            for c in range(2):
                block = lax.rem(i - place[1] + 4, 4) + 4 * jnp.abs(c - place[2])
                at = pl.ds(pl.multiple_of(block * 128, 128), 128)
                dq[at, head * 128 : head * 128 + 128] = out[c * 128 : c * 128 + 128, :].astype(BF16)
        for c in range(2):
            block = lax.rem(i - place[1] + 4, 4) + 4 * jnp.abs(c - place[2])
            dots[pl.ds(block, 1), :] = dot[:, c * 128 : c * 128 + 128] * (1.0 / LOG2E)

    @pl.when(place[0] == 1)
    def _():
        for i in range(4):
            queries(0, i)

    @pl.when(place[0] == 0)
    def _():
        for i in range(4):
            queries(1024, i)

    done(dq)
    for b in range(8):
        rows = slice(b * 128, b * 128 + 128)
        z, c = spot(place, b)
        at = pl.ds(pl.multiple_of(1024 + z * 256 + c * 128, 128), 128)
        key_grad = dk_acc[at, :] * (1.0 / LOG2E)
        dk[rows, :] = key_grad
        dv[rows, :] = dv_acc[at, :]
        dots[8 + b : 9 + b, :] = row_sums(key_grad * keys[at, :].astype(F32))
        key_grad = dk_acc[rows, :] * (1.0 / LOG2E)
        d_low[rows, :128] = key_grad.astype(BF16)
        d_low[rows, 128:] = dv_acc[rows, :].astype(BF16)
        dots[16 + b : 17 + b, :] = row_sums(key_grad * keys[rows, :].astype(F32))


def unproject_body(
    ready, done, place, dq, dk, dv, d_got, q_raw, k_raw, squares, dots, dots_got, cos, sin,
    gain_q, gain_k, x_turned, gains, d_made, sent, sums,
):
    sums[...] = jnp.zeros_like(sums)
    ready(dq, dk, dv, d_got, q_raw, k_raw, cos, sin)

    def step(b, carry):
        rows = pl.ds(pl.multiple_of(b * 128, 128), 128)
        cosine, sine = cos[rows, :], sin[rows, :]
        r = column(root(squares[pl.ds(b, 1), :], 2048.0))
        mean = column(dots[pl.ds(b, 1), :]) * (1.0 / 2048.0)
        for head in range(2):
            lanes = slice(head * 128, head * 128 + 128)
            turn = dq[rows, lanes].astype(F32)
            d_norm = turn * cosine - pltpu.roll(turn, 64, 1) * sine
            hat = q_raw[rows, lanes] * r
            sums[0:1, lanes] += jnp.sum(d_norm * hat, axis=0, keepdims=True)
            d_made[rows, lanes] = (r * (d_norm * gain_q[:, lanes] - hat * mean)).astype(BF16)
        r = column(root(squares[pl.ds(b + 8, 1), :], 1024.0))
        mean = column(dots[pl.ds(b + 8, 1), :] + dots_got[pl.ds(b, 1), :]) * (1.0 / 1024.0)
        turn = dk[rows, :] + d_got[rows, :128].astype(F32)
        d_norm = turn * cosine - pltpu.roll(turn, 64, 1) * sine
        hat = k_raw[rows, :] * r
        sums[0:1, 256:] += jnp.sum(d_norm * hat, axis=0, keepdims=True)
        d_made[rows, 256:384] = (r * (d_norm * gain_k[...] - hat * mean)).astype(BF16)
        d_made[rows, 384:] = (dv[rows, :] + d_got[rows, 128:].astype(F32)).astype(BF16)
        return carry

    lax.fori_loop(0, 8, step, 0)
    done(d_made)
    ready(x_turned, gains)

    def grad(t, carry):
        rows = pl.ds(pl.multiple_of(t * 256, 256), 256)
        sent[rows, :512] = jnp.dot(
            x_turned[rows, :], d_made[...], preferred_element_type=F32
        ).astype(BF16)
        sent[rows, 512:] = gains[rows, :]
        return carry

    lax.fori_loop(0, 4, grad, 0)
    extra = 0.0
    for lo, width, each, first in ((0, 256, 16, 0), (256, 128, 8, 16)):
        row = lax.broadcasted_iota(jnp.int32, (128, width), 0) // 8
        lane = lax.broadcasted_iota(jnp.int32, (128, width), 1) // each
        spread = jnp.where(row == lane, sums[0:1, lo : lo + width], 0.0).astype(BF16)
        lane = lax.broadcasted_iota(jnp.int32, (width, 128), 0) % each + first
        pick = jnp.where(lane == lax.broadcasted_iota(jnp.int32, (width, 128), 1), 1.0, 0.0)
        extra = extra + jnp.dot(spread, pick.astype(BF16), preferred_element_type=F32)
    rows = pl.ds(pl.multiple_of((place[1] * 2 + place[2]) * 128, 128), 128)
    sent[rows, 512:] = (gains[rows, :].astype(F32) + extra).astype(BF16)


def input_body(ready, done, d_made, weight, dx_mine, dx_part):
    ready(d_made, weight)

    def step(t, carry):
        at = pl.ds(pl.multiple_of(t * 256, 256), 256)
        far = pl.ds(pl.multiple_of(512 + t * 256, 256), 256)
        dx_part[at, :] = lax.dot_general(
            d_made[far, :], weight[...], NT, preferred_element_type=F32
        ).astype(BF16)
        dx_mine[at, :] = lax.dot_general(
            d_made[at, :], weight[...], NT, preferred_element_type=F32
        )
        return carry

    lax.fori_loop(0, 2, step, 0)


def expand_body(ready, done, h_all, weight, packed, gate, up, expanded, m_mine, m_part, down):
    ready(h_all, weight)
    done(h_all)
    def widen(n, carry):
        lanes = pl.ds(pl.multiple_of(n * 256, 256), 256)
        upper = pl.ds(pl.multiple_of(768 + n * 256, 256), 256)
        g = jnp.dot(h_all[...], weight[:, lanes], preferred_element_type=F32)
        u = jnp.dot(h_all[...], weight[:, upper], preferred_element_type=F32)
        gate[:, lanes] = g
        up[:, lanes] = u
        expanded[:, lanes] = (g * jax.nn.sigmoid(g) * u).astype(BF16)
        return carry

    lax.fori_loop(0, 3, widen, 0)
    done(gate, up, expanded)
    ready(packed)
    for f in range(8):
        down[f * 96 : f * 96 + 96, :768] = packed[f * 128 : f * 128 + 96, :]
        for m in range(3):
            down[f * 96 + m * 32 : f * 96 + m * 32 + 32, 768:] = packed[
                f * 128 + 96 : f * 128 + 128, m * 256 : m * 256 + 256
            ]
    done(down)

    def narrow(n, carry):
        lanes = pl.ds(pl.multiple_of(n * 256, 256), 256)
        m = jnp.dot(expanded[...], down[:, lanes], preferred_element_type=F32)
        m_mine[:, lanes] = m[:256]
        m_part[:, lanes] = m[256:].astype(BF16)
        return carry

    lax.fori_loop(0, 4, narrow, 0)


def expand_back_body(ready, done, dm_all, gate, up, weight, down, d_gu, dh_mine, dh_part):
    ready(dm_all, gate, up, down)
    done(dm_all)

    def widen(n, carry):
        lanes = pl.ds(pl.multiple_of(n * 256, 256), 256)
        upper = pl.ds(pl.multiple_of(768 + n * 256, 256), 256)
        de = lax.dot_general(dm_all[...], down[lanes, :], NT, preferred_element_type=F32)
        g = gate[:, lanes]
        sig = jax.nn.sigmoid(g)
        d_gu[:, lanes] = (de * up[:, lanes] * sig * (1.0 + g * (1.0 - sig))).astype(BF16)
        d_gu[:, upper] = (de * (g * sig)).astype(BF16)
        return carry

    lax.fori_loop(0, 3, widen, 0)
    done(d_gu)
    ready(weight)

    def narrow(n, carry):
        lanes = pl.ds(pl.multiple_of(n * 256, 256), 256)
        dh = lax.dot_general(d_gu[...], weight[lanes, :], NT, preferred_element_type=F32)
        dh_mine[:, lanes] = dh[:256]
        dh_part[:, lanes] = dh[256:].astype(BF16)
        return carry

    lax.fori_loop(0, 4, narrow, 0)


def expand_grad_body(ready, done, h_turned, d_gu, expanded, dm_all, out, expanded_t):
    ready(expanded)
    expanded_t[...] = jnp.transpose(expanded[...].astype(F32)).astype(BF16)

    ready(h_turned, d_gu, dm_all)

    def widen(n, carry):
        lanes = pl.ds(pl.multiple_of(n * 256, 256), 256)
        out[:, lanes] = jnp.dot(
            h_turned[...], d_gu[:, lanes], preferred_element_type=F32
        ).astype(BF16)
        return carry

    lax.fori_loop(0, 6, widen, 0)
    for n in range(4):
        made = jnp.dot(
            expanded_t[...], dm_all[:, n * 256 : n * 256 + 256], preferred_element_type=F32
        ).astype(BF16)
        for f in range(16):
            if n < 3:
                out[f * 64 : f * 64 + 48, 1536 + n * 256 : 1792 + n * 256] = made[
                    f * 48 : f * 48 + 48
                ]
                continue
            for m in range(3):
                out[f * 64 + 48 : f * 64 + 64, 1536 + m * 256 : 1792 + m * 256] = made[
                    f * 48 + m * 16 : f * 48 + m * 16 + 16
                ]


def norm_scale(values):
    return lax.rsqrt(jnp.mean(values * values, axis=-1, keepdims=True) + EPS)


def norm_back(upstream, normed, scaling):
    return scaling * (upstream - normed * jnp.mean(upstream * normed, axis=-1, keepdims=True))


def rotary_tables(first, z, c):
    half = DH // 2
    k = jnp.arange(4, dtype=jnp.int32)
    starts = jnp.concatenate([((z + k) % 4) * 256 + c * 128, ((z + k) % 4) * 256 + (1 - c) * 128])
    places = (first + starts[:, None] + jnp.arange(128, dtype=jnp.int32)[None, :]).reshape(1024)
    inverse = THETA ** (-(jnp.arange(half, dtype=F32) * (2.0 / DH)))
    angles = places.astype(F32)[:, None] * inverse[None, :]
    cosine, sine = jnp.cos(angles), jnp.sin(angles)
    return (
        jnp.concatenate([cosine, cosine], axis=-1),
        jnp.concatenate([-sine, sine], axis=-1),
    )


def dot(a, b):
    return jnp.dot(a, b, preferred_element_type=F32)


def dot_nt(a, b):
    return lax.dot_general(a, b, NT, preferred_element_type=F32)


def dot_tn(a, b):
    return lax.dot_general(a, b, (((0,), (0,)), ((), ())), preferred_element_type=F32)


def on_device(
    tokens, out_grad, w_query, w_key, w_value, w_out, w_gate, w_up, w_down,
    gain_query, gain_key, gain_attn, gain_mlp,
):
    seq = lax.axis_index("seq")
    xh, zc = seq // 8, seq % 8
    z, c = zc // 2, zc % 2
    quarter = (z % 2) * 2 + c
    place = jnp.stack([xh, z, c]).astype(jnp.int32)
    inputs = tokens[0]

    def columns(weight, width):
        return lax.dynamic_slice_in_dim(weight, zc * width, width, 1)

    def spread(block):
        return lax.all_to_all(
            jnp.broadcast_to(block[None], (8,) + block.shape),
            "fsdp", split_axis=0, concat_axis=0, tiled=True,
        ).reshape(8 * block.shape[0], block.shape[1])

    x_blocks = gather_group(inputs)
    weight = spread(
        jnp.concatenate(
            [columns(w_query, 256), columns(w_key, 128), columns(w_value, 128)], axis=1
        )
    )
    w_out_rows = lax.ppermute(
        after(lax.dynamic_slice_in_dim(w_out, zc * 32, 32, 0), weight),
        ("seq", "fsdp"),
        TURN,
    )

    def quarters(weight):
        part = lax.dynamic_slice_in_dim(weight.reshape(128, 8, 384), quarter * 96, 96, 2)
        return part.reshape(128, 768)

    down = lax.dynamic_slice_in_dim(w_down, quarter * 96, 96, 0)
    packed = jnp.concatenate(
        [
            down[:, :768],
            jnp.concatenate([down[m * 32 : m * 32 + 32, 768:] for m in range(3)], axis=1),
        ],
        axis=0,
    )
    w_narrow = lax.all_gather(packed, "fsdp", axis=0, tiled=True)
    w_wide = jnp.concatenate([quarters(w_gate), quarters(w_up)], axis=1)
    weight, w_wide = lax.optimization_barrier((weight, w_wide))

    cosine, sine = rotary_tables(xh * 1024, z, c)
    gain_q = lax.dynamic_slice_in_dim(gain_query, zc * 256, 256, 0)[None]
    gain_k = lax.dynamic_slice_in_dim(gain_key, zc * 128, 128, 0)[None]
    x_all, q_raw, k_raw, q_rot, kv_rot, squares = kernel_call(
        project_body,
        [
            *in_hbm(
                0, shaped((1024, 256), F32), shaped((1024, 128), F32),
                shaped((1024, 256), BF16), shaped((1024, 256), BF16),
            ),
            shaped((16, 128), F32),
        ],
        [x_blocks, weight, gain_q, gain_k, cosine, sine],
        flops=2 * 1024 * 1024 * 512, nbytes=9 << 20,
    )

    kv_low = swap(kv_rot, LOW_TO_HIGH)
    squares = sum_group(squares)
    squares_low = swap(squares[8:], LOW_TO_HIGH)
    kv_low, squares, squares_low, w_wide, w_narrow, w_out_rows = lax.optimization_barrier(
        (kv_low, squares, squares_low, w_wide, w_narrow, w_out_rows)
    )
    w_wide = lax.all_gather(w_wide, "fsdp", axis=0, tiled=True)
    w_out_rows = spread(w_out_rows)
    out_raw, mixed, mixed_turned, q_tiles, keys, vals, logs = kernel_call(
        attend_body,
        [
            *in_hbm(
                shaped((1024, 256), F32), shaped((1024, 256), BF16), shaped((256, 1024), BF16),
                shaped((8, 256, 128), BF16), shaped((2048, 128), BF16), shaped((2048, 128), BF16),
            ),
            shaped((8, 256), F32),
        ],
        [place, *in_hbm(q_rot, kv_rot), kv_low, squares, squares_low],
        [pltpu.VMEM((128, 2048), BF16)],
        flops=4 * 1024 * 2048 * 256, nbytes=9 << 20,
    )
    a_mine, a_part = kernel_call(
        output_body,
        [shaped((512, 1024), F32), shaped((512, 1024), BF16)],
        [*in_hbm(mixed), w_out_rows],
        flops=2 * 1024 * 1024 * 256, nbytes=5 << 20,
    )
    x_turned = x_all.T

    attended = scatter_group(a_mine, a_part)
    attended, x_turned = lax.optimization_barrier((attended, x_turned))
    attn_scale = norm_scale(attended)
    attn_hat = attended * attn_scale
    hidden_state = inputs.astype(F32) + attn_hat * gain_attn
    h_all, gate, up, expanded, m_mine, m_part, w_down_rows = kernel_call(
        expand_body,
        [
            0, shaped((512, 768), F32), shaped((512, 768), F32), shaped((512, 768), BF16),
            shaped((256, 1024), F32), shaped((256, 1024), BF16), shaped((768, 1024), BF16),
        ],
        [
            gather_pair(hidden_state.astype(BF16)), *in_hbm(w_wide, w_narrow),
        ],
        flops=2 * 512 * 2304 * 1024, nbytes=12 << 20,
    )
    projected, _ = scatter_pair(m_mine, m_part)
    mlp_scale = norm_scale(projected)
    mlp_hat = projected * mlp_scale
    output = (hidden_state + mlp_hat * gain_mlp).astype(BF16)[None]

    upstream = out_grad[0].astype(F32)
    grad_gain_mlp = jnp.sum(upstream * mlp_hat, axis=0)
    d_projected = norm_back(upstream * gain_mlp, mlp_hat, mlp_scale).astype(BF16)
    n = jnp.arange(1024, dtype=jnp.int32)
    source = ((n // 8) % 16) * 64 + (n // 128) * 8 + n % 8
    order = (n[None, :] == source[:, None]).astype(BF16)
    h_turned = dot_nt(order, h_all).astype(BF16)
    d_blocks = gather_pair(d_projected)
    d_blocks[3], h_turned = lax.optimization_barrier((d_blocks[3], h_turned))
    dm_all, d_gu, dh_mine, dh_part = kernel_call(
        expand_back_body,
        [
            0, shaped((512, 1536), BF16), shaped((256, 1024), F32), shaped((256, 1024), BF16),
        ],
        [d_blocks, gate, up, w_wide, w_down_rows],
        flops=2 * 512 * 2304 * 1024, nbytes=12 << 20,
    )

    far = dh_mine[128:] + swap(dh_part[128:], CORE_SWAP).astype(F32)
    far, d_gu, dm_all = lax.optimization_barrier((far.astype(BF16), d_gu, dm_all))
    far = swap(far, Z_SWAP)
    (grad_mlp,) = kernel_call(
        expand_grad_body,
        in_hbm(shaped((1024, 2304), BF16)),
        [h_turned, d_gu, expanded, dm_all],
        [pltpu.VMEM((768, 512), BF16)],
        flops=2 * 512 * 2304 * 1024, nbytes=9 << 20,
    )
    far, grad_mlp = lax.optimization_barrier((far, grad_mlp))
    grad_mlp = lax.psum_scatter(grad_mlp, "fsdp", scatter_dimension=0, tiled=True)
    d_hidden = upstream + dh_mine[:128] + swap(dh_part[:128], CORE_SWAP).astype(F32)
    d_hidden = d_hidden + far.astype(F32)

    grad_gain_attn = jnp.sum(d_hidden * attn_hat, axis=0)
    d_attended = norm_back(d_hidden * gain_attn, attn_hat, attn_scale).astype(BF16)
    d_tiles, deltas, grad_out = kernel_call(
        output_back_body,
        [shaped((8, 256, 128), BF16), shaped((8, 2, 128), F32), shaped((256, 1024), BF16)],
        [place, *in_hbm(out_raw, w_out_rows, gather_group(d_attended), mixed_turned)],
        flops=4 * 1024 * 1024 * 256, nbytes=6 << 20,
    )
    fsdp = lax.axis_index("fsdp")

    def halve(value, rows, bit, axis, pairs):
        parts = value.reshape(-1, 2, rows, 1024)
        given = jnp.where(bit == 1, parts[:, 0], parts[:, 1])
        mine = jnp.where(bit == 1, parts[:, 1], parts[:, 0]).astype(F32)
        return (mine + lax.ppermute(given, axis, pairs).astype(F32)).astype(BF16)

    grad_out = halve(grad_out, 32, fsdp % 2, "fsdp", [(i, i ^ 1) for i in range(8)])
    dq, dk, dv, d_low, dots = kernel_call(
        attend_back_body,
        [
            *in_hbm(
                shaped((1024, 256), BF16), shaped((1024, 128), F32), shaped((1024, 128), F32),
                shaped((1024, 256), BF16),
            ),
            shaped((24, 128), F32),
        ],
        [place, *in_hbm(q_tiles, keys, vals), logs, d_tiles, deltas],
        [
            pltpu.VMEM((128, 2048), BF16), pltpu.VMEM((2048, 128), F32),
            pltpu.VMEM((2048, 128), F32),
        ],
        flops=10 * 1024 * 2048 * 256, nbytes=8 << 20,
    )
    dots, grad_out = lax.optimization_barrier((dots, grad_out))
    grad_out = halve(grad_out, 32, fsdp // 2 % 2, "fsdp", [(i, i ^ 2) for i in range(8)])
    grad_out = halve(grad_out, 32, fsdp // 4, "fsdp", [(i, i ^ 4) for i in range(8)])
    d_got = swap(d_low, HIGH_TO_LOW)
    dots = sum_group(dots)
    dots_got = swap(dots[16:], HIGH_TO_LOW)

    gains = jnp.concatenate([grad_gain_attn.reshape(128, 8), grad_gain_mlp.reshape(128, 8)], axis=1)
    gains = jnp.broadcast_to(
        jnp.pad(gains.astype(BF16), ((0, 0), (24, 88)))[:, None, :], (128, 8, 128)
    ).reshape(1024, 128)
    d_made, sent = kernel_call(
        unproject_body,
        [*in_hbm(shaped((1024, 512), BF16)), shaped((1024, 640), BF16)],
        [
            place, *in_hbm(dq, dk, dv), d_got, *in_hbm(q_raw, k_raw), squares, dots, dots_got, cosine, sine,
            gain_q, gain_k, *in_hbm(x_turned), gains,
        ],
        [pltpu.VMEM((8, 384), F32)],
        flops=2 * 1024 * 1024 * 512, nbytes=9 << 20,
    )

    def halves(value, upper):
        low, high = value[: value.shape[0] // 2], value[value.shape[0] // 2 :]
        return jnp.where(upper, high, low), jnp.where(upper, low, high)

    mine, given = halves(grad_mlp, xh == 1)
    mine = mine.astype(F32) + swap(given, X_SWAP).astype(F32)
    got_wide = lax.all_to_all(
        grad_mlp[:, :1536].reshape(16, 8, 1536), "seq", split_axis=0, concat_axis=0, tiled=True
    )
    sent, got_wide, grad_mlp, grad_out = lax.optimization_barrier(
        (sent, got_wide, grad_mlp, grad_out)
    )
    grad_down = jnp.concatenate(
        [
            piece
            for h in (0, 64)
            for piece in [
                jnp.concatenate(
                    [
                        grad_mlp[h : h + 48, 1536:],
                        jnp.concatenate(
                            [
                                grad_mlp[h + 48 : h + 64, 1536 + m * 256 : 1792 + m * 256]
                                for m in range(3)
                            ],
                            axis=0,
                        ),
                    ],
                    axis=1,
                )
            ]
        ],
        axis=0,
    ).reshape(4, 24, 1024)
    grad_down = sum(
        lax.ppermute(
            lax.dynamic_index_in_dim(grad_down, (xh * 2 + z // 2) ^ other, 0, keepdims=False),
            ("seq", "fsdp"),
            down_home(other),
        ).astype(F32)
        for other in range(4)
    )
    got_made = lax.all_to_all(
        sent.reshape(128, 8, 640), ("seq", "fsdp"), split_axis=0, concat_axis=0, tiled=True
    )
    dx_mine, dx_part = kernel_call(
        input_body,
        in_hbm(shaped((512, 1024), F32), shaped((512, 1024), BF16)),
        [*in_hbm(after(d_made, sent)), weight],
        flops=2 * 1024 * 1024 * 512, nbytes=5 << 20,
    )
    rows = [slice(k * 128, k * 128 + 128) for k in range(4)]
    pieces = [dx_mine[r] + swap(dx_part[r], CORE_SWAP).astype(F32) for r in rows]
    far = [piece.astype(BF16) for piece in pieces[1:]]
    got_made, grad_down, grad_out, far = lax.optimization_barrier(
        (got_made, grad_down, grad_out, far)
    )
    grad_out = grad_out.reshape(2, 16, 1024)
    own = jnp.where(xh == 1, grad_out[1], grad_out[0])
    given = jnp.where(xh == 1, grad_out[0], grad_out[1])
    own = swap(own, out_home(False))
    grad_out = own.astype(F32) + swap(after(given, own), out_home(True)).astype(F32)
    d_inputs = pieces[0] + sum(
        swap(piece, to_z(k)).astype(F32) for k, piece in enumerate(far, 1)
    )
    summed = jnp.sum(got_made.reshape(2, 8, 8, 8, 640).astype(F32), axis=(0, 2))
    gains = jnp.sum(summed[:, 0, 512:], axis=0)

    def take(first, width):
        return summed[:, :, first : first + width].swapaxes(0, 1).reshape(8, 8 * width)

    wide = jnp.sum(got_wide.reshape(2, 2, 4, 8, 2, 8, 96).astype(F32), axis=(0, 1))
    wide = wide.transpose(2, 1, 3, 0, 4).reshape(2, 8, 3072)
    return (
        output,
        (d_hidden + d_inputs).astype(BF16)[None],
        take(0, 256),
        take(256, 128),
        take(384, 128),
        grad_out.astype(F32),
        wide[0],
        wide[1],
        grad_down.astype(F32),
        gains[:16],
        gains[16:24],
        gains[24:32],
        gains[32:40],
    )


def solution(mesh):
    rows = P("fsdp", "seq", None)
    weight = P("fsdp", None)
    grad = P(("seq", "fsdp"), None)
    gain = P(("seq", "fsdp"))
    return jax.shard_map(
        on_device,
        mesh=mesh,
        in_specs=(rows,) * 2 + (weight,) * 7 + (P(),) * 4,
        out_specs=(rows,) * 2 + (grad,) * 7 + (gain,) * 4,
        check_vma=False,
    )
```

```python
import functools
import math

import jax
import jax.numpy as jnp
from jax import lax
from jax.experimental import pallas as pl
from jax.experimental.pallas import tpu as pltpu
from jax.sharding import PartitionSpec as P

BF16 = jnp.bfloat16
F32 = jnp.float32
DH = 128
EPS = 1e-06
THETA = 1000000.0
MASKED = -1e30
LOG2E = math.log2(math.e)
QUERY_SCALE = DH ** (-0.5) * LOG2E
VMEM_BYTES = 20 * 1024 * 1024
VMEM = pl.BlockSpec(memory_space=pltpu.VMEM)
SMEM = pl.BlockSpec(memory_space=pltpu.SMEM)
ANY = pl.BlockSpec(memory_space=pl.ANY)
SMALL = 64 * 1024
WAIT_FLOPS = 12 * 10**9
NT = (((1,), (1,)), ((), ()))

SEQ_PLACES = [(xh, z, c) for xh in range(2) for z in range(4) for c in range(2)]


def seq_index(xh, z, c):
    return xh * 8 + (z % 4) * 2 + c


CORE_SWAP = [(i, i ^ 1) for i in range(16)]
LOW_TO_HIGH = [(i, i + 8) for i in range(8)]
HIGH_TO_LOW = [(i + 8, i) for i in range(8)]
X_SWAP = [(i, i ^ 8) for i in range(16)]


def from_z(k):
    return [(seq_index(xh, z + k, c), seq_index(xh, z, c)) for xh, z, c in SEQ_PLACES]


def to_z(k):
    return [(seq_index(xh, z, c), seq_index(xh, z + k, c)) for xh, z, c in SEQ_PLACES]


def across(pairs):
    return [(seq * 8 + f, to_seq * 8 + to_f) for seq, f, to_seq, to_f in pairs]


TURN = across(
    (xh * 8 + a, f, xh * 8 + f, a) for xh in range(2) for a in range(8) for f in range(8)
)
Z_SWAP = [(i, i ^ 2) for i in range(16)]
FAR_SWAP = [(i, i ^ 4) for i in range(16)]


def out_home(other):
    return [(xh * 8 + a, 2 * a + (xh ^ other)) for xh in range(2) for a in range(8)]


def down_home(other):
    return across(
        (seq_index(own // 2, 2 * (own % 2) + zl, c), f, 2 * f + zl, 4 * c + (own ^ other))
        for own in range(4) for zl in range(2) for c in range(2) for f in range(8)
    )


def swap(value, pairs):
    return lax.ppermute(value, "seq", pairs)


def after(value, *others):
    return lax.optimization_barrier((value, *others))[0]


def gather_group(block):
    far = {k: swap(block, from_z(k)) for k in (2, 1, 3)}
    mine = [block, far[1], far[2], far[3]]
    return mine + [swap(v, CORE_SWAP) for v in mine]


def scatter_group(mine, part):
    rows = [slice(k * 128, k * 128 + 128) for k in range(4)]
    out = None
    for k in (2, 1, 3, 0):
        piece = mine[rows[k]] + swap(part[rows[k]], CORE_SWAP).astype(F32)
        if k:
            piece = swap(piece.astype(BF16), to_z(k)).astype(F32)
        out = piece if out is None else out + piece
    return out


def gather_pair(block):
    mine = [block, swap(block, Z_SWAP)]
    return mine + [swap(v, CORE_SWAP) for v in mine]


def scatter_pair(mine, part, later=()):
    far = mine[128:] + swap(part[128:], CORE_SWAP).astype(F32)
    far, *later = lax.optimization_barrier((far.astype(BF16), *later))
    far = swap(far, Z_SWAP).astype(F32)
    return mine[:128] + swap(part[:128], CORE_SWAP).astype(F32) + far, later


def sum_group(rows):
    groups = rows.shape[0] // 8
    other = swap(rows, CORE_SWAP).reshape(groups, 2, 4, 128)
    pair = rows.reshape(groups, 2, 4, 128) + jnp.concatenate([other[:, 1:], other[:, :1]], axis=1)
    odd = lax.axis_index("seq") // 2 % 2 == 1
    got = swap(pair, Z_SWAP)
    up = jnp.concatenate([got[:, :, 3:], got[:, :, :3]], axis=2)
    down = jnp.concatenate([got[:, :, 1:], got[:, :, :1]], axis=2)
    pair = pair + jnp.where(odd, down, up)
    got = swap(pair, FAR_SWAP)
    pair = pair + jnp.concatenate([got[:, :, 2:], got[:, :, :2]], axis=2)
    return pair.reshape(rows.shape)


def column(row):
    return jnp.transpose(jnp.broadcast_to(row, (128, 128)))


def row_sums(values):
    return jnp.sum(jnp.transpose(values), axis=0, keepdims=True)


def shaped(shape, dtype):
    return jax.ShapeDtypeStruct(shape, dtype)


class Kept:
    def __init__(self, value):
        self.value = value


def in_hbm(*values):
    return [Kept(v) for v in values]


def kernel_call(body, outs, inputs, scratch=(), flops=0, nbytes=0):
    hbm_outs = [isinstance(o, Kept) for o in outs]
    hbm_ins = [isinstance(x, Kept) for x in inputs]
    outs = [o.value if isinstance(o, Kept) else o for o in outs]
    inputs = [x.value if isinstance(x, Kept) else x for x in inputs]
    groups = [x if isinstance(x, list) else [x] for x in inputs]
    flat = [a for group in groups for a in group]
    joined = [
        shaped((sum(a.shape[0] for a in group),) + group[0].shape[1:], group[0].dtype)
        for group in groups
    ]

    def large(s):
        return math.prod(s.shape) * s.dtype.itemsize >= SMALL

    def where(s):
        return ANY if large(s) else SMEM if s.dtype == jnp.int32 else VMEM

    out_shapes = [joined[o] if isinstance(o, int) else o for o in outs]
    in_buffers = [pltpu.VMEM(s.shape, s.dtype) for s in joined if large(s)]
    out_buffers = [
        pltpu.VMEM(o.shape, o.dtype) for o in outs if not isinstance(o, int) and large(o)
    ]

    def whole(*refs):
        refs = list(refs)

        def pull(count):
            taken = refs[:count]
            del refs[:count]
            return taken

        in_refs, out_refs = pull(len(flat)), pull(len(outs))
        in_space, out_space = pull(len(in_buffers)), pull(len(out_buffers))
        own, (in_sem, out_sem) = pull(len(scratch)), refs
        loads, ins, at = {}, [], 0
        for group, s in zip(groups, joined):
            if not large(s):
                ins.append(in_refs[at])
                at += 1
                continue
            space, row = in_space.pop(0), 0
            loads[id(space)] = []
            for a in group:
                copy = pltpu.make_async_copy(
                    in_refs[at], space.at[pl.ds(row, a.shape[0])], in_sem.at[at]
                )
                copy.start()
                loads[id(space)].append(copy)
                row, at = row + a.shape[0], at + 1
            ins.append(space)
        made, stores = [], {}
        for k, (o, s, ref) in enumerate(zip(outs, out_shapes, out_refs)):
            if not large(s):
                made.append(ref)
                continue
            space = ins[o] if isinstance(o, int) else out_space.pop(0)
            stores[id(space)] = pltpu.make_async_copy(space, ref, out_sem.at[k])
            if not isinstance(o, int):
                made.append(space)
        started = []

        def ready(*spaces):
            for space in spaces:
                for copy in loads.pop(id(space), ()):
                    copy.wait()

        def done(*spaces):
            for space in spaces:
                copy = stores.pop(id(space))
                copy.start()
                started.append(copy)

        body(ready, done, *ins, *made, *own)
        for key in list(stores):
            copy = stores.pop(key)
            copy.start()
            started.append(copy)
        for copy in started:
            copy.wait()

    shapes = [pltpu.HBM(s.shape, s.dtype) if hbm else s for s, hbm in zip(out_shapes, hbm_outs)]
    return pl.pallas_call(
        whole,
        out_shape=tuple(shapes),
        in_specs=[where(s) for group, s in zip(groups, joined) for _ in group],
        out_specs=tuple(where(s) for s in out_shapes),
        scratch_shapes=[
            *in_buffers, *out_buffers, *scratch,
            pltpu.SemaphoreType.DMA((len(flat),)), pltpu.SemaphoreType.DMA((len(outs),)),
        ],
        compiler_params=pltpu.CompilerParams(vmem_limit_bytes=VMEM_BYTES),
        cost_estimate=pl.CostEstimate(flops=flops, bytes_accessed=nbytes, transcendentals=0),
    )(
        *[
            pltpu.with_memory_space_constraint(a, pltpu.HBM) if hbm else a
            for group, hbm in zip(groups, hbm_ins)
            for a in group
        ],
    )


def root(total, width):
    return lax.rsqrt(total * (1.0 / width) + EPS)


def project_body(
    ready, done, x_all, weight, gain_q, gain_k, cos, sin,
    q_raw, k_raw, q_rot, kv_rot, squares,
):
    ready(x_all, weight, cos, sin)
    done(x_all)

    def step(t, carry):
        at = pl.multiple_of(t * 256, 256)
        made = jnp.dot(x_all[pl.ds(at, 256), :], weight[...], preferred_element_type=F32)
        for part in range(2):
            rows = pl.ds(at + part * 128, 128)
            block = t * 2 + part
            here = made[part * 128 : part * 128 + 128]
            q, k = here[:, :256], here[:, 256:384]
            kv_rot[rows, 128:] = here[:, 384:].astype(BF16)
            q_raw[rows, :] = q
            k_raw[rows, :] = k
            squares[pl.ds(block, 1), :] = row_sums(
                q[:, :128] * q[:, :128] + q[:, 128:] * q[:, 128:]
            )
            squares[pl.ds(block + 8, 1), :] = row_sums(k * k)
            cosine, sine = cos[rows, :], sin[rows, :]
            for head in range(2):
                lanes = slice(head * 128, head * 128 + 128)
                turn = q[:, lanes] * gain_q[:, lanes]
                q_rot[rows, lanes] = (turn * cosine + pltpu.roll(turn, 64, 1) * sine).astype(BF16)
            turn = k * gain_k[...]
            kv_rot[rows, :128] = (turn * cosine + pltpu.roll(turn, 64, 1) * sine).astype(BF16)
        return carry

    lax.fori_loop(0, 4, step, 0)


def spot(place, block):
    z = lax.rem(place[1] + block % 4, 4)
    c = place[2] if block < 4 else 1 - place[2]
    return z, c


def diagonal():
    query = lax.broadcasted_iota(jnp.int32, (256, 512), 1) % 256
    return lax.broadcasted_iota(jnp.int32, (256, 512), 0) <= query


def attend_body(
    ready, done, place, q_rot, kv_rot, kv_low, squares, squares_low,
    out_raw, out_low, out_turned, q_tiles, keys, vals, logs, vals_t,
):
    ready(q_rot, kv_rot, kv_low)
    for b in range(8):
        rows = slice(b * 128, b * 128 + 128)
        z, c = spot(place, b)
        r = column(root(squares[b : b + 1, :], 2048.0)) * QUERY_SCALE
        inner = pl.ds(pl.multiple_of(c * 128, 128), 128)
        for head in range(2):
            q = q_rot[rows, head * 128 : head * 128 + 128].astype(F32)
            q_tiles[z * 2 + head, inner, :] = (q * r).astype(BF16)
        at = pl.ds(pl.multiple_of(1024 + z * 256 + c * 128, 128), 128)
        r = column(root(squares[8 + b : 9 + b, :], 1024.0))
        keys[at, :] = (kv_rot[rows, :128].astype(F32) * r).astype(BF16)
        vals[at, :] = kv_rot[rows, 128:]
        r = column(root(squares_low[b : b + 1, :], 1024.0))
        keys[rows, :] = (kv_low[rows, :128].astype(F32) * r).astype(BF16)
        vals[rows, :] = kv_low[rows, 128:]
    done(q_tiles, keys, vals)
    vals_t[...] = jnp.transpose(vals[...].astype(F32)).astype(BF16)

    def queries(first, i):
        at_diagonal = 1024 + i * 256
        q = q_tiles[i * 2 : i * 2 + 2].reshape(512, 128)
        ranges = [(lo, lo + 256) for lo in range(first, at_diagonal + 256, 256)]
        scores = [
            lax.dot_general(keys[lo:hi, :], q, NT, preferred_element_type=F32) for lo, hi in ranges
        ]
        scores[-1] = jnp.where(diagonal(), scores[-1], MASKED)
        top = functools.reduce(jnp.maximum, [jnp.max(s, axis=0, keepdims=True) for s in scores])
        total, acc = 0.0, 0.0
        for s, (lo, hi) in zip(scores, ranges):
            p = jnp.exp2(s - top)
            total = total + jnp.sum(p, axis=0, keepdims=True)
            acc = acc + jnp.dot(vals_t[:, lo:hi], p.astype(BF16), preferred_element_type=F32)
        acc = acc / total
        log = top + jnp.log2(total)
        for head in range(2):
            turned = acc[:, head * 256 : head * 256 + 256]
            out = jnp.transpose(turned)
            turned = turned.astype(BF16)
            logs[i * 2 + head : i * 2 + head + 1, :] = log[:, head * 256 : head * 256 + 256]
            for c in range(2):
                block = lax.rem(i - place[1] + 4, 4) + 4 * jnp.abs(c - place[2])
                at = pl.ds(pl.multiple_of(block * 128, 128), 128)
                lanes = slice(head * 128, head * 128 + 128)
                out_raw[at, lanes] = out[c * 128 : c * 128 + 128, :]
                out_low[at, lanes] = out[c * 128 : c * 128 + 128, :].astype(BF16)
                out_turned[lanes, at] = turned[:, c * 128 : c * 128 + 128]

    @pl.when(place[0] == 1)
    def _():
        for i in range(4):
            queries(0, i)

    @pl.when(place[0] == 0)
    def _():
        for i in range(4):
            queries(1024, i)

    done(out_raw, out_low, out_turned)


def output_body(ready, done, mixed, w_out, a_mine, a_part):
    ready(mixed, w_out)

    def project(t, carry):
        at = pl.ds(pl.multiple_of(t * 256, 256), 256)
        far = pl.ds(pl.multiple_of(512 + t * 256, 256), 256)
        a_part[at, :] = jnp.dot(mixed[far, :], w_out[...], preferred_element_type=F32).astype(BF16)
        a_mine[at, :] = jnp.dot(mixed[at, :], w_out[...], preferred_element_type=F32)
        return carry

    lax.fori_loop(0, 2, project, 0)


def output_back_body(
    ready, done, place, out_raw, w_out, da_all, mixed_turned, d_tiles, deltas, grad_out
):
    ready(out_raw, w_out, da_all)
    for b in range(8):
        rows = slice(b * 128, b * 128 + 128)
        z, c = spot(place, b)
        inner = pl.ds(pl.multiple_of(c * 128, 128), 128)
        d_out = lax.dot_general(
            da_all[rows, :], w_out[...], NT, preferred_element_type=F32
        ).astype(BF16)
        for head in range(2):
            lanes = slice(head * 128, head * 128 + 128)
            grad = d_out[:, lanes]
            d_tiles[z * 2 + head, inner, :] = grad
            deltas[z * 2 + head, pl.ds(c, 1), :] = row_sums(grad.astype(F32) * out_raw[rows, lanes])
    done(d_tiles)
    ready(mixed_turned)
    for m in range(4):
        lanes = slice(m * 256, m * 256 + 256)
        made = jnp.dot(mixed_turned[...], da_all[:, lanes], preferred_element_type=F32).astype(BF16)
        for j in range(2):
            for f in range(8):
                to, at = f * 32 + j * 16, j * 128 + f * 16
                grad_out[to : to + 16, lanes] = made[at : at + 16]


def attend_back_body(
    ready, done, place, q_tiles, keys, vals, logs, d_tiles, deltas,
    dq, dk, dv, d_low, dots, keys_t, dk_acc, dv_acc,
):
    ready(keys)
    keys_t[...] = jnp.transpose(keys[...].astype(F32)).astype(BF16)
    dk_acc[...] = jnp.zeros_like(dk_acc)
    dv_acc[...] = jnp.zeros_like(dv_acc)
    ready(q_tiles, vals, d_tiles)

    def queries(first, i):
        at_diagonal = 1024 + i * 256
        q = q_tiles[i * 2 : i * 2 + 2].reshape(512, 128)
        grad = d_tiles[i * 2 : i * 2 + 2].reshape(512, 128)
        log = jnp.concatenate([logs[i * 2 : i * 2 + 1, :], logs[i * 2 + 1 : i * 2 + 2, :]], axis=1)
        delta = jnp.concatenate(
            [deltas[i * 2 + head, c : c + 1, :] for head in range(2) for c in range(2)], axis=1
        )
        total = 0.0
        for lo in range(first, at_diagonal + 256, 256):
            at = slice(lo, lo + 256)
            k, v = keys[at, :], vals[at, :]
            s = lax.dot_general(k, q, NT, preferred_element_type=F32)
            p = jnp.exp2(s - log)
            if lo == at_diagonal:
                p = jnp.where(diagonal(), p, 0.0)
            dp = lax.dot_general(v, grad, NT, preferred_element_type=F32)
            ds = (p * (dp - delta)).astype(BF16)
            dv_acc[at, :] += jnp.dot(p.astype(BF16), grad, preferred_element_type=F32)
            dk_acc[at, :] += jnp.dot(ds, q, preferred_element_type=F32)
            total = total + jnp.dot(keys_t[:, at], ds, preferred_element_type=F32)
        dot = total * jnp.transpose(q.astype(F32))
        dot = jnp.sum(dot[:, :256] + dot[:, 256:], axis=0, keepdims=True)
        for head in range(2):
            out = jnp.transpose(total[:, head * 256 : head * 256 + 256]) * DH ** (-0.5)
            for c in range(2):
                block = lax.rem(i - place[1] + 4, 4) + 4 * jnp.abs(c - place[2])
                at = pl.ds(pl.multiple_of(block * 128, 128), 128)
                dq[at, head * 128 : head * 128 + 128] = out[c * 128 : c * 128 + 128, :].astype(BF16)
        for c in range(2):
            block = lax.rem(i - place[1] + 4, 4) + 4 * jnp.abs(c - place[2])
            dots[pl.ds(block, 1), :] = dot[:, c * 128 : c * 128 + 128] * (1.0 / LOG2E)

    @pl.when(place[0] == 1)
    def _():
        for i in range(4):
            queries(0, i)

    @pl.when(place[0] == 0)
    def _():
        for i in range(4):
            queries(1024, i)

    done(dq)
    for b in range(8):
        rows = slice(b * 128, b * 128 + 128)
        z, c = spot(place, b)
        at = pl.ds(pl.multiple_of(1024 + z * 256 + c * 128, 128), 128)
        key_grad = dk_acc[at, :] * (1.0 / LOG2E)
        dk[rows, :] = key_grad
        dv[rows, :] = dv_acc[at, :]
        dots[8 + b : 9 + b, :] = row_sums(key_grad * keys[at, :].astype(F32))
        key_grad = dk_acc[rows, :] * (1.0 / LOG2E)
        d_low[rows, :128] = key_grad.astype(BF16)
        d_low[rows, 128:] = dv_acc[rows, :].astype(BF16)
        dots[16 + b : 17 + b, :] = row_sums(key_grad * keys[rows, :].astype(F32))


def unproject_body(
    ready, done, place, dq, dk, dv, d_got, q_raw, k_raw, squares, dots, dots_got, cos, sin,
    gain_q, gain_k, x_turned, gains, d_made, sent, sums,
):
    sums[...] = jnp.zeros_like(sums)
    ready(dq, dk, dv, d_got, q_raw, k_raw, cos, sin)

    def step(b, carry):
        rows = pl.ds(pl.multiple_of(b * 128, 128), 128)
        cosine, sine = cos[rows, :], sin[rows, :]
        r = column(root(squares[pl.ds(b, 1), :], 2048.0))
        mean = column(dots[pl.ds(b, 1), :]) * (1.0 / 2048.0)
        for head in range(2):
            lanes = slice(head * 128, head * 128 + 128)
            turn = dq[rows, lanes].astype(F32)
            d_norm = turn * cosine - pltpu.roll(turn, 64, 1) * sine
            hat = q_raw[rows, lanes] * r
            sums[0:1, lanes] += jnp.sum(d_norm * hat, axis=0, keepdims=True)
            d_made[rows, lanes] = (r * (d_norm * gain_q[:, lanes] - hat * mean)).astype(BF16)
        r = column(root(squares[pl.ds(b + 8, 1), :], 1024.0))
        mean = column(dots[pl.ds(b + 8, 1), :] + dots_got[pl.ds(b, 1), :]) * (1.0 / 1024.0)
        turn = dk[rows, :] + d_got[rows, :128].astype(F32)
        d_norm = turn * cosine - pltpu.roll(turn, 64, 1) * sine
        hat = k_raw[rows, :] * r
        sums[0:1, 256:] += jnp.sum(d_norm * hat, axis=0, keepdims=True)
        d_made[rows, 256:384] = (r * (d_norm * gain_k[...] - hat * mean)).astype(BF16)
        d_made[rows, 384:] = (dv[rows, :] + d_got[rows, 128:].astype(F32)).astype(BF16)
        return carry

    lax.fori_loop(0, 8, step, 0)
    done(d_made)
    ready(x_turned, gains)

    def grad(t, carry):
        rows = pl.ds(pl.multiple_of(t * 256, 256), 256)
        sent[rows, :512] = jnp.dot(
            x_turned[rows, :], d_made[...], preferred_element_type=F32
        ).astype(BF16)
        sent[rows, 512:] = gains[rows, :]
        return carry

    lax.fori_loop(0, 4, grad, 0)
    extra = 0.0
    for lo, width, each, first in ((0, 256, 16, 0), (256, 128, 8, 16)):
        row = lax.broadcasted_iota(jnp.int32, (128, width), 0)
        lane = lax.broadcasted_iota(jnp.int32, (128, width), 1) // each
        here = row // 8 % 2 * 8 + row // 16 == lane
        spread = jnp.where(here, sums[0:1, lo : lo + width], 0.0).astype(BF16)
        lane = lax.broadcasted_iota(jnp.int32, (width, 128), 0) % each + first
        pick = jnp.where(lane == lax.broadcasted_iota(jnp.int32, (width, 128), 1), 1.0, 0.0)
        extra = extra + jnp.dot(spread, pick.astype(BF16), preferred_element_type=F32)
    for f in range(8):
        rows = pl.ds(pl.multiple_of(f * 128 + (place[1] * 2 + place[2]) * 16, 16), 16)
        added = gains[rows, :].astype(F32) + extra[f * 16 : f * 16 + 16]
        sent[rows, 512:] = added.astype(BF16)


def input_body(ready, done, d_made, weight, dx_mine, dx_part):
    ready(d_made, weight)

    def step(t, carry):
        at = pl.ds(pl.multiple_of(t * 256, 256), 256)
        far = pl.ds(pl.multiple_of(512 + t * 256, 256), 256)
        dx_part[at, :] = lax.dot_general(
            d_made[far, :], weight[...], NT, preferred_element_type=F32
        ).astype(BF16)
        dx_mine[at, :] = lax.dot_general(
            d_made[at, :], weight[...], NT, preferred_element_type=F32
        )
        return carry

    lax.fori_loop(0, 2, step, 0)


def expand_body(ready, done, h_all, weight, packed, gate, up, expanded, m_mine, m_part, down):
    ready(h_all, weight)
    done(h_all)
    def widen(n, carry):
        lanes = pl.ds(pl.multiple_of(n * 256, 256), 256)
        upper = pl.ds(pl.multiple_of(768 + n * 256, 256), 256)
        g = jnp.dot(h_all[...], weight[:, lanes], preferred_element_type=F32)
        u = jnp.dot(h_all[...], weight[:, upper], preferred_element_type=F32)
        gate[:, lanes] = g
        up[:, lanes] = u
        expanded[:, lanes] = (g * jax.nn.sigmoid(g) * u).astype(BF16)
        return carry

    lax.fori_loop(0, 3, widen, 0)
    done(gate, up, expanded)
    ready(packed)
    for f in range(8):
        down[f * 96 : f * 96 + 96, :768] = packed[f * 128 : f * 128 + 96, :]
        for m in range(3):
            down[f * 96 + m * 32 : f * 96 + m * 32 + 32, 768:] = packed[
                f * 128 + 96 : f * 128 + 128, m * 256 : m * 256 + 256
            ]
    done(down)

    def narrow(n, carry):
        lanes = pl.ds(pl.multiple_of(n * 256, 256), 256)
        m = jnp.dot(expanded[...], down[:, lanes], preferred_element_type=F32)
        m_mine[:, lanes] = m[:256]
        m_part[:, lanes] = m[256:].astype(BF16)
        return carry

    lax.fori_loop(0, 4, narrow, 0)


def expand_back_body(ready, done, dm_all, gate, up, weight, down, d_gu, dh_mine, dh_part):
    ready(dm_all, gate, up, down)
    done(dm_all)

    def widen(n, carry):
        lanes = pl.ds(pl.multiple_of(n * 256, 256), 256)
        upper = pl.ds(pl.multiple_of(768 + n * 256, 256), 256)
        de = lax.dot_general(dm_all[...], down[lanes, :], NT, preferred_element_type=F32)
        g = gate[:, lanes]
        sig = jax.nn.sigmoid(g)
        d_gu[:, lanes] = (de * up[:, lanes] * sig * (1.0 + g * (1.0 - sig))).astype(BF16)
        d_gu[:, upper] = (de * (g * sig)).astype(BF16)
        return carry

    lax.fori_loop(0, 3, widen, 0)
    done(d_gu)
    ready(weight)

    def narrow(n, carry):
        lanes = pl.ds(pl.multiple_of(n * 256, 256), 256)
        dh = lax.dot_general(d_gu[...], weight[lanes, :], NT, preferred_element_type=F32)
        dh_mine[:, lanes] = dh[:256]
        dh_part[:, lanes] = dh[256:].astype(BF16)
        return carry

    lax.fori_loop(0, 4, narrow, 0)


def expand_grad_body(ready, done, h_turned, d_gu, expanded, dm_all, out, expanded_t):
    ready(expanded)
    expanded_t[...] = jnp.transpose(expanded[...].astype(F32)).astype(BF16)

    ready(h_turned, d_gu, dm_all)

    def widen(n, carry):
        lanes = pl.ds(pl.multiple_of(n * 256, 256), 256)
        out[:, lanes] = jnp.dot(
            h_turned[...], d_gu[:, lanes], preferred_element_type=F32
        ).astype(BF16)
        return carry

    lax.fori_loop(0, 6, widen, 0)
    for n in range(4):
        made = jnp.dot(
            expanded_t[...], dm_all[:, n * 256 : n * 256 + 256], preferred_element_type=F32
        ).astype(BF16)
        for f in range(16):
            if n < 3:
                out[f * 64 : f * 64 + 48, 1536 + n * 256 : 1792 + n * 256] = made[
                    f * 48 : f * 48 + 48
                ]
                continue
            for m in range(3):
                out[f * 64 + 48 : f * 64 + 64, 1536 + m * 256 : 1792 + m * 256] = made[
                    f * 48 + m * 16 : f * 48 + m * 16 + 16
                ]


def collect_body(ready, done, got, grad_mlp, out):
    ready(got)
    total = got[:128, :].astype(F32)
    for f in range(1, 8):
        total = total + got[f * 128 : f * 128 + 128, :].astype(F32)
    out[:, :640] = total.astype(BF16)
    ready(grad_mlp)
    out[:, 640:] = grad_mlp[:, :1536]


def norm_scale(values):
    return lax.rsqrt(jnp.mean(values * values, axis=-1, keepdims=True) + EPS)


def norm_back(upstream, normed, scaling):
    return scaling * (upstream - normed * jnp.mean(upstream * normed, axis=-1, keepdims=True))


def rotary_tables(first, z, c):
    half = DH // 2
    k = jnp.arange(4, dtype=jnp.int32)
    starts = jnp.concatenate([((z + k) % 4) * 256 + c * 128, ((z + k) % 4) * 256 + (1 - c) * 128])
    places = (first + starts[:, None] + jnp.arange(128, dtype=jnp.int32)[None, :]).reshape(1024)
    inverse = THETA ** (-(jnp.arange(half, dtype=F32) * (2.0 / DH)))
    angles = places.astype(F32)[:, None] * inverse[None, :]
    cosine, sine = jnp.cos(angles), jnp.sin(angles)
    return (
        jnp.concatenate([cosine, cosine], axis=-1),
        jnp.concatenate([-sine, sine], axis=-1),
    )


def dot(a, b):
    return jnp.dot(a, b, preferred_element_type=F32)


def dot_nt(a, b):
    return lax.dot_general(a, b, NT, preferred_element_type=F32)


def dot_tn(a, b):
    return lax.dot_general(a, b, (((0,), (0,)), ((), ())), preferred_element_type=F32)


def on_device(
    tokens, out_grad, w_query, w_key, w_value, w_out, w_gate, w_up, w_down,
    gain_query, gain_key, gain_attn, gain_mlp,
):
    seq = lax.axis_index("seq")
    xh, zc = seq // 8, seq % 8
    z, c = zc // 2, zc % 2
    quarter = (z % 2) * 2 + c
    place = jnp.stack([xh, z, c]).astype(jnp.int32)
    inputs = tokens[0]

    def columns(weight, width):
        return lax.dynamic_slice_in_dim(weight, zc * width, width, 1)

    def spread(block):
        return lax.all_to_all(
            jnp.broadcast_to(block[None], (8,) + block.shape),
            "fsdp", split_axis=0, concat_axis=0, tiled=True,
        ).reshape(8 * block.shape[0], block.shape[1])

    x_blocks = gather_group(inputs)
    weight = spread(
        jnp.concatenate(
            [columns(w_query, 256), columns(w_key, 128), columns(w_value, 128)], axis=1
        )
    )
    w_out_rows = lax.ppermute(
        after(lax.dynamic_slice_in_dim(w_out, zc * 32, 32, 0), weight),
        ("seq", "fsdp"),
        TURN,
    )

    def quarters(weight):
        part = lax.dynamic_slice_in_dim(weight.reshape(128, 8, 384), quarter * 96, 96, 2)
        return part.reshape(128, 768)

    down = lax.dynamic_slice_in_dim(w_down, quarter * 96, 96, 0)
    packed = jnp.concatenate(
        [
            down[:, :768],
            jnp.concatenate([down[m * 32 : m * 32 + 32, 768:] for m in range(3)], axis=1),
        ],
        axis=0,
    )
    w_narrow = lax.all_gather(packed, "fsdp", axis=0, tiled=True)
    w_wide = jnp.concatenate([quarters(w_gate), quarters(w_up)], axis=1)
    weight, w_wide = lax.optimization_barrier((weight, w_wide))

    cosine, sine = rotary_tables(xh * 1024, z, c)
    gain_q = lax.dynamic_slice_in_dim(gain_query, zc * 256, 256, 0)[None]
    gain_k = lax.dynamic_slice_in_dim(gain_key, zc * 128, 128, 0)[None]
    x_all, q_raw, k_raw, q_rot, kv_rot, squares = kernel_call(
        project_body,
        [
            *in_hbm(
                0, shaped((1024, 256), F32), shaped((1024, 128), F32),
                shaped((1024, 256), BF16), shaped((1024, 256), BF16),
            ),
            shaped((16, 128), F32),
        ],
        [x_blocks, weight, gain_q, gain_k, cosine, sine],
        flops=2 * 1024 * 1024 * 512, nbytes=9 << 20,
    )

    kv_low = swap(kv_rot, LOW_TO_HIGH)
    squares = sum_group(squares)
    squares_low = swap(squares[8:], LOW_TO_HIGH)
    kv_low, squares, squares_low, w_wide, w_narrow, w_out_rows = lax.optimization_barrier(
        (kv_low, squares, squares_low, w_wide, w_narrow, w_out_rows)
    )
    w_wide = lax.all_gather(w_wide, "fsdp", axis=0, tiled=True)
    w_out_rows = spread(w_out_rows)
    out_raw, mixed, mixed_turned, q_tiles, keys, vals, logs = kernel_call(
        attend_body,
        [
            *in_hbm(
                shaped((1024, 256), F32), shaped((1024, 256), BF16), shaped((256, 1024), BF16),
                shaped((8, 256, 128), BF16), shaped((2048, 128), BF16), shaped((2048, 128), BF16),
            ),
            shaped((8, 256), F32),
        ],
        [place, *in_hbm(q_rot, kv_rot), kv_low, squares, squares_low],
        [pltpu.VMEM((128, 2048), BF16)],
        flops=4 * 1024 * 2048 * 256, nbytes=9 << 20,
    )
    a_mine, a_part = kernel_call(
        output_body,
        [shaped((512, 1024), F32), shaped((512, 1024), BF16)],
        [*in_hbm(mixed), w_out_rows],
        flops=2 * 1024 * 1024 * 256, nbytes=5 << 20,
    )
    n = jnp.arange(1024, dtype=jnp.int32)
    source = ((n // 8) % 16) * 64 + (n // 128) * 8 + n % 8
    order = (n[None, :] == source[:, None]).astype(BF16)
    x_turned = dot_nt(order, x_all).astype(BF16)

    attended = scatter_group(a_mine, a_part)
    attended, x_turned = lax.optimization_barrier((attended, x_turned))
    attn_scale = norm_scale(attended)
    attn_hat = attended * attn_scale
    hidden_state = inputs.astype(F32) + attn_hat * gain_attn
    h_all, gate, up, expanded, m_mine, m_part, w_down_rows = kernel_call(
        expand_body,
        [
            0, shaped((512, 768), F32), shaped((512, 768), F32), shaped((512, 768), BF16),
            shaped((256, 1024), F32), shaped((256, 1024), BF16), shaped((768, 1024), BF16),
        ],
        [
            gather_pair(hidden_state.astype(BF16)), *in_hbm(w_wide, w_narrow),
        ],
        flops=2 * 512 * 2304 * 1024, nbytes=12 << 20,
    )
    projected, _ = scatter_pair(m_mine, m_part)
    mlp_scale = norm_scale(projected)
    mlp_hat = projected * mlp_scale
    output = (hidden_state + mlp_hat * gain_mlp).astype(BF16)[None]

    upstream = out_grad[0].astype(F32)
    grad_gain_mlp = jnp.sum(upstream * mlp_hat, axis=0)
    d_projected = norm_back(upstream * gain_mlp, mlp_hat, mlp_scale).astype(BF16)
    h_turned = dot_nt(order, h_all).astype(BF16)
    d_blocks = gather_pair(d_projected)
    d_blocks[3], h_turned = lax.optimization_barrier((d_blocks[3], h_turned))
    dm_all, d_gu, dh_mine, dh_part = kernel_call(
        expand_back_body,
        [
            0, shaped((512, 1536), BF16), shaped((256, 1024), F32), shaped((256, 1024), BF16),
        ],
        [d_blocks, gate, up, w_wide, w_down_rows],
        flops=2 * 512 * 2304 * 1024, nbytes=12 << 20,
    )

    far = dh_mine[128:] + swap(dh_part[128:], CORE_SWAP).astype(F32)
    far, d_gu, dm_all = lax.optimization_barrier((far.astype(BF16), d_gu, dm_all))
    far = swap(far, Z_SWAP)
    (grad_mlp,) = kernel_call(
        expand_grad_body,
        in_hbm(shaped((1024, 2304), BF16)),
        [h_turned, d_gu, expanded, dm_all],
        [pltpu.VMEM((768, 512), BF16)],
        flops=2 * 512 * 2304 * 1024, nbytes=9 << 20,
    )
    far, grad_mlp = lax.optimization_barrier((far, grad_mlp))
    grad_mlp = lax.psum_scatter(grad_mlp, "fsdp", scatter_dimension=0, tiled=True)
    d_hidden = upstream + dh_mine[:128] + swap(dh_part[:128], CORE_SWAP).astype(F32)
    d_hidden = d_hidden + far.astype(F32)

    grad_gain_attn = jnp.sum(d_hidden * attn_hat, axis=0)
    d_attended = norm_back(d_hidden * gain_attn, attn_hat, attn_scale).astype(BF16)
    d_tiles, deltas, grad_out = kernel_call(
        output_back_body,
        [shaped((8, 256, 128), BF16), shaped((8, 2, 128), F32), shaped((256, 1024), BF16)],
        [place, *in_hbm(out_raw, w_out_rows, gather_group(d_attended), mixed_turned)],
        flops=4 * 1024 * 1024 * 256, nbytes=6 << 20,
    )
    fsdp = lax.axis_index("fsdp")

    def halve(value, rows, bit, axis, pairs):
        parts = value.reshape(-1, 2, rows, 1024)
        given = jnp.where(bit == 1, parts[:, 0], parts[:, 1])
        mine = jnp.where(bit == 1, parts[:, 1], parts[:, 0]).astype(F32)
        return (mine + lax.ppermute(given, axis, pairs).astype(F32)).astype(BF16)

    grad_out = halve(grad_out, 32, fsdp % 2, "fsdp", [(i, i ^ 1) for i in range(8)])
    dq, dk, dv, d_low, dots = kernel_call(
        attend_back_body,
        [
            *in_hbm(
                shaped((1024, 256), BF16), shaped((1024, 128), F32), shaped((1024, 128), F32),
                shaped((1024, 256), BF16),
            ),
            shaped((24, 128), F32),
        ],
        [place, *in_hbm(q_tiles, keys, vals), logs, d_tiles, deltas],
        [
            pltpu.VMEM((128, 2048), BF16), pltpu.VMEM((2048, 128), F32),
            pltpu.VMEM((2048, 128), F32),
        ],
        flops=10 * 1024 * 2048 * 256, nbytes=8 << 20,
    )
    dots, grad_out = lax.optimization_barrier((dots, grad_out))
    grad_out = halve(grad_out, 32, fsdp // 2 % 2, "fsdp", [(i, i ^ 2) for i in range(8)])
    grad_out = halve(grad_out, 32, fsdp // 4, "fsdp", [(i, i ^ 4) for i in range(8)])
    d_got = swap(d_low, HIGH_TO_LOW)
    dots = sum_group(dots)
    dots_got = swap(dots[16:], HIGH_TO_LOW)

    gains = jnp.concatenate([grad_gain_attn.reshape(128, 8), grad_gain_mlp.reshape(128, 8)], axis=1)
    gains = gains.reshape(16, 8, 16).swapaxes(0, 1).reshape(128, 16)
    gains = jnp.broadcast_to(
        jnp.pad(gains.astype(BF16), ((0, 0), (24, 88)))[:, None, :], (128, 8, 128)
    ).reshape(1024, 128)
    d_made, sent = kernel_call(
        unproject_body,
        [*in_hbm(shaped((1024, 512), BF16)), shaped((1024, 640), BF16)],
        [
            place, *in_hbm(dq, dk, dv), d_got, *in_hbm(q_raw, k_raw), squares, dots, dots_got, cosine, sine,
            gain_q, gain_k, *in_hbm(x_turned), gains,
        ],
        [pltpu.VMEM((8, 384), F32)],
        flops=2 * 1024 * 1024 * 512, nbytes=9 << 20,
    )

    def halves(value, upper):
        low, high = value[: value.shape[0] // 2], value[value.shape[0] // 2 :]
        return jnp.where(upper, high, low), jnp.where(upper, low, high)

    mine, given = halves(grad_mlp, xh == 1)
    mine = mine.astype(F32) + swap(given, X_SWAP).astype(F32)
    sent, grad_out = lax.optimization_barrier((sent, grad_out))
    grad_mlp = after(grad_mlp, sent)
    grad_down = jnp.concatenate(
        [
            piece
            for h in (0, 64)
            for piece in [
                jnp.concatenate(
                    [
                        grad_mlp[h : h + 48, 1536:],
                        jnp.concatenate(
                            [
                                grad_mlp[h + 48 : h + 64, 1536 + m * 256 : 1792 + m * 256]
                                for m in range(3)
                            ],
                            axis=0,
                        ),
                    ],
                    axis=1,
                )
            ]
        ],
        axis=0,
    ).reshape(4, 24, 1024)
    grad_down = sum(
        lax.ppermute(
            lax.dynamic_index_in_dim(grad_down, (xh * 2 + z // 2) ^ other, 0, keepdims=False),
            ("seq", "fsdp"),
            down_home(other),
        ).astype(F32)
        for other in range(4)
    )
    got_made = lax.all_to_all(
        sent.reshape(8, 128, 640), "fsdp", split_axis=0, concat_axis=0, tiled=True
    )
    dx_mine, dx_part = kernel_call(
        input_body,
        in_hbm(shaped((512, 1024), F32), shaped((512, 1024), BF16)),
        [*in_hbm(after(d_made, sent)), weight],
        flops=2 * 1024 * 1024 * 512, nbytes=5 << 20,
    )
    rows = [slice(k * 128, k * 128 + 128) for k in range(4)]
    pieces = [dx_mine[r] + swap(dx_part[r], CORE_SWAP).astype(F32) for r in rows]
    far = [piece.astype(BF16) for piece in pieces[1:]]
    (collected,) = kernel_call(
        collect_body,
        [shaped((128, 2176), BF16)],
        [got_made.reshape(1024, 640), grad_mlp],
        flops=WAIT_FLOPS, nbytes=3 << 20,
    )
    got = lax.all_to_all(
        collected.reshape(16, 8, 2176), "seq", split_axis=0, concat_axis=0, tiled=True
    )
    grad_out = grad_out.reshape(2, 16, 1024)
    own = jnp.where(xh == 1, grad_out[1], grad_out[0])
    given = jnp.where(xh == 1, grad_out[0], grad_out[1])
    own = swap(own, out_home(False))
    grad_out = own.astype(F32) + swap(given, out_home(True)).astype(F32)
    d_inputs = pieces[0] + sum(
        swap(piece, to_z(k)).astype(F32) for k, piece in enumerate(far, 1)
    )
    got = got.reshape(2, 8, 8, 2176).astype(F32)
    summed = got[0, :, :, :640] + got[1, :, :, :640]
    gains = jnp.sum(summed[:, 0, 512:], axis=0)

    def take(first, width):
        return summed[:, :, first : first + width].swapaxes(0, 1).reshape(8, 8 * width)

    wide = jnp.sum(got[:, :, :, 640:].reshape(2, 2, 4, 8, 2, 8, 96), axis=(0, 1))
    wide = wide.transpose(2, 1, 3, 0, 4).reshape(2, 8, 3072)
    return (
        output,
        (d_hidden + d_inputs).astype(BF16)[None],
        take(0, 256),
        take(256, 128),
        take(384, 128),
        grad_out.astype(F32),
        wide[0],
        wide[1],
        grad_down.astype(F32),
        gains[:16],
        gains[16:24],
        gains[24:32],
        gains[32:40],
    )


def solution(mesh):
    rows = P("fsdp", "seq", None)
    weight = P("fsdp", None)
    grad = P(("seq", "fsdp"), None)
    gain = P(("seq", "fsdp"))
    return jax.shard_map(
        on_device,
        mesh=mesh,
        in_specs=(rows,) * 2 + (weight,) * 7 + (P(),) * 4,
        out_specs=(rows,) * 2 + (grad,) * 7 + (gain,) * 4,
        check_vma=False,
    )
```

```python
import functools
import math

import jax
import jax.numpy as jnp
from jax import lax
from jax.experimental import pallas as pl
from jax.experimental.pallas import tpu as pltpu
from jax.sharding import PartitionSpec as P

BF16 = jnp.bfloat16
F32 = jnp.float32
DH = 128
EPS = 1e-06
THETA = 1000000.0
MASKED = -1e30
LOG2E = math.log2(math.e)
QUERY_SCALE = DH ** (-0.5) * LOG2E
VMEM_BYTES = 20 * 1024 * 1024
VMEM = pl.BlockSpec(memory_space=pltpu.VMEM)
SMEM = pl.BlockSpec(memory_space=pltpu.SMEM)
ANY = pl.BlockSpec(memory_space=pl.ANY)
SMALL = 64 * 1024
WAIT_FLOPS = 12 * 10**9
NT = (((1,), (1,)), ((), ()))

SEQ_PLACES = [(xh, z, c) for xh in range(2) for z in range(4) for c in range(2)]


def seq_index(xh, z, c):
    return xh * 8 + (z % 4) * 2 + c


CORE_SWAP = [(i, i ^ 1) for i in range(16)]
LOW_TO_HIGH = [(i, i + 8) for i in range(8)]
HIGH_TO_LOW = [(i + 8, i) for i in range(8)]
X_SWAP = [(i, i ^ 8) for i in range(16)]


def from_z(k):
    return [(seq_index(xh, z + k, c), seq_index(xh, z, c)) for xh, z, c in SEQ_PLACES]


def to_z(k):
    return [(seq_index(xh, z, c), seq_index(xh, z + k, c)) for xh, z, c in SEQ_PLACES]


def across(pairs):
    return [(seq * 8 + f, to_seq * 8 + to_f) for seq, f, to_seq, to_f in pairs]


TURN = across(
    (xh * 8 + a, f, xh * 8 + f, a) for xh in range(2) for a in range(8) for f in range(8)
)
Z_SWAP = [(i, i ^ 2) for i in range(16)]
FAR_SWAP = [(i, i ^ 4) for i in range(16)]


def out_home(other):
    return [(xh * 8 + a, 2 * a + (xh ^ other)) for xh in range(2) for a in range(8)]


def down_home(other):
    return across(
        (seq_index(own // 2, 2 * (own % 2) + zl, c), f, 2 * f + zl, 4 * c + (own ^ other))
        for own in range(4) for zl in range(2) for c in range(2) for f in range(8)
    )


def swap(value, pairs):
    return lax.ppermute(value, "seq", pairs)


def after(value, *others):
    return lax.optimization_barrier((value, *others))[0]


def gather_group(block):
    far = {k: swap(block, from_z(k)) for k in (2, 1, 3)}
    mine = [block, far[1], far[2], far[3]]
    return mine + [swap(v, CORE_SWAP) for v in mine]


def scatter_group(mine, part):
    rows = [slice(k * 128, k * 128 + 128) for k in range(4)]
    out = None
    for k in (2, 1, 3, 0):
        piece = mine[rows[k]] + swap(part[rows[k]], CORE_SWAP).astype(F32)
        if k:
            piece = swap(piece.astype(BF16), to_z(k)).astype(F32)
        out = piece if out is None else out + piece
    return out


def gather_pair(block):
    mine = [block, swap(block, Z_SWAP)]
    return mine + [swap(v, CORE_SWAP) for v in mine]


def scatter_pair(mine, part, later=()):
    far = mine[128:] + swap(part[128:], CORE_SWAP).astype(F32)
    far, *later = lax.optimization_barrier((far.astype(BF16), *later))
    far = swap(far, Z_SWAP).astype(F32)
    return mine[:128] + swap(part[:128], CORE_SWAP).astype(F32) + far, later


def sum_group(rows):
    groups = rows.shape[0] // 8
    other = swap(rows, CORE_SWAP).reshape(groups, 2, 4, 128)
    pair = rows.reshape(groups, 2, 4, 128) + jnp.concatenate([other[:, 1:], other[:, :1]], axis=1)
    odd = lax.axis_index("seq") // 2 % 2 == 1
    got = swap(pair, Z_SWAP)
    up = jnp.concatenate([got[:, :, 3:], got[:, :, :3]], axis=2)
    down = jnp.concatenate([got[:, :, 1:], got[:, :, :1]], axis=2)
    pair = pair + jnp.where(odd, down, up)
    got = swap(pair, FAR_SWAP)
    pair = pair + jnp.concatenate([got[:, :, 2:], got[:, :, :2]], axis=2)
    return pair.reshape(rows.shape)


def column(row):
    return jnp.transpose(jnp.broadcast_to(row, (128, 128)))


def row_sums(values):
    return jnp.sum(jnp.transpose(values), axis=0, keepdims=True)


def shaped(shape, dtype):
    return jax.ShapeDtypeStruct(shape, dtype)


class Kept:
    def __init__(self, value):
        self.value = value


def in_hbm(*values):
    return [Kept(v) for v in values]


def kernel_call(body, outs, inputs, scratch=(), flops=0, nbytes=0):
    hbm_outs = [isinstance(o, Kept) for o in outs]
    hbm_ins = [isinstance(x, Kept) for x in inputs]
    outs = [o.value if isinstance(o, Kept) else o for o in outs]
    inputs = [x.value if isinstance(x, Kept) else x for x in inputs]
    groups = [x if isinstance(x, list) else [x] for x in inputs]
    flat = [a for group in groups for a in group]
    joined = [
        shaped((sum(a.shape[0] for a in group),) + group[0].shape[1:], group[0].dtype)
        for group in groups
    ]

    def large(s):
        return math.prod(s.shape) * s.dtype.itemsize >= SMALL

    def where(s):
        return ANY if large(s) else SMEM if s.dtype == jnp.int32 else VMEM

    out_shapes = [joined[o] if isinstance(o, int) else o for o in outs]
    in_buffers = [pltpu.VMEM(s.shape, s.dtype) for s in joined if large(s)]
    out_buffers = [
        pltpu.VMEM(o.shape, o.dtype) for o in outs if not isinstance(o, int) and large(o)
    ]

    def whole(*refs):
        refs = list(refs)

        def pull(count):
            taken = refs[:count]
            del refs[:count]
            return taken

        in_refs, out_refs = pull(len(flat)), pull(len(outs))
        in_space, out_space = pull(len(in_buffers)), pull(len(out_buffers))
        own, (in_sem, out_sem) = pull(len(scratch)), refs
        loads, ins, at = {}, [], 0
        for group, s in zip(groups, joined):
            if not large(s):
                ins.append(in_refs[at])
                at += 1
                continue
            space, row = in_space.pop(0), 0
            loads[id(space)] = []
            for a in group:
                copy = pltpu.make_async_copy(
                    in_refs[at], space.at[pl.ds(row, a.shape[0])], in_sem.at[at]
                )
                copy.start()
                loads[id(space)].append(copy)
                row, at = row + a.shape[0], at + 1
            ins.append(space)
        made, stores = [], {}
        for k, (o, s, ref) in enumerate(zip(outs, out_shapes, out_refs)):
            if not large(s):
                made.append(ref)
                continue
            space = ins[o] if isinstance(o, int) else out_space.pop(0)
            stores[id(space)] = pltpu.make_async_copy(space, ref, out_sem.at[k])
            if not isinstance(o, int):
                made.append(space)
        started = []

        def ready(*spaces):
            for space in spaces:
                for copy in loads.pop(id(space), ()):
                    copy.wait()

        def done(*spaces):
            for space in spaces:
                copy = stores.pop(id(space))
                copy.start()
                started.append(copy)

        body(ready, done, *ins, *made, *own)
        for key in list(stores):
            copy = stores.pop(key)
            copy.start()
            started.append(copy)
        for copy in started:
            copy.wait()

    shapes = [pltpu.HBM(s.shape, s.dtype) if hbm else s for s, hbm in zip(out_shapes, hbm_outs)]
    return pl.pallas_call(
        whole,
        out_shape=tuple(shapes),
        in_specs=[where(s) for group, s in zip(groups, joined) for _ in group],
        out_specs=tuple(where(s) for s in out_shapes),
        scratch_shapes=[
            *in_buffers, *out_buffers, *scratch,
            pltpu.SemaphoreType.DMA((len(flat),)), pltpu.SemaphoreType.DMA((len(outs),)),
        ],
        compiler_params=pltpu.CompilerParams(vmem_limit_bytes=VMEM_BYTES),
        cost_estimate=pl.CostEstimate(flops=flops, bytes_accessed=nbytes, transcendentals=0),
    )(
        *[
            pltpu.with_memory_space_constraint(a, pltpu.HBM) if hbm else a
            for group, hbm in zip(groups, hbm_ins)
            for a in group
        ],
    )


def root(total, width):
    return lax.rsqrt(total * (1.0 / width) + EPS)


def project_body(
    ready, done, x_all, weight, gain_q, gain_k, cos, sin,
    q_raw, k_raw, q_rot, kv_rot, squares,
):
    ready(x_all, weight, cos, sin)
    done(x_all)

    def step(t, carry):
        at = pl.multiple_of(t * 256, 256)
        made = jnp.dot(x_all[pl.ds(at, 256), :], weight[...], preferred_element_type=F32)
        for part in range(2):
            rows = pl.ds(at + part * 128, 128)
            block = t * 2 + part
            here = made[part * 128 : part * 128 + 128]
            q, k = here[:, :256], here[:, 256:384]
            kv_rot[rows, 128:] = here[:, 384:].astype(BF16)
            q_raw[rows, :] = q
            k_raw[rows, :] = k
            squares[pl.ds(block, 1), :] = row_sums(
                q[:, :128] * q[:, :128] + q[:, 128:] * q[:, 128:]
            )
            squares[pl.ds(block + 8, 1), :] = row_sums(k * k)
            cosine, sine = cos[rows, :], sin[rows, :]
            for head in range(2):
                lanes = slice(head * 128, head * 128 + 128)
                turn = q[:, lanes] * gain_q[:, lanes]
                q_rot[rows, lanes] = (turn * cosine + pltpu.roll(turn, 64, 1) * sine).astype(BF16)
            turn = k * gain_k[...]
            kv_rot[rows, :128] = (turn * cosine + pltpu.roll(turn, 64, 1) * sine).astype(BF16)
        return carry

    lax.fori_loop(0, 4, step, 0)


def spot(place, block):
    z = lax.rem(place[1] + block % 4, 4)
    c = place[2] if block < 4 else 1 - place[2]
    return z, c


def diagonal():
    query = lax.broadcasted_iota(jnp.int32, (256, 512), 1) % 256
    return lax.broadcasted_iota(jnp.int32, (256, 512), 0) <= query


def attend_body(
    ready, done, place, q_rot, kv_rot, kv_low, squares, squares_low,
    out_raw, out_low, out_turned, q_tiles, keys, vals, logs, vals_t,
):
    ready(q_rot, kv_rot, kv_low)
    for b in range(8):
        rows = slice(b * 128, b * 128 + 128)
        z, c = spot(place, b)
        r = column(root(squares[b : b + 1, :], 2048.0)) * QUERY_SCALE
        inner = pl.ds(pl.multiple_of(c * 128, 128), 128)
        for head in range(2):
            q = q_rot[rows, head * 128 : head * 128 + 128].astype(F32)
            q_tiles[z * 2 + head, inner, :] = (q * r).astype(BF16)
        at = pl.ds(pl.multiple_of(1024 + z * 256 + c * 128, 128), 128)
        r = column(root(squares[8 + b : 9 + b, :], 1024.0))
        keys[at, :] = (kv_rot[rows, :128].astype(F32) * r).astype(BF16)
        vals[at, :] = kv_rot[rows, 128:]
        r = column(root(squares_low[b : b + 1, :], 1024.0))
        keys[rows, :] = (kv_low[rows, :128].astype(F32) * r).astype(BF16)
        vals[rows, :] = kv_low[rows, 128:]
    done(q_tiles, keys, vals)
    vals_t[...] = jnp.transpose(vals[...].astype(F32)).astype(BF16)

    def queries(first, i):
        at_diagonal = 1024 + i * 256
        q = q_tiles[i * 2 : i * 2 + 2].reshape(512, 128)
        ranges = [(lo, lo + 256) for lo in range(first, at_diagonal + 256, 256)]
        scores = [
            lax.dot_general(keys[lo:hi, :], q, NT, preferred_element_type=F32) for lo, hi in ranges
        ]
        scores[-1] = jnp.where(diagonal(), scores[-1], MASKED)
        top = functools.reduce(jnp.maximum, [jnp.max(s, axis=0, keepdims=True) for s in scores])
        total, acc = 0.0, 0.0
        for s, (lo, hi) in zip(scores, ranges):
            p = jnp.exp2(s - top)
            total = total + jnp.sum(p, axis=0, keepdims=True)
            acc = acc + jnp.dot(vals_t[:, lo:hi], p.astype(BF16), preferred_element_type=F32)
        acc = acc / total
        log = top + jnp.log2(total)
        for head in range(2):
            turned = acc[:, head * 256 : head * 256 + 256]
            out = jnp.transpose(turned)
            turned = turned.astype(BF16)
            logs[i * 2 + head : i * 2 + head + 1, :] = log[:, head * 256 : head * 256 + 256]
            for c in range(2):
                block = lax.rem(i - place[1] + 4, 4) + 4 * jnp.abs(c - place[2])
                at = pl.ds(pl.multiple_of(block * 128, 128), 128)
                lanes = slice(head * 128, head * 128 + 128)
                out_raw[at, lanes] = out[c * 128 : c * 128 + 128, :]
                out_low[at, lanes] = out[c * 128 : c * 128 + 128, :].astype(BF16)
                out_turned[lanes, at] = turned[:, c * 128 : c * 128 + 128]

    @pl.when(place[0] == 1)
    def _():
        for i in range(4):
            queries(0, i)

    @pl.when(place[0] == 0)
    def _():
        for i in range(4):
            queries(1024, i)

    done(out_raw, out_low, out_turned)


def output_body(ready, done, place, mixed, w_own, w_got, a_mine, a_part, w_out):
    ready(w_own, w_got)
    w_out[pl.ds(pl.multiple_of(place[3] * 128, 128), 128), :] = w_own[...]
    w_out[pl.ds(pl.multiple_of((1 - place[3]) * 128, 128), 128), :] = w_got[...]
    done(w_out)
    ready(mixed)

    def project(t, carry):
        at = pl.ds(pl.multiple_of(t * 256, 256), 256)
        far = pl.ds(pl.multiple_of(512 + t * 256, 256), 256)
        a_part[at, :] = jnp.dot(mixed[far, :], w_out[...], preferred_element_type=F32).astype(BF16)
        a_mine[at, :] = jnp.dot(mixed[at, :], w_out[...], preferred_element_type=F32)
        return carry

    lax.fori_loop(0, 2, project, 0)


def output_back_body(
    ready, done, place, out_raw, w_out, da_all, mixed_turned, d_tiles, deltas, grad_out
):
    ready(out_raw, w_out, da_all)
    for b in range(8):
        rows = slice(b * 128, b * 128 + 128)
        z, c = spot(place, b)
        inner = pl.ds(pl.multiple_of(c * 128, 128), 128)
        d_out = lax.dot_general(
            da_all[rows, :], w_out[...], NT, preferred_element_type=F32
        ).astype(BF16)
        for head in range(2):
            lanes = slice(head * 128, head * 128 + 128)
            grad = d_out[:, lanes]
            d_tiles[z * 2 + head, inner, :] = grad
            deltas[z * 2 + head, pl.ds(c, 1), :] = row_sums(grad.astype(F32) * out_raw[rows, lanes])
    done(d_tiles)
    ready(mixed_turned)
    for m in range(4):
        lanes = slice(m * 256, m * 256 + 256)
        made = jnp.dot(mixed_turned[...], da_all[:, lanes], preferred_element_type=F32).astype(BF16)
        for j in range(2):
            for f in range(8):
                to, at = f * 32 + j * 16, j * 128 + f * 16
                grad_out[to : to + 16, lanes] = made[at : at + 16]


def attend_back_body(
    ready, done, place, q_tiles, keys, vals, logs, d_tiles, deltas,
    dq, dk, dv, d_low, dots, keys_t, dk_acc, dv_acc,
):
    ready(keys)
    keys_t[...] = jnp.transpose(keys[...].astype(F32)).astype(BF16)
    dk_acc[...] = jnp.zeros_like(dk_acc)
    dv_acc[...] = jnp.zeros_like(dv_acc)
    ready(q_tiles, vals, d_tiles)

    def queries(first, i):
        at_diagonal = 1024 + i * 256
        q = q_tiles[i * 2 : i * 2 + 2].reshape(512, 128)
        grad = d_tiles[i * 2 : i * 2 + 2].reshape(512, 128)
        log = jnp.concatenate([logs[i * 2 : i * 2 + 1, :], logs[i * 2 + 1 : i * 2 + 2, :]], axis=1)
        delta = jnp.concatenate(
            [deltas[i * 2 + head, c : c + 1, :] for head in range(2) for c in range(2)], axis=1
        )
        total = 0.0
        for lo in range(first, at_diagonal + 256, 256):
            at = slice(lo, lo + 256)
            k, v = keys[at, :], vals[at, :]
            s = lax.dot_general(k, q, NT, preferred_element_type=F32)
            p = jnp.exp2(s - log)
            if lo == at_diagonal:
                p = jnp.where(diagonal(), p, 0.0)
            dp = lax.dot_general(v, grad, NT, preferred_element_type=F32)
            ds = (p * (dp - delta)).astype(BF16)
            dv_acc[at, :] += jnp.dot(p.astype(BF16), grad, preferred_element_type=F32)
            dk_acc[at, :] += jnp.dot(ds, q, preferred_element_type=F32)
            total = total + jnp.dot(keys_t[:, at], ds, preferred_element_type=F32)
        dot = total * jnp.transpose(q.astype(F32))
        dot = jnp.sum(dot[:, :256] + dot[:, 256:], axis=0, keepdims=True)
        for head in range(2):
            out = jnp.transpose(total[:, head * 256 : head * 256 + 256]) * DH ** (-0.5)
            for c in range(2):
                block = lax.rem(i - place[1] + 4, 4) + 4 * jnp.abs(c - place[2])
                at = pl.ds(pl.multiple_of(block * 128, 128), 128)
                dq[at, head * 128 : head * 128 + 128] = out[c * 128 : c * 128 + 128, :].astype(BF16)
        for c in range(2):
            block = lax.rem(i - place[1] + 4, 4) + 4 * jnp.abs(c - place[2])
            dots[pl.ds(block, 1), :] = dot[:, c * 128 : c * 128 + 128] * (1.0 / LOG2E)

    @pl.when(place[0] == 1)
    def _():
        for i in range(4):
            queries(0, i)

    @pl.when(place[0] == 0)
    def _():
        for i in range(4):
            queries(1024, i)

    done(dq)
    for b in range(8):
        rows = slice(b * 128, b * 128 + 128)
        z, c = spot(place, b)
        at = pl.ds(pl.multiple_of(1024 + z * 256 + c * 128, 128), 128)
        key_grad = dk_acc[at, :] * (1.0 / LOG2E)
        dk[rows, :] = key_grad
        dv[rows, :] = dv_acc[at, :]
        dots[8 + b : 9 + b, :] = row_sums(key_grad * keys[at, :].astype(F32))
        key_grad = dk_acc[rows, :] * (1.0 / LOG2E)
        d_low[rows, :128] = key_grad.astype(BF16)
        d_low[rows, 128:] = dv_acc[rows, :].astype(BF16)
        dots[16 + b : 17 + b, :] = row_sums(key_grad * keys[rows, :].astype(F32))


def unproject_body(
    ready, done, place, dq, dk, dv, d_got, q_raw, k_raw, squares, dots, dots_got, cos, sin,
    gain_q, gain_k, x_turned, gains, d_made, sent, sums,
):
    sums[...] = jnp.zeros_like(sums)
    ready(dq, dk, dv, d_got, q_raw, k_raw, cos, sin)

    def step(b, carry):
        rows = pl.ds(pl.multiple_of(b * 128, 128), 128)
        cosine, sine = cos[rows, :], sin[rows, :]
        r = column(root(squares[pl.ds(b, 1), :], 2048.0))
        mean = column(dots[pl.ds(b, 1), :]) * (1.0 / 2048.0)
        for head in range(2):
            lanes = slice(head * 128, head * 128 + 128)
            turn = dq[rows, lanes].astype(F32)
            d_norm = turn * cosine - pltpu.roll(turn, 64, 1) * sine
            hat = q_raw[rows, lanes] * r
            sums[0:1, lanes] += jnp.sum(d_norm * hat, axis=0, keepdims=True)
            d_made[rows, lanes] = (r * (d_norm * gain_q[:, lanes] - hat * mean)).astype(BF16)
        r = column(root(squares[pl.ds(b + 8, 1), :], 1024.0))
        mean = column(dots[pl.ds(b + 8, 1), :] + dots_got[pl.ds(b, 1), :]) * (1.0 / 1024.0)
        turn = dk[rows, :] + d_got[rows, :128].astype(F32)
        d_norm = turn * cosine - pltpu.roll(turn, 64, 1) * sine
        hat = k_raw[rows, :] * r
        sums[0:1, 256:] += jnp.sum(d_norm * hat, axis=0, keepdims=True)
        d_made[rows, 256:384] = (r * (d_norm * gain_k[...] - hat * mean)).astype(BF16)
        d_made[rows, 384:] = (dv[rows, :] + d_got[rows, 128:].astype(F32)).astype(BF16)
        return carry

    lax.fori_loop(0, 8, step, 0)
    done(d_made)
    ready(x_turned, gains)

    def grad(t, carry):
        rows = pl.ds(pl.multiple_of(t * 256, 256), 256)
        sent[rows, :512] = jnp.dot(
            x_turned[rows, :], d_made[...], preferred_element_type=F32
        ).astype(BF16)
        sent[rows, 512:] = gains[rows, :]
        return carry

    lax.fori_loop(0, 4, grad, 0)
    extra = 0.0
    for lo, width, each, first in ((0, 256, 16, 0), (256, 128, 8, 16)):
        row = lax.broadcasted_iota(jnp.int32, (128, width), 0)
        lane = lax.broadcasted_iota(jnp.int32, (128, width), 1) // each
        here = row // 8 % 2 * 8 + row // 16 == lane
        spread = jnp.where(here, sums[0:1, lo : lo + width], 0.0).astype(BF16)
        lane = lax.broadcasted_iota(jnp.int32, (width, 128), 0) % each + first
        pick = jnp.where(lane == lax.broadcasted_iota(jnp.int32, (width, 128), 1), 1.0, 0.0)
        extra = extra + jnp.dot(spread, pick.astype(BF16), preferred_element_type=F32)
    for f in range(8):
        rows = pl.ds(pl.multiple_of(f * 128 + (place[1] * 2 + place[2]) * 16, 16), 16)
        added = gains[rows, :].astype(F32) + extra[f * 16 : f * 16 + 16]
        sent[rows, 512:] = added.astype(BF16)


def input_body(ready, done, d_made, weight, dx_mine, dx_part):
    ready(d_made, weight)

    def step(t, carry):
        at = pl.ds(pl.multiple_of(t * 256, 256), 256)
        far = pl.ds(pl.multiple_of(512 + t * 256, 256), 256)
        dx_part[at, :] = lax.dot_general(
            d_made[far, :], weight[...], NT, preferred_element_type=F32
        ).astype(BF16)
        dx_mine[at, :] = lax.dot_general(
            d_made[at, :], weight[...], NT, preferred_element_type=F32
        )
        return carry

    lax.fori_loop(0, 2, step, 0)


def expand_body(ready, done, h_all, weight, packed, gate, up, expanded, m_mine, m_part, down):
    ready(h_all, weight)
    done(h_all)
    def widen(n, carry):
        lanes = pl.ds(pl.multiple_of(n * 256, 256), 256)
        upper = pl.ds(pl.multiple_of(768 + n * 256, 256), 256)
        g = jnp.dot(h_all[...], weight[:, lanes], preferred_element_type=F32)
        u = jnp.dot(h_all[...], weight[:, upper], preferred_element_type=F32)
        gate[:, lanes] = g
        up[:, lanes] = u
        expanded[:, lanes] = (g * jax.nn.sigmoid(g) * u).astype(BF16)
        return carry

    lax.fori_loop(0, 3, widen, 0)
    done(gate, up, expanded)
    ready(packed)
    for f in range(8):
        down[f * 96 : f * 96 + 96, :768] = packed[f * 128 : f * 128 + 96, :]
        for m in range(3):
            down[f * 96 + m * 32 : f * 96 + m * 32 + 32, 768:] = packed[
                f * 128 + 96 : f * 128 + 128, m * 256 : m * 256 + 256
            ]
    done(down)

    def narrow(n, carry):
        lanes = pl.ds(pl.multiple_of(n * 256, 256), 256)
        m = jnp.dot(expanded[...], down[:, lanes], preferred_element_type=F32)
        m_mine[:, lanes] = m[:256]
        m_part[:, lanes] = m[256:].astype(BF16)
        return carry

    lax.fori_loop(0, 4, narrow, 0)


def expand_back_body(ready, done, dm_all, gate, up, weight, down, d_gu, dh_mine, dh_part):
    ready(dm_all, gate, up, down)
    done(dm_all)

    def widen(n, carry):
        lanes = pl.ds(pl.multiple_of(n * 256, 256), 256)
        upper = pl.ds(pl.multiple_of(768 + n * 256, 256), 256)
        de = lax.dot_general(dm_all[...], down[lanes, :], NT, preferred_element_type=F32)
        g = gate[:, lanes]
        sig = jax.nn.sigmoid(g)
        d_gu[:, lanes] = (de * up[:, lanes] * sig * (1.0 + g * (1.0 - sig))).astype(BF16)
        d_gu[:, upper] = (de * (g * sig)).astype(BF16)
        return carry

    lax.fori_loop(0, 3, widen, 0)
    done(d_gu)
    ready(weight)

    def narrow(n, carry):
        lanes = pl.ds(pl.multiple_of(n * 256, 256), 256)
        dh = lax.dot_general(d_gu[...], weight[lanes, :], NT, preferred_element_type=F32)
        dh_mine[:, lanes] = dh[:256]
        dh_part[:, lanes] = dh[256:].astype(BF16)
        return carry

    lax.fori_loop(0, 4, narrow, 0)


def expand_grad_body(ready, done, h_turned, d_gu, expanded, dm_all, out, expanded_t):
    ready(expanded)
    expanded_t[...] = jnp.transpose(expanded[...].astype(F32)).astype(BF16)

    ready(h_turned, d_gu, dm_all)

    def widen(n, carry):
        lanes = pl.ds(pl.multiple_of(n * 256, 256), 256)
        out[:, lanes] = jnp.dot(
            h_turned[...], d_gu[:, lanes], preferred_element_type=F32
        ).astype(BF16)
        return carry

    lax.fori_loop(0, 6, widen, 0)
    for n in range(4):
        made = jnp.dot(
            expanded_t[...], dm_all[:, n * 256 : n * 256 + 256], preferred_element_type=F32
        ).astype(BF16)
        for f in range(16):
            if n < 3:
                out[f * 64 : f * 64 + 48, 1536 + n * 256 : 1792 + n * 256] = made[
                    f * 48 : f * 48 + 48
                ]
                continue
            for m in range(3):
                out[f * 64 + 48 : f * 64 + 64, 1536 + m * 256 : 1792 + m * 256] = made[
                    f * 48 + m * 16 : f * 48 + m * 16 + 16
                ]


def collect_body(ready, done, got, grad_mlp, out):
    ready(got)
    total = got[:128, :].astype(F32)
    for f in range(1, 8):
        total = total + got[f * 128 : f * 128 + 128, :].astype(F32)
    out[:, :640] = total.astype(BF16)
    ready(grad_mlp)
    out[:, 640:] = grad_mlp[:, :1536]


def norm_scale(values):
    return lax.rsqrt(jnp.mean(values * values, axis=-1, keepdims=True) + EPS)


def norm_back(upstream, normed, scaling):
    return scaling * (upstream - normed * jnp.mean(upstream * normed, axis=-1, keepdims=True))


def rotary_tables(first, z, c):
    half = DH // 2
    k = jnp.arange(4, dtype=jnp.int32)
    starts = jnp.concatenate([((z + k) % 4) * 256 + c * 128, ((z + k) % 4) * 256 + (1 - c) * 128])
    places = (first + starts[:, None] + jnp.arange(128, dtype=jnp.int32)[None, :]).reshape(1024)
    inverse = THETA ** (-(jnp.arange(half, dtype=F32) * (2.0 / DH)))
    angles = places.astype(F32)[:, None] * inverse[None, :]
    cosine, sine = jnp.cos(angles), jnp.sin(angles)
    return (
        jnp.concatenate([cosine, cosine], axis=-1),
        jnp.concatenate([-sine, sine], axis=-1),
    )


def dot(a, b):
    return jnp.dot(a, b, preferred_element_type=F32)


def dot_nt(a, b):
    return lax.dot_general(a, b, NT, preferred_element_type=F32)


def dot_tn(a, b):
    return lax.dot_general(a, b, (((0,), (0,)), ((), ())), preferred_element_type=F32)


def on_device(
    tokens, out_grad, w_query, w_key, w_value, w_out, w_gate, w_up, w_down,
    gain_query, gain_key, gain_attn, gain_mlp,
):
    seq = lax.axis_index("seq")
    xh, zc = seq // 8, seq % 8
    z, c = zc // 2, zc % 2
    quarter = (z % 2) * 2 + c
    fsdp = lax.axis_index("fsdp")
    place = jnp.stack([xh, z, c, fsdp // 4]).astype(jnp.int32)
    inputs = tokens[0]

    def columns(weight, width):
        return lax.dynamic_slice_in_dim(weight, zc * width, width, 1)

    def spread(block):
        return lax.all_to_all(
            jnp.broadcast_to(block[None], (8,) + block.shape),
            "fsdp", split_axis=0, concat_axis=0, tiled=True,
        ).reshape(8 * block.shape[0], block.shape[1])

    x_blocks = gather_group(inputs)
    weight = spread(
        jnp.concatenate(
            [columns(w_query, 256), columns(w_key, 128), columns(w_value, 128)], axis=1
        )
    )
    w_out_rows = lax.ppermute(
        after(lax.dynamic_slice_in_dim(w_out, zc * 32, 32, 0), weight),
        ("seq", "fsdp"),
        TURN,
    )

    def quarters(weight):
        part = lax.dynamic_slice_in_dim(weight.reshape(128, 8, 384), quarter * 96, 96, 2)
        return part.reshape(128, 768)

    down = lax.dynamic_slice_in_dim(w_down, quarter * 96, 96, 0)
    packed = jnp.concatenate(
        [
            down[:, :768],
            jnp.concatenate([down[m * 32 : m * 32 + 32, 768:] for m in range(3)], axis=1),
        ],
        axis=0,
    )
    w_narrow = lax.all_gather(packed, "fsdp", axis=0, tiled=True)
    w_wide = jnp.concatenate([quarters(w_gate), quarters(w_up)], axis=1)
    weight, w_wide = lax.optimization_barrier((weight, w_wide))

    cosine, sine = rotary_tables(xh * 1024, z, c)
    gain_q = lax.dynamic_slice_in_dim(gain_query, zc * 256, 256, 0)[None]
    gain_k = lax.dynamic_slice_in_dim(gain_key, zc * 128, 128, 0)[None]
    x_all, q_raw, k_raw, q_rot, kv_rot, squares = kernel_call(
        project_body,
        [
            *in_hbm(
                0, shaped((1024, 256), F32), shaped((1024, 128), F32),
                shaped((1024, 256), BF16), shaped((1024, 256), BF16),
            ),
            shaped((16, 128), F32),
        ],
        [x_blocks, weight, gain_q, gain_k, cosine, sine],
        flops=2 * 1024 * 1024 * 512, nbytes=9 << 20,
    )

    kv_low = swap(kv_rot, LOW_TO_HIGH)
    squares = sum_group(squares)
    squares_low = swap(squares[8:], LOW_TO_HIGH)
    for bit in (1, 2):
        got = lax.ppermute(w_out_rows, "fsdp", [(i, i ^ bit) for i in range(8)])
        upper = fsdp // bit % 2 == 1
        w_out_rows = jnp.concatenate(
            [jnp.where(upper, got, w_out_rows), jnp.where(upper, w_out_rows, got)], axis=0
        )
    kv_low, squares, squares_low, w_wide, w_narrow, w_out_rows = lax.optimization_barrier(
        (kv_low, squares, squares_low, w_wide, w_narrow, w_out_rows)
    )
    w_wide = lax.all_gather(w_wide, "fsdp", axis=0, tiled=True)
    w_out_got = lax.ppermute(w_out_rows, "fsdp", [(i, i ^ 4) for i in range(8)])
    out_raw, mixed, mixed_turned, q_tiles, keys, vals, logs = kernel_call(
        attend_body,
        [
            *in_hbm(
                shaped((1024, 256), F32), shaped((1024, 256), BF16), shaped((256, 1024), BF16),
                shaped((8, 256, 128), BF16), shaped((2048, 128), BF16), shaped((2048, 128), BF16),
            ),
            shaped((8, 256), F32),
        ],
        [place, *in_hbm(q_rot, kv_rot), kv_low, squares, squares_low],
        [pltpu.VMEM((128, 2048), BF16)],
        flops=4 * 1024 * 2048 * 256, nbytes=9 << 20,
    )
    a_mine, a_part, w_out_rows = kernel_call(
        output_body,
        [shaped((512, 1024), F32), shaped((512, 1024), BF16), *in_hbm(shaped((256, 1024), BF16))],
        [place, *in_hbm(mixed), w_out_rows, w_out_got],
        flops=2 * 1024 * 1024 * 256, nbytes=5 << 20,
    )
    n = jnp.arange(1024, dtype=jnp.int32)
    source = ((n // 8) % 16) * 64 + (n // 128) * 8 + n % 8
    order = (n[None, :] == source[:, None]).astype(BF16)
    x_turned = dot_nt(order, x_all).astype(BF16)

    attended = scatter_group(a_mine, a_part)
    attended, x_turned = lax.optimization_barrier((attended, x_turned))
    attn_scale = norm_scale(attended)
    attn_hat = attended * attn_scale
    hidden_state = inputs.astype(F32) + attn_hat * gain_attn
    h_all, gate, up, expanded, m_mine, m_part, w_down_rows = kernel_call(
        expand_body,
        [
            0, shaped((512, 768), F32), shaped((512, 768), F32), shaped((512, 768), BF16),
            shaped((256, 1024), F32), shaped((256, 1024), BF16), shaped((768, 1024), BF16),
        ],
        [
            gather_pair(hidden_state.astype(BF16)), *in_hbm(w_wide, w_narrow),
        ],
        flops=2 * 512 * 2304 * 1024, nbytes=12 << 20,
    )
    projected, _ = scatter_pair(m_mine, m_part)
    mlp_scale = norm_scale(projected)
    mlp_hat = projected * mlp_scale
    output = (hidden_state + mlp_hat * gain_mlp).astype(BF16)[None]

    upstream = out_grad[0].astype(F32)
    grad_gain_mlp = jnp.sum(upstream * mlp_hat, axis=0)
    d_projected = norm_back(upstream * gain_mlp, mlp_hat, mlp_scale).astype(BF16)
    h_turned = dot_nt(order, h_all).astype(BF16)
    d_blocks = gather_pair(d_projected)
    d_blocks[3], h_turned = lax.optimization_barrier((d_blocks[3], h_turned))
    dm_all, d_gu, dh_mine, dh_part = kernel_call(
        expand_back_body,
        [
            0, shaped((512, 1536), BF16), shaped((256, 1024), F32), shaped((256, 1024), BF16),
        ],
        [d_blocks, gate, up, w_wide, w_down_rows],
        flops=2 * 512 * 2304 * 1024, nbytes=12 << 20,
    )

    far = dh_mine[128:] + swap(dh_part[128:], CORE_SWAP).astype(F32)
    far, d_gu, dm_all = lax.optimization_barrier((far.astype(BF16), d_gu, dm_all))
    far = swap(far, Z_SWAP)
    (grad_mlp,) = kernel_call(
        expand_grad_body,
        in_hbm(shaped((1024, 2304), BF16)),
        [h_turned, d_gu, expanded, dm_all],
        [pltpu.VMEM((768, 512), BF16)],
        flops=2 * 512 * 2304 * 1024, nbytes=9 << 20,
    )
    far, grad_mlp = lax.optimization_barrier((far, grad_mlp))
    grad_mlp = lax.psum_scatter(grad_mlp, "fsdp", scatter_dimension=0, tiled=True)
    d_hidden = upstream + dh_mine[:128] + swap(dh_part[:128], CORE_SWAP).astype(F32)
    d_hidden = d_hidden + far.astype(F32)

    grad_gain_attn = jnp.sum(d_hidden * attn_hat, axis=0)
    d_attended = norm_back(d_hidden * gain_attn, attn_hat, attn_scale).astype(BF16)
    d_tiles, deltas, grad_out = kernel_call(
        output_back_body,
        [shaped((8, 256, 128), BF16), shaped((8, 2, 128), F32), shaped((256, 1024), BF16)],
        [place, *in_hbm(out_raw, w_out_rows, gather_group(d_attended), mixed_turned)],
        flops=4 * 1024 * 1024 * 256, nbytes=6 << 20,
    )
    def halve(value, rows, bit, axis, pairs):
        parts = value.reshape(-1, 2, rows, 1024)
        given = jnp.where(bit == 1, parts[:, 0], parts[:, 1])
        mine = jnp.where(bit == 1, parts[:, 1], parts[:, 0]).astype(F32)
        return (mine + lax.ppermute(given, axis, pairs).astype(F32)).astype(BF16)

    grad_out = halve(grad_out, 32, fsdp % 2, "fsdp", [(i, i ^ 1) for i in range(8)])
    dq, dk, dv, d_low, dots = kernel_call(
        attend_back_body,
        [
            *in_hbm(
                shaped((1024, 256), BF16), shaped((1024, 128), F32), shaped((1024, 128), F32),
                shaped((1024, 256), BF16),
            ),
            shaped((24, 128), F32),
        ],
        [place, *in_hbm(q_tiles, keys, vals), logs, d_tiles, deltas],
        [
            pltpu.VMEM((128, 2048), BF16), pltpu.VMEM((2048, 128), F32),
            pltpu.VMEM((2048, 128), F32),
        ],
        flops=10 * 1024 * 2048 * 256, nbytes=8 << 20,
    )
    dots, grad_out = lax.optimization_barrier((dots, grad_out))
    grad_out = halve(grad_out, 32, fsdp // 2 % 2, "fsdp", [(i, i ^ 2) for i in range(8)])
    d_got = swap(d_low, HIGH_TO_LOW)
    dots = sum_group(dots)
    dots_got = swap(dots[16:], HIGH_TO_LOW)

    gains = jnp.concatenate([grad_gain_attn.reshape(128, 8), grad_gain_mlp.reshape(128, 8)], axis=1)
    gains = gains.reshape(16, 8, 16).swapaxes(0, 1).reshape(128, 16)
    gains = jnp.broadcast_to(
        jnp.pad(gains.astype(BF16), ((0, 0), (24, 88)))[:, None, :], (128, 8, 128)
    ).reshape(1024, 128)
    d_made, sent = kernel_call(
        unproject_body,
        [*in_hbm(shaped((1024, 512), BF16)), shaped((1024, 640), BF16)],
        [
            place, *in_hbm(dq, dk, dv), d_got, *in_hbm(q_raw, k_raw), squares, dots, dots_got, cosine, sine,
            gain_q, gain_k, *in_hbm(x_turned), gains,
        ],
        [pltpu.VMEM((8, 384), F32)],
        flops=2 * 1024 * 1024 * 512, nbytes=9 << 20,
    )

    def halves(value, upper):
        low, high = value[: value.shape[0] // 2], value[value.shape[0] // 2 :]
        return jnp.where(upper, high, low), jnp.where(upper, low, high)

    mine, given = halves(grad_mlp, xh == 1)
    mine = mine.astype(F32) + swap(given, X_SWAP).astype(F32)
    sent, grad_out = lax.optimization_barrier((sent, grad_out))
    grad_out = halve(grad_out, 32, fsdp // 4, "fsdp", [(i, i ^ 4) for i in range(8)])
    grad_mlp = after(grad_mlp, sent)
    grad_down = jnp.concatenate(
        [
            piece
            for h in (0, 64)
            for piece in [
                jnp.concatenate(
                    [
                        grad_mlp[h : h + 48, 1536:],
                        jnp.concatenate(
                            [
                                grad_mlp[h + 48 : h + 64, 1536 + m * 256 : 1792 + m * 256]
                                for m in range(3)
                            ],
                            axis=0,
                        ),
                    ],
                    axis=1,
                )
            ]
        ],
        axis=0,
    ).reshape(4, 24, 1024)
    grad_down = sum(
        lax.ppermute(
            lax.dynamic_index_in_dim(grad_down, (xh * 2 + z // 2) ^ other, 0, keepdims=False),
            ("seq", "fsdp"),
            down_home(other),
        ).astype(F32)
        for other in range(4)
    )
    got_made = lax.all_to_all(
        sent.reshape(8, 128, 640), "fsdp", split_axis=0, concat_axis=0, tiled=True
    )
    dx_mine, dx_part = kernel_call(
        input_body,
        in_hbm(shaped((512, 1024), F32), shaped((512, 1024), BF16)),
        [*in_hbm(after(d_made, sent)), weight],
        flops=2 * 1024 * 1024 * 512, nbytes=5 << 20,
    )
    rows = [slice(k * 128, k * 128 + 128) for k in range(4)]
    pieces = [dx_mine[r] + swap(dx_part[r], CORE_SWAP).astype(F32) for r in rows]
    far = [piece.astype(BF16) for piece in pieces[1:]]
    (collected,) = kernel_call(
        collect_body,
        [shaped((128, 2176), BF16)],
        [got_made.reshape(1024, 640), grad_mlp],
        flops=WAIT_FLOPS, nbytes=3 << 20,
    )
    got = lax.all_to_all(
        collected.reshape(16, 8, 2176), "seq", split_axis=0, concat_axis=0, tiled=True
    )
    grad_out = grad_out.reshape(2, 16, 1024)
    own = jnp.where(xh == 1, grad_out[1], grad_out[0])
    given = jnp.where(xh == 1, grad_out[0], grad_out[1])
    own = swap(own, out_home(False))
    grad_out = own.astype(F32) + swap(given, out_home(True)).astype(F32)
    d_inputs = pieces[0] + sum(
        swap(piece, to_z(k)).astype(F32) for k, piece in enumerate(far, 1)
    )
    got = got.reshape(2, 8, 8, 2176).astype(F32)
    summed = got[0, :, :, :640] + got[1, :, :, :640]
    gains = jnp.sum(summed[:, 0, 512:], axis=0)

    def take(first, width):
        return summed[:, :, first : first + width].swapaxes(0, 1).reshape(8, 8 * width)

    wide = jnp.sum(got[:, :, :, 640:].reshape(2, 2, 4, 8, 2, 8, 96), axis=(0, 1))
    wide = wide.transpose(2, 1, 3, 0, 4).reshape(2, 8, 3072)
    return (
        output,
        (d_hidden + d_inputs).astype(BF16)[None],
        take(0, 256),
        take(256, 128),
        take(384, 128),
        grad_out.astype(F32),
        wide[0],
        wide[1],
        grad_down.astype(F32),
        gains[:16],
        gains[16:24],
        gains[24:32],
        gains[32:40],
    )


def solution(mesh):
    rows = P("fsdp", "seq", None)
    weight = P("fsdp", None)
    grad = P(("seq", "fsdp"), None)
    gain = P(("seq", "fsdp"))
    return jax.shard_map(
        on_device,
        mesh=mesh,
        in_specs=(rows,) * 2 + (weight,) * 7 + (P(),) * 4,
        out_specs=(rows,) * 2 + (grad,) * 7 + (gain,) * 4,
        check_vma=False,
    )
```

```python
import functools
import math

import jax
import jax.numpy as jnp
from jax import lax
from jax.experimental import pallas as pl
from jax.experimental.pallas import tpu as pltpu
from jax.sharding import PartitionSpec as P

BF16 = jnp.bfloat16
F32 = jnp.float32
DH = 128
EPS = 1e-06
THETA = 1000000.0
MASKED = -1e30
LOG2E = math.log2(math.e)
QUERY_SCALE = DH ** (-0.5) * LOG2E
VMEM_BYTES = 20 * 1024 * 1024
VMEM = pl.BlockSpec(memory_space=pltpu.VMEM)
SMEM = pl.BlockSpec(memory_space=pltpu.SMEM)
ANY = pl.BlockSpec(memory_space=pl.ANY)
SMALL = 64 * 1024
WAIT_FLOPS = 12 * 10**9
NT = (((1,), (1,)), ((), ()))

SEQ_PLACES = [(xh, z, c) for xh in range(2) for z in range(4) for c in range(2)]


def seq_index(xh, z, c):
    return xh * 8 + (z % 4) * 2 + c


CORE_SWAP = [(i, i ^ 1) for i in range(16)]
LOW_TO_HIGH = [(i, i + 8) for i in range(8)]
HIGH_TO_LOW = [(i + 8, i) for i in range(8)]
X_SWAP = [(i, i ^ 8) for i in range(16)]


def from_z(k):
    return [(seq_index(xh, z + k, c), seq_index(xh, z, c)) for xh, z, c in SEQ_PLACES]


def to_z(k):
    return [(seq_index(xh, z, c), seq_index(xh, z + k, c)) for xh, z, c in SEQ_PLACES]


def across(pairs):
    return [(seq * 8 + f, to_seq * 8 + to_f) for seq, f, to_seq, to_f in pairs]


TURN = across(
    (xh * 8 + a, f, xh * 8 + f, a) for xh in range(2) for a in range(8) for f in range(8)
)
Z_SWAP = [(i, i ^ 2) for i in range(16)]
FAR_SWAP = [(i, i ^ 4) for i in range(16)]


def out_home(other):
    return [(xh * 8 + a, 2 * a + (xh ^ other)) for xh in range(2) for a in range(8)]


def down_home(other):
    return across(
        (seq_index(own // 2, 2 * (own % 2) + zl, c), f, 2 * f + zl, 4 * c + (own ^ other))
        for own in range(4) for zl in range(2) for c in range(2) for f in range(8)
    )


def swap(value, pairs):
    return lax.ppermute(value, "seq", pairs)


def after(value, *others):
    return lax.optimization_barrier((value, *others))[0]


def gather_group(block):
    far = {k: swap(block, from_z(k)) for k in (2, 1, 3)}
    mine = [block, far[1], far[2], far[3]]
    return mine + [swap(v, CORE_SWAP) for v in mine]


def scatter_group(mine, part):
    rows = [slice(k * 128, k * 128 + 128) for k in range(4)]
    out = None
    for k in (2, 1, 3, 0):
        piece = mine[rows[k]] + swap(part[rows[k]], CORE_SWAP).astype(F32)
        if k:
            piece = swap(piece.astype(BF16), to_z(k)).astype(F32)
        out = piece if out is None else out + piece
    return out


def gather_pair(block):
    mine = [block, swap(block, Z_SWAP)]
    return mine + [swap(v, CORE_SWAP) for v in mine]


def scatter_pair(mine, part, later=()):
    far = mine[128:] + swap(part[128:], CORE_SWAP).astype(F32)
    far, *later = lax.optimization_barrier((far.astype(BF16), *later))
    far = swap(far, Z_SWAP).astype(F32)
    return mine[:128] + swap(part[:128], CORE_SWAP).astype(F32) + far, later


def sum_group(rows):
    groups = rows.shape[0] // 8
    other = swap(rows, CORE_SWAP).reshape(groups, 2, 4, 128)
    pair = rows.reshape(groups, 2, 4, 128) + jnp.concatenate([other[:, 1:], other[:, :1]], axis=1)
    odd = lax.axis_index("seq") // 2 % 2 == 1
    got = swap(pair, Z_SWAP)
    up = jnp.concatenate([got[:, :, 3:], got[:, :, :3]], axis=2)
    down = jnp.concatenate([got[:, :, 1:], got[:, :, :1]], axis=2)
    pair = pair + jnp.where(odd, down, up)
    got = swap(pair, FAR_SWAP)
    pair = pair + jnp.concatenate([got[:, :, 2:], got[:, :, :2]], axis=2)
    return pair.reshape(rows.shape)


def column(row):
    return jnp.transpose(jnp.broadcast_to(row, (128, 128)))


def row_sums(values):
    return jnp.sum(jnp.transpose(values), axis=0, keepdims=True)


def shaped(shape, dtype):
    return jax.ShapeDtypeStruct(shape, dtype)


class Kept:
    def __init__(self, value):
        self.value = value


def in_hbm(*values):
    return [Kept(v) for v in values]


def kernel_call(body, outs, inputs, scratch=(), flops=0, nbytes=0):
    hbm_outs = [isinstance(o, Kept) for o in outs]
    hbm_ins = [isinstance(x, Kept) for x in inputs]
    outs = [o.value if isinstance(o, Kept) else o for o in outs]
    inputs = [x.value if isinstance(x, Kept) else x for x in inputs]
    groups = [x if isinstance(x, list) else [x] for x in inputs]
    flat = [a for group in groups for a in group]
    joined = [
        shaped((sum(a.shape[0] for a in group),) + group[0].shape[1:], group[0].dtype)
        for group in groups
    ]

    def large(s):
        return math.prod(s.shape) * s.dtype.itemsize >= SMALL

    def where(s):
        return ANY if large(s) else SMEM if s.dtype == jnp.int32 else VMEM

    out_shapes = [joined[o] if isinstance(o, int) else o for o in outs]
    in_buffers = [pltpu.VMEM(s.shape, s.dtype) for s in joined if large(s)]
    out_buffers = [
        pltpu.VMEM(o.shape, o.dtype) for o in outs if not isinstance(o, int) and large(o)
    ]

    def whole(*refs):
        refs = list(refs)

        def pull(count):
            taken = refs[:count]
            del refs[:count]
            return taken

        in_refs, out_refs = pull(len(flat)), pull(len(outs))
        in_space, out_space = pull(len(in_buffers)), pull(len(out_buffers))
        own, (in_sem, out_sem) = pull(len(scratch)), refs
        loads, ins, at = {}, [], 0
        for group, s in zip(groups, joined):
            if not large(s):
                ins.append(in_refs[at])
                at += 1
                continue
            space, row = in_space.pop(0), 0
            loads[id(space)] = []
            for a in group:
                copy = pltpu.make_async_copy(
                    in_refs[at], space.at[pl.ds(row, a.shape[0])], in_sem.at[at]
                )
                copy.start()
                loads[id(space)].append(copy)
                row, at = row + a.shape[0], at + 1
            ins.append(space)
        made, stores = [], {}
        for k, (o, s, ref) in enumerate(zip(outs, out_shapes, out_refs)):
            if not large(s):
                made.append(ref)
                continue
            space = ins[o] if isinstance(o, int) else out_space.pop(0)
            stores[id(space)] = pltpu.make_async_copy(space, ref, out_sem.at[k])
            if not isinstance(o, int):
                made.append(space)
        started = []

        def ready(*spaces):
            for space in spaces:
                for copy in loads.pop(id(space), ()):
                    copy.wait()

        def done(*spaces):
            for space in spaces:
                copy = stores.pop(id(space))
                copy.start()
                started.append(copy)

        body(ready, done, *ins, *made, *own)
        for key in list(stores):
            copy = stores.pop(key)
            copy.start()
            started.append(copy)
        for copy in started:
            copy.wait()

    shapes = [pltpu.HBM(s.shape, s.dtype) if hbm else s for s, hbm in zip(out_shapes, hbm_outs)]
    return pl.pallas_call(
        whole,
        out_shape=tuple(shapes),
        in_specs=[where(s) for group, s in zip(groups, joined) for _ in group],
        out_specs=tuple(where(s) for s in out_shapes),
        scratch_shapes=[
            *in_buffers, *out_buffers, *scratch,
            pltpu.SemaphoreType.DMA((len(flat),)), pltpu.SemaphoreType.DMA((len(outs),)),
        ],
        compiler_params=pltpu.CompilerParams(vmem_limit_bytes=VMEM_BYTES),
        cost_estimate=pl.CostEstimate(flops=flops, bytes_accessed=nbytes, transcendentals=0),
    )(
        *[
            pltpu.with_memory_space_constraint(a, pltpu.HBM) if hbm else a
            for group, hbm in zip(groups, hbm_ins)
            for a in group
        ],
    )


def root(total, width):
    return lax.rsqrt(total * (1.0 / width) + EPS)


def project_body(
    ready, done, x_all, weight, gain_q, gain_k, cos, sin,
    q_raw, k_raw, q_rot, kv_rot, squares,
):
    ready(x_all, weight, cos, sin)
    done(x_all)

    def step(t, carry):
        at = pl.multiple_of(t * 256, 256)
        made = jnp.dot(x_all[pl.ds(at, 256), :], weight[...], preferred_element_type=F32)
        for part in range(2):
            rows = pl.ds(at + part * 128, 128)
            block = t * 2 + part
            here = made[part * 128 : part * 128 + 128]
            q, k = here[:, :256], here[:, 256:384]
            kv_rot[rows, 128:] = here[:, 384:].astype(BF16)
            q_raw[rows, :] = q
            k_raw[rows, :] = k
            squares[pl.ds(block, 1), :] = row_sums(
                q[:, :128] * q[:, :128] + q[:, 128:] * q[:, 128:]
            )
            squares[pl.ds(block + 8, 1), :] = row_sums(k * k)
            cosine, sine = cos[rows, :], sin[rows, :]
            for head in range(2):
                lanes = slice(head * 128, head * 128 + 128)
                turn = q[:, lanes] * gain_q[:, lanes]
                q_rot[rows, lanes] = (turn * cosine + pltpu.roll(turn, 64, 1) * sine).astype(BF16)
            turn = k * gain_k[...]
            kv_rot[rows, :128] = (turn * cosine + pltpu.roll(turn, 64, 1) * sine).astype(BF16)
        return carry

    lax.fori_loop(0, 4, step, 0)


def spot(place, block):
    z = lax.rem(place[1] + block % 4, 4)
    c = place[2] if block < 4 else 1 - place[2]
    return z, c


def diagonal():
    query = lax.broadcasted_iota(jnp.int32, (256, 512), 1) % 256
    return lax.broadcasted_iota(jnp.int32, (256, 512), 0) <= query


def attend_body(
    ready, done, place, q_rot, kv_rot, kv_low, squares, squares_low,
    out_raw, out_low, out_turned, q_tiles, keys, vals, logs, vals_t,
):
    ready(q_rot, kv_rot, kv_low)
    for b in range(8):
        rows = slice(b * 128, b * 128 + 128)
        z, c = spot(place, b)
        r = column(root(squares[b : b + 1, :], 2048.0)) * QUERY_SCALE
        inner = pl.ds(pl.multiple_of(c * 128, 128), 128)
        for head in range(2):
            q = q_rot[rows, head * 128 : head * 128 + 128].astype(F32)
            q_tiles[z * 2 + head, inner, :] = (q * r).astype(BF16)
        at = pl.ds(pl.multiple_of(1024 + z * 256 + c * 128, 128), 128)
        r = column(root(squares[8 + b : 9 + b, :], 1024.0))
        keys[at, :] = (kv_rot[rows, :128].astype(F32) * r).astype(BF16)
        vals[at, :] = kv_rot[rows, 128:]
        r = column(root(squares_low[b : b + 1, :], 1024.0))
        keys[rows, :] = (kv_low[rows, :128].astype(F32) * r).astype(BF16)
        vals[rows, :] = kv_low[rows, 128:]
    done(q_tiles, keys, vals)
    vals_t[...] = jnp.transpose(vals[...].astype(F32)).astype(BF16)

    def queries(first, i):
        at_diagonal = 1024 + i * 256
        q = q_tiles[i * 2 : i * 2 + 2].reshape(512, 128)
        ranges = [(lo, lo + 256) for lo in range(first, at_diagonal + 256, 256)]
        scores = [
            lax.dot_general(keys[lo:hi, :], q, NT, preferred_element_type=F32) for lo, hi in ranges
        ]
        scores[-1] = jnp.where(diagonal(), scores[-1], MASKED)
        top = functools.reduce(jnp.maximum, [jnp.max(s, axis=0, keepdims=True) for s in scores])
        total, acc = 0.0, 0.0
        for s, (lo, hi) in zip(scores, ranges):
            p = jnp.exp2(s - top)
            total = total + jnp.sum(p, axis=0, keepdims=True)
            acc = acc + jnp.dot(vals_t[:, lo:hi], p.astype(BF16), preferred_element_type=F32)
        acc = acc / total
        log = top + jnp.log2(total)
        for head in range(2):
            turned = acc[:, head * 256 : head * 256 + 256]
            out = jnp.transpose(turned)
            turned = turned.astype(BF16)
            logs[i * 2 + head : i * 2 + head + 1, :] = log[:, head * 256 : head * 256 + 256]
            for c in range(2):
                block = lax.rem(i - place[1] + 4, 4) + 4 * jnp.abs(c - place[2])
                at = pl.ds(pl.multiple_of(block * 128, 128), 128)
                lanes = slice(head * 128, head * 128 + 128)
                out_raw[at, lanes] = out[c * 128 : c * 128 + 128, :]
                out_low[at, lanes] = out[c * 128 : c * 128 + 128, :].astype(BF16)
                out_turned[lanes, at] = turned[:, c * 128 : c * 128 + 128]

    @pl.when(place[0] == 1)
    def _():
        for i in range(4):
            queries(0, i)

    @pl.when(place[0] == 0)
    def _():
        for i in range(4):
            queries(1024, i)

    done(out_raw, out_low, out_turned)


def output_body(ready, done, place, mixed, w_own, w_got, a_mine, a_part, w_out):
    ready(w_own, w_got)
    w_out[pl.ds(pl.multiple_of(place[3] * 128, 128), 128), :] = w_own[...]
    w_out[pl.ds(pl.multiple_of((1 - place[3]) * 128, 128), 128), :] = w_got[...]
    done(w_out)
    ready(mixed)

    def project(t, carry):
        at = pl.ds(pl.multiple_of(t * 256, 256), 256)
        far = pl.ds(pl.multiple_of(512 + t * 256, 256), 256)
        a_part[at, :] = jnp.dot(mixed[far, :], w_out[...], preferred_element_type=F32).astype(BF16)
        a_mine[at, :] = jnp.dot(mixed[at, :], w_out[...], preferred_element_type=F32)
        return carry

    lax.fori_loop(0, 2, project, 0)


def output_back_body(
    ready, done, place, out_raw, w_out, da_all, mixed_turned, d_tiles, deltas, grad_out
):
    ready(out_raw, w_out, da_all)
    for b in range(8):
        rows = slice(b * 128, b * 128 + 128)
        z, c = spot(place, b)
        inner = pl.ds(pl.multiple_of(c * 128, 128), 128)
        d_out = lax.dot_general(
            da_all[rows, :], w_out[...], NT, preferred_element_type=F32
        ).astype(BF16)
        for head in range(2):
            lanes = slice(head * 128, head * 128 + 128)
            grad = d_out[:, lanes]
            d_tiles[z * 2 + head, inner, :] = grad
            deltas[z * 2 + head, pl.ds(c, 1), :] = row_sums(grad.astype(F32) * out_raw[rows, lanes])
    done(d_tiles)
    ready(mixed_turned)
    for m in range(4):
        lanes = slice(m * 256, m * 256 + 256)
        made = jnp.dot(mixed_turned[...], da_all[:, lanes], preferred_element_type=F32).astype(BF16)
        for j in range(2):
            for f in range(8):
                to, at = f * 32 + j * 16, j * 128 + f * 16
                grad_out[to : to + 16, lanes] = made[at : at + 16]


def attend_back_body(
    ready, done, place, q_tiles, keys, vals, logs, d_tiles, deltas,
    dq, dk, dv, d_low, dots, keys_t, dk_acc, dv_acc,
):
    ready(keys)
    keys_t[...] = jnp.transpose(keys[...].astype(F32)).astype(BF16)
    dk_acc[...] = jnp.zeros_like(dk_acc)
    dv_acc[...] = jnp.zeros_like(dv_acc)
    ready(q_tiles, vals, d_tiles)

    def queries(first, i):
        at_diagonal = 1024 + i * 256
        q = q_tiles[i * 2 : i * 2 + 2].reshape(512, 128)
        grad = d_tiles[i * 2 : i * 2 + 2].reshape(512, 128)
        log = jnp.concatenate([logs[i * 2 : i * 2 + 1, :], logs[i * 2 + 1 : i * 2 + 2, :]], axis=1)
        delta = jnp.concatenate(
            [deltas[i * 2 + head, c : c + 1, :] for head in range(2) for c in range(2)], axis=1
        )
        total = 0.0
        for lo in range(first, at_diagonal + 256, 256):
            at = slice(lo, lo + 256)
            k, v = keys[at, :], vals[at, :]
            s = lax.dot_general(k, q, NT, preferred_element_type=F32)
            p = jnp.exp2(s - log)
            if lo == at_diagonal:
                p = jnp.where(diagonal(), p, 0.0)
            dp = lax.dot_general(v, grad, NT, preferred_element_type=F32)
            ds = (p * (dp - delta)).astype(BF16)
            dv_acc[at, :] += jnp.dot(p.astype(BF16), grad, preferred_element_type=F32)
            dk_acc[at, :] += jnp.dot(ds, q, preferred_element_type=F32)
            total = total + jnp.dot(keys_t[:, at], ds, preferred_element_type=F32)
        dot = total * jnp.transpose(q.astype(F32))
        dot = jnp.sum(dot[:, :256] + dot[:, 256:], axis=0, keepdims=True)
        for head in range(2):
            out = jnp.transpose(total[:, head * 256 : head * 256 + 256]) * DH ** (-0.5)
            for c in range(2):
                block = lax.rem(i - place[1] + 4, 4) + 4 * jnp.abs(c - place[2])
                at = pl.ds(pl.multiple_of(block * 128, 128), 128)
                dq[at, head * 128 : head * 128 + 128] = out[c * 128 : c * 128 + 128, :].astype(BF16)
        for c in range(2):
            block = lax.rem(i - place[1] + 4, 4) + 4 * jnp.abs(c - place[2])
            dots[pl.ds(block, 1), :] = dot[:, c * 128 : c * 128 + 128] * (1.0 / LOG2E)

    @pl.when(place[0] == 1)
    def _():
        for i in range(4):
            queries(0, i)

    @pl.when(place[0] == 0)
    def _():
        for i in range(4):
            queries(1024, i)

    done(dq)
    for b in range(8):
        rows = slice(b * 128, b * 128 + 128)
        z, c = spot(place, b)
        at = pl.ds(pl.multiple_of(1024 + z * 256 + c * 128, 128), 128)
        key_grad = dk_acc[at, :] * (1.0 / LOG2E)
        dk[rows, :] = key_grad
        dv[rows, :] = dv_acc[at, :]
        dots[8 + b : 9 + b, :] = row_sums(key_grad * keys[at, :].astype(F32))
        key_grad = dk_acc[rows, :] * (1.0 / LOG2E)
        d_low[rows, :128] = key_grad.astype(BF16)
        d_low[rows, 128:] = dv_acc[rows, :].astype(BF16)
        dots[16 + b : 17 + b, :] = row_sums(key_grad * keys[rows, :].astype(F32))


def unproject_body(
    ready, done, place, dq, dk, dv, d_got, q_raw, k_raw, squares, dots, dots_got, cos, sin,
    gain_q, gain_k, x_turned, gains, d_made, sent, sums,
):
    sums[...] = jnp.zeros_like(sums)
    ready(dq, dk, dv, d_got, q_raw, k_raw, cos, sin)

    def step(b, carry):
        rows = pl.ds(pl.multiple_of(b * 128, 128), 128)
        cosine, sine = cos[rows, :], sin[rows, :]
        r = column(root(squares[pl.ds(b, 1), :], 2048.0))
        mean = column(dots[pl.ds(b, 1), :]) * (1.0 / 2048.0)
        for head in range(2):
            lanes = slice(head * 128, head * 128 + 128)
            turn = dq[rows, lanes].astype(F32)
            d_norm = turn * cosine - pltpu.roll(turn, 64, 1) * sine
            hat = q_raw[rows, lanes] * r
            sums[0:1, lanes] += jnp.sum(d_norm * hat, axis=0, keepdims=True)
            d_made[rows, lanes] = (r * (d_norm * gain_q[:, lanes] - hat * mean)).astype(BF16)
        r = column(root(squares[pl.ds(b + 8, 1), :], 1024.0))
        mean = column(dots[pl.ds(b + 8, 1), :] + dots_got[pl.ds(b, 1), :]) * (1.0 / 1024.0)
        turn = dk[rows, :] + d_got[rows, :128].astype(F32)
        d_norm = turn * cosine - pltpu.roll(turn, 64, 1) * sine
        hat = k_raw[rows, :] * r
        sums[0:1, 256:] += jnp.sum(d_norm * hat, axis=0, keepdims=True)
        d_made[rows, 256:384] = (r * (d_norm * gain_k[...] - hat * mean)).astype(BF16)
        d_made[rows, 384:] = (dv[rows, :] + d_got[rows, 128:].astype(F32)).astype(BF16)
        return carry

    lax.fori_loop(0, 8, step, 0)
    done(d_made)
    ready(x_turned, gains)

    def grad(t, carry):
        rows = pl.ds(pl.multiple_of(t * 256, 256), 256)
        sent[rows, :512] = jnp.dot(
            x_turned[rows, :], d_made[...], preferred_element_type=F32
        ).astype(BF16)
        sent[rows, 512:] = gains[rows, :]
        return carry

    lax.fori_loop(0, 4, grad, 0)
    extra = 0.0
    for lo, width, each, first in ((0, 256, 16, 0), (256, 128, 8, 16)):
        row = lax.broadcasted_iota(jnp.int32, (128, width), 0)
        lane = lax.broadcasted_iota(jnp.int32, (128, width), 1) // each
        here = row // 8 % 2 * 8 + row // 16 == lane
        spread = jnp.where(here, sums[0:1, lo : lo + width], 0.0).astype(BF16)
        lane = lax.broadcasted_iota(jnp.int32, (width, 128), 0) % each + first
        pick = jnp.where(lane == lax.broadcasted_iota(jnp.int32, (width, 128), 1), 1.0, 0.0)
        extra = extra + jnp.dot(spread, pick.astype(BF16), preferred_element_type=F32)
    for f in range(8):
        rows = pl.ds(pl.multiple_of(f * 128 + (place[1] * 2 + place[2]) * 16, 16), 16)
        added = gains[rows, :].astype(F32) + extra[f * 16 : f * 16 + 16]
        sent[rows, 512:] = added.astype(BF16)


def input_body(ready, done, d_made, weight, dx_mine, dx_part):
    ready(d_made, weight)

    def step(t, carry):
        at = pl.ds(pl.multiple_of(t * 256, 256), 256)
        far = pl.ds(pl.multiple_of(512 + t * 256, 256), 256)
        dx_part[at, :] = lax.dot_general(
            d_made[far, :], weight[...], NT, preferred_element_type=F32
        ).astype(BF16)
        dx_mine[at, :] = lax.dot_general(
            d_made[at, :], weight[...], NT, preferred_element_type=F32
        )
        return carry

    lax.fori_loop(0, 2, step, 0)


def expand_body(ready, done, h_all, weight, packed, gate, up, expanded, m_mine, m_part, down):
    ready(h_all, weight)
    done(h_all)
    def widen(n, carry):
        lanes = pl.ds(pl.multiple_of(n * 256, 256), 256)
        upper = pl.ds(pl.multiple_of(768 + n * 256, 256), 256)
        g = jnp.dot(h_all[...], weight[:, lanes], preferred_element_type=F32)
        u = jnp.dot(h_all[...], weight[:, upper], preferred_element_type=F32)
        gate[:, lanes] = g
        up[:, lanes] = u
        expanded[:, lanes] = (g * jax.nn.sigmoid(g) * u).astype(BF16)
        return carry

    lax.fori_loop(0, 3, widen, 0)
    done(gate, up, expanded)
    ready(packed)
    for f in range(8):
        down[f * 96 : f * 96 + 96, :768] = packed[f * 128 : f * 128 + 96, :]
        for m in range(3):
            down[f * 96 + m * 32 : f * 96 + m * 32 + 32, 768:] = packed[
                f * 128 + 96 : f * 128 + 128, m * 256 : m * 256 + 256
            ]
    done(down)

    def narrow(n, carry):
        lanes = pl.ds(pl.multiple_of(n * 256, 256), 256)
        m = jnp.dot(expanded[...], down[:, lanes], preferred_element_type=F32)
        m_mine[:, lanes] = m[:256]
        m_part[:, lanes] = m[256:].astype(BF16)
        return carry

    lax.fori_loop(0, 4, narrow, 0)


def expand_back_body(ready, done, dm_all, gate, up, weight, down, d_gu, dh_mine, dh_part):
    ready(dm_all, gate, up, down)
    done(dm_all)

    def widen(n, carry):
        lanes = pl.ds(pl.multiple_of(n * 256, 256), 256)
        upper = pl.ds(pl.multiple_of(768 + n * 256, 256), 256)
        de = lax.dot_general(dm_all[...], down[lanes, :], NT, preferred_element_type=F32)
        g = gate[:, lanes]
        sig = jax.nn.sigmoid(g)
        d_gu[:, lanes] = (de * up[:, lanes] * sig * (1.0 + g * (1.0 - sig))).astype(BF16)
        d_gu[:, upper] = (de * (g * sig)).astype(BF16)
        return carry

    lax.fori_loop(0, 3, widen, 0)
    done(d_gu)
    ready(weight)

    def narrow(n, carry):
        lanes = pl.ds(pl.multiple_of(n * 256, 256), 256)
        dh = lax.dot_general(d_gu[...], weight[lanes, :], NT, preferred_element_type=F32)
        dh_mine[:, lanes] = dh[:256]
        dh_part[:, lanes] = dh[256:].astype(BF16)
        return carry

    lax.fori_loop(0, 4, narrow, 0)


def expand_grad_body(ready, done, h_turned, d_gu, expanded, dm_all, out, expanded_t):
    ready(expanded)
    expanded_t[...] = jnp.transpose(expanded[...].astype(F32)).astype(BF16)

    ready(h_turned, d_gu, dm_all)

    def widen(n, carry):
        lanes = pl.ds(pl.multiple_of(n * 256, 256), 256)
        out[:, lanes] = jnp.dot(
            h_turned[...], d_gu[:, lanes], preferred_element_type=F32
        ).astype(BF16)
        return carry

    lax.fori_loop(0, 6, widen, 0)
    for n in range(4):
        made = jnp.dot(
            expanded_t[...], dm_all[:, n * 256 : n * 256 + 256], preferred_element_type=F32
        ).astype(BF16)
        for f in range(16):
            if n < 3:
                out[f * 64 : f * 64 + 48, 1536 + n * 256 : 1792 + n * 256] = made[
                    f * 48 : f * 48 + 48
                ]
                continue
            for m in range(3):
                out[f * 64 + 48 : f * 64 + 64, 1536 + m * 256 : 1792 + m * 256] = made[
                    f * 48 + m * 16 : f * 48 + m * 16 + 16
                ]


def collect_body(ready, done, got, grad_mlp, out):
    ready(got)
    total = got[:128, :].astype(F32)
    for f in range(1, 8):
        total = total + got[f * 128 : f * 128 + 128, :].astype(F32)
    out[:, :640] = total.astype(BF16)
    ready(grad_mlp)
    out[:, 640:] = grad_mlp[:, :1536]


def norm_scale(values):
    return lax.rsqrt(jnp.mean(values * values, axis=-1, keepdims=True) + EPS)


def norm_back(upstream, normed, scaling):
    return scaling * (upstream - normed * jnp.mean(upstream * normed, axis=-1, keepdims=True))


def rotary_tables(first, z, c):
    half = DH // 2
    k = jnp.arange(4, dtype=jnp.int32)
    starts = jnp.concatenate([((z + k) % 4) * 256 + c * 128, ((z + k) % 4) * 256 + (1 - c) * 128])
    places = (first + starts[:, None] + jnp.arange(128, dtype=jnp.int32)[None, :]).reshape(1024)
    inverse = THETA ** (-(jnp.arange(half, dtype=F32) * (2.0 / DH)))
    angles = places.astype(F32)[:, None] * inverse[None, :]
    cosine, sine = jnp.cos(angles), jnp.sin(angles)
    return (
        jnp.concatenate([cosine, cosine], axis=-1),
        jnp.concatenate([-sine, sine], axis=-1),
    )


def dot(a, b):
    return jnp.dot(a, b, preferred_element_type=F32)


def dot_nt(a, b):
    return lax.dot_general(a, b, NT, preferred_element_type=F32)


def dot_tn(a, b):
    return lax.dot_general(a, b, (((0,), (0,)), ((), ())), preferred_element_type=F32)


def on_device(
    tokens, out_grad, w_query, w_key, w_value, w_out, w_gate, w_up, w_down,
    gain_query, gain_key, gain_attn, gain_mlp,
):
    seq = lax.axis_index("seq")
    xh, zc = seq // 8, seq % 8
    z, c = zc // 2, zc % 2
    quarter = (z % 2) * 2 + c
    fsdp = lax.axis_index("fsdp")
    place = jnp.stack([xh, z, c, fsdp // 4]).astype(jnp.int32)
    inputs = tokens[0]

    def columns(weight, width):
        return lax.dynamic_slice_in_dim(weight, zc * width, width, 1)

    def spread(block):
        return lax.all_to_all(
            jnp.broadcast_to(block[None], (8,) + block.shape),
            "fsdp", split_axis=0, concat_axis=0, tiled=True,
        ).reshape(8 * block.shape[0], block.shape[1])

    x_blocks = gather_group(inputs)
    weight = spread(
        jnp.concatenate(
            [columns(w_query, 256), columns(w_key, 128), columns(w_value, 128)], axis=1
        )
    )
    w_out_rows = lax.ppermute(
        after(lax.dynamic_slice_in_dim(w_out, zc * 32, 32, 0), weight),
        ("seq", "fsdp"),
        TURN,
    )

    def quarters(weight):
        part = lax.dynamic_slice_in_dim(weight.reshape(128, 8, 384), quarter * 96, 96, 2)
        return part.reshape(128, 768)

    down = lax.dynamic_slice_in_dim(w_down, quarter * 96, 96, 0)
    packed = jnp.concatenate(
        [
            down[:, :768],
            jnp.concatenate([down[m * 32 : m * 32 + 32, 768:] for m in range(3)], axis=1),
        ],
        axis=0,
    )
    w_narrow = lax.all_gather(packed, "fsdp", axis=0, tiled=True)
    w_wide = jnp.concatenate([quarters(w_gate), quarters(w_up)], axis=1)
    weight, w_wide = lax.optimization_barrier((weight, w_wide))

    cosine, sine = rotary_tables(xh * 1024, z, c)
    gain_q = lax.dynamic_slice_in_dim(gain_query, zc * 256, 256, 0)[None]
    gain_k = lax.dynamic_slice_in_dim(gain_key, zc * 128, 128, 0)[None]
    x_all, q_raw, k_raw, q_rot, kv_rot, squares = kernel_call(
        project_body,
        [
            *in_hbm(
                0, shaped((1024, 256), F32), shaped((1024, 128), F32),
                shaped((1024, 256), BF16), shaped((1024, 256), BF16),
            ),
            shaped((16, 128), F32),
        ],
        [x_blocks, weight, gain_q, gain_k, cosine, sine],
        flops=2 * 1024 * 1024 * 512, nbytes=9 << 20,
    )

    kv_low = swap(kv_rot, LOW_TO_HIGH)
    squares = sum_group(squares)
    squares_low = swap(squares[8:], LOW_TO_HIGH)
    for bit in (1, 2):
        got = lax.ppermute(w_out_rows, "fsdp", [(i, i ^ bit) for i in range(8)])
        upper = fsdp // bit % 2 == 1
        w_out_rows = jnp.concatenate(
            [jnp.where(upper, got, w_out_rows), jnp.where(upper, w_out_rows, got)], axis=0
        )
    kv_low, squares, squares_low, w_wide, w_narrow, w_out_rows = lax.optimization_barrier(
        (kv_low, squares, squares_low, w_wide, w_narrow, w_out_rows)
    )
    w_wide = lax.all_gather(w_wide, "fsdp", axis=0, tiled=True)
    w_out_got = lax.ppermute(w_out_rows, "fsdp", [(i, i ^ 4) for i in range(8)])
    out_raw, mixed, mixed_turned, q_tiles, keys, vals, logs = kernel_call(
        attend_body,
        [
            *in_hbm(
                shaped((1024, 256), F32), shaped((1024, 256), BF16), shaped((256, 1024), BF16),
                shaped((8, 256, 128), BF16), shaped((2048, 128), BF16), shaped((2048, 128), BF16),
            ),
            shaped((8, 256), F32),
        ],
        [place, *in_hbm(q_rot, kv_rot), kv_low, squares, squares_low],
        [pltpu.VMEM((128, 2048), BF16)],
        flops=4 * 1024 * 2048 * 256, nbytes=9 << 20,
    )
    a_mine, a_part, w_out_rows = kernel_call(
        output_body,
        [shaped((512, 1024), F32), shaped((512, 1024), BF16), *in_hbm(shaped((256, 1024), BF16))],
        [place, *in_hbm(mixed), w_out_rows, w_out_got],
        flops=2 * 1024 * 1024 * 256, nbytes=5 << 20,
    )
    n = jnp.arange(1024, dtype=jnp.int32)
    source = ((n // 8) % 16) * 64 + (n // 128) * 8 + n % 8
    order = (n[None, :] == source[:, None]).astype(BF16)
    x_turned = dot_nt(order, x_all).astype(BF16)

    attended = scatter_group(a_mine, a_part)
    attended, x_turned = lax.optimization_barrier((attended, x_turned))
    attn_scale = norm_scale(attended)
    attn_hat = attended * attn_scale
    hidden_state = inputs.astype(F32) + attn_hat * gain_attn
    h_all, gate, up, expanded, m_mine, m_part, w_down_rows = kernel_call(
        expand_body,
        [
            0, shaped((512, 768), F32), shaped((512, 768), F32), shaped((512, 768), BF16),
            shaped((256, 1024), F32), shaped((256, 1024), BF16), shaped((768, 1024), BF16),
        ],
        [
            gather_pair(hidden_state.astype(BF16)), *in_hbm(w_wide, w_narrow),
        ],
        flops=2 * 512 * 2304 * 1024, nbytes=12 << 20,
    )
    projected, _ = scatter_pair(m_mine, m_part)
    mlp_scale = norm_scale(projected)
    mlp_hat = projected * mlp_scale
    output = (hidden_state + mlp_hat * gain_mlp).astype(BF16)[None]

    upstream = out_grad[0].astype(F32)
    grad_gain_mlp = jnp.sum(upstream * mlp_hat, axis=0)
    d_projected = norm_back(upstream * gain_mlp, mlp_hat, mlp_scale).astype(BF16)
    h_turned = dot_nt(order, h_all).astype(BF16)
    d_blocks = gather_pair(d_projected)
    d_blocks[3], h_turned = lax.optimization_barrier((d_blocks[3], h_turned))
    dm_all, d_gu, dh_mine, dh_part = kernel_call(
        expand_back_body,
        [
            0, shaped((512, 1536), BF16), shaped((256, 1024), F32), shaped((256, 1024), BF16),
        ],
        [d_blocks, gate, up, w_wide, w_down_rows],
        flops=2 * 512 * 2304 * 1024, nbytes=12 << 20,
    )

    far = dh_mine[128:] + swap(dh_part[128:], CORE_SWAP).astype(F32)
    far, d_gu, dm_all = lax.optimization_barrier((far.astype(BF16), d_gu, dm_all))
    far = swap(far, Z_SWAP)
    (grad_mlp,) = kernel_call(
        expand_grad_body,
        in_hbm(shaped((1024, 2304), BF16)),
        [h_turned, d_gu, expanded, dm_all],
        [pltpu.VMEM((768, 512), BF16)],
        flops=2 * 512 * 2304 * 1024, nbytes=9 << 20,
    )
    far, grad_mlp = lax.optimization_barrier((far, grad_mlp))
    grad_mlp = lax.psum_scatter(grad_mlp, "fsdp", scatter_dimension=0, tiled=True)
    d_hidden = upstream + dh_mine[:128] + swap(dh_part[:128], CORE_SWAP).astype(F32)
    d_hidden = d_hidden + far.astype(F32)

    grad_gain_attn = jnp.sum(d_hidden * attn_hat, axis=0)
    d_attended = norm_back(d_hidden * gain_attn, attn_hat, attn_scale).astype(BF16)
    d_tiles, deltas, grad_out = kernel_call(
        output_back_body,
        [shaped((8, 256, 128), BF16), shaped((8, 2, 128), F32), shaped((256, 1024), BF16)],
        [place, *in_hbm(out_raw, w_out_rows, gather_group(d_attended), mixed_turned)],
        flops=4 * 1024 * 1024 * 256, nbytes=6 << 20,
    )
    def halve(value, rows, bit, axis, pairs):
        parts = value.reshape(-1, 2, rows, 1024)
        given = jnp.where(bit == 1, parts[:, 0], parts[:, 1])
        mine = jnp.where(bit == 1, parts[:, 1], parts[:, 0]).astype(F32)
        return (mine + lax.ppermute(given, axis, pairs).astype(F32)).astype(BF16)

    grad_out = halve(grad_out, 32, fsdp % 2, "fsdp", [(i, i ^ 1) for i in range(8)])
    dq, dk, dv, d_low, dots = kernel_call(
        attend_back_body,
        [
            *in_hbm(
                shaped((1024, 256), BF16), shaped((1024, 128), F32), shaped((1024, 128), F32),
                shaped((1024, 256), BF16),
            ),
            shaped((24, 128), F32),
        ],
        [place, *in_hbm(q_tiles, keys, vals), logs, d_tiles, deltas],
        [
            pltpu.VMEM((128, 2048), BF16), pltpu.VMEM((2048, 128), F32),
            pltpu.VMEM((2048, 128), F32),
        ],
        flops=10 * 1024 * 2048 * 256, nbytes=8 << 20,
    )
    dots, grad_out = lax.optimization_barrier((dots, grad_out))
    grad_out = halve(grad_out, 32, fsdp // 2 % 2, "fsdp", [(i, i ^ 2) for i in range(8)])
    grad_out = halve(grad_out, 32, fsdp // 4, "fsdp", [(i, i ^ 4) for i in range(8)])
    d_got = swap(d_low, HIGH_TO_LOW)
    dots = sum_group(dots)
    dots_got = swap(dots[16:], HIGH_TO_LOW)

    gains = jnp.concatenate([grad_gain_attn.reshape(128, 8), grad_gain_mlp.reshape(128, 8)], axis=1)
    gains = gains.reshape(16, 8, 16).swapaxes(0, 1).reshape(128, 16)
    gains = jnp.broadcast_to(
        jnp.pad(gains.astype(BF16), ((0, 0), (24, 88)))[:, None, :], (128, 8, 128)
    ).reshape(1024, 128)
    d_made, sent = kernel_call(
        unproject_body,
        [*in_hbm(shaped((1024, 512), BF16)), shaped((1024, 640), BF16)],
        [
            place, *in_hbm(dq, dk, dv), d_got, *in_hbm(q_raw, k_raw), squares, dots, dots_got, cosine, sine,
            gain_q, gain_k, *in_hbm(x_turned), gains,
        ],
        [pltpu.VMEM((8, 384), F32)],
        flops=2 * 1024 * 1024 * 512, nbytes=9 << 20,
    )

    def halves(value, upper):
        low, high = value[: value.shape[0] // 2], value[value.shape[0] // 2 :]
        return jnp.where(upper, high, low), jnp.where(upper, low, high)

    mine, given = halves(grad_mlp, xh == 1)
    mine = mine.astype(F32) + swap(given, X_SWAP).astype(F32)
    sent, grad_out = lax.optimization_barrier((sent, grad_out))
    grad_mlp = after(grad_mlp, sent)
    grad_down = jnp.concatenate(
        [
            piece
            for h in (0, 64)
            for piece in [
                jnp.concatenate(
                    [
                        grad_mlp[h : h + 48, 1536:],
                        jnp.concatenate(
                            [
                                grad_mlp[h + 48 : h + 64, 1536 + m * 256 : 1792 + m * 256]
                                for m in range(3)
                            ],
                            axis=0,
                        ),
                    ],
                    axis=1,
                )
            ]
        ],
        axis=0,
    ).reshape(4, 24, 1024)
    grad_down = sum(
        lax.ppermute(
            lax.dynamic_index_in_dim(grad_down, (xh * 2 + z // 2) ^ other, 0, keepdims=False),
            ("seq", "fsdp"),
            down_home(other),
        ).astype(F32)
        for other in range(4)
    )
    got_made = lax.all_to_all(
        sent.reshape(8, 128, 640), "fsdp", split_axis=0, concat_axis=0, tiled=True
    )
    dx_mine, dx_part = kernel_call(
        input_body,
        in_hbm(shaped((512, 1024), F32), shaped((512, 1024), BF16)),
        [*in_hbm(after(d_made, sent)), weight],
        flops=2 * 1024 * 1024 * 512, nbytes=5 << 20,
    )
    rows = [slice(k * 128, k * 128 + 128) for k in range(4)]
    pieces = [dx_mine[r] + swap(dx_part[r], CORE_SWAP).astype(F32) for r in rows]
    far = [piece.astype(BF16) for piece in pieces[1:]]
    (collected,) = kernel_call(
        collect_body,
        [shaped((128, 2176), BF16)],
        [got_made.reshape(1024, 640), grad_mlp],
        flops=WAIT_FLOPS, nbytes=3 << 20,
    )
    got = lax.all_to_all(
        collected.reshape(16, 8, 2176), "seq", split_axis=0, concat_axis=0, tiled=True
    )
    grad_out = grad_out.reshape(2, 16, 1024)
    own = jnp.where(xh == 1, grad_out[1], grad_out[0])
    given = jnp.where(xh == 1, grad_out[0], grad_out[1])
    own = swap(own, out_home(False))
    grad_out = own.astype(F32) + swap(given, out_home(True)).astype(F32)
    d_inputs = pieces[0] + sum(
        swap(piece, to_z(k)).astype(F32) for k, piece in enumerate(far, 1)
    )
    got = got.reshape(2, 8, 8, 2176).astype(F32)
    summed = got[0, :, :, :640] + got[1, :, :, :640]
    gains = jnp.sum(summed[:, 0, 512:], axis=0)

    def take(first, width):
        return summed[:, :, first : first + width].swapaxes(0, 1).reshape(8, 8 * width)

    wide = jnp.sum(got[:, :, :, 640:].reshape(2, 2, 4, 8, 2, 8, 96), axis=(0, 1))
    wide = wide.transpose(2, 1, 3, 0, 4).reshape(2, 8, 3072)
    return (
        output,
        (d_hidden + d_inputs).astype(BF16)[None],
        take(0, 256),
        take(256, 128),
        take(384, 128),
        grad_out.astype(F32),
        wide[0],
        wide[1],
        grad_down.astype(F32),
        gains[:16],
        gains[16:24],
        gains[24:32],
        gains[32:40],
    )


def solution(mesh):
    rows = P("fsdp", "seq", None)
    weight = P("fsdp", None)
    grad = P(("seq", "fsdp"), None)
    gain = P(("seq", "fsdp"))
    return jax.shard_map(
        on_device,
        mesh=mesh,
        in_specs=(rows,) * 2 + (weight,) * 7 + (P(),) * 4,
        out_specs=(rows,) * 2 + (grad,) * 7 + (gain,) * 4,
        check_vma=False,
    )
```

```python
import functools
import math

import jax
import jax.numpy as jnp
from jax import lax
from jax.experimental import pallas as pl
from jax.experimental.pallas import tpu as pltpu
from jax.sharding import PartitionSpec as P

BF16 = jnp.bfloat16
F32 = jnp.float32
DH = 128
EPS = 1e-06
THETA = 1000000.0
MASKED = -1e30
LOG2E = math.log2(math.e)
QUERY_SCALE = DH ** (-0.5) * LOG2E
VMEM_BYTES = 20 * 1024 * 1024
VMEM = pl.BlockSpec(memory_space=pltpu.VMEM)
SMEM = pl.BlockSpec(memory_space=pltpu.SMEM)
ANY = pl.BlockSpec(memory_space=pl.ANY)
SMALL = 64 * 1024
WAIT_FLOPS = 12 * 10**9
NT = (((1,), (1,)), ((), ()))

SEQ_PLACES = [(xh, z, c) for xh in range(2) for z in range(4) for c in range(2)]


def seq_index(xh, z, c):
    return xh * 8 + (z % 4) * 2 + c


CORE_SWAP = [(i, i ^ 1) for i in range(16)]
LOW_TO_HIGH = [(i, i + 8) for i in range(8)]
HIGH_TO_LOW = [(i + 8, i) for i in range(8)]
X_SWAP = [(i, i ^ 8) for i in range(16)]


def from_z(k):
    return [(seq_index(xh, z + k, c), seq_index(xh, z, c)) for xh, z, c in SEQ_PLACES]


def to_z(k):
    return [(seq_index(xh, z, c), seq_index(xh, z + k, c)) for xh, z, c in SEQ_PLACES]


def across(pairs):
    return [(seq * 8 + f, to_seq * 8 + to_f) for seq, f, to_seq, to_f in pairs]


TURN = across(
    (xh * 8 + a, f, xh * 8 + f, a) for xh in range(2) for a in range(8) for f in range(8)
)
Z_SWAP = [(i, i ^ 2) for i in range(16)]
FAR_SWAP = [(i, i ^ 4) for i in range(16)]


def out_home(other):
    return [(xh * 8 + a, 2 * a + (xh ^ other)) for xh in range(2) for a in range(8)]


def down_home(other):
    return across(
        (seq_index(own // 2, 2 * (own % 2) + zl, c), f, 2 * f + zl, 4 * c + (own ^ other))
        for own in range(4) for zl in range(2) for c in range(2) for f in range(8)
    )


def swap(value, pairs):
    return lax.ppermute(value, "seq", pairs)


def after(value, *others):
    return lax.optimization_barrier((value, *others))[0]


def gather_group(block):
    far = {k: swap(block, from_z(k)) for k in (2, 1, 3)}
    mine = [block, far[1], far[2], far[3]]
    return mine + [swap(v, CORE_SWAP) for v in mine]


def scatter_group(mine, part):
    rows = [slice(k * 128, k * 128 + 128) for k in range(4)]
    out = None
    for k in (2, 1, 3, 0):
        piece = mine[rows[k]] + swap(part[rows[k]], CORE_SWAP).astype(F32)
        if k:
            piece = swap(piece.astype(BF16), to_z(k)).astype(F32)
        out = piece if out is None else out + piece
    return out


def gather_pair(block):
    mine = [block, swap(block, Z_SWAP)]
    return mine + [swap(v, CORE_SWAP) for v in mine]


def scatter_pair(mine, part, later=()):
    far = mine[128:] + swap(part[128:], CORE_SWAP).astype(F32)
    far, *later = lax.optimization_barrier((far.astype(BF16), *later))
    far = swap(far, Z_SWAP).astype(F32)
    return mine[:128] + swap(part[:128], CORE_SWAP).astype(F32) + far, later


def sum_group(rows):
    groups = rows.shape[0] // 8
    other = swap(rows, CORE_SWAP).reshape(groups, 2, 4, 128)
    pair = rows.reshape(groups, 2, 4, 128) + jnp.concatenate([other[:, 1:], other[:, :1]], axis=1)
    odd = lax.axis_index("seq") // 2 % 2 == 1
    got = swap(pair, Z_SWAP)
    up = jnp.concatenate([got[:, :, 3:], got[:, :, :3]], axis=2)
    down = jnp.concatenate([got[:, :, 1:], got[:, :, :1]], axis=2)
    pair = pair + jnp.where(odd, down, up)
    got = swap(pair, FAR_SWAP)
    pair = pair + jnp.concatenate([got[:, :, 2:], got[:, :, :2]], axis=2)
    return pair.reshape(rows.shape)


def column(row):
    return jnp.transpose(jnp.broadcast_to(row, (128, 128)))


def row_sums(values):
    return jnp.sum(jnp.transpose(values), axis=0, keepdims=True)


def shaped(shape, dtype):
    return jax.ShapeDtypeStruct(shape, dtype)


class Kept:
    def __init__(self, value):
        self.value = value


def in_hbm(*values):
    return [Kept(v) for v in values]


def kernel_call(body, outs, inputs, scratch=(), flops=0, nbytes=0):
    hbm_outs = [isinstance(o, Kept) for o in outs]
    hbm_ins = [isinstance(x, Kept) for x in inputs]
    outs = [o.value if isinstance(o, Kept) else o for o in outs]
    inputs = [x.value if isinstance(x, Kept) else x for x in inputs]
    groups = [x if isinstance(x, list) else [x] for x in inputs]
    flat = [a for group in groups for a in group]
    joined = [
        shaped((sum(a.shape[0] for a in group),) + group[0].shape[1:], group[0].dtype)
        for group in groups
    ]

    def large(s):
        return math.prod(s.shape) * s.dtype.itemsize >= SMALL

    def where(s):
        return ANY if large(s) else SMEM if s.dtype == jnp.int32 else VMEM

    out_shapes = [joined[o] if isinstance(o, int) else o for o in outs]
    in_buffers = [pltpu.VMEM(s.shape, s.dtype) for s in joined if large(s)]
    out_buffers = [
        pltpu.VMEM(o.shape, o.dtype) for o in outs if not isinstance(o, int) and large(o)
    ]

    def whole(*refs):
        refs = list(refs)

        def pull(count):
            taken = refs[:count]
            del refs[:count]
            return taken

        in_refs, out_refs = pull(len(flat)), pull(len(outs))
        in_space, out_space = pull(len(in_buffers)), pull(len(out_buffers))
        own, (in_sem, out_sem) = pull(len(scratch)), refs
        loads, ins, at = {}, [], 0
        for group, s in zip(groups, joined):
            if not large(s):
                ins.append(in_refs[at])
                at += 1
                continue
            space, row = in_space.pop(0), 0
            loads[id(space)] = []
            for a in group:
                copy = pltpu.make_async_copy(
                    in_refs[at], space.at[pl.ds(row, a.shape[0])], in_sem.at[at]
                )
                copy.start()
                loads[id(space)].append(copy)
                row, at = row + a.shape[0], at + 1
            ins.append(space)
        made, stores = [], {}
        for k, (o, s, ref) in enumerate(zip(outs, out_shapes, out_refs)):
            if not large(s):
                made.append(ref)
                continue
            space = ins[o] if isinstance(o, int) else out_space.pop(0)
            stores[id(space)] = pltpu.make_async_copy(space, ref, out_sem.at[k])
            if not isinstance(o, int):
                made.append(space)
        started = []

        def ready(*spaces):
            for space in spaces:
                for copy in loads.pop(id(space), ()):
                    copy.wait()

        def done(*spaces):
            for space in spaces:
                copy = stores.pop(id(space))
                copy.start()
                started.append(copy)

        body(ready, done, *ins, *made, *own)
        for key in list(stores):
            copy = stores.pop(key)
            copy.start()
            started.append(copy)
        for copy in started:
            copy.wait()

    shapes = [pltpu.HBM(s.shape, s.dtype) if hbm else s for s, hbm in zip(out_shapes, hbm_outs)]
    return pl.pallas_call(
        whole,
        out_shape=tuple(shapes),
        in_specs=[where(s) for group, s in zip(groups, joined) for _ in group],
        out_specs=tuple(where(s) for s in out_shapes),
        scratch_shapes=[
            *in_buffers, *out_buffers, *scratch,
            pltpu.SemaphoreType.DMA((len(flat),)), pltpu.SemaphoreType.DMA((len(outs),)),
        ],
        compiler_params=pltpu.CompilerParams(vmem_limit_bytes=VMEM_BYTES),
        cost_estimate=pl.CostEstimate(flops=flops, bytes_accessed=nbytes, transcendentals=0),
    )(
        *[
            pltpu.with_memory_space_constraint(a, pltpu.HBM) if hbm else a
            for group, hbm in zip(groups, hbm_ins)
            for a in group
        ],
    )


def root(total, width):
    return lax.rsqrt(total * (1.0 / width) + EPS)


def project_body(
    ready, done, x_all, weight, gain_q, gain_k, cos, sin,
    q_raw, k_raw, q_rot, kv_rot, squares,
):
    ready(x_all, weight, cos, sin)
    done(x_all)

    def step(t, carry):
        at = pl.multiple_of(t * 256, 256)
        made = jnp.dot(x_all[pl.ds(at, 256), :], weight[...], preferred_element_type=F32)
        for part in range(2):
            rows = pl.ds(at + part * 128, 128)
            block = t * 2 + part
            here = made[part * 128 : part * 128 + 128]
            q, k = here[:, :256], here[:, 256:384]
            kv_rot[rows, 128:] = here[:, 384:].astype(BF16)
            q_raw[rows, :] = q
            k_raw[rows, :] = k
            squares[pl.ds(block, 1), :] = row_sums(
                q[:, :128] * q[:, :128] + q[:, 128:] * q[:, 128:]
            )
            squares[pl.ds(block + 8, 1), :] = row_sums(k * k)
            cosine, sine = cos[rows, :], sin[rows, :]
            for head in range(2):
                lanes = slice(head * 128, head * 128 + 128)
                turn = q[:, lanes] * gain_q[:, lanes]
                q_rot[rows, lanes] = (turn * cosine + pltpu.roll(turn, 64, 1) * sine).astype(BF16)
            turn = k * gain_k[...]
            kv_rot[rows, :128] = (turn * cosine + pltpu.roll(turn, 64, 1) * sine).astype(BF16)
        return carry

    lax.fori_loop(0, 4, step, 0)


def spot(place, block):
    z = lax.rem(place[1] + block % 4, 4)
    c = place[2] if block < 4 else 1 - place[2]
    return z, c


def diagonal():
    query = lax.broadcasted_iota(jnp.int32, (256, 512), 1) % 256
    return lax.broadcasted_iota(jnp.int32, (256, 512), 0) <= query


def attend_body(
    ready, done, place, q_rot, kv_rot, kv_low, squares, squares_low,
    out_raw, out_low, out_turned, q_tiles, keys, vals, logs, vals_t,
):
    ready(q_rot, kv_rot, kv_low)
    for b in range(8):
        rows = slice(b * 128, b * 128 + 128)
        z, c = spot(place, b)
        r = column(root(squares[b : b + 1, :], 2048.0)) * QUERY_SCALE
        inner = pl.ds(pl.multiple_of(c * 128, 128), 128)
        for head in range(2):
            q = q_rot[rows, head * 128 : head * 128 + 128].astype(F32)
            q_tiles[z * 2 + head, inner, :] = (q * r).astype(BF16)
        at = pl.ds(pl.multiple_of(1024 + z * 256 + c * 128, 128), 128)
        r = column(root(squares[8 + b : 9 + b, :], 1024.0))
        keys[at, :] = (kv_rot[rows, :128].astype(F32) * r).astype(BF16)
        vals[at, :] = kv_rot[rows, 128:]
        r = column(root(squares_low[b : b + 1, :], 1024.0))
        keys[rows, :] = (kv_low[rows, :128].astype(F32) * r).astype(BF16)
        vals[rows, :] = kv_low[rows, 128:]
    done(q_tiles, keys, vals)
    vals_t[...] = jnp.transpose(vals[...].astype(F32)).astype(BF16)

    def queries(first, i):
        at_diagonal = 1024 + i * 256
        q = q_tiles[i * 2 : i * 2 + 2].reshape(512, 128)
        ranges = [(lo, lo + 256) for lo in range(first, at_diagonal + 256, 256)]
        scores = [
            lax.dot_general(keys[lo:hi, :], q, NT, preferred_element_type=F32) for lo, hi in ranges
        ]
        scores[-1] = jnp.where(diagonal(), scores[-1], MASKED)
        top = functools.reduce(jnp.maximum, [jnp.max(s, axis=0, keepdims=True) for s in scores])
        total, acc = 0.0, 0.0
        for s, (lo, hi) in zip(scores, ranges):
            p = jnp.exp2(s - top)
            total = total + jnp.sum(p, axis=0, keepdims=True)
            acc = acc + jnp.dot(vals_t[:, lo:hi], p.astype(BF16), preferred_element_type=F32)
        acc = acc / total
        log = top + jnp.log2(total)
        for head in range(2):
            turned = acc[:, head * 256 : head * 256 + 256]
            out = jnp.transpose(turned)
            turned = turned.astype(BF16)
            logs[i * 2 + head : i * 2 + head + 1, :] = log[:, head * 256 : head * 256 + 256]
            for c in range(2):
                block = lax.rem(i - place[1] + 4, 4) + 4 * jnp.abs(c - place[2])
                at = pl.ds(pl.multiple_of(block * 128, 128), 128)
                lanes = slice(head * 128, head * 128 + 128)
                out_raw[at, lanes] = out[c * 128 : c * 128 + 128, :]
                out_low[at, lanes] = out[c * 128 : c * 128 + 128, :].astype(BF16)
                out_turned[lanes, at] = turned[:, c * 128 : c * 128 + 128]

    @pl.when(place[0] == 1)
    def _():
        for i in range(4):
            queries(0, i)

    @pl.when(place[0] == 0)
    def _():
        for i in range(4):
            queries(1024, i)

    done(out_raw, out_low, out_turned)


def output_body(ready, done, place, mixed, w_own, w_got, a_mine, a_part, w_out):
    ready(w_own, w_got)
    w_out[pl.ds(pl.multiple_of(place[3] * 128, 128), 128), :] = w_own[...]
    w_out[pl.ds(pl.multiple_of((1 - place[3]) * 128, 128), 128), :] = w_got[...]
    done(w_out)
    ready(mixed)

    def project(t, carry):
        at = pl.ds(pl.multiple_of(t * 256, 256), 256)
        far = pl.ds(pl.multiple_of(512 + t * 256, 256), 256)
        a_part[at, :] = jnp.dot(mixed[far, :], w_out[...], preferred_element_type=F32).astype(BF16)
        a_mine[at, :] = jnp.dot(mixed[at, :], w_out[...], preferred_element_type=F32)
        return carry

    lax.fori_loop(0, 2, project, 0)


def output_back_body(
    ready, done, place, out_raw, w_out, da_all, mixed_turned, d_tiles, deltas, grad_out
):
    ready(out_raw, w_out, da_all)
    for b in range(8):
        rows = slice(b * 128, b * 128 + 128)
        z, c = spot(place, b)
        inner = pl.ds(pl.multiple_of(c * 128, 128), 128)
        d_out = lax.dot_general(
            da_all[rows, :], w_out[...], NT, preferred_element_type=F32
        ).astype(BF16)
        for head in range(2):
            lanes = slice(head * 128, head * 128 + 128)
            grad = d_out[:, lanes]
            d_tiles[z * 2 + head, inner, :] = grad
            deltas[z * 2 + head, pl.ds(c, 1), :] = row_sums(grad.astype(F32) * out_raw[rows, lanes])
    done(d_tiles)
    ready(mixed_turned)
    for m in range(4):
        lanes = slice(m * 256, m * 256 + 256)
        made = jnp.dot(mixed_turned[...], da_all[:, lanes], preferred_element_type=F32).astype(BF16)
        for j in range(2):
            for f in range(8):
                to, at = f * 32 + j * 16, j * 128 + f * 16
                grad_out[to : to + 16, lanes] = made[at : at + 16]


def attend_back_body(
    ready, done, place, q_tiles, keys, vals, logs, d_tiles, deltas,
    dq, dk, dv, d_low, dots, keys_t, dk_acc, dv_acc,
):
    ready(keys)
    keys_t[...] = jnp.transpose(keys[...].astype(F32)).astype(BF16)
    dk_acc[...] = jnp.zeros_like(dk_acc)
    dv_acc[...] = jnp.zeros_like(dv_acc)
    ready(q_tiles, vals, d_tiles)

    def queries(first, i):
        at_diagonal = 1024 + i * 256
        q = q_tiles[i * 2 : i * 2 + 2].reshape(512, 128)
        grad = d_tiles[i * 2 : i * 2 + 2].reshape(512, 128)
        log = jnp.concatenate([logs[i * 2 : i * 2 + 1, :], logs[i * 2 + 1 : i * 2 + 2, :]], axis=1)
        delta = jnp.concatenate(
            [deltas[i * 2 + head, c : c + 1, :] for head in range(2) for c in range(2)], axis=1
        )
        total = 0.0
        for lo in range(first, at_diagonal + 256, 256):
            at = slice(lo, lo + 256)
            k, v = keys[at, :], vals[at, :]
            s = lax.dot_general(k, q, NT, preferred_element_type=F32)
            p = jnp.exp2(s - log)
            if lo == at_diagonal:
                p = jnp.where(diagonal(), p, 0.0)
            dp = lax.dot_general(v, grad, NT, preferred_element_type=F32)
            ds = (p * (dp - delta)).astype(BF16)
            dv_acc[at, :] += jnp.dot(p.astype(BF16), grad, preferred_element_type=F32)
            dk_acc[at, :] += jnp.dot(ds, q, preferred_element_type=F32)
            total = total + jnp.dot(keys_t[:, at], ds, preferred_element_type=F32)
        dot = total * jnp.transpose(q.astype(F32))
        dot = jnp.sum(dot[:, :256] + dot[:, 256:], axis=0, keepdims=True)
        for head in range(2):
            out = jnp.transpose(total[:, head * 256 : head * 256 + 256]) * DH ** (-0.5)
            for c in range(2):
                block = lax.rem(i - place[1] + 4, 4) + 4 * jnp.abs(c - place[2])
                at = pl.ds(pl.multiple_of(block * 128, 128), 128)
                dq[at, head * 128 : head * 128 + 128] = out[c * 128 : c * 128 + 128, :].astype(BF16)
        for c in range(2):
            block = lax.rem(i - place[1] + 4, 4) + 4 * jnp.abs(c - place[2])
            dots[pl.ds(block, 1), :] = dot[:, c * 128 : c * 128 + 128] * (1.0 / LOG2E)

    @pl.when(place[0] == 1)
    def _():
        for i in range(4):
            queries(0, i)

    @pl.when(place[0] == 0)
    def _():
        for i in range(4):
            queries(1024, i)

    done(dq)
    for b in range(8):
        rows = slice(b * 128, b * 128 + 128)
        z, c = spot(place, b)
        at = pl.ds(pl.multiple_of(1024 + z * 256 + c * 128, 128), 128)
        key_grad = dk_acc[at, :] * (1.0 / LOG2E)
        dk[rows, :] = key_grad
        dv[rows, :] = dv_acc[at, :]
        dots[8 + b : 9 + b, :] = row_sums(key_grad * keys[at, :].astype(F32))
        key_grad = dk_acc[rows, :] * (1.0 / LOG2E)
        d_low[rows, :128] = key_grad.astype(BF16)
        d_low[rows, 128:] = dv_acc[rows, :].astype(BF16)
        dots[16 + b : 17 + b, :] = row_sums(key_grad * keys[rows, :].astype(F32))


def unproject_body(
    ready, done, place, dq, dk, dv, d_got, q_raw, k_raw, squares, dots, dots_got, cos, sin,
    gain_q, gain_k, x_turned, gains, d_made, sent, sums,
):
    sums[...] = jnp.zeros_like(sums)
    ready(dq, dk, dv, d_got, q_raw, k_raw, cos, sin)

    def step(b, carry):
        rows = pl.ds(pl.multiple_of(b * 128, 128), 128)
        cosine, sine = cos[rows, :], sin[rows, :]
        r = column(root(squares[pl.ds(b, 1), :], 2048.0))
        mean = column(dots[pl.ds(b, 1), :]) * (1.0 / 2048.0)
        for head in range(2):
            lanes = slice(head * 128, head * 128 + 128)
            turn = dq[rows, lanes].astype(F32)
            d_norm = turn * cosine - pltpu.roll(turn, 64, 1) * sine
            hat = q_raw[rows, lanes] * r
            sums[0:1, lanes] += jnp.sum(d_norm * hat, axis=0, keepdims=True)
            d_made[rows, lanes] = (r * (d_norm * gain_q[:, lanes] - hat * mean)).astype(BF16)
        r = column(root(squares[pl.ds(b + 8, 1), :], 1024.0))
        mean = column(dots[pl.ds(b + 8, 1), :] + dots_got[pl.ds(b, 1), :]) * (1.0 / 1024.0)
        turn = dk[rows, :] + d_got[rows, :128].astype(F32)
        d_norm = turn * cosine - pltpu.roll(turn, 64, 1) * sine
        hat = k_raw[rows, :] * r
        sums[0:1, 256:] += jnp.sum(d_norm * hat, axis=0, keepdims=True)
        d_made[rows, 256:384] = (r * (d_norm * gain_k[...] - hat * mean)).astype(BF16)
        d_made[rows, 384:] = (dv[rows, :] + d_got[rows, 128:].astype(F32)).astype(BF16)
        return carry

    lax.fori_loop(0, 8, step, 0)
    done(d_made)
    ready(x_turned, gains)

    def grad(t, carry):
        rows = pl.ds(pl.multiple_of(t * 256, 256), 256)
        sent[rows, :512] = jnp.dot(
            x_turned[rows, :], d_made[...], preferred_element_type=F32
        ).astype(BF16)
        sent[rows, 512:] = gains[rows, :]
        return carry

    lax.fori_loop(0, 4, grad, 0)
    extra = 0.0
    for lo, width, each, first in ((0, 256, 16, 0), (256, 128, 8, 16)):
        row = lax.broadcasted_iota(jnp.int32, (128, width), 0)
        lane = lax.broadcasted_iota(jnp.int32, (128, width), 1) // each
        here = row // 8 % 2 * 8 + row // 16 == lane
        spread = jnp.where(here, sums[0:1, lo : lo + width], 0.0).astype(BF16)
        lane = lax.broadcasted_iota(jnp.int32, (width, 128), 0) % each + first
        pick = jnp.where(lane == lax.broadcasted_iota(jnp.int32, (width, 128), 1), 1.0, 0.0)
        extra = extra + jnp.dot(spread, pick.astype(BF16), preferred_element_type=F32)
    for f in range(8):
        rows = pl.ds(pl.multiple_of(f * 128 + (place[1] * 2 + place[2]) * 16, 16), 16)
        added = gains[rows, :].astype(F32) + extra[f * 16 : f * 16 + 16]
        sent[rows, 512:] = added.astype(BF16)


def input_body(ready, done, d_made, weight, dx_mine, dx_part):
    ready(d_made, weight)

    def step(t, carry):
        at = pl.ds(pl.multiple_of(t * 256, 256), 256)
        far = pl.ds(pl.multiple_of(512 + t * 256, 256), 256)
        dx_part[at, :] = lax.dot_general(
            d_made[far, :], weight[...], NT, preferred_element_type=F32
        ).astype(BF16)
        dx_mine[at, :] = lax.dot_general(
            d_made[at, :], weight[...], NT, preferred_element_type=F32
        )
        return carry

    lax.fori_loop(0, 2, step, 0)


def expand_body(ready, done, h_all, weight, packed, gate, up, expanded, m_mine, m_part, down):
    ready(h_all, weight)
    done(h_all)
    def widen(n, carry):
        lanes = pl.ds(pl.multiple_of(n * 256, 256), 256)
        upper = pl.ds(pl.multiple_of(768 + n * 256, 256), 256)
        g = jnp.dot(h_all[...], weight[:, lanes], preferred_element_type=F32)
        u = jnp.dot(h_all[...], weight[:, upper], preferred_element_type=F32)
        gate[:, lanes] = g
        up[:, lanes] = u
        expanded[:, lanes] = (g * jax.nn.sigmoid(g) * u).astype(BF16)
        return carry

    lax.fori_loop(0, 3, widen, 0)
    done(gate, up, expanded)
    ready(packed)
    for f in range(8):
        down[f * 96 : f * 96 + 96, :768] = packed[f * 128 : f * 128 + 96, :]
        for m in range(3):
            down[f * 96 + m * 32 : f * 96 + m * 32 + 32, 768:] = packed[
                f * 128 + 96 : f * 128 + 128, m * 256 : m * 256 + 256
            ]
    done(down)

    def narrow(n, carry):
        lanes = pl.ds(pl.multiple_of(n * 256, 256), 256)
        m = jnp.dot(expanded[...], down[:, lanes], preferred_element_type=F32)
        m_mine[:, lanes] = m[:256]
        m_part[:, lanes] = m[256:].astype(BF16)
        return carry

    lax.fori_loop(0, 4, narrow, 0)


def expand_back_body(ready, done, dm_all, gate, up, weight, down, d_gu, dh_mine, dh_part):
    ready(dm_all, gate, up, down)
    done(dm_all)

    def widen(n, carry):
        lanes = pl.ds(pl.multiple_of(n * 256, 256), 256)
        upper = pl.ds(pl.multiple_of(768 + n * 256, 256), 256)
        de = lax.dot_general(dm_all[...], down[lanes, :], NT, preferred_element_type=F32)
        g = gate[:, lanes]
        sig = jax.nn.sigmoid(g)
        d_gu[:, lanes] = (de * up[:, lanes] * sig * (1.0 + g * (1.0 - sig))).astype(BF16)
        d_gu[:, upper] = (de * (g * sig)).astype(BF16)
        return carry

    lax.fori_loop(0, 3, widen, 0)
    done(d_gu)
    ready(weight)

    def narrow(n, carry):
        lanes = pl.ds(pl.multiple_of(n * 256, 256), 256)
        dh = lax.dot_general(d_gu[...], weight[lanes, :], NT, preferred_element_type=F32)
        dh_mine[:, lanes] = dh[:256]
        dh_part[:, lanes] = dh[256:].astype(BF16)
        return carry

    lax.fori_loop(0, 4, narrow, 0)


def expand_grad_body(ready, done, h_turned, d_gu, expanded, dm_all, out, expanded_t):
    ready(expanded)
    expanded_t[...] = jnp.transpose(expanded[...].astype(F32)).astype(BF16)

    ready(h_turned, d_gu, dm_all)

    def widen(n, carry):
        lanes = pl.ds(pl.multiple_of(n * 256, 256), 256)
        out[:, lanes] = jnp.dot(
            h_turned[...], d_gu[:, lanes], preferred_element_type=F32
        ).astype(BF16)
        return carry

    lax.fori_loop(0, 6, widen, 0)
    for n in range(4):
        made = jnp.dot(
            expanded_t[...], dm_all[:, n * 256 : n * 256 + 256], preferred_element_type=F32
        ).astype(BF16)
        for f in range(16):
            if n < 3:
                out[f * 64 : f * 64 + 48, 1536 + n * 256 : 1792 + n * 256] = made[
                    f * 48 : f * 48 + 48
                ]
                continue
            for m in range(3):
                out[f * 64 + 48 : f * 64 + 64, 1536 + m * 256 : 1792 + m * 256] = made[
                    f * 48 + m * 16 : f * 48 + m * 16 + 16
                ]


def collect_body(ready, done, got, grad_mlp, out):
    ready(got)
    total = got[:128, :].astype(F32)
    for f in range(1, 8):
        total = total + got[f * 128 : f * 128 + 128, :].astype(F32)
    out[:, :640] = total.astype(BF16)
    ready(grad_mlp)
    out[:, 640:] = grad_mlp[:, :1536]


def norm_scale(values):
    return lax.rsqrt(jnp.mean(values * values, axis=-1, keepdims=True) + EPS)


def norm_back(upstream, normed, scaling):
    return scaling * (upstream - normed * jnp.mean(upstream * normed, axis=-1, keepdims=True))


def rotary_tables(first, z, c):
    half = DH // 2
    k = jnp.arange(4, dtype=jnp.int32)
    starts = jnp.concatenate([((z + k) % 4) * 256 + c * 128, ((z + k) % 4) * 256 + (1 - c) * 128])
    places = (first + starts[:, None] + jnp.arange(128, dtype=jnp.int32)[None, :]).reshape(1024)
    inverse = THETA ** (-(jnp.arange(half, dtype=F32) * (2.0 / DH)))
    angles = places.astype(F32)[:, None] * inverse[None, :]
    cosine, sine = jnp.cos(angles), jnp.sin(angles)
    return (
        jnp.concatenate([cosine, cosine], axis=-1),
        jnp.concatenate([-sine, sine], axis=-1),
    )


def dot(a, b):
    return jnp.dot(a, b, preferred_element_type=F32)


def dot_nt(a, b):
    return lax.dot_general(a, b, NT, preferred_element_type=F32)


def dot_tn(a, b):
    return lax.dot_general(a, b, (((0,), (0,)), ((), ())), preferred_element_type=F32)


def on_device(
    tokens, out_grad, w_query, w_key, w_value, w_out, w_gate, w_up, w_down,
    gain_query, gain_key, gain_attn, gain_mlp,
):
    seq = lax.axis_index("seq")
    xh, zc = seq // 8, seq % 8
    z, c = zc // 2, zc % 2
    quarter = (z % 2) * 2 + c
    fsdp = lax.axis_index("fsdp")
    place = jnp.stack([xh, z, c, fsdp // 4]).astype(jnp.int32)
    inputs = tokens[0]

    def columns(weight, width):
        return lax.dynamic_slice_in_dim(weight, zc * width, width, 1)

    def spread(block):
        return lax.all_to_all(
            jnp.broadcast_to(block[None], (8,) + block.shape),
            "fsdp", split_axis=0, concat_axis=0, tiled=True,
        ).reshape(8 * block.shape[0], block.shape[1])

    x_blocks = gather_group(inputs)
    weight = spread(
        jnp.concatenate(
            [columns(w_query, 256), columns(w_key, 128), columns(w_value, 128)], axis=1
        )
    )
    w_out_rows = lax.ppermute(
        after(lax.dynamic_slice_in_dim(w_out, zc * 32, 32, 0), weight),
        ("seq", "fsdp"),
        TURN,
    )

    def quarters(weight):
        part = lax.dynamic_slice_in_dim(weight.reshape(128, 8, 384), quarter * 96, 96, 2)
        return part.reshape(128, 768)

    down = lax.dynamic_slice_in_dim(w_down, quarter * 96, 96, 0)
    packed = jnp.concatenate(
        [
            down[:, :768],
            jnp.concatenate([down[m * 32 : m * 32 + 32, 768:] for m in range(3)], axis=1),
        ],
        axis=0,
    )
    w_narrow = lax.all_gather(packed, "fsdp", axis=0, tiled=True)
    w_wide = jnp.concatenate([quarters(w_gate), quarters(w_up)], axis=1)
    weight, w_wide = lax.optimization_barrier((weight, w_wide))

    cosine, sine = rotary_tables(xh * 1024, z, c)
    gain_q = lax.dynamic_slice_in_dim(gain_query, zc * 256, 256, 0)[None]
    gain_k = lax.dynamic_slice_in_dim(gain_key, zc * 128, 128, 0)[None]
    x_all, q_raw, k_raw, q_rot, kv_rot, squares = kernel_call(
        project_body,
        [
            *in_hbm(
                0, shaped((1024, 256), F32), shaped((1024, 128), F32),
                shaped((1024, 256), BF16), shaped((1024, 256), BF16),
            ),
            shaped((16, 128), F32),
        ],
        [x_blocks, weight, gain_q, gain_k, cosine, sine],
        flops=2 * 1024 * 1024 * 512, nbytes=9 << 20,
    )

    kv_low = swap(kv_rot, LOW_TO_HIGH)
    squares = sum_group(squares)
    squares_low = swap(squares[8:], LOW_TO_HIGH)
    for bit in (1, 2):
        got = lax.ppermute(w_out_rows, "fsdp", [(i, i ^ bit) for i in range(8)])
        upper = fsdp // bit % 2 == 1
        w_out_rows = jnp.concatenate(
            [jnp.where(upper, got, w_out_rows), jnp.where(upper, w_out_rows, got)], axis=0
        )
    kv_low, squares, squares_low, w_wide, w_narrow, w_out_rows = lax.optimization_barrier(
        (kv_low, squares, squares_low, w_wide, w_narrow, w_out_rows)
    )
    w_wide = lax.all_gather(w_wide, "fsdp", axis=0, tiled=True)
    w_out_got = lax.ppermute(w_out_rows, "fsdp", [(i, i ^ 4) for i in range(8)])
    out_raw, mixed, mixed_turned, q_tiles, keys, vals, logs = kernel_call(
        attend_body,
        [
            *in_hbm(
                shaped((1024, 256), F32), shaped((1024, 256), BF16), shaped((256, 1024), BF16),
                shaped((8, 256, 128), BF16), shaped((2048, 128), BF16), shaped((2048, 128), BF16),
            ),
            shaped((8, 256), F32),
        ],
        [place, *in_hbm(q_rot, kv_rot), kv_low, squares, squares_low],
        [pltpu.VMEM((128, 2048), BF16)],
        flops=4 * 1024 * 2048 * 256, nbytes=9 << 20,
    )
    a_mine, a_part, w_out_rows = kernel_call(
        output_body,
        [shaped((512, 1024), F32), shaped((512, 1024), BF16), *in_hbm(shaped((256, 1024), BF16))],
        [place, *in_hbm(mixed), w_out_rows, w_out_got],
        flops=2 * 1024 * 1024 * 256, nbytes=5 << 20,
    )
    n = jnp.arange(1024, dtype=jnp.int32)
    source = ((n // 8) % 16) * 64 + (n // 128) * 8 + n % 8
    order = (n[None, :] == source[:, None]).astype(BF16)
    x_turned = dot_nt(order, x_all).astype(BF16)

    attended = scatter_group(a_mine, a_part)
    attended, x_turned = lax.optimization_barrier((attended, x_turned))
    attn_scale = norm_scale(attended)
    attn_hat = attended * attn_scale
    hidden_state = inputs.astype(F32) + attn_hat * gain_attn
    h_all, gate, up, expanded, m_mine, m_part, w_down_rows = kernel_call(
        expand_body,
        [
            0, shaped((512, 768), F32), shaped((512, 768), F32), shaped((512, 768), BF16),
            shaped((256, 1024), F32), shaped((256, 1024), BF16), shaped((768, 1024), BF16),
        ],
        [
            gather_pair(hidden_state.astype(BF16)), *in_hbm(w_wide, w_narrow),
        ],
        flops=2 * 512 * 2304 * 1024, nbytes=12 << 20,
    )
    projected, _ = scatter_pair(m_mine, m_part)
    mlp_scale = norm_scale(projected)
    mlp_hat = projected * mlp_scale
    output = (hidden_state + mlp_hat * gain_mlp).astype(BF16)[None]

    upstream = out_grad[0].astype(F32)
    grad_gain_mlp = jnp.sum(upstream * mlp_hat, axis=0)
    d_projected = norm_back(upstream * gain_mlp, mlp_hat, mlp_scale).astype(BF16)
    h_turned = dot_nt(order, h_all).astype(BF16)
    d_blocks = gather_pair(d_projected)
    d_blocks[3], h_turned = lax.optimization_barrier((d_blocks[3], h_turned))
    dm_all, d_gu, dh_mine, dh_part = kernel_call(
        expand_back_body,
        [
            0, shaped((512, 1536), BF16), shaped((256, 1024), F32), shaped((256, 1024), BF16),
        ],
        [d_blocks, gate, up, w_wide, w_down_rows],
        flops=2 * 512 * 2304 * 1024, nbytes=12 << 20,
    )

    far = dh_mine[128:] + swap(dh_part[128:], CORE_SWAP).astype(F32)
    far, d_gu, dm_all = lax.optimization_barrier((far.astype(BF16), d_gu, dm_all))
    far = swap(far, Z_SWAP)
    (grad_mlp,) = kernel_call(
        expand_grad_body,
        in_hbm(shaped((1024, 2304), BF16)),
        [h_turned, d_gu, expanded, dm_all],
        [pltpu.VMEM((768, 512), BF16)],
        flops=2 * 512 * 2304 * 1024, nbytes=9 << 20,
    )
    far, grad_mlp = lax.optimization_barrier((far, grad_mlp))
    grad_mlp = lax.psum_scatter(grad_mlp, "fsdp", scatter_dimension=0, tiled=True)
    d_hidden = upstream + dh_mine[:128] + swap(dh_part[:128], CORE_SWAP).astype(F32)
    d_hidden = d_hidden + far.astype(F32)

    grad_gain_attn = jnp.sum(d_hidden * attn_hat, axis=0)
    d_attended = norm_back(d_hidden * gain_attn, attn_hat, attn_scale).astype(BF16)
    d_tiles, deltas, grad_out = kernel_call(
        output_back_body,
        [shaped((8, 256, 128), BF16), shaped((8, 2, 128), F32), shaped((256, 1024), BF16)],
        [place, *in_hbm(out_raw, w_out_rows, gather_group(d_attended), mixed_turned)],
        flops=4 * 1024 * 1024 * 256, nbytes=6 << 20,
    )
    def halve(value, rows, bit, axis, pairs):
        parts = value.reshape(-1, 2, rows, 1024)
        given = jnp.where(bit == 1, parts[:, 0], parts[:, 1])
        mine = jnp.where(bit == 1, parts[:, 1], parts[:, 0]).astype(F32)
        return (mine + lax.ppermute(given, axis, pairs).astype(F32)).astype(BF16)

    grad_out = halve(grad_out, 128, fsdp // 4, "fsdp", [(i, i ^ 4) for i in range(8)])
    dq, dk, dv, d_low, dots = kernel_call(
        attend_back_body,
        [
            *in_hbm(
                shaped((1024, 256), BF16), shaped((1024, 128), F32), shaped((1024, 128), F32),
                shaped((1024, 256), BF16),
            ),
            shaped((24, 128), F32),
        ],
        [place, *in_hbm(q_tiles, keys, vals), logs, d_tiles, deltas],
        [
            pltpu.VMEM((128, 2048), BF16), pltpu.VMEM((2048, 128), F32),
            pltpu.VMEM((2048, 128), F32),
        ],
        flops=10 * 1024 * 2048 * 256, nbytes=8 << 20,
    )
    dots, grad_out = lax.optimization_barrier((dots, grad_out))
    grad_out = halve(grad_out, 32, fsdp % 2, "fsdp", [(i, i ^ 1) for i in range(8)])
    grad_out = halve(grad_out, 32, fsdp // 2 % 2, "fsdp", [(i, i ^ 2) for i in range(8)])
    d_got = swap(d_low, HIGH_TO_LOW)
    dots = sum_group(dots)
    dots_got = swap(dots[16:], HIGH_TO_LOW)

    gains = jnp.concatenate([grad_gain_attn.reshape(128, 8), grad_gain_mlp.reshape(128, 8)], axis=1)
    gains = gains.reshape(16, 8, 16).swapaxes(0, 1).reshape(128, 16)
    gains = jnp.broadcast_to(
        jnp.pad(gains.astype(BF16), ((0, 0), (24, 88)))[:, None, :], (128, 8, 128)
    ).reshape(1024, 128)
    d_made, sent = kernel_call(
        unproject_body,
        [*in_hbm(shaped((1024, 512), BF16)), shaped((1024, 640), BF16)],
        [
            place, *in_hbm(dq, dk, dv), d_got, *in_hbm(q_raw, k_raw), squares, dots, dots_got, cosine, sine,
            gain_q, gain_k, *in_hbm(x_turned), gains,
        ],
        [pltpu.VMEM((8, 384), F32)],
        flops=2 * 1024 * 1024 * 512, nbytes=9 << 20,
    )

    def halves(value, upper):
        low, high = value[: value.shape[0] // 2], value[value.shape[0] // 2 :]
        return jnp.where(upper, high, low), jnp.where(upper, low, high)

    mine, given = halves(grad_mlp, xh == 1)
    mine = mine.astype(F32) + swap(given, X_SWAP).astype(F32)
    sent, grad_out = lax.optimization_barrier((sent, grad_out))
    grad_mlp = after(grad_mlp, sent)
    grad_down = jnp.concatenate(
        [
            piece
            for h in (0, 64)
            for piece in [
                jnp.concatenate(
                    [
                        grad_mlp[h : h + 48, 1536:],
                        jnp.concatenate(
                            [
                                grad_mlp[h + 48 : h + 64, 1536 + m * 256 : 1792 + m * 256]
                                for m in range(3)
                            ],
                            axis=0,
                        ),
                    ],
                    axis=1,
                )
            ]
        ],
        axis=0,
    ).reshape(4, 24, 1024)
    grad_down = sum(
        lax.ppermute(
            lax.dynamic_index_in_dim(grad_down, (xh * 2 + z // 2) ^ other, 0, keepdims=False),
            ("seq", "fsdp"),
            down_home(other),
        ).astype(F32)
        for other in range(4)
    )
    got_made = lax.all_to_all(
        sent.reshape(8, 128, 640), "fsdp", split_axis=0, concat_axis=0, tiled=True
    )
    dx_mine, dx_part = kernel_call(
        input_body,
        in_hbm(shaped((512, 1024), F32), shaped((512, 1024), BF16)),
        [*in_hbm(after(d_made, sent)), weight],
        flops=2 * 1024 * 1024 * 512, nbytes=5 << 20,
    )
    rows = [slice(k * 128, k * 128 + 128) for k in range(4)]
    pieces = [dx_mine[r] + swap(dx_part[r], CORE_SWAP).astype(F32) for r in rows]
    far = [piece.astype(BF16) for piece in pieces[1:]]
    (collected,) = kernel_call(
        collect_body,
        [shaped((128, 2176), BF16)],
        [got_made.reshape(1024, 640), grad_mlp],
        flops=WAIT_FLOPS, nbytes=3 << 20,
    )
    got = lax.all_to_all(
        collected.reshape(16, 8, 2176), "seq", split_axis=0, concat_axis=0, tiled=True
    )
    grad_out = grad_out.reshape(2, 16, 1024)
    own = jnp.where(xh == 1, grad_out[1], grad_out[0])
    given = jnp.where(xh == 1, grad_out[0], grad_out[1])
    own = swap(own, out_home(False))
    grad_out = own.astype(F32) + swap(given, out_home(True)).astype(F32)
    d_inputs = pieces[0] + sum(
        swap(piece, to_z(k)).astype(F32) for k, piece in enumerate(far, 1)
    )
    got = got.reshape(2, 8, 8, 2176).astype(F32)
    summed = got[0, :, :, :640] + got[1, :, :, :640]
    gains = jnp.sum(summed[:, 0, 512:], axis=0)

    def take(first, width):
        return summed[:, :, first : first + width].swapaxes(0, 1).reshape(8, 8 * width)

    wide = jnp.sum(got[:, :, :, 640:].reshape(2, 2, 4, 8, 2, 8, 96), axis=(0, 1))
    wide = wide.transpose(2, 1, 3, 0, 4).reshape(2, 8, 3072)
    return (
        output,
        (d_hidden + d_inputs).astype(BF16)[None],
        take(0, 256),
        take(256, 128),
        take(384, 128),
        grad_out.astype(F32),
        wide[0],
        wide[1],
        grad_down.astype(F32),
        gains[:16],
        gains[16:24],
        gains[24:32],
        gains[32:40],
    )


def solution(mesh):
    rows = P("fsdp", "seq", None)
    weight = P("fsdp", None)
    grad = P(("seq", "fsdp"), None)
    gain = P(("seq", "fsdp"))
    return jax.shard_map(
        on_device,
        mesh=mesh,
        in_specs=(rows,) * 2 + (weight,) * 7 + (P(),) * 4,
        out_specs=(rows,) * 2 + (grad,) * 7 + (gain,) * 4,
        check_vma=False,
    )
```
